32 devices in a mesh: chan: 8 (over z, y), win: 4 (over x, core).
Axes of the slice: x: 2, y: 2, z: 4, core: 2. Of those that a mesh axis runs over, the one named last changes fastest.
Arguments:
- spectra: bfloat16 [8, 2560, 2, 512], P('win', 'chan')
- counts: int32 [8], P('chan'), may hold values from 160 to 320, as said below
- partner: int32 [1, 8], replicated, may hold values from 0 to 7, as said below
Outputs:
- corr: float32 [8, 1, 16, 160, 320], P('chan', None, None, 'win')
The draws below stay inside these ranges and needn't reach their ends.
Inputs may be any that keep to these rules, and one draw needn't show every extreme that they name: `counts`: every block has at least 160 live channels and some block has all 320. partner[q, b] = b XOR t_q for distinct nonzero round numbers t_q, so every round pairs the blocks among themselves.
All inputs are finite; a program needn't handle non-finite values.
Results may differ from the reference program's by a relative error of at most 0.0049.
Values may be sent and summed in bfloat16 or wider, within the bound.
No kernel may reach another device: no remote copies, remote signals or barrier semaphores. Data moves between devices by JAX's collectives and lax.ppermute only.
A program may use at most 64 MiB of HBM per device.

```python
import math
import jax
import jax.numpy as jnp
from jax import lax

CB = 320
FREQS = 512
LAGS = 16
SRC = 160
ROUNDS = 1
WINDOWS = 8
BLOCKS = 8
CHANNELS = 2560


def draw_spectra(key, part):
    key = jax.random.fold_in(key, 11)
    first, second = jax.random.split(key)
    noise = jax.random.normal(first, (WINDOWS, CHANNELS, 2, FREQS), jnp.float32)
    levels = jnp.exp(jax.random.uniform(second, (WINDOWS, CHANNELS, 1, 1), jnp.float32, 0.0, math.log(10.0)))
    return (noise * levels).astype(jnp.bfloat16)


def draw_counts(key, part):
    key = jax.random.fold_in(key, 23)
    first, second = jax.random.split(key)
    drawn = jax.random.randint(first, (BLOCKS,), CB // 2, CB + 1)
    full = jax.random.randint(second, (), 0, BLOCKS)
    return jnp.where(jnp.arange(BLOCKS) == full, CB, drawn).astype(jnp.int32)


def draw_partner(key, part):
    key = jax.random.fold_in(key, 37)
    order = jax.random.permutation(key, BLOCKS - 1) + 1
    picked = order[:ROUNDS].astype(jnp.int32)
    channel_blocks = jnp.arange(BLOCKS, dtype=jnp.int32)
    return jnp.bitwise_xor(channel_blocks[None, :], picked[:, None]).astype(jnp.int32)


def setup_inputs(seed: int = 0) -> dict:
    key_list = jax.random.split(jax.random.key(seed), 4)
    spectra = draw_spectra(jax.random.fold_in(key_list[3], 71), 0)
    counts = draw_counts(jax.random.fold_in(key_list[3], 71), 0)
    partner = draw_partner(jax.random.fold_in(key_list[3], 71), 0)
    return {"spectra": spectra, "counts": counts, "partner": partner}


def spectral_whitening(spectra, counts):
    values = spectra.astype(jnp.float32)
    block_positions = jnp.arange(CHANNELS, dtype=jnp.int32) % CB
    owners = jnp.arange(CHANNELS, dtype=jnp.int32) // CB
    valid = (block_positions < counts[owners]).astype(jnp.float32)
    freq = jnp.arange(FREQS, dtype=jnp.float32)
    taper = 0.75 - 0.25 * jnp.cos(2.0 * math.pi * (freq + 0.5) / FREQS)
    power = lax.optimization_barrier(jnp.mean(values * values, axis=(2, 3)))
    scale = valid[None, :] / jnp.sqrt(power + 1e-05)
    return (values * taper * scale[:, :, None, None]).astype(jnp.bfloat16)

def lag_table():
    freq = jnp.arange(FREQS, dtype=jnp.float32) + FREQS // 4
    delay = jnp.arange(LAGS, dtype=jnp.float32) - LAGS // 2
    phase = 2.0 * math.pi * freq[:, None] * delay[None, :] / (4.0 * FREQS)
    norm = 1.0 / math.sqrt(2.0 * FREQS)
    return jnp.stack([jnp.cos(phase), -jnp.sin(phase)]) * norm

def blended_sources(sources, table):
    src = sources.astype(jnp.float32)
    first = src[:, :, 0][:, :, None, :]
    second = src[:, :, 1][:, :, None, :]
    cos_part = table[0].T[None, None]
    sin_part = table[1].T[None, None]
    real_mix = first * cos_part + second * sin_part
    imag_mix = second * cos_part - first * sin_part
    return jnp.stack([real_mix, imag_mix], axis=3).astype(jnp.bfloat16)

def reference(spectra, counts, partner):
    white = spectral_whitening(spectra, counts).reshape(WINDOWS, BLOCKS, CB, 2, FREQS)
    table = lag_table()
    rounds_out = []
    for step in range(ROUNDS):

        def per_block(block):
            other = partner[step, block]
            receiver_blocks = lax.dynamic_index_in_dim(white, other, 1, keepdims=False)
            mine = lax.dynamic_index_in_dim(white, block, 1, keepdims=False)
            mixed_spectra = blended_sources(mine[:, :SRC], table)
            return jnp.einsum('kidtb,katb->dia', mixed_spectra.astype(jnp.float32), receiver_blocks.astype(jnp.float32))
        rounds_out.append(lax.map(per_block, jnp.arange(BLOCKS, dtype=jnp.int32)))
    return jnp.stack(rounds_out, axis=1) / math.sqrt(WINDOWS)
```

```python
import functools
import math

import jax
import jax.numpy as jnp
import numpy as np
from jax import lax
from jax.experimental import pallas as pl
from jax.experimental.pallas import tpu as pltpu
from jax.sharding import PartitionSpec as P

LAGS = 16
SRC = 160
HALF = LAGS // 2
VMEM_LIMIT = 48 * 1024 * 1024


def from_partner(value, axis, stride):
    return lax.ppermute(value, axis, [(i, i ^ 1 << stride) for i in range(lax.axis_size(axis))])


def whiten_local(spectra, count):
    values = spectra.astype(jnp.float32)
    block_size = spectra.shape[1]
    freqs = spectra.shape[3]
    valid = (jnp.arange(block_size, dtype=jnp.int32) < count).astype(jnp.float32)
    freq = jnp.arange(freqs, dtype=jnp.float32)
    taper = 0.75 - 0.25 * jnp.cos(2.0 * math.pi * (freq + 0.5) / freqs)
    power = jnp.mean(values * values, axis=(2, 3))
    scale = valid[None, :] / jnp.sqrt(power + 1e-05)
    return (values * taper * scale[:, :, None, None]).astype(jnp.bfloat16)


def shift_tables(freqs):
    freq = np.arange(freqs, dtype=np.float64) + freqs // 4
    shift = np.arange(1, HALF + 1, dtype=np.float64)
    phase = 2.0 * np.pi * shift[:, None] * freq[None, :] / (4.0 * freqs)
    rows = lambda v: np.broadcast_to(v.astype(np.float32)[:, None, :], (HALF, 8, freqs)).copy()
    return rows(np.cos(phase)), rows(np.sin(phase))


def mix(m_ref, piece, cos_ref, sin_ref):
    rows, width = piece.shape
    freqs = width // 2
    pad = (-rows) % 16
    for start in range(0, freqs, 128):
        low = slice(start, start + 128)
        high = slice(freqs + start, freqs + start + 128)
        real_raw, imag_raw = piece[:, low], piece[:, high]
        real = real_raw.astype(jnp.float32).reshape(rows // 8, 8, 128)
        imag = imag_raw.astype(jnp.float32).reshape(rows // 8, 8, 128)
        for m in range(1, HALF + 1):
            c, s = cos_ref[m - 1, :, low], sin_ref[m - 1, :, low]
            rc, rs, ic, si = real * c, real * s, imag * c, imag * s
            later = ((rc - si).reshape(rows, 128), (ic + rs).reshape(rows, 128))
            earlier = ((rc + si).reshape(rows, 128), (ic - rs).reshape(rows, 128))
            if m < HALF:
                place = 2 * (m - 1) * rows
                for a, b, cols in zip(later, earlier, (low, high)):
                    both = jnp.concatenate([a, b], axis=0).astype(jnp.bfloat16)
                    m_ref[place:place + 2 * rows, cols] = both
            else:
                place = 14 * rows
                still = (real.reshape(rows, 128), imag.reshape(rows, 128))
                for a, b, cols in zip(still, earlier, (low, high)):
                    both = jnp.concatenate([a, b], axis=0).astype(jnp.bfloat16)
                    m_ref[place:place + 2 * rows, cols] = both
                place = 16 * rows
                fill = jnp.zeros((pad, 128), jnp.float32)
                for a, cols in zip(later, (low, high)):
                    last = jnp.concatenate([a, fill], axis=0) if pad else a
                    m_ref[place:place + rows + pad, cols] = last.astype(jnp.bfloat16)


def terms_kernel(final, scale, x_ref, lhs_ref, recv_ref, cos_ref, sin_ref, *refs):
    if final:
        part_ref, back_keep, back_send, own_keep, own_send, m_ref, acc_ref = refs
    else:
        acc_ref, m_ref = refs
    step = pl.program_id(0)
    x = x_ref[0]
    rows = recv_ref.shape[2]
    lhs = lhs_ref[0]
    for place in range(2):
        q = x if place == 0 else 1 - x
        mix(m_ref.at[place], recv_ref[0, q], cos_ref, sin_ref)
        term = lax.dot_general(
            lhs, m_ref[place], (((1,), (1,)), ((), ())), preferred_element_type=jnp.float32
        )

        @pl.when(step == 0)
        def _():
            if final:
                acc_ref[place] = part_ref[place] + term
            else:
                acc_ref[place] = term

        @pl.when(step > 0)
        def _():
            acc_ref[place] += term

    if final:

        @pl.when(step == pl.num_programs(0) - 1)
        def _():
            half = SRC // 2
            wide = LAGS * rows
            back_keep[...] = acc_ref[0, SRC:, :wide] * scale
            back_send[...] = (acc_ref[1, SRC:, :wide] * scale).astype(jnp.bfloat16)
            for place in range(2):
                q = x if place == 0 else 1 - x
                for group, out in ((x, own_keep), (1 - x, own_send)):
                    line = pl.ds(pl.multiple_of(group * half, 16), half)
                    mine = acc_ref[place, line, :]
                    value = jnp.concatenate(
                        [mine[:, :wide - rows], mine[:, wide:wide + rows]], axis=1
                    )
                    out[q] = (value * scale).astype(out.dtype)


def terms(x, lhs, recv, part, scale):
    windows, channels, width = lhs.shape
    _, groups, rows, _ = recv.shape
    freqs = width // 2
    cos, sin = shift_tables(freqs)
    columns = LAGS * rows + rows + (-rows) % 16
    final = part is not None
    table_spec = pl.BlockSpec((HALF, 8, freqs), lambda w, s: (0, 0, 0))
    part_spec = pl.BlockSpec((2, channels, columns), lambda w, s: (0, 0, 0))
    in_specs = [
        pl.BlockSpec((1, channels, width), lambda w, s: (w, 0, 0)),
        pl.BlockSpec((1, groups, rows, width), lambda w, s: (w, 0, 0, 0)),
        table_spec,
        table_spec,
    ]
    operands = [lhs, recv, jnp.asarray(cos), jnp.asarray(sin)]
    mixed = pltpu.VMEM((2, columns, width), jnp.bfloat16)
    wide = LAGS * rows
    if final:
        in_specs.append(part_spec)
        operands.append(part)
        whole2 = lambda w, s: (0, 0)
        whole3 = lambda w, s: (0, 0, 0)
        out_specs = [
            pl.BlockSpec((channels - SRC, wide), whole2),
            pl.BlockSpec((channels - SRC, wide), whole2),
            pl.BlockSpec((2, SRC // 2, wide), whole3),
            pl.BlockSpec((2, SRC // 2, wide), whole3),
        ]
        out_shape = [
            jax.ShapeDtypeStruct((channels - SRC, wide), jnp.float32),
            jax.ShapeDtypeStruct((channels - SRC, wide), jnp.bfloat16),
            jax.ShapeDtypeStruct((2, SRC // 2, wide), jnp.float32),
            jax.ShapeDtypeStruct((2, SRC // 2, wide), jnp.bfloat16),
        ]
        scratch = [mixed, pltpu.VMEM((2, channels, columns), jnp.float32)]
    else:
        out_specs = part_spec
        out_shape = jax.ShapeDtypeStruct((2, channels, columns), jnp.float32)
        scratch = [mixed]
    return pl.pallas_call(
        functools.partial(terms_kernel, final, scale),
        grid_spec=pltpu.PrefetchScalarGridSpec(
            num_scalar_prefetch=1,
            grid=(windows,),
            in_specs=in_specs,
            out_specs=out_specs,
            scratch_shapes=scratch,
        ),
        out_shape=out_shape,
        compiler_params=pltpu.CompilerParams(vmem_limit_bytes=VMEM_LIMIT),
        cost_estimate=pl.CostEstimate(
            flops=2 * windows * channels * 2 * columns * width,
            bytes_accessed=2 * (lhs.size + recv.size) + 8 * channels * columns,
            transcendentals=0,
        ),
        name="terms_final" if final else "terms_first",
    )(x, *operands)


def place_kernel(core_ref, own_ref, other_ref, back_ref, out_ref):
    lags, mine, channels = out_ref.shape
    own = own_ref[...].astype(jnp.float32)
    other = other_ref[...].astype(jnp.float32)
    swap = core_ref[0] != 0
    first = jnp.where(swap, other, own)
    second = jnp.where(swap, own, other)
    back = back_ref[...].astype(jnp.float32).T
    for j in range(lags):
        if j == lags - 2:
            lag = HALF
        elif j == lags - 1:
            lag = 0
        else:
            lag = HALF + (j // 2 + 1) * (-1 if j % 2 else 1)
        cols = slice(j * mine, (j + 1) * mine)
        reverse = 2 * HALF - lag if j < lags - 1 else 0
        near = jnp.concatenate(
            [first[0, :, cols], second[0, :, cols], first[1, :, cols], second[1, :, cols]],
            axis=1,
        )
        out_ref[reverse, :, :4 * mine] = near
        out_ref[lag, :, 4 * mine:] = back[j * mine:(j + 1) * mine, :]


def place(core, own, other, back):
    groups, mine, wide = own.shape
    lags = wide // mine
    channels = SRC + back.shape[0]
    vmem = pl.BlockSpec(memory_space=pltpu.VMEM)
    return pl.pallas_call(
        place_kernel,
        in_specs=[pl.BlockSpec(memory_space=pltpu.SMEM), vmem, vmem, vmem],
        out_specs=vmem,
        out_shape=jax.ShapeDtypeStruct((lags, mine, channels), jnp.float32),
        compiler_params=pltpu.CompilerParams(vmem_limit_bytes=VMEM_LIMIT),
        name="place_lags",
    )(core, own, other, back)


def pair_body(spectra, counts, partner):
    blocks = lax.axis_size("chan")
    groups = lax.axis_size("win")
    windows, channels, two, freqs = spectra.shape
    scale = 1.0 / (math.sqrt(2.0 * freqs) * math.sqrt(windows * groups))
    mine = SRC // groups
    spot = lax.axis_index("win")
    x, core = spot // 2, spot % 2
    x_arg = x.astype(jnp.int32)[None]
    core_arg = core.astype(jnp.int32)[None]

    white = whiten_local(spectra, counts[0]).reshape(windows, channels, two * freqs)
    sources = white[:, :SRC].reshape(windows, groups // 2, 2, mine, two * freqs)
    straight = lax.dynamic_index_in_dim(sources, core, 2, keepdims=False)
    crossed = lax.dynamic_index_in_dim(sources, 1 - core, 2, keepdims=False)

    other_core = [(i, i ^ 1) for i in range(groups)]
    other_chip = [(i, i ^ 2) for i in range(groups)]

    def for_round(t):
        to_partner = [(i, i ^ t) for i in range(blocks)]
        to_partner_core = [
            (i * groups + g, (i ^ t) * groups + (g ^ 1))
            for i in range(blocks)
            for g in range(groups)
        ]

        def run(white, straight, crossed):
            recv1 = lax.ppermute(straight, "chan", to_partner)
            recv2 = lax.ppermute(crossed, ("chan", "win"), to_partner_core)
            sibling = lax.ppermute(white, "win", other_core)
            part = terms(x_arg, white, recv1, None, scale)
            back_keep, back_send, own_keep, own_send = terms(x_arg, sibling, recv2, part, scale)
            back_recv = lax.ppermute(back_send, "win", other_chip)
            own_recv = lax.ppermute(own_send, "win", other_chip)
            back = (back_keep + back_recv.astype(jnp.float32)).astype(jnp.bfloat16)
            back = lax.ppermute(back, "chan", to_partner)
            own = own_keep + own_recv.astype(jnp.float32)
            own = own.reshape(2, 2, mine, LAGS * mine)
            here = lax.dynamic_index_in_dim(own, core, 1, keepdims=False)
            away = lax.dynamic_index_in_dim(own, 1 - core, 1, keepdims=False)
            other = lax.ppermute(away.astype(jnp.bfloat16), "win", other_core)
            return place(core_arg, here, other, back)

        return run

    rounds = partner[0, 0]
    out = lax.switch(rounds - 1, [for_round(t) for t in range(1, blocks)], white, straight, crossed)
    return out[None, None]


def lag_table(freqs, lags):
    freq = jnp.arange(freqs, dtype=jnp.float32) + freqs // 4
    delay = jnp.arange(lags, dtype=jnp.float32) - lags // 2
    phase = 2.0 * math.pi * freq[:, None] * delay[None, :] / (4.0 * freqs)
    norm = 1.0 / math.sqrt(2.0 * freqs)
    return jnp.stack([jnp.cos(phase), -jnp.sin(phase)]) * norm


def blended_sources(sources, table):
    src = sources.astype(jnp.float32)
    first = src[:, :, 0][:, :, None, :]
    second = src[:, :, 1][:, :, None, :]
    cos_part = table[0].T[None, None]
    sin_part = table[1].T[None, None]
    real_mix = first * cos_part + second * sin_part
    imag_mix = second * cos_part - first * sin_part
    return jnp.stack([real_mix, imag_mix], axis=3).astype(jnp.bfloat16)


def pair_terms(sources, receiver_blocks, table):
    wins, count, two, freqs = sources.shape
    lags = table.shape[2]
    group = math.gcd(count, 32)
    flat_recv = receiver_blocks.reshape(wins, receiver_blocks.shape[1], two * freqs)
    grouped = jnp.moveaxis(sources.reshape(wins, count // group, group, two, freqs), 1, 0)

    def one_group(piece):
        mixed_spectra = blended_sources(piece, table).reshape(wins, group * lags, two * freqs)
        out = jnp.einsum(
            "wmx,wrx->mr", mixed_spectra, flat_recv, preferred_element_type=jnp.float32
        )
        return out.reshape(group, lags, receiver_blocks.shape[1])

    out = lax.map(one_group, grouped).reshape(count, lags, receiver_blocks.shape[1])
    return jnp.transpose(out, (1, 0, 2))


def route_blocks(values, round_flags, levels):
    for level in range(levels):
        moved = from_partner(values, "chan", level)
        values = jnp.where((round_flags >> level) % 2 == 1, moved, values)
    return values


def general_body(spectra, counts, partner):
    white = whiten_local(spectra, counts[0])
    table = lag_table(spectra.shape[3], LAGS)
    levels = lax.axis_size("chan").bit_length() - 1
    windows = spectra.shape[0] * lax.axis_size("win")
    receiver_blocks = route_blocks(white, partner[0, 0], levels)
    out = pair_terms(white[:, :SRC], receiver_blocks, table)
    stacked = lax.psum_scatter(out, "win", scatter_dimension=1, tiled=True)
    return (stacked / math.sqrt(windows))[None, None]


def solution(mesh):
    body = pair_body if mesh.shape["win"] == 4 else general_body
    return jax.shard_map(
        body,
        mesh=mesh,
        in_specs=(P("win", "chan", None, None), P("chan"), P()),
        out_specs=P("chan", None, None, "win", None),
        check_vma=False,
    )
```

```python
import functools
import math

import jax
import jax.numpy as jnp
import numpy as np
from jax import lax
from jax.experimental import pallas as pl
from jax.experimental.pallas import tpu as pltpu
from jax.sharding import PartitionSpec as P

LAGS = 16
SRC = 160
HALF = LAGS // 2
VMEM_LIMIT = 48 * 1024 * 1024


def from_partner(value, axis, stride):
    return lax.ppermute(value, axis, [(i, i ^ 1 << stride) for i in range(lax.axis_size(axis))])


def whiten_local(spectra, count):
    values = spectra.astype(jnp.float32)
    block_size = spectra.shape[1]
    freqs = spectra.shape[3]
    valid = (jnp.arange(block_size, dtype=jnp.int32) < count).astype(jnp.float32)
    freq = jnp.arange(freqs, dtype=jnp.float32)
    taper = 0.75 - 0.25 * jnp.cos(2.0 * math.pi * (freq + 0.5) / freqs)
    power = jnp.mean(values * values, axis=(2, 3))
    scale = valid[None, :] / jnp.sqrt(power + 1e-05)
    return (values * taper * scale[:, :, None, None]).astype(jnp.bfloat16)


def shift_tables(freqs):
    freq = np.arange(freqs, dtype=np.float64) + freqs // 4
    shift = np.arange(1, HALF + 1, dtype=np.float64)
    phase = 2.0 * np.pi * shift[:, None] * freq[None, :] / (4.0 * freqs)
    rows = lambda v: np.broadcast_to(v.astype(np.float32)[:, None, :], (HALF, 8, freqs)).copy()
    return rows(np.cos(phase)), rows(np.sin(phase))


def place_of_core():
    spot = lax.axis_index("win")
    return spot // 2, spot % 2


def whole():
    return pl.BlockSpec(memory_space=pltpu.VMEM)


def kernel_params():
    return pltpu.CompilerParams(vmem_limit_bytes=VMEM_LIMIT)


def whiten_kernel(count_ref, raw_ref, taper_ref, white_ref, *piece_refs):
    _, core = place_of_core()
    windows, channels, width = raw_ref.shape
    step = SRC // 2
    mine = step // 2
    for w in range(windows):
        for start in range(0, channels, step):
            block = slice(start, start + step)
            values = raw_ref[w, block, :].astype(jnp.float32)
            power = jnp.sum(values * values, axis=1, keepdims=True) * (1.0 / width)
            row = start + lax.broadcasted_iota(jnp.int32, (step, 1), 0)
            valid = (row < count_ref[0]).astype(jnp.float32)
            scale = valid / jnp.sqrt(power + 1e-05)
            values = values * taper_ref[...] * scale
            white_ref[w, block, :] = values.astype(jnp.bfloat16)
            if start < SRC:
                low, high = values[:mine], values[mine:]
                first = core == 0
                near = jnp.where(first, low, high)
                far = jnp.where(first, high, low)
                place = 0
                for i in range(0, len(piece_refs), 2):
                    rows = piece_refs[i].shape[2]
                    part = slice(place, place + rows)
                    piece_refs[i][w, start // step] = near[part].astype(jnp.bfloat16)
                    piece_refs[i + 1][w, start // step] = far[part].astype(jnp.bfloat16)
                    place += rows


def whiten(spectra, counts, chunks):
    windows, channels, two, freqs = spectra.shape
    width = two * freqs
    freq = np.arange(freqs, dtype=np.float64)
    taper = 0.75 - 0.25 * np.cos(2.0 * np.pi * (freq + 0.5) / freqs)
    taper = np.tile(taper.astype(np.float32), two)[None, :]
    out_shape = [jax.ShapeDtypeStruct((windows, channels, width), jnp.bfloat16)]
    for rows in chunks:
        out_shape += [jax.ShapeDtypeStruct((windows, 2, rows, width), jnp.bfloat16)] * 2
    return pl.pallas_call(
        whiten_kernel,
        in_specs=[pl.BlockSpec(memory_space=pltpu.SMEM), whole(), whole()],
        out_specs=[whole()] * len(out_shape),
        out_shape=out_shape,
        compiler_params=kernel_params(),
        name="whiten",
    )(counts, spectra.reshape(windows, channels, width), jnp.asarray(taper))


def mix(m_ref, base, extra, piece, cos_ref, sin_ref):
    rows, width = piece.shape
    freqs = width // 2
    for start in range(0, freqs, 128):
        low = slice(start, start + 128)
        high = slice(freqs + start, freqs + start + 128)
        real_raw, imag_raw = piece[:, low], piece[:, high]
        real = real_raw.astype(jnp.float32).reshape(rows // 8, 8, 128)
        imag = imag_raw.astype(jnp.float32).reshape(rows // 8, 8, 128)
        for m in range(1, HALF + 1):
            c, s = cos_ref[m - 1, :, low], sin_ref[m - 1, :, low]
            rc, rs, ic, si = real * c, real * s, imag * c, imag * s
            later = (rc - si, ic + rs)
            earlier = (rc + si, ic - rs)
            first = later if m < HALF else (real, imag)
            row = base + 2 * (m - 1) * rows
            for a, b, cols in zip(first, earlier, (low, high)):
                both = jnp.concatenate([a, b], axis=0).reshape(2 * rows, 128)
                m_ref[row:row + 2 * rows, cols] = both.astype(jnp.bfloat16)
            if m == HALF:
                for a, cols in zip(later, (low, high)):
                    m_ref[extra:extra + rows, cols] = a.reshape(rows, 128).astype(jnp.bfloat16)


def times(lhs, rhs):
    return lax.dot_general(
        lhs, rhs, (((1,), (1,)), ((), ())), preferred_element_type=jnp.float32
    )


def terms_kernel(
    scale, near_ref, far_ref, near_recv, far_recv, cos_ref, sin_ref,
    back_keep, back_send, own_keep, own_send, m_ref, main_ref, extra_ref,
):
    x, core = place_of_core()
    rows = near_recv.shape[2]
    wide = LAGS * rows
    step = 0
    for lhs_ref, recv_ref in ((near_ref, near_recv), (far_ref, far_recv)):
        for w in range(lhs_ref.shape[0]):
            mixed = m_ref.at[step % 2]
            for place in range(2):
                q = x if place == 0 else 1 - x
                base, extra = place * wide, 2 * wide + place * rows
                mix(mixed, base, extra, recv_ref[w, q], cos_ref, sin_ref)
            main = times(lhs_ref[w], mixed[:2 * wide])
            last = times(lhs_ref[w, :SRC], mixed[2 * wide:])
            if step == 0:
                main_ref[...] = main
                extra_ref[...] = last
            else:
                main_ref[...] += main
                extra_ref[...] += last
            step += 1

    back_keep[...] = main_ref[SRC:, :wide] * scale
    back_send[...] = (main_ref[SRC:, wide:] * scale).astype(jnp.bfloat16)
    mine = SRC // 4
    for place in range(2):
        q = x if place == 0 else 1 - x
        for group, out in ((x, own_keep), (1 - x, own_send)):
            for side in range(2):
                spot = core if side == 0 else 1 - core
                line = pl.ds(pl.multiple_of((2 * group + spot) * mine, 8), mine)
                front = main_ref[line, place * wide:(place + 1) * wide]
                last = extra_ref[line, place * rows:(place + 1) * rows]
                value = jnp.concatenate([front[:, :wide - rows], last], axis=1)
                out[side, q] = (value * scale).astype(out.dtype)


def terms(near, far, near_recv, far_recv, scale):
    windows, channels, width = near.shape
    rows = near_recv.shape[2]
    wide = LAGS * rows
    cos, sin = shift_tables(width // 2)
    mine = SRC // 4
    return pl.pallas_call(
        functools.partial(terms_kernel, scale),
        in_specs=[whole()] * 6,
        out_specs=[whole()] * 4,
        out_shape=[
            jax.ShapeDtypeStruct((channels - SRC, wide), jnp.float32),
            jax.ShapeDtypeStruct((channels - SRC, wide), jnp.bfloat16),
            jax.ShapeDtypeStruct((2, 2, mine, wide), jnp.float32),
            jax.ShapeDtypeStruct((2, 2, mine, wide), jnp.bfloat16),
        ],
        scratch_shapes=[
            pltpu.VMEM((2, 2 * wide + 2 * rows, width), jnp.bfloat16),
            pltpu.VMEM((channels, 2 * wide), jnp.float32),
            pltpu.VMEM((SRC, 2 * rows), jnp.float32),
        ],
        compiler_params=kernel_params(),
        cost_estimate=pl.CostEstimate(
            flops=2 * 2 * windows * channels * 2 * wide * width,
            bytes_accessed=4 * (near.size + near_recv.size),
            transcendentals=0,
        ),
        name="terms",
    )(near, far, near_recv, far_recv, jnp.asarray(cos), jnp.asarray(sin))


def after_kernel(*refs):
    del refs


def after(done, values):
    count = len(values)
    anywhere = pl.BlockSpec(memory_space=pl.ANY)
    return pl.pallas_call(
        after_kernel,
        in_specs=[anywhere] * (count + len(done)),
        out_specs=[anywhere] * count,
        out_shape=[jax.ShapeDtypeStruct(v.shape, v.dtype) for v in values],
        input_output_aliases={i: i for i in range(count)},
        name="after",
    )(*values, *done)


def place_kernel(chunks, *refs):
    out_ref = refs[-1]
    _, core = place_of_core()
    lags, mine, channels = out_ref.shape
    swap = core != 0
    sides, backs = [], []
    for i in range(len(chunks)):
        own = refs[3 * i][...].astype(jnp.float32)
        other = refs[3 * i + 1][...].astype(jnp.float32)
        sides.append((jnp.where(swap, other, own), jnp.where(swap, own, other)))
        backs.append(refs[3 * i + 2][...].astype(jnp.float32).T)
    for j in range(lags):
        if j == lags - 2:
            lag = HALF
        elif j == lags - 1:
            lag = 0
        else:
            lag = HALF + (j // 2 + 1) * (-1 if j % 2 else 1)
        reverse = 2 * HALF - lag if j < lags - 1 else 0
        near = []
        for q in range(2):
            for side in range(2):
                for i, rows in enumerate(chunks):
                    near.append(sides[i][side][q, :, j * rows:(j + 1) * rows])
        out_ref[reverse, :, :SRC] = jnp.concatenate(near, axis=1)
        far = [backs[i][j * rows:(j + 1) * rows] for i, rows in enumerate(chunks)]
        out_ref[lag, :, SRC:] = jnp.concatenate(far, axis=0)


def place(chunks, parts, channels):
    mine = sum(chunks)
    return pl.pallas_call(
        functools.partial(place_kernel, chunks),
        in_specs=[whole()] * len(parts),
        out_specs=whole(),
        out_shape=jax.ShapeDtypeStruct((LAGS, mine, channels), jnp.float32),
        compiler_params=kernel_params(),
        name="place_lags",
    )(*parts)


def pair_body(spectra, counts, partner):
    blocks = lax.axis_size("chan")
    groups = lax.axis_size("win")
    windows, channels, two, freqs = spectra.shape
    scale = 1.0 / (math.sqrt(2.0 * freqs) * math.sqrt(windows * groups))
    chunks = (24, 16)

    white, *pieces = whiten(spectra, counts, chunks)
    other_core = [(i, i ^ 1) for i in range(groups)]
    other_chip = [(i, i ^ 2) for i in range(groups)]

    def for_round(t):
        to_partner = [(i, i ^ t) for i in range(blocks)]
        to_partner_core = [
            (i * groups + g, (i ^ t) * groups + (g ^ 1))
            for i in range(blocks)
            for g in range(groups)
        ]

        def run(white, *pieces):
            arrived = []
            for i in range(len(chunks)):
                straight, crossed = pieces[2 * i:2 * i + 2]
                if i:
                    straight, crossed = after(arrived[-1], (straight, crossed))
                straight = lax.ppermute(straight, "chan", to_partner)
                crossed = lax.ppermute(crossed, ("chan", "win"), to_partner_core)
                arrived.append((straight, crossed))
                if i == 0:
                    sibling = lax.ppermute(white, "win", other_core)
            parts = []
            for recv in arrived:
                back_keep, back_send, own_keep, own_send = terms(white, sibling, *recv, scale)
                back_recv = lax.ppermute(back_send, "win", other_chip)
                back = (back_keep + back_recv.astype(jnp.float32)).astype(jnp.bfloat16)
                back = lax.ppermute(back, "chan", to_partner)
                own_recv = lax.ppermute(own_send, "win", other_chip).astype(jnp.float32)
                here = own_keep[0] + own_recv[0]
                away = (own_keep[1] + own_recv[1]).astype(jnp.bfloat16)
                other = lax.ppermute(away, "win", other_core)
                parts += [here, other, back]
            return place(chunks, parts, channels)

        return run

    rounds = partner[0, 0]
    out = lax.switch(rounds - 1, [for_round(t) for t in range(1, blocks)], white, *pieces)
    return out[None, None]


def lag_table(freqs, lags):
    freq = jnp.arange(freqs, dtype=jnp.float32) + freqs // 4
    delay = jnp.arange(lags, dtype=jnp.float32) - lags // 2
    phase = 2.0 * math.pi * freq[:, None] * delay[None, :] / (4.0 * freqs)
    norm = 1.0 / math.sqrt(2.0 * freqs)
    return jnp.stack([jnp.cos(phase), -jnp.sin(phase)]) * norm


def blended_sources(sources, table):
    src = sources.astype(jnp.float32)
    first = src[:, :, 0][:, :, None, :]
    second = src[:, :, 1][:, :, None, :]
    cos_part = table[0].T[None, None]
    sin_part = table[1].T[None, None]
    real_mix = first * cos_part + second * sin_part
    imag_mix = second * cos_part - first * sin_part
    return jnp.stack([real_mix, imag_mix], axis=3).astype(jnp.bfloat16)


def pair_terms(sources, receiver_blocks, table):
    wins, count, two, freqs = sources.shape
    lags = table.shape[2]
    group = math.gcd(count, 32)
    flat_recv = receiver_blocks.reshape(wins, receiver_blocks.shape[1], two * freqs)
    grouped = jnp.moveaxis(sources.reshape(wins, count // group, group, two, freqs), 1, 0)

    def one_group(piece):
        mixed_spectra = blended_sources(piece, table).reshape(wins, group * lags, two * freqs)
        out = jnp.einsum(
            "wmx,wrx->mr", mixed_spectra, flat_recv, preferred_element_type=jnp.float32
        )
        return out.reshape(group, lags, receiver_blocks.shape[1])

    out = lax.map(one_group, grouped).reshape(count, lags, receiver_blocks.shape[1])
    return jnp.transpose(out, (1, 0, 2))


def route_blocks(values, round_flags, levels):
    for level in range(levels):
        moved = from_partner(values, "chan", level)
        values = jnp.where((round_flags >> level) % 2 == 1, moved, values)
    return values


def general_body(spectra, counts, partner):
    white = whiten_local(spectra, counts[0])
    table = lag_table(spectra.shape[3], LAGS)
    levels = lax.axis_size("chan").bit_length() - 1
    windows = spectra.shape[0] * lax.axis_size("win")
    receiver_blocks = route_blocks(white, partner[0, 0], levels)
    out = pair_terms(white[:, :SRC], receiver_blocks, table)
    stacked = lax.psum_scatter(out, "win", scatter_dimension=1, tiled=True)
    return (stacked / math.sqrt(windows))[None, None]


def solution(mesh):
    body = pair_body if mesh.shape["win"] == 4 else general_body
    return jax.shard_map(
        body,
        mesh=mesh,
        in_specs=(P("win", "chan", None, None), P("chan"), P()),
        out_specs=P("chan", None, None, "win", None),
        check_vma=False,
    )
```

```python
import functools
import math

import jax
import jax.numpy as jnp
import numpy as np
from jax import lax
from jax.experimental import pallas as pl
from jax.experimental.pallas import tpu as pltpu
from jax.sharding import PartitionSpec as P

LAGS = 16
SRC = 160
HALF = LAGS // 2
VMEM_LIMIT = 48 * 1024 * 1024


def from_partner(value, axis, stride):
    return lax.ppermute(value, axis, [(i, i ^ 1 << stride) for i in range(lax.axis_size(axis))])


def whiten_local(spectra, count):
    values = spectra.astype(jnp.float32)
    block_size = spectra.shape[1]
    freqs = spectra.shape[3]
    valid = (jnp.arange(block_size, dtype=jnp.int32) < count).astype(jnp.float32)
    freq = jnp.arange(freqs, dtype=jnp.float32)
    taper = 0.75 - 0.25 * jnp.cos(2.0 * math.pi * (freq + 0.5) / freqs)
    power = jnp.mean(values * values, axis=(2, 3))
    scale = valid[None, :] / jnp.sqrt(power + 1e-05)
    return (values * taper * scale[:, :, None, None]).astype(jnp.bfloat16)


def shift_tables(freqs):
    freq = np.arange(freqs, dtype=np.float64) + freqs // 4
    shift = np.arange(1, HALF + 1, dtype=np.float64)
    phase = 2.0 * np.pi * shift[:, None] * freq[None, :] / (4.0 * freqs)
    return np.cos(phase).astype(np.float32), np.sin(phase).astype(np.float32)


def place_of_core():
    spot = lax.axis_index("win")
    return spot // 2, spot % 2


def whole():
    return pl.BlockSpec(memory_space=pltpu.VMEM)


def kernel_params():
    return pltpu.CompilerParams(vmem_limit_bytes=VMEM_LIMIT)


def whiten_kernel(count_ref, raw_ref, taper_ref, white_ref, *piece_refs):
    _, core = place_of_core()
    windows, channels, width = raw_ref.shape
    step = SRC // 2
    mine = step // 2
    for w in range(windows):
        for start in range(0, channels, step):
            block = slice(start, start + step)
            values = raw_ref[w, block, :].astype(jnp.float32)
            power = jnp.sum(values * values, axis=1, keepdims=True) * (1.0 / width)
            row = start + lax.broadcasted_iota(jnp.int32, (step, 1), 0)
            valid = (row < count_ref[0]).astype(jnp.float32)
            scale = valid / jnp.sqrt(power + 1e-05)
            values = values * taper_ref[...] * scale
            white_ref[w, block, :] = values.astype(jnp.bfloat16)
            if start < SRC:
                low, high = values[:mine], values[mine:]
                first = core == 0
                near = jnp.where(first, low, high)
                far = jnp.where(first, high, low)
                place = 0
                for i in range(0, len(piece_refs), 2):
                    rows = piece_refs[i].shape[2]
                    part = slice(place, place + rows)
                    piece_refs[i][w, start // step] = near[part].astype(jnp.bfloat16)
                    piece_refs[i + 1][w, start // step] = far[part].astype(jnp.bfloat16)
                    place += rows


def keep_kernel(*refs):
    del refs


def keep(values):
    return pl.pallas_call(
        keep_kernel,
        in_specs=[whole()] * len(values),
        out_specs=[whole()] * len(values),
        out_shape=[jax.ShapeDtypeStruct(v.shape, v.dtype) for v in values],
        input_output_aliases={i: i for i in range(len(values))},
        compiler_params=kernel_params(),
        name="keep",
    )(*values)


def whiten(spectra, counts, chunks):
    windows, channels, two, freqs = spectra.shape
    width = two * freqs
    freq = np.arange(freqs, dtype=np.float64)
    taper = 0.75 - 0.25 * np.cos(2.0 * np.pi * (freq + 0.5) / freqs)
    taper = np.tile(taper.astype(np.float32), two)[None, :]
    out_shape = [jax.ShapeDtypeStruct((windows, channels, width), jnp.bfloat16)]
    for rows in chunks:
        out_shape += [jax.ShapeDtypeStruct((windows, 2, rows, width), jnp.bfloat16)] * 2
    tables = [jnp.asarray(v) for v in shift_tables(freqs)]
    spectra, taper, count, *tables = keep(
        [spectra, jnp.asarray(taper), counts.reshape(1, 1), *tables]
    )
    pieces = pl.pallas_call(
        whiten_kernel,
        in_specs=[whole()] * 3,
        out_specs=[whole()] * len(out_shape),
        out_shape=out_shape,
        compiler_params=kernel_params(),
        name="whiten",
    )(count, spectra.reshape(windows, channels, width), taper)
    return tables, pieces


def mix(m_ref, base, extra, piece, cos_ref, sin_ref, low, high):
    real, imag = (piece[:, cols].astype(jnp.float32) for cols in (low, high))
    rows = real.shape[0]
    fill = jnp.zeros(((-rows) % 16, 128), jnp.float32)

    def put(row, values, cols):
        line = pl.ds(pl.multiple_of(row, 16), sum(v.shape[0] for v in values))
        m_ref[line, cols] = jnp.concatenate(values, axis=0).astype(jnp.bfloat16)

    for m in range(1, HALF + 1):
        c, s = cos_ref[m - 1:m, low], sin_ref[m - 1:m, low]
        rc, rs, ic, si = real * c, real * s, imag * c, imag * s
        later = (rc - si, ic + rs)
        earlier = (rc + si, ic - rs)
        first = later if m < HALF else (real, imag)
        for a, b, cols in zip(first, earlier, (low, high)):
            put(base + 2 * (m - 1) * rows, [a, b], cols)
        if m == HALF:
            for a, cols in zip(later, (low, high)):
                put(extra, [a, fill] if fill.shape[0] else [a], cols)


def times(lhs, rhs):
    return lax.dot_general(
        lhs, rhs, (((1,), (1,)), ((), ())), preferred_element_type=jnp.float32
    )


def terms_kernel(
    scale, near_ref, far_ref, near_recv, far_recv, cos_ref, sin_ref,
    back_keep, back_send, own_keep, own_send, m_ref, main_ref, extra_ref,
):
    x, core = place_of_core()
    windows, _, rows, width = near_recv.shape
    freqs = width // 2
    wide = LAGS * rows
    stride = rows + (-rows) % 16
    tile = 256
    main_ref[...] = jnp.zeros_like(main_ref)
    extra_ref[...] = jnp.zeros_like(extra_ref)
    for lhs_ref, recv_ref in ((near_ref, near_recv), (far_ref, far_recv)):

        @pl.loop(0, windows)
        def _(w):
            @pl.loop(0, 2 * (freqs // 128))
            def _(i):
                place, start = i // (freqs // 128), i % (freqs // 128) * 128
                q = jnp.where(place == 0, x, 1 - x)
                low = pl.ds(pl.multiple_of(start, 128), 128)
                high = pl.ds(pl.multiple_of(freqs + start, 128), 128)
                base, extra = place * wide, 2 * wide + place * stride
                mix(m_ref, base, extra, recv_ref.at[w, q], cos_ref, sin_ref, low, high)

            @pl.loop(0, 2 * wide // tile)
            def _(n):
                line = pl.ds(pl.multiple_of(n * tile, tile), tile)
                main_ref[:, line] += times(lhs_ref[w], m_ref[line, :])

            extra_ref[...] += times(lhs_ref[w, :SRC], m_ref[2 * wide:, :])

    back_keep[...] = main_ref[SRC:, :wide] * scale
    back_send[...] = (main_ref[SRC:, wide:] * scale).astype(jnp.bfloat16)
    mine = SRC // 4
    for place in range(2):
        q = x if place == 0 else 1 - x
        for group, out in ((x, own_keep), (1 - x, own_send)):
            for side in range(2):
                spot = core if side == 0 else 1 - core
                line = pl.ds(pl.multiple_of((2 * group + spot) * mine, 8), mine)
                front = main_ref[line, place * wide:(place + 1) * wide]
                last = extra_ref[line, place * stride:place * stride + rows]
                value = jnp.concatenate([front[:, :wide - rows], last], axis=1)
                out[side, q] = (value * scale).astype(out.dtype)


def terms(near, far, near_recv, far_recv, tables, scale):
    windows, channels, width = near.shape
    rows = near_recv.shape[2]
    wide = LAGS * rows
    stride = rows + (-rows) % 16
    mine = SRC // 4
    return pl.pallas_call(
        functools.partial(terms_kernel, scale),
        in_specs=[whole()] * 6,
        out_specs=[whole()] * 4,
        out_shape=[
            jax.ShapeDtypeStruct((channels - SRC, wide), jnp.float32),
            jax.ShapeDtypeStruct((channels - SRC, wide), jnp.bfloat16),
            jax.ShapeDtypeStruct((2, 2, mine, wide), jnp.float32),
            jax.ShapeDtypeStruct((2, 2, mine, wide), jnp.bfloat16),
        ],
        scratch_shapes=[
            pltpu.VMEM((2 * wide + 2 * stride, width), jnp.bfloat16),
            pltpu.VMEM((channels, 2 * wide), jnp.float32),
            pltpu.VMEM((SRC, 2 * stride), jnp.float32),
        ],
        compiler_params=kernel_params(),
        cost_estimate=pl.CostEstimate(
            flops=2 * 2 * windows * channels * 2 * wide * width,
            bytes_accessed=4 * (near.size + near_recv.size),
            transcendentals=0,
        ),
        name="terms",
    )(near, far, near_recv, far_recv, *tables)


def place_kernel(chunks, *refs):
    out_ref = refs[-1]
    _, core = place_of_core()
    lags, mine, channels = out_ref.shape
    swap = core != 0
    sides, backs = [], []
    for i in range(len(chunks)):
        own = refs[3 * i][...].astype(jnp.float32)
        other = refs[3 * i + 1][...].astype(jnp.float32)
        sides.append((jnp.where(swap, other, own), jnp.where(swap, own, other)))
        backs.append(refs[3 * i + 2][...].astype(jnp.float32).T)
    for j in range(lags):
        if j == lags - 2:
            lag = HALF
        elif j == lags - 1:
            lag = 0
        else:
            lag = HALF + (j // 2 + 1) * (-1 if j % 2 else 1)
        reverse = 2 * HALF - lag if j < lags - 1 else 0
        near = []
        for q in range(2):
            for side in range(2):
                for i, rows in enumerate(chunks):
                    near.append(sides[i][side][q, :, j * rows:(j + 1) * rows])
        out_ref[reverse, :, :SRC] = jnp.concatenate(near, axis=1)
        far = [backs[i][j * rows:(j + 1) * rows] for i, rows in enumerate(chunks)]
        out_ref[lag, :, SRC:] = jnp.concatenate(far, axis=0)


def place(chunks, parts, channels):
    mine = sum(chunks)
    return pl.pallas_call(
        functools.partial(place_kernel, chunks),
        in_specs=[whole()] * len(parts),
        out_specs=whole(),
        out_shape=jax.ShapeDtypeStruct((LAGS, mine, channels), jnp.float32),
        compiler_params=kernel_params(),
        name="place_lags",
    )(*parts)


def pair_body(spectra, counts, partner):
    blocks = lax.axis_size("chan")
    groups = lax.axis_size("win")
    windows, channels, two, freqs = spectra.shape
    scale = 1.0 / (math.sqrt(2.0 * freqs) * math.sqrt(windows * groups))
    chunks = (24, 16)

    tables, (white, *pieces) = whiten(spectra, counts, chunks)
    other_core = [(i, i ^ 1) for i in range(groups)]
    other_chip = [(i, i ^ 2) for i in range(groups)]

    def for_round(t):
        to_partner = [(i, i ^ t) for i in range(blocks)]
        to_partner_core = [
            (i * groups + g, (i ^ t) * groups + (g ^ 1))
            for i in range(blocks)
            for g in range(groups)
        ]

        def run(tables, white, *pieces):
            sibling = lax.ppermute(white, "win", other_core)
            arrived = []
            for i in range(len(chunks)):
                straight, crossed = pieces[2 * i:2 * i + 2]
                straight = lax.ppermute(straight, "chan", to_partner)
                crossed = lax.ppermute(crossed, ("chan", "win"), to_partner_core)
                arrived.append((straight, crossed))
            parts = []
            for recv in arrived:
                back_keep, back_send, own_keep, own_send = terms(
                    white, sibling, *recv, tables, scale
                )
                back_recv = lax.ppermute(back_send, "win", other_chip)
                back = (back_keep + back_recv.astype(jnp.float32)).astype(jnp.bfloat16)
                back = lax.ppermute(back, "chan", to_partner)
                own_recv = lax.ppermute(own_send, "win", other_chip).astype(jnp.float32)
                here = own_keep[0] + own_recv[0]
                away = (own_keep[1] + own_recv[1]).astype(jnp.bfloat16)
                other = lax.ppermute(away, "win", other_core)
                parts += [here, other, back]
            return parts

        return run

    rounds = partner[0, 0]
    branches = [for_round(t) for t in range(1, blocks)]
    parts = lax.switch(rounds - 1, branches, tables, white, *pieces)
    return place(chunks, parts, channels)[None, None]


def lag_table(freqs, lags):
    freq = jnp.arange(freqs, dtype=jnp.float32) + freqs // 4
    delay = jnp.arange(lags, dtype=jnp.float32) - lags // 2
    phase = 2.0 * math.pi * freq[:, None] * delay[None, :] / (4.0 * freqs)
    norm = 1.0 / math.sqrt(2.0 * freqs)
    return jnp.stack([jnp.cos(phase), -jnp.sin(phase)]) * norm


def blended_sources(sources, table):
    src = sources.astype(jnp.float32)
    first = src[:, :, 0][:, :, None, :]
    second = src[:, :, 1][:, :, None, :]
    cos_part = table[0].T[None, None]
    sin_part = table[1].T[None, None]
    real_mix = first * cos_part + second * sin_part
    imag_mix = second * cos_part - first * sin_part
    return jnp.stack([real_mix, imag_mix], axis=3).astype(jnp.bfloat16)


def pair_terms(sources, receiver_blocks, table):
    wins, count, two, freqs = sources.shape
    lags = table.shape[2]
    group = math.gcd(count, 32)
    flat_recv = receiver_blocks.reshape(wins, receiver_blocks.shape[1], two * freqs)
    grouped = jnp.moveaxis(sources.reshape(wins, count // group, group, two, freqs), 1, 0)

    def one_group(piece):
        mixed_spectra = blended_sources(piece, table).reshape(wins, group * lags, two * freqs)
        out = jnp.einsum(
            "wmx,wrx->mr", mixed_spectra, flat_recv, preferred_element_type=jnp.float32
        )
        return out.reshape(group, lags, receiver_blocks.shape[1])

    out = lax.map(one_group, grouped).reshape(count, lags, receiver_blocks.shape[1])
    return jnp.transpose(out, (1, 0, 2))


def route_blocks(values, round_flags, levels):
    for level in range(levels):
        moved = from_partner(values, "chan", level)
        values = jnp.where((round_flags >> level) % 2 == 1, moved, values)
    return values


def general_body(spectra, counts, partner):
    white = whiten_local(spectra, counts[0])
    table = lag_table(spectra.shape[3], LAGS)
    levels = lax.axis_size("chan").bit_length() - 1
    windows = spectra.shape[0] * lax.axis_size("win")
    receiver_blocks = route_blocks(white, partner[0, 0], levels)
    out = pair_terms(white[:, :SRC], receiver_blocks, table)
    stacked = lax.psum_scatter(out, "win", scatter_dimension=1, tiled=True)
    return (stacked / math.sqrt(windows))[None, None]


def solution(mesh):
    body = pair_body if mesh.shape["win"] == 4 else general_body
    return jax.shard_map(
        body,
        mesh=mesh,
        in_specs=(P("win", "chan", None, None), P("chan"), P()),
        out_specs=P("chan", None, None, "win", None),
        check_vma=False,
    )
```

```python
import functools
import math

import jax
import jax.numpy as jnp
import numpy as np
from jax import lax
from jax.experimental import pallas as pl
from jax.experimental.pallas import tpu as pltpu
from jax.sharding import PartitionSpec as P

LAGS = 16
SRC = 160
HALF = LAGS // 2
VMEM_LIMIT = 48 * 1024 * 1024


def from_partner(value, axis, stride):
    return lax.ppermute(value, axis, [(i, i ^ 1 << stride) for i in range(lax.axis_size(axis))])


def whiten_local(spectra, count):
    values = spectra.astype(jnp.float32)
    block_size = spectra.shape[1]
    freqs = spectra.shape[3]
    valid = (jnp.arange(block_size, dtype=jnp.int32) < count).astype(jnp.float32)
    freq = jnp.arange(freqs, dtype=jnp.float32)
    taper = 0.75 - 0.25 * jnp.cos(2.0 * math.pi * (freq + 0.5) / freqs)
    power = jnp.mean(values * values, axis=(2, 3))
    scale = valid[None, :] / jnp.sqrt(power + 1e-05)
    return (values * taper * scale[:, :, None, None]).astype(jnp.bfloat16)


def shift_tables(freqs):
    freq = np.arange(freqs, dtype=np.float64) + freqs // 4
    shift = np.arange(1, HALF + 1, dtype=np.float64)
    phase = 2.0 * np.pi * shift[:, None] * freq[None, :] / (4.0 * freqs)
    return np.cos(phase).astype(np.float32), np.sin(phase).astype(np.float32)


def place_of_core():
    spot = lax.axis_index("win")
    return spot // 2, spot % 2


def whole():
    return pl.BlockSpec(memory_space=pltpu.VMEM)


def anywhere():
    return pl.BlockSpec(memory_space=pl.ANY)


def kernel_params():
    return pltpu.CompilerParams(vmem_limit_bytes=VMEM_LIMIT)


def fetch_kernel(source_ref, out_ref, sem):
    copy = pltpu.make_async_copy(source_ref, out_ref, sem)
    copy.start()
    copy.wait()


def fetch(value):
    return pl.pallas_call(
        fetch_kernel,
        in_specs=[anywhere()],
        out_specs=whole(),
        out_shape=jax.ShapeDtypeStruct(value.shape, value.dtype),
        scratch_shapes=[pltpu.SemaphoreType.DMA],
        compiler_params=kernel_params(),
        name="fetch",
    )(value)


def whiten_kernel(count_ref, raw_ref, taper_ref, white_ref, near_ref, far_ref, count, sem):
    copy = pltpu.make_async_copy(count_ref, count, sem)
    copy.start()
    _, core = place_of_core()
    windows, channels, width = raw_ref.shape
    mine = SRC // 4
    step = 2 * mine

    def block(w, index, send):
        line = pl.ds(pl.multiple_of(index * step, step), step)
        values = raw_ref[w, line, :].astype(jnp.float32)
        power = jnp.sum(values * values, axis=1, keepdims=True) * (1.0 / width)
        row = index * step + lax.broadcasted_iota(jnp.int32, (step, 1), 0)
        valid = (row < count[0]).astype(jnp.float32)
        scale = valid / jnp.sqrt(power + 1e-05)
        values = values * taper_ref[...] * scale
        white_ref[w, line, :] = values.astype(jnp.bfloat16)
        if send:
            low, high = values[:mine], values[mine:]
            first = core == 0
            near_ref[w, index] = jnp.where(first, low, high).astype(jnp.bfloat16)
            far_ref[w, index] = jnp.where(first, high, low).astype(jnp.bfloat16)

    copy.wait()

    @pl.loop(0, windows * 2)
    def _(i):
        block(i // 2, i % 2, True)

    @pl.loop(0, windows * (channels // step - 2))
    def _(i):
        rest = channels // step - 2
        block(i // rest, 2 + i % rest, False)


def whiten(spectra, counts):
    windows, channels, two, freqs = spectra.shape
    width = two * freqs
    freq = np.arange(freqs, dtype=np.float64)
    taper = 0.75 - 0.25 * np.cos(2.0 * np.pi * (freq + 0.5) / freqs)
    taper = np.tile(taper.astype(np.float32), two)[None, :]
    piece = jax.ShapeDtypeStruct((windows, 2, SRC // 4, width), jnp.bfloat16)
    return pl.pallas_call(
        whiten_kernel,
        in_specs=[anywhere(), whole(), whole()],
        out_specs=[whole()] * 3,
        out_shape=[
            jax.ShapeDtypeStruct((windows, channels, width), jnp.bfloat16), piece, piece
        ],
        scratch_shapes=[pltpu.SMEM((1,), jnp.int32), pltpu.SemaphoreType.DMA],
        compiler_params=kernel_params(),
        name="whiten",
    )(counts, fetch(spectra).reshape(windows, channels, width), jnp.asarray(taper))


def mix(m_ref, piece, cos_ref, sin_ref):
    rows, width = piece.shape
    freqs = width // 2
    vrow = v_row(rows)
    for start in range(0, freqs, 128):
        low = slice(start, start + 128)
        high = slice(freqs + start, freqs + start + 128)
        real = piece[:, low].astype(jnp.float32)
        imag = piece[:, high].astype(jnp.float32)
        for m in range(0, HALF, 2):
            c = [cos_ref[m + i:m + i + 1, low] for i in range(2)]
            s = [sin_ref[m + i:m + i + 1, low] for i in range(2)]
            line = slice(m * rows, (m + 2) * rows)
            vline = slice(vrow + m * rows, vrow + (m + 2) * rows)

            def put(where, cols, values):
                m_ref[where, cols] = jnp.concatenate(values, axis=0).astype(jnp.bfloat16)

            put(line, low, [real * v for v in c])
            put(line, high, [imag * v for v in c])
            put(vline, low, [imag * -v for v in s])
            put(vline, high, [real * v for v in s])
        fill = jnp.zeros((vrow - (HALF + 1) * rows, 128), jnp.float32)
        for value, cols in ((real, low), (imag, high)):
            still = jnp.concatenate([value, fill], axis=0).astype(jnp.bfloat16)
            m_ref[HALF * rows:vrow, cols] = still


def v_row(rows):
    return -(-(HALF + 1) * rows // 128) * 128


def times(lhs, rhs):
    return lax.dot_general(
        lhs, rhs, (((1,), (1,)), ((), ())), preferred_element_type=jnp.float32
    )


def terms_kernel(
    second, scale, both_ref, near_recv, far_recv, cos_ref, sin_ref, *refs
):
    if second:
        _, _, back_ref, keep_ref, send_ref, recv_ref, even_ref, odd_ref, acc_ref = refs
    else:
        back_ref, keep_ref, send_ref, recv_ref, even_ref, odd_ref, acc_ref = refs
    x, core = place_of_core()
    windows, _, rows, _ = near_recv.shape
    steps = 2 * windows
    vrow = v_row(rows)
    wide = HALF * rows
    q = x if second else 1 - x
    for w in range(windows):
        recv_ref[w] = near_recv[w, q]
        recv_ref[windows + w] = far_recv[w, q]

    mix(even_ref, recv_ref.at[0], cos_ref, sin_ref)
    acc_ref[...] = jnp.zeros_like(acc_ref)

    @pl.loop(0, steps, step=2)
    def _(w):
        acc_ref[...] += times(both_ref[w], even_ref[...])
        mix(odd_ref, recv_ref.at[w + 1], cos_ref, sin_ref)
        acc_ref[...] += times(both_ref[w + 1], odd_ref[...])
        mix(even_ref, recv_ref.at[jnp.minimum(w + 2, steps - 1)], cos_ref, sin_ref)

    def split(line):
        u, v = acc_ref[line, :wide] * scale, acc_ref[line, vrow:vrow + wide] * scale
        still = acc_ref[line, wide:wide + rows] * scale
        return u + v, u - v, still

    plus, minus, still = split(pl.ds(SRC, acc_ref.shape[0] - SRC))
    back = jnp.concatenate([minus, plus[:, :wide - rows], still], axis=1)
    back_ref[...] = back.astype(back_ref.dtype)
    mine = SRC // 4
    for group, out in ((x, keep_ref), (1 - x, send_ref)):
        for side in range(2):
            spot = core if side == 0 else 1 - core
            line = pl.ds(pl.multiple_of((2 * group + spot) * mine, 8), mine)
            plus, minus, still = split(line)
            value = jnp.concatenate([plus, minus[:, :wide - rows], still], axis=1)
            out[1 if second else 0, side] = value.astype(out.dtype)


def terms(both, near_recv, far_recv, tables, scale, first=None):
    steps, channels, width = both.shape
    rows = near_recv.shape[2]
    wide = 2 * HALF * rows
    columns = v_row(rows) + HALF * rows
    mine = SRC // 4
    second = first is not None
    own = () if first is None else tuple(first)
    return pl.pallas_call(
        functools.partial(terms_kernel, second, scale),
        in_specs=[whole()] * 5 + [anywhere()] * len(own),
        out_specs=[whole()] * 3,
        out_shape=[
            jax.ShapeDtypeStruct(
                (channels - SRC, wide), jnp.float32 if second else jnp.bfloat16
            ),
            jax.ShapeDtypeStruct((2, 2, mine, wide), jnp.float32),
            jax.ShapeDtypeStruct((2, 2, mine, wide), jnp.bfloat16),
        ],
        input_output_aliases={5: 1, 6: 2} if second else {},
        scratch_shapes=[
            pltpu.VMEM((steps, rows, width), jnp.bfloat16),
            pltpu.VMEM((columns, width), jnp.bfloat16),
            pltpu.VMEM((columns, width), jnp.bfloat16),
            pltpu.VMEM((channels, columns), jnp.float32),
        ],
        compiler_params=kernel_params(),
        cost_estimate=pl.CostEstimate(
            flops=2 * steps * channels * columns * width,
            bytes_accessed=2 * both.size,
            transcendentals=0,
        ),
        name="terms_second" if second else "terms_first",
    )(both, near_recv, far_recv, *tables, *own)


def place_kernel(here_ref, other_ref, back_ref, out_ref, block_ref, sems):
    x, core = place_of_core()
    lags, mine, channels = block_ref.shape
    swap = core != 0
    sides = []
    for q in range(2):
        index = jnp.where(x == q, 1, 0)
        own, other = here_ref[index], other_ref[index].astype(jnp.float32)
        sides += [jnp.where(swap, other, own), jnp.where(swap, own, other)]
    back = back_ref[...].astype(jnp.float32).T
    copies = []
    for j in range(lags):
        lag = HALF - 1 - j if j < HALF else j + 1 if j < lags - 1 else HALF
        cols = slice(j * mine, (j + 1) * mine)
        block_ref[lag, :, :SRC] = jnp.concatenate([v[:, cols] for v in sides], axis=1)
        block_ref[lag, :, SRC:] = back[cols]
        copies.append(pltpu.make_async_copy(block_ref.at[lag], out_ref.at[lag], sems.at[lag]))
        copies[-1].start()
    for copy in copies:
        copy.wait()


def place(here, other, back):
    _, mine, wide = here.shape
    shape = (wide // mine, mine, SRC + back.shape[0])
    return pl.pallas_call(
        place_kernel,
        in_specs=[whole()] * 3,
        out_specs=anywhere(),
        out_shape=jax.ShapeDtypeStruct(shape, jnp.float32),
        scratch_shapes=[
            pltpu.VMEM(shape, jnp.float32), pltpu.SemaphoreType.DMA((shape[0],))
        ],
        compiler_params=kernel_params(),
        name="place_lags",
    )(here, other, back)


def pair_body(spectra, counts, partner):
    blocks = lax.axis_size("chan")
    groups = lax.axis_size("win")
    windows, channels, two, freqs = spectra.shape
    scale = 1.0 / (math.sqrt(2.0 * freqs) * math.sqrt(windows * groups))
    other_core = [(i, i ^ 1) for i in range(groups)]
    other_chip = [(i, i ^ 2) for i in range(groups)]

    def to_partner(t):
        return [(i, i ^ t) for i in range(blocks)]

    def to_partner_core(t):
        return [
            (i * groups + g, (i ^ t) * groups + (g ^ 1))
            for i in range(blocks)
            for g in range(groups)
        ]

    def send_sources(t, white, near, far):
        sibling = lax.ppermute(white, "win", other_core)
        near = lax.ppermute(near, "chan", to_partner(t))
        far = lax.ppermute(far, ("chan", "win"), to_partner_core(t))
        return jnp.concatenate([white, sibling]), near, far

    def send_terms(t, back, keep, send):
        back = lax.ppermute(back, "chan", to_partner(t))
        recv = lax.ppermute(send, "win", other_chip).astype(jnp.float32)
        total = keep + recv[::-1]
        away = total[:, 1].astype(jnp.bfloat16)
        return total[:, 0], lax.ppermute(away, "win", other_core), back

    def by_round(run, *values):
        branches = [functools.partial(run, t) for t in range(1, blocks)]
        return lax.switch(partner[0, 0] - 1, branches, *values)

    tables = [jnp.asarray(v) for v in shift_tables(freqs)]
    sources = by_round(send_sources, *whiten(spectra, counts))
    back_send, *own = terms(*sources, tables, scale)
    back_recv = lax.ppermute(back_send, "win", other_chip)
    back_keep, *own = terms(*sources, tables, scale, own)
    back = (back_keep + back_recv.astype(jnp.float32)).astype(jnp.bfloat16)
    return place(*by_round(send_terms, back, *own))[None, None]


def lag_table(freqs, lags):
    freq = jnp.arange(freqs, dtype=jnp.float32) + freqs // 4
    delay = jnp.arange(lags, dtype=jnp.float32) - lags // 2
    phase = 2.0 * math.pi * freq[:, None] * delay[None, :] / (4.0 * freqs)
    norm = 1.0 / math.sqrt(2.0 * freqs)
    return jnp.stack([jnp.cos(phase), -jnp.sin(phase)]) * norm


def blended_sources(sources, table):
    src = sources.astype(jnp.float32)
    first = src[:, :, 0][:, :, None, :]
    second = src[:, :, 1][:, :, None, :]
    cos_part = table[0].T[None, None]
    sin_part = table[1].T[None, None]
    real_mix = first * cos_part + second * sin_part
    imag_mix = second * cos_part - first * sin_part
    return jnp.stack([real_mix, imag_mix], axis=3).astype(jnp.bfloat16)


def pair_terms(sources, receiver_blocks, table):
    wins, count, two, freqs = sources.shape
    lags = table.shape[2]
    group = math.gcd(count, 32)
    flat_recv = receiver_blocks.reshape(wins, receiver_blocks.shape[1], two * freqs)
    grouped = jnp.moveaxis(sources.reshape(wins, count // group, group, two, freqs), 1, 0)

    def one_group(piece):
        mixed_spectra = blended_sources(piece, table).reshape(wins, group * lags, two * freqs)
        out = jnp.einsum(
            "wmx,wrx->mr", mixed_spectra, flat_recv, preferred_element_type=jnp.float32
        )
        return out.reshape(group, lags, receiver_blocks.shape[1])

    out = lax.map(one_group, grouped).reshape(count, lags, receiver_blocks.shape[1])
    return jnp.transpose(out, (1, 0, 2))


def route_blocks(values, round_flags, levels):
    for level in range(levels):
        moved = from_partner(values, "chan", level)
        values = jnp.where((round_flags >> level) % 2 == 1, moved, values)
    return values


def general_body(spectra, counts, partner):
    white = whiten_local(spectra, counts[0])
    table = lag_table(spectra.shape[3], LAGS)
    levels = lax.axis_size("chan").bit_length() - 1
    windows = spectra.shape[0] * lax.axis_size("win")
    receiver_blocks = route_blocks(white, partner[0, 0], levels)
    out = pair_terms(white[:, :SRC], receiver_blocks, table)
    stacked = lax.psum_scatter(out, "win", scatter_dimension=1, tiled=True)
    return (stacked / math.sqrt(windows))[None, None]


def solution(mesh):
    body = pair_body if mesh.shape["win"] == 4 else general_body
    return jax.shard_map(
        body,
        mesh=mesh,
        in_specs=(P("win", "chan", None, None), P("chan"), P()),
        out_specs=P("chan", None, None, "win", None),
        check_vma=False,
    )
```

```python
import functools
import math

import jax
import jax.numpy as jnp
import numpy as np
from jax import lax
from jax.experimental import pallas as pl
from jax.experimental.pallas import tpu as pltpu
from jax.sharding import PartitionSpec as P

LAGS = 16
SRC = 160
HALF = LAGS // 2
VMEM_LIMIT = 16 * 1024 * 1024


def from_partner(value, axis, stride):
    return lax.ppermute(value, axis, [(i, i ^ 1 << stride) for i in range(lax.axis_size(axis))])


def whiten_local(spectra, count):
    values = spectra.astype(jnp.float32)
    block_size = spectra.shape[1]
    freqs = spectra.shape[3]
    valid = (jnp.arange(block_size, dtype=jnp.int32) < count).astype(jnp.float32)
    freq = jnp.arange(freqs, dtype=jnp.float32)
    taper = 0.75 - 0.25 * jnp.cos(2.0 * math.pi * (freq + 0.5) / freqs)
    power = jnp.mean(values * values, axis=(2, 3))
    scale = valid[None, :] / jnp.sqrt(power + 1e-05)
    return (values * taper * scale[:, :, None, None]).astype(jnp.bfloat16)


def shift_tables(freqs):
    freq = np.arange(freqs, dtype=np.float64) + freqs // 4
    shift = np.arange(1, HALF + 1, dtype=np.float64)
    phase = 2.0 * np.pi * shift[:, None] * freq[None, :] / (4.0 * freqs)
    return np.cos(phase).astype(np.float32), np.sin(phase).astype(np.float32)


def place_of_core():
    spot = lax.axis_index("win")
    return spot // 2, spot % 2


def whole():
    return pl.BlockSpec(memory_space=pltpu.VMEM)


def anywhere():
    return pl.BlockSpec(memory_space=pl.ANY)


def kernel_params():
    return pltpu.CompilerParams(vmem_limit_bytes=VMEM_LIMIT)


def fetch_kernel(source_ref, out_ref, sems):
    windows, parts = out_ref.shape[0], sems.shape[1]
    step = out_ref.shape[1] // parts
    copies = []
    for w in range(windows):
        for i in range(parts):
            part = (w, pl.ds(i * step, step))
            copies.append(
                pltpu.make_async_copy(source_ref.at[part], out_ref.at[part], sems.at[w, i])
            )
            copies[-1].start()
    for copy in copies:
        copy.wait()


def fetch(value):
    return pl.pallas_call(
        fetch_kernel,
        in_specs=[pl.BlockSpec(memory_space=pltpu.HBM)],
        out_specs=whole(),
        out_shape=jax.ShapeDtypeStruct(value.shape, value.dtype),
        scratch_shapes=[pltpu.SemaphoreType.DMA((value.shape[0], 4))],
        compiler_params=kernel_params(),
        name="fetch",
    )(pltpu.with_memory_space_constraint(value, pltpu.HBM))


def whiten_kernel(count_ref, raw_ref, taper_ref, white_ref, near_ref, far_ref, count, sem):
    copy = pltpu.make_async_copy(count_ref, count, sem)
    copy.start()
    _, core = place_of_core()
    windows, channels, width = raw_ref.shape
    mine = SRC // 4
    step = 2 * mine

    copy.wait()
    for w in range(windows):
        for index in range(channels // step):
            line = slice(index * step, (index + 1) * step)
            values = raw_ref[w, line, :].astype(jnp.float32)
            power = jnp.sum(values * values, axis=1, keepdims=True) * (1.0 / width)
            row = index * step + lax.broadcasted_iota(jnp.int32, (step, 1), 0)
            valid = (row < count[0]).astype(jnp.float32)
            scale = valid / jnp.sqrt(power + 1e-05)
            values = values * taper_ref[...] * scale
            white_ref[w, line, :] = values.astype(jnp.bfloat16)
            if index * step < SRC:
                low, high = values[:mine], values[mine:]
                first = core == 0
                near_ref[w, index] = jnp.where(first, low, high).astype(jnp.bfloat16)
                far_ref[w, index] = jnp.where(first, high, low).astype(jnp.bfloat16)


def whiten(spectra, counts):
    windows, channels, two, freqs = spectra.shape
    width = two * freqs
    freq = np.arange(freqs, dtype=np.float64)
    taper = 0.75 - 0.25 * np.cos(2.0 * np.pi * (freq + 0.5) / freqs)
    taper = np.tile(taper.astype(np.float32), two)[None, :]
    piece = jax.ShapeDtypeStruct((windows, 2, SRC // 4, width), jnp.bfloat16)
    return pl.pallas_call(
        whiten_kernel,
        in_specs=[anywhere(), whole(), whole()],
        out_specs=[whole()] * 3,
        out_shape=[
            jax.ShapeDtypeStruct((windows, channels, width), jnp.bfloat16), piece, piece
        ],
        scratch_shapes=[pltpu.SMEM((1,), jnp.int32), pltpu.SemaphoreType.DMA],
        compiler_params=kernel_params(),
        name="whiten",
    )(counts, fetch(spectra).reshape(windows, channels, width), jnp.asarray(taper))


def mix(m_ref, piece, cos_ref, sin_ref, start):
    rows, width = piece.shape
    freqs = width // 2
    vrow = v_row(rows)
    low = slice(start, start + 128)
    high = slice(freqs + start, freqs + start + 128)
    real = piece[:, low].astype(jnp.float32)
    imag = piece[:, high].astype(jnp.float32)

    def put(where, cols, values):
        m_ref[where, cols] = jnp.concatenate(values, axis=0).astype(jnp.bfloat16)

    for m in range(0, HALF, 2):
        c = [cos_ref[m + i:m + i + 1, low] for i in range(2)]
        s = [sin_ref[m + i:m + i + 1, low] for i in range(2)]
        line = slice(m * rows, (m + 2) * rows)
        vline = slice(vrow + m * rows, vrow + (m + 2) * rows)
        put(line, low, [real * v for v in c])
        put(line, high, [imag * v for v in c])
        put(vline, low, [imag * -v for v in s])
        put(vline, high, [real * v for v in s])
    fill = jnp.zeros((vrow - (HALF + 1) * rows, 128), jnp.float32)
    for value, cols in ((real, low), (imag, high)):
        put(slice(HALF * rows, vrow), cols, [value, fill])


def v_row(rows):
    return -(-(HALF + 1) * rows // 128) * 128


def times(lhs, rhs):
    return lax.dot_general(
        lhs, rhs, (((1,), (1,)), ((), ())), preferred_element_type=jnp.float32
    )


def terms_kernel(second, scale, both_ref, recv_ref, cos_ref, sin_ref, *refs):
    if second:
        refs = refs[4:]
    back_ref, *own_refs, even_ref, odd_ref, acc_ref = refs
    x, core = place_of_core()
    steps, _, rows, width = recv_ref.shape
    vrow = v_row(rows)
    wide = HALF * rows
    starts = range(0, width // 2, 128)
    q = x if second else 1 - x
    for start in starts:
        mix(even_ref, recv_ref.at[0, q], cos_ref, sin_ref, start)
    acc_ref[...] = jnp.zeros_like(acc_ref)

    def multiply(w, now_ref, next_ref, later):
        columns = now_ref.shape[0]
        todo = list(starts)
        for tile in range(0, columns, 256):
            cols = slice(tile, min(tile + 256, columns))
            acc_ref[:, cols] += times(both_ref[w], now_ref[cols, :])
            for start in todo[:2]:
                mix(next_ref, recv_ref.at[later, q], cos_ref, sin_ref, start)
            todo = todo[2:]

    @pl.loop(0, steps, step=2)
    def _(w):
        multiply(w, even_ref, odd_ref, w + 1)
        multiply(w + 1, odd_ref, even_ref, jnp.minimum(w + 2, steps - 1))

    def split(line):
        u, v = acc_ref[line, :wide] * scale, acc_ref[line, vrow:vrow + wide] * scale
        still = acc_ref[line, wide:wide + rows] * scale
        return u + v, u - v, still

    plus, minus, still = split(pl.ds(SRC, acc_ref.shape[0] - SRC))
    back = jnp.concatenate([minus, plus[:, :wide - rows], still], axis=1)
    back_ref[...] = back.astype(back_ref.dtype)
    mine = SRC // 4
    for i, out in enumerate(own_refs):
        group, spot = (x, 1 - x)[i // 2], (core, 1 - core)[i % 2]
        line = pl.ds(pl.multiple_of((2 * group + spot) * mine, 8), mine)
        plus, minus, still = split(line)
        value = jnp.concatenate([plus, minus[:, :wide - rows], still], axis=1)
        out[1 if second else 0] = value.astype(out.dtype)


def terms(both, recv, tables, scale, first=None):
    steps, channels, width = both.shape
    rows = recv.shape[2]
    wide = 2 * HALF * rows
    columns = v_row(rows) + HALF * rows
    mine = SRC // 4
    second = first is not None
    own = () if first is None else tuple(first)
    return pl.pallas_call(
        functools.partial(terms_kernel, second, scale),
        in_specs=[whole()] * 4 + [anywhere()] * len(own),
        out_specs=[whole()] * 5,
        out_shape=[
            jax.ShapeDtypeStruct(
                (channels - SRC, wide), jnp.float32 if second else jnp.bfloat16
            ),
            jax.ShapeDtypeStruct((2, mine, wide), jnp.float32),
        ] + [jax.ShapeDtypeStruct((2, mine, wide), jnp.bfloat16)] * 3,
        input_output_aliases={4 + i: 1 + i for i in range(len(own))},
        scratch_shapes=[
            pltpu.VMEM((columns, width), jnp.bfloat16),
            pltpu.VMEM((columns, width), jnp.bfloat16),
            pltpu.VMEM((channels, columns), jnp.float32),
        ],
        compiler_params=kernel_params(),
        cost_estimate=pl.CostEstimate(
            flops=2 * steps * channels * columns * width,
            bytes_accessed=2 * both.size,
            transcendentals=0,
        ),
        name="terms_second" if second else "terms_first",
    )(both, recv, *tables, *own)


def place_kernel(here_ref, away_ref, back_ref, out_ref, block_ref, sems):
    x, core = place_of_core()
    lags, mine, channels = block_ref.shape
    swap = core != 0
    sides = []
    for q in range(2):
        index = jnp.where(x == q, 1, 0)
        own = here_ref[index] + away_ref[3 - index].astype(jnp.float32)
        other = away_ref[index].astype(jnp.float32) + away_ref[5 - index].astype(jnp.float32)
        sides += [jnp.where(swap, other, own), jnp.where(swap, own, other)]
    back = back_ref[...].T
    copies = []
    for j in range(lags):
        lag = HALF - 1 - j if j < HALF else j + 1 if j < lags - 1 else HALF
        cols = slice(j * mine, (j + 1) * mine)
        block_ref[lag, :, :SRC] = jnp.concatenate([v[:, cols] for v in sides], axis=1)
        block_ref[lag, :, SRC:] = back[cols]
        copies.append(pltpu.make_async_copy(block_ref.at[lag], out_ref.at[lag], sems.at[lag]))
        copies[-1].start()
    for copy in copies:
        copy.wait()


def place(here, away, back):
    _, mine, wide = here.shape
    shape = (wide // mine, mine, SRC + back.shape[0])
    return pl.pallas_call(
        place_kernel,
        in_specs=[whole()] * 3,
        out_specs=anywhere(),
        out_shape=jax.ShapeDtypeStruct(shape, jnp.float32),
        scratch_shapes=[
            pltpu.VMEM(shape, jnp.float32), pltpu.SemaphoreType.DMA((shape[0],))
        ],
        compiler_params=kernel_params(),
        name="place_lags",
    )(here, away, back)


def pair_body(spectra, counts, partner):
    blocks = lax.axis_size("chan")
    groups = lax.axis_size("win")
    windows, channels, two, freqs = spectra.shape
    scale = 1.0 / (math.sqrt(2.0 * freqs) * math.sqrt(windows * groups))
    other_core = [(i, i ^ 1) for i in range(groups)]
    other_chip = [(i, i ^ 2) for i in range(groups)]
    other_both = [(i, i ^ 3) for i in range(groups)]

    def to_partner(t):
        return [(i, i ^ t) for i in range(blocks)]

    def to_partner_core(t):
        return [
            (i * groups + g, (i ^ t) * groups + (g ^ 1))
            for i in range(blocks)
            for g in range(groups)
        ]

    def send_sources(t, white, near, far):
        sibling = lax.ppermute(white, "win", other_core)
        near = lax.ppermute(near, "chan", to_partner(t))
        far = lax.ppermute(far, ("chan", "win"), to_partner_core(t))
        return jnp.concatenate([white, sibling]), jnp.concatenate([near, far])

    def send_terms(t, back, here, core, chip, cross):
        back = lax.ppermute(back, "chan", to_partner(t))
        core = lax.ppermute(core, "win", other_core)
        chip = lax.ppermute(chip, "win", other_chip)
        cross = lax.ppermute(cross, "win", other_both)
        return here, jnp.concatenate([core, chip, cross]), back.astype(jnp.float32)

    def by_round(run, *values):
        branches = [functools.partial(run, t) for t in range(1, blocks)]
        return lax.switch(partner[0, 0] - 1, branches, *values)

    tables = [jnp.asarray(v) for v in shift_tables(freqs)]
    sources = by_round(send_sources, *whiten(spectra, counts))
    back_send, *own = terms(*sources, tables, scale)
    back_recv = lax.ppermute(back_send, "win", other_chip)
    back_keep, *own = terms(*sources, tables, scale, own)
    back = (back_keep + back_recv.astype(jnp.float32)).astype(jnp.bfloat16)
    return place(*by_round(send_terms, back, *own))[None, None]


def lag_table(freqs, lags):
    freq = jnp.arange(freqs, dtype=jnp.float32) + freqs // 4
    delay = jnp.arange(lags, dtype=jnp.float32) - lags // 2
    phase = 2.0 * math.pi * freq[:, None] * delay[None, :] / (4.0 * freqs)
    norm = 1.0 / math.sqrt(2.0 * freqs)
    return jnp.stack([jnp.cos(phase), -jnp.sin(phase)]) * norm


def blended_sources(sources, table):
    src = sources.astype(jnp.float32)
    first = src[:, :, 0][:, :, None, :]
    second = src[:, :, 1][:, :, None, :]
    cos_part = table[0].T[None, None]
    sin_part = table[1].T[None, None]
    real_mix = first * cos_part + second * sin_part
    imag_mix = second * cos_part - first * sin_part
    return jnp.stack([real_mix, imag_mix], axis=3).astype(jnp.bfloat16)


def pair_terms(sources, receiver_blocks, table):
    wins, count, two, freqs = sources.shape
    lags = table.shape[2]
    group = math.gcd(count, 32)
    flat_recv = receiver_blocks.reshape(wins, receiver_blocks.shape[1], two * freqs)
    grouped = jnp.moveaxis(sources.reshape(wins, count // group, group, two, freqs), 1, 0)

    def one_group(piece):
        mixed_spectra = blended_sources(piece, table).reshape(wins, group * lags, two * freqs)
        out = jnp.einsum(
            "wmx,wrx->mr", mixed_spectra, flat_recv, preferred_element_type=jnp.float32
        )
        return out.reshape(group, lags, receiver_blocks.shape[1])

    out = lax.map(one_group, grouped).reshape(count, lags, receiver_blocks.shape[1])
    return jnp.transpose(out, (1, 0, 2))


def route_blocks(values, round_flags, levels):
    for level in range(levels):
        moved = from_partner(values, "chan", level)
        values = jnp.where((round_flags >> level) % 2 == 1, moved, values)
    return values


def general_body(spectra, counts, partner):
    white = whiten_local(spectra, counts[0])
    table = lag_table(spectra.shape[3], LAGS)
    levels = lax.axis_size("chan").bit_length() - 1
    windows = spectra.shape[0] * lax.axis_size("win")
    receiver_blocks = route_blocks(white, partner[0, 0], levels)
    out = pair_terms(white[:, :SRC], receiver_blocks, table)
    stacked = lax.psum_scatter(out, "win", scatter_dimension=1, tiled=True)
    return (stacked / math.sqrt(windows))[None, None]


def solution(mesh):
    body = pair_body if mesh.shape["win"] == 4 else general_body
    return jax.shard_map(
        body,
        mesh=mesh,
        in_specs=(P("win", "chan", None, None), P("chan"), P()),
        out_specs=P("chan", None, None, "win", None),
        check_vma=False,
    )
```

```python
import functools
import math

import jax
import jax.numpy as jnp
import numpy as np
from jax import lax
from jax.experimental import pallas as pl
from jax.experimental.pallas import tpu as pltpu
from jax.sharding import PartitionSpec as P

LAGS = 16
SRC = 160
HALF = LAGS // 2
VMEM_LIMIT = 16 * 1024 * 1024


def from_partner(value, axis, stride):
    return lax.ppermute(value, axis, [(i, i ^ 1 << stride) for i in range(lax.axis_size(axis))])


def whiten_local(spectra, count):
    values = spectra.astype(jnp.float32)
    block_size = spectra.shape[1]
    freqs = spectra.shape[3]
    valid = (jnp.arange(block_size, dtype=jnp.int32) < count).astype(jnp.float32)
    freq = jnp.arange(freqs, dtype=jnp.float32)
    taper = 0.75 - 0.25 * jnp.cos(2.0 * math.pi * (freq + 0.5) / freqs)
    power = jnp.mean(values * values, axis=(2, 3))
    scale = valid[None, :] / jnp.sqrt(power + 1e-05)
    return (values * taper * scale[:, :, None, None]).astype(jnp.bfloat16)


def shift_tables(freqs):
    freq = np.arange(freqs, dtype=np.float64) + freqs // 4
    shift = np.arange(1, HALF + 1, dtype=np.float64)
    phase = 2.0 * np.pi * shift[:, None] * freq[None, :] / (4.0 * freqs)
    return np.cos(phase).astype(np.float32), np.sin(phase).astype(np.float32)


def place_of_core():
    spot = lax.axis_index("win")
    return spot // 2, spot % 2


def whole():
    return pl.BlockSpec(memory_space=pltpu.VMEM)


def anywhere():
    return pl.BlockSpec(memory_space=pl.ANY)


def kernel_params():
    return pltpu.CompilerParams(vmem_limit_bytes=VMEM_LIMIT)


def fetch_kernel(source_ref, out_ref, sems):
    windows, parts = out_ref.shape[0], sems.shape[1]
    step = out_ref.shape[1] // parts
    copies = []
    for w in range(windows):
        for i in range(parts):
            part = (w, pl.ds(i * step, step))
            copies.append(
                pltpu.make_async_copy(source_ref.at[part], out_ref.at[part], sems.at[w, i])
            )
            copies[-1].start()
    for copy in copies:
        copy.wait()


def fetch(value):
    return pl.pallas_call(
        fetch_kernel,
        in_specs=[pl.BlockSpec(memory_space=pltpu.HBM)],
        out_specs=whole(),
        out_shape=jax.ShapeDtypeStruct(value.shape, value.dtype),
        scratch_shapes=[pltpu.SemaphoreType.DMA((value.shape[0], 4))],
        compiler_params=kernel_params(),
        name="fetch",
    )(pltpu.with_memory_space_constraint(value, pltpu.HBM))


def whiten_kernel(count_ref, raw_ref, taper_ref, white_ref, near_ref, far_ref, count, sem):
    copy = pltpu.make_async_copy(count_ref, count, sem)
    copy.start()
    _, core = place_of_core()
    windows, channels, width = raw_ref.shape
    mine = SRC // 4
    step = 2 * mine

    copy.wait()
    for w in range(windows):
        for index in range(channels // step):
            line = slice(index * step, (index + 1) * step)
            values = raw_ref[w, line, :].astype(jnp.float32)
            power = jnp.sum(values * values, axis=1, keepdims=True) * (1.0 / width)
            row = index * step + lax.broadcasted_iota(jnp.int32, (step, 1), 0)
            valid = (row < count[0]).astype(jnp.float32)
            scale = valid / jnp.sqrt(power + 1e-05)
            values = values * taper_ref[...] * scale
            white_ref[w, line, :] = values.astype(jnp.bfloat16)
            if index * step < SRC:
                low, high = values[:mine], values[mine:]
                first = core == 0
                near_ref[w, index] = jnp.where(first, low, high).astype(jnp.bfloat16)
                far_ref[w, index] = jnp.where(first, high, low).astype(jnp.bfloat16)


def whiten(spectra, counts):
    windows, channels, two, freqs = spectra.shape
    width = two * freqs
    freq = np.arange(freqs, dtype=np.float64)
    taper = 0.75 - 0.25 * np.cos(2.0 * np.pi * (freq + 0.5) / freqs)
    taper = np.tile(taper.astype(np.float32), two)[None, :]
    piece = jax.ShapeDtypeStruct((windows, 2, SRC // 4, width), jnp.bfloat16)
    return pl.pallas_call(
        whiten_kernel,
        in_specs=[anywhere(), whole(), whole()],
        out_specs=[whole()] * 3,
        out_shape=[
            jax.ShapeDtypeStruct((windows, channels, width), jnp.bfloat16), piece, piece
        ],
        scratch_shapes=[pltpu.SMEM((1,), jnp.int32), pltpu.SemaphoreType.DMA],
        compiler_params=kernel_params(),
        name="whiten",
    )(counts, fetch(spectra).reshape(windows, channels, width), jnp.asarray(taper))


def mix(m_ref, piece, cos_ref, sin_ref, start):
    rows, width = piece.shape
    freqs = width // 2
    vrow = v_row(rows)
    low = slice(start, start + 128)
    high = slice(freqs + start, freqs + start + 128)
    real = piece[:, low].astype(jnp.float32)
    imag = piece[:, high].astype(jnp.float32)

    def put(where, cols, values):
        m_ref[where, cols] = jnp.concatenate(values, axis=0).astype(jnp.bfloat16)

    for m in range(0, HALF, 2):
        c = [cos_ref[m + i:m + i + 1, low] for i in range(2)]
        s = [sin_ref[m + i:m + i + 1, low] for i in range(2)]
        line = slice(m * rows, (m + 2) * rows)
        vline = slice(vrow + m * rows, vrow + (m + 2) * rows)
        put(line, low, [real * v for v in c])
        put(line, high, [imag * v for v in c])
        put(vline, low, [imag * -v for v in s])
        put(vline, high, [real * v for v in s])
    fill = jnp.zeros((vrow - (HALF + 1) * rows, 128), jnp.float32)
    for value, cols in ((real, low), (imag, high)):
        put(slice(HALF * rows, vrow), cols, [value, fill])


def v_row(rows):
    return -(-(HALF + 1) * rows // 128) * 128


def times(lhs, rhs):
    return lax.dot_general(
        lhs, rhs, (((1,), (1,)), ((), ())), preferred_element_type=jnp.float32
    )


def terms_kernel(second, scale, both_ref, recv_ref, cos_ref, sin_ref, *refs):
    if second:
        refs = refs[4:]
    back_ref, *own_refs, even_ref, odd_ref, acc_ref = refs
    x, core = place_of_core()
    steps, _, rows, width = recv_ref.shape
    vrow = v_row(rows)
    wide = HALF * rows
    starts = range(0, width // 2, 128)
    q = x if second else 1 - x
    for start in starts:
        mix(even_ref, recv_ref.at[0, q], cos_ref, sin_ref, start)
    acc_ref[...] = jnp.zeros_like(acc_ref)

    def multiply(w, now_ref, next_ref, later):
        columns = now_ref.shape[0]
        todo = list(starts)
        for tile in range(0, columns, 256):
            cols = slice(tile, min(tile + 256, columns))
            acc_ref[:, cols] += times(both_ref[w], now_ref[cols, :])
            for start in todo[:2]:
                mix(next_ref, recv_ref.at[later, q], cos_ref, sin_ref, start)
            todo = todo[2:]

    @pl.loop(0, steps, step=2)
    def _(w):
        multiply(w, even_ref, odd_ref, w + 1)
        multiply(w + 1, odd_ref, even_ref, jnp.minimum(w + 2, steps - 1))

    def split(line):
        u, v = acc_ref[line, :wide] * scale, acc_ref[line, vrow:vrow + wide] * scale
        still = acc_ref[line, wide:wide + rows] * scale
        return u + v, u - v, still

    plus, minus, still = split(pl.ds(SRC, acc_ref.shape[0] - SRC))
    back = jnp.concatenate([minus, plus[:, :wide - rows], still], axis=1)
    back_ref[...] = back.astype(back_ref.dtype)
    mine = SRC // 4
    for i, out in enumerate(own_refs):
        group, spot = (x, 1 - x)[i // 2], (core, 1 - core)[i % 2]
        line = pl.ds(pl.multiple_of((2 * group + spot) * mine, 8), mine)
        plus, minus, still = split(line)
        value = jnp.concatenate([plus, minus[:, :wide - rows], still], axis=1)
        out[1 if second else 0] = value.astype(out.dtype)


def terms(both, recv, tables, scale, first=None):
    steps, channels, width = both.shape
    rows = recv.shape[2]
    wide = 2 * HALF * rows
    columns = v_row(rows) + HALF * rows
    mine = SRC // 4
    second = first is not None
    own = () if first is None else tuple(first)
    return pl.pallas_call(
        functools.partial(terms_kernel, second, scale),
        in_specs=[whole()] * 4 + [anywhere()] * len(own),
        out_specs=[whole()] * 5,
        out_shape=[
            jax.ShapeDtypeStruct(
                (channels - SRC, wide), jnp.float32 if second else jnp.bfloat16
            ),
            jax.ShapeDtypeStruct((2, mine, wide), jnp.float32),
        ] + [jax.ShapeDtypeStruct((2, mine, wide), jnp.bfloat16)] * 3,
        input_output_aliases={4 + i: 1 + i for i in range(len(own))},
        scratch_shapes=[
            pltpu.VMEM((columns, width), jnp.bfloat16),
            pltpu.VMEM((columns, width), jnp.bfloat16),
            pltpu.VMEM((channels, columns), jnp.float32),
        ],
        compiler_params=kernel_params(),
        cost_estimate=pl.CostEstimate(
            flops=2 * steps * channels * columns * width,
            bytes_accessed=2 * both.size,
            transcendentals=0,
        ),
        name="terms_second" if second else "terms_first",
    )(both, recv, *tables, *own)


def place_kernel(
    here_ref, core_ref, chip_ref, cross_ref, back_ref, out_ref, block_ref, sems
):
    x, core = place_of_core()
    lags, mine, channels = block_ref.shape
    swap = core != 0
    sides = []
    for q in range(2):
        index = jnp.where(x == q, 1, 0)
        own = here_ref[index] + chip_ref[1 - index].astype(jnp.float32)
        other = core_ref[index].astype(jnp.float32) + cross_ref[1 - index].astype(jnp.float32)
        sides += [jnp.where(swap, other, own), jnp.where(swap, own, other)]
    back = back_ref[...].T
    copies = []
    for j in range(lags):
        lag = HALF - 1 - j if j < HALF else j + 1 if j < lags - 1 else HALF
        cols = slice(j * mine, (j + 1) * mine)
        block_ref[lag, :, :SRC] = jnp.concatenate([v[:, cols] for v in sides], axis=1)
        block_ref[lag, :, SRC:] = back[cols]
        copies.append(pltpu.make_async_copy(block_ref.at[lag], out_ref.at[lag], sems.at[lag]))
        copies[-1].start()
    for copy in copies:
        copy.wait()


def place(here, core, chip, cross, back):
    _, mine, wide = here.shape
    shape = (wide // mine, mine, SRC + back.shape[0])
    return pl.pallas_call(
        place_kernel,
        in_specs=[whole()] * 5,
        out_specs=anywhere(),
        out_shape=jax.ShapeDtypeStruct(shape, jnp.float32),
        scratch_shapes=[
            pltpu.VMEM(shape, jnp.float32), pltpu.SemaphoreType.DMA((shape[0],))
        ],
        compiler_params=kernel_params(),
        name="place_lags",
    )(here, core, chip, cross, back)


def pair_body(spectra, counts, partner):
    blocks = lax.axis_size("chan")
    groups = lax.axis_size("win")
    windows, channels, two, freqs = spectra.shape
    scale = 1.0 / (math.sqrt(2.0 * freqs) * math.sqrt(windows * groups))
    other_core = [(i, i ^ 1) for i in range(groups)]
    other_chip = [(i, i ^ 2) for i in range(groups)]
    other_both = [(i, i ^ 3) for i in range(groups)]

    def to_partner(t):
        return [(i, i ^ t) for i in range(blocks)]

    def to_partner_core(t):
        return [
            (i * groups + g, (i ^ t) * groups + (g ^ 1))
            for i in range(blocks)
            for g in range(groups)
        ]

    def send_sources(t, white, near, far):
        sibling = lax.ppermute(white, "win", other_core)
        near = lax.ppermute(near, "chan", to_partner(t))
        far = lax.ppermute(far, ("chan", "win"), to_partner_core(t))
        return jnp.concatenate([white, sibling]), jnp.concatenate([near, far])

    def send_terms(t, back):
        return lax.ppermute(back, "chan", to_partner(t)).astype(jnp.float32)

    def by_round(run, *values):
        branches = [functools.partial(run, t) for t in range(1, blocks)]
        return lax.switch(partner[0, 0] - 1, branches, *values)

    tables = [jnp.asarray(v) for v in shift_tables(freqs)]
    sources = by_round(send_sources, *whiten(spectra, counts))
    back_send, *own = terms(*sources, tables, scale)
    back_recv = lax.ppermute(back_send, "win", other_chip)
    back_keep, here, core, chip, cross = terms(*sources, tables, scale, own)
    away = [
        lax.ppermute(value, "win", to)
        for value, to in ((core, other_core), (chip, other_chip), (cross, other_both))
    ]
    back = (back_keep + back_recv.astype(jnp.float32)).astype(jnp.bfloat16)
    back = by_round(send_terms, back)
    return place(here, *away, back)[None, None]


def lag_table(freqs, lags):
    freq = jnp.arange(freqs, dtype=jnp.float32) + freqs // 4
    delay = jnp.arange(lags, dtype=jnp.float32) - lags // 2
    phase = 2.0 * math.pi * freq[:, None] * delay[None, :] / (4.0 * freqs)
    norm = 1.0 / math.sqrt(2.0 * freqs)
    return jnp.stack([jnp.cos(phase), -jnp.sin(phase)]) * norm


def blended_sources(sources, table):
    src = sources.astype(jnp.float32)
    first = src[:, :, 0][:, :, None, :]
    second = src[:, :, 1][:, :, None, :]
    cos_part = table[0].T[None, None]
    sin_part = table[1].T[None, None]
    real_mix = first * cos_part + second * sin_part
    imag_mix = second * cos_part - first * sin_part
    return jnp.stack([real_mix, imag_mix], axis=3).astype(jnp.bfloat16)


def pair_terms(sources, receiver_blocks, table):
    wins, count, two, freqs = sources.shape
    lags = table.shape[2]
    group = math.gcd(count, 32)
    flat_recv = receiver_blocks.reshape(wins, receiver_blocks.shape[1], two * freqs)
    grouped = jnp.moveaxis(sources.reshape(wins, count // group, group, two, freqs), 1, 0)

    def one_group(piece):
        mixed_spectra = blended_sources(piece, table).reshape(wins, group * lags, two * freqs)
        out = jnp.einsum(
            "wmx,wrx->mr", mixed_spectra, flat_recv, preferred_element_type=jnp.float32
        )
        return out.reshape(group, lags, receiver_blocks.shape[1])

    out = lax.map(one_group, grouped).reshape(count, lags, receiver_blocks.shape[1])
    return jnp.transpose(out, (1, 0, 2))


def route_blocks(values, round_flags, levels):
    for level in range(levels):
        moved = from_partner(values, "chan", level)
        values = jnp.where((round_flags >> level) % 2 == 1, moved, values)
    return values


def general_body(spectra, counts, partner):
    white = whiten_local(spectra, counts[0])
    table = lag_table(spectra.shape[3], LAGS)
    levels = lax.axis_size("chan").bit_length() - 1
    windows = spectra.shape[0] * lax.axis_size("win")
    receiver_blocks = route_blocks(white, partner[0, 0], levels)
    out = pair_terms(white[:, :SRC], receiver_blocks, table)
    stacked = lax.psum_scatter(out, "win", scatter_dimension=1, tiled=True)
    return (stacked / math.sqrt(windows))[None, None]


def solution(mesh):
    body = pair_body if mesh.shape["win"] == 4 else general_body
    return jax.shard_map(
        body,
        mesh=mesh,
        in_specs=(P("win", "chan", None, None), P("chan"), P()),
        out_specs=P("chan", None, None, "win", None),
        check_vma=False,
    )
```

```python
import functools
import math

import jax
import jax.numpy as jnp
import numpy as np
from jax import lax
from jax.experimental import pallas as pl
from jax.experimental.pallas import tpu as pltpu
from jax.sharding import PartitionSpec as P

LAGS = 16
SRC = 160
HALF = LAGS // 2
VMEM_LIMIT = 16 * 1024 * 1024


def from_partner(value, axis, stride):
    return lax.ppermute(value, axis, [(i, i ^ 1 << stride) for i in range(lax.axis_size(axis))])


def whiten_local(spectra, count):
    values = spectra.astype(jnp.float32)
    block_size = spectra.shape[1]
    freqs = spectra.shape[3]
    valid = (jnp.arange(block_size, dtype=jnp.int32) < count).astype(jnp.float32)
    freq = jnp.arange(freqs, dtype=jnp.float32)
    taper = 0.75 - 0.25 * jnp.cos(2.0 * math.pi * (freq + 0.5) / freqs)
    power = jnp.mean(values * values, axis=(2, 3))
    scale = valid[None, :] / jnp.sqrt(power + 1e-05)
    return (values * taper * scale[:, :, None, None]).astype(jnp.bfloat16)


def shift_tables(freqs):
    freq = np.arange(freqs, dtype=np.float64) + freqs // 4
    shift = np.arange(1, HALF + 1, dtype=np.float64)
    phase = 2.0 * np.pi * shift[:, None] * freq[None, :] / (4.0 * freqs)
    return np.cos(phase).astype(np.float32), np.sin(phase).astype(np.float32)


def place_of_core():
    spot = lax.axis_index("win")
    return spot // 2, spot % 2


def whole():
    return pl.BlockSpec(memory_space=pltpu.VMEM)


def anywhere():
    return pl.BlockSpec(memory_space=pl.ANY)


def kernel_params():
    return pltpu.CompilerParams(vmem_limit_bytes=VMEM_LIMIT)


def fetch_kernel(source_ref, out_ref, sems):
    windows, parts = out_ref.shape[0], sems.shape[1]
    step = out_ref.shape[1] // parts
    copies = []
    for w in range(windows):
        for i in range(parts):
            part = (w, pl.ds(i * step, step))
            copies.append(
                pltpu.make_async_copy(source_ref.at[part], out_ref.at[part], sems.at[w, i])
            )
            copies[-1].start()
    for copy in copies:
        copy.wait()


def fetch(value):
    return pl.pallas_call(
        fetch_kernel,
        in_specs=[pl.BlockSpec(memory_space=pltpu.HBM)],
        out_specs=whole(),
        out_shape=jax.ShapeDtypeStruct(value.shape, value.dtype),
        scratch_shapes=[pltpu.SemaphoreType.DMA((value.shape[0], 4))],
        compiler_params=kernel_params(),
        name="fetch",
    )(pltpu.with_memory_space_constraint(value, pltpu.HBM))


def whiten_kernel(count_ref, raw_ref, taper_ref, white_ref, *refs):
    *piece_refs, count, sem = refs
    copy = pltpu.make_async_copy(count_ref, count, sem)
    copy.start()
    x, core = place_of_core()
    windows, channels, width = raw_ref.shape
    mine = SRC // 4
    step = 2 * mine
    copy.wait()
    for w in range(windows):
        for index in range(channels // step):
            block = (1 - x, x)[index] if index * step < SRC else index
            begin = block * step
            line = pl.ds(pl.multiple_of(begin, step), step)
            values = raw_ref[w, line, :].astype(jnp.float32)
            power = jnp.sum(values * values, axis=1, keepdims=True) * (1.0 / width)
            row = begin + lax.broadcasted_iota(jnp.int32, (step, 1), 0)
            valid = (row < count[0]).astype(jnp.float32)
            scale = valid / jnp.sqrt(power + 1e-05)
            values = values * taper_ref[...] * scale
            white_ref[w, line, :] = values.astype(jnp.bfloat16)
            if index * step < SRC:
                low, high = values[:mine], values[mine:]
                first = core == 0
                near_ref, far_ref = piece_refs[2 * index:2 * index + 2]
                near_ref[w] = jnp.where(first, low, high).astype(jnp.bfloat16)
                far_ref[w] = jnp.where(first, high, low).astype(jnp.bfloat16)


def whiten(spectra, counts):
    windows, channels, two, freqs = spectra.shape
    width = two * freqs
    freq = np.arange(freqs, dtype=np.float64)
    taper = 0.75 - 0.25 * np.cos(2.0 * np.pi * (freq + 0.5) / freqs)
    taper = np.tile(taper.astype(np.float32), two)[None, :]
    piece = jax.ShapeDtypeStruct((windows, SRC // 4, width), jnp.bfloat16)
    return pl.pallas_call(
        whiten_kernel,
        in_specs=[anywhere(), whole(), whole()],
        out_specs=[whole()] * 5,
        out_shape=[jax.ShapeDtypeStruct((windows, channels, width), jnp.bfloat16)]
        + [piece] * 4,
        scratch_shapes=[pltpu.SMEM((1,), jnp.int32), pltpu.SemaphoreType.DMA],
        compiler_params=kernel_params(),
        name="whiten",
    )(counts, fetch(spectra).reshape(windows, channels, width), jnp.asarray(taper))


def mix(m_ref, piece, cos_ref, sin_ref, start):
    rows, width = piece.shape
    freqs = width // 2
    vrow = v_row(rows)
    low = slice(start, start + 128)
    high = slice(freqs + start, freqs + start + 128)
    real = piece[:, low].astype(jnp.float32)
    imag = piece[:, high].astype(jnp.float32)

    def put(where, cols, values):
        m_ref[where, cols] = jnp.concatenate(values, axis=0).astype(jnp.bfloat16)

    for m in range(0, HALF, 2):
        c = [cos_ref[m + i:m + i + 1, low] for i in range(2)]
        s = [sin_ref[m + i:m + i + 1, low] for i in range(2)]
        line = slice(m * rows, (m + 2) * rows)
        vline = slice(vrow + m * rows, vrow + (m + 2) * rows)
        put(line, low, [real * v for v in c])
        put(line, high, [imag * v for v in c])
        put(vline, low, [imag * -v for v in s])
        put(vline, high, [real * v for v in s])
    fill = jnp.zeros((vrow - (HALF + 1) * rows, 128), jnp.float32)
    for value, cols in ((real, low), (imag, high)):
        put(slice(HALF * rows, vrow), cols, [value, fill])


def v_row(rows):
    return -(-(HALF + 1) * rows // 128) * 128


def times(lhs, rhs):
    return lax.dot_general(
        lhs, rhs, (((1,), (1,)), ((), ())), preferred_element_type=jnp.float32
    )


def terms_kernel(second, scale, recv_ref, cos_ref, sin_ref, *refs):
    if second:
        white_ref, sibling_ref, _, _, _, _, back_ref, *own_refs, even_ref, odd_ref, acc_ref = refs
    else:
        both_ref, back_ref, *own_refs, even_ref, acc_ref = refs
    x, core = place_of_core()
    steps, rows, width = recv_ref.shape
    vrow = v_row(rows)
    wide = HALF * rows
    tile = 256
    starts = range(0, width // 2, 128)

    def multiply(lhs_ref, now_ref, next_ref, later):
        todo = list(starts)
        for n in range(0, acc_ref.shape[1], tile):
            cols = slice(n, min(n + tile, acc_ref.shape[1]))
            acc_ref[:, cols] += times(lhs_ref[...], now_ref[cols, :])
            for start in todo[:2]:
                mix(next_ref, recv_ref.at[later], cos_ref, sin_ref, start)
            todo = todo[2:]

    acc_ref[...] = jnp.zeros_like(acc_ref)
    if second:
        for start in starts:
            mix(even_ref, recv_ref.at[0], cos_ref, sin_ref, start)

        half = steps // 2

        @pl.loop(0, half)
        def _(w):
            multiply(white_ref.at[w], even_ref, odd_ref, half + w)
            multiply(sibling_ref.at[w], odd_ref, even_ref, jnp.minimum(w + 1, half - 1))
    else:
        even_ref[vrow + wide:, :] = jnp.zeros_like(even_ref[vrow + wide:, :])

        @pl.loop(0, steps)
        def _(w):
            for start in starts:
                mix(even_ref, recv_ref.at[w], cos_ref, sin_ref, start)

            @pl.loop(0, acc_ref.shape[1], step=tile)
            def _(n):
                cols = pl.ds(pl.multiple_of(n, tile), tile)
                acc_ref[:, cols] += times(both_ref[w], even_ref[cols, :])

    def split(line):
        u, v = acc_ref[line, :wide] * scale, acc_ref[line, vrow:vrow + wide] * scale
        still = acc_ref[line, wide:wide + rows] * scale
        return u + v, u - v, still

    plus, minus, still = split(pl.ds(SRC, acc_ref.shape[0] - SRC))
    back = jnp.concatenate([minus, plus[:, :wide - rows], still], axis=1)
    back_ref[...] = back.astype(back_ref.dtype)
    mine = SRC // 4
    for i, out in enumerate(own_refs):
        group, spot = (x, 1 - x)[i // 2], (core, 1 - core)[i % 2]
        line = pl.ds(pl.multiple_of((2 * group + spot) * mine, 8), mine)
        plus, minus, still = split(line)
        value = jnp.concatenate([plus, minus[:, :wide - rows], still], axis=1)
        out[1 if second else 0] = value.astype(out.dtype)


def terms(lhs, recv, tables, scale, first=None):
    steps, rows, width = recv.shape
    channels = lhs[0].shape[1]
    wide = 2 * HALF * rows
    columns = v_row(rows) + HALF * rows
    mine = SRC // 4
    second = first is not None
    own = tuple(first) if second else ()
    if not second:
        columns += (-columns) % 256
    return pl.pallas_call(
        functools.partial(terms_kernel, second, scale),
        in_specs=[whole()] * (3 + len(lhs)) + [anywhere()] * len(own),
        out_specs=[whole()] * 5,
        out_shape=[
            jax.ShapeDtypeStruct(
                (channels - SRC, wide), jnp.float32 if second else jnp.bfloat16
            ),
            jax.ShapeDtypeStruct((2, mine, wide), jnp.float32),
        ] + [jax.ShapeDtypeStruct((2, mine, wide), jnp.bfloat16)] * 3,
        input_output_aliases={3 + len(lhs) + i: 1 + i for i in range(len(own))},
        scratch_shapes=[pltpu.VMEM((columns, width), jnp.bfloat16)] * (2 if second else 1)
        + [pltpu.VMEM((channels, columns), jnp.float32)],
        compiler_params=kernel_params(),
        cost_estimate=pl.CostEstimate(
            flops=2 * steps * channels * columns * width,
            bytes_accessed=2 * steps * channels * width,
            transcendentals=0,
        ),
        name="terms_second" if second else "terms_first",
    )(recv, *tables, *lhs, *own)


def place_kernel(
    here_ref, core_ref, chip_ref, cross_ref, back_ref, out_ref, block_ref, sems
):
    x, core = place_of_core()
    lags, mine, channels = block_ref.shape
    swap = core != 0
    sides = []
    for q in range(2):
        index = jnp.where(x == q, 1, 0)
        own = here_ref[index] + chip_ref[1 - index].astype(jnp.float32)
        other = core_ref[index].astype(jnp.float32) + cross_ref[1 - index].astype(jnp.float32)
        sides += [jnp.where(swap, other, own), jnp.where(swap, own, other)]
    back = back_ref[...].astype(jnp.float32).T
    copies = []
    for j in range(lags):
        lag = HALF - 1 - j if j < HALF else j + 1 if j < lags - 1 else HALF
        cols = slice(j * mine, (j + 1) * mine)
        block_ref[lag, :, :SRC] = jnp.concatenate([v[:, cols] for v in sides], axis=1)
        block_ref[lag, :, SRC:] = back[cols]
        copies.append(pltpu.make_async_copy(block_ref.at[lag], out_ref.at[lag], sems.at[lag]))
        copies[-1].start()
    for copy in copies:
        copy.wait()


def place(here, core, chip, cross, back):
    _, mine, wide = here.shape
    shape = (wide // mine, mine, SRC + back.shape[0])
    return pl.pallas_call(
        place_kernel,
        in_specs=[whole()] * 5,
        out_specs=anywhere(),
        out_shape=jax.ShapeDtypeStruct(shape, jnp.float32),
        scratch_shapes=[
            pltpu.VMEM(shape, jnp.float32), pltpu.SemaphoreType.DMA((shape[0],))
        ],
        compiler_params=kernel_params(),
        name="place_lags",
    )(here, core, chip, cross, back)


def pair_body(spectra, counts, partner):
    blocks = lax.axis_size("chan")
    groups = lax.axis_size("win")
    windows, channels, two, freqs = spectra.shape
    scale = 1.0 / (math.sqrt(2.0 * freqs) * math.sqrt(windows * groups))
    other_core = [(i, i ^ 1) for i in range(groups)]
    other_chip = [(i, i ^ 2) for i in range(groups)]
    other_both = [(i, i ^ 3) for i in range(groups)]

    def to_partner(t):
        return [(i, i ^ t) for i in range(blocks)]

    def to_partner_core(t):
        return [
            (i * groups + g, (i ^ t) * groups + (g ^ 1))
            for i in range(blocks)
            for g in range(groups)
        ]

    def send_sources(t, near, far):
        near = lax.ppermute(near, "chan", to_partner(t))
        far = lax.ppermute(far, ("chan", "win"), to_partner_core(t))
        return jnp.concatenate([near, far])

    def send_more(t, near, far, white, sibling, recv):
        second = send_sources(t, near, far)
        both = jnp.concatenate([white, sibling])
        back, *own = terms([both], recv, tables, scale)
        back = lax.ppermute(back, "win", other_chip).astype(jnp.float32)
        return second, back, own

    def send_terms(t, back, core, chip, cross):
        back = lax.ppermute(back, "chan", to_partner(t))
        core = lax.ppermute(core, "win", other_core)
        chip = lax.ppermute(chip, "win", other_chip)
        cross = lax.ppermute(cross, "win", other_both)
        return core, chip, cross, back

    def by_round(run, *values):
        branches = [functools.partial(run, t) for t in range(1, blocks)]
        return lax.switch(partner[0, 0] - 1, branches, *values)

    tables = [jnp.asarray(v) for v in shift_tables(freqs)]
    white, near, far, near_more, far_more = whiten(spectra, counts)
    sibling = lax.ppermute(white, "win", other_core)
    recv = by_round(send_sources, near, far)
    recv, back_recv, own = by_round(send_more, near_more, far_more, white, sibling, recv)
    back_keep, here, *away = terms([white, sibling], recv, tables, scale, own)
    back = (back_keep + back_recv).astype(jnp.bfloat16)
    return place(here, *by_round(send_terms, back, *away))[None, None]


def lag_table(freqs, lags):
    freq = jnp.arange(freqs, dtype=jnp.float32) + freqs // 4
    delay = jnp.arange(lags, dtype=jnp.float32) - lags // 2
    phase = 2.0 * math.pi * freq[:, None] * delay[None, :] / (4.0 * freqs)
    norm = 1.0 / math.sqrt(2.0 * freqs)
    return jnp.stack([jnp.cos(phase), -jnp.sin(phase)]) * norm


def blended_sources(sources, table):
    src = sources.astype(jnp.float32)
    first = src[:, :, 0][:, :, None, :]
    second = src[:, :, 1][:, :, None, :]
    cos_part = table[0].T[None, None]
    sin_part = table[1].T[None, None]
    real_mix = first * cos_part + second * sin_part
    imag_mix = second * cos_part - first * sin_part
    return jnp.stack([real_mix, imag_mix], axis=3).astype(jnp.bfloat16)


def pair_terms(sources, receiver_blocks, table):
    wins, count, two, freqs = sources.shape
    lags = table.shape[2]
    group = math.gcd(count, 32)
    flat_recv = receiver_blocks.reshape(wins, receiver_blocks.shape[1], two * freqs)
    grouped = jnp.moveaxis(sources.reshape(wins, count // group, group, two, freqs), 1, 0)

    def one_group(piece):
        mixed_spectra = blended_sources(piece, table).reshape(wins, group * lags, two * freqs)
        out = jnp.einsum(
            "wmx,wrx->mr", mixed_spectra, flat_recv, preferred_element_type=jnp.float32
        )
        return out.reshape(group, lags, receiver_blocks.shape[1])

    out = lax.map(one_group, grouped).reshape(count, lags, receiver_blocks.shape[1])
    return jnp.transpose(out, (1, 0, 2))


def route_blocks(values, round_flags, levels):
    for level in range(levels):
        moved = from_partner(values, "chan", level)
        values = jnp.where((round_flags >> level) % 2 == 1, moved, values)
    return values


def general_body(spectra, counts, partner):
    white = whiten_local(spectra, counts[0])
    table = lag_table(spectra.shape[3], LAGS)
    levels = lax.axis_size("chan").bit_length() - 1
    windows = spectra.shape[0] * lax.axis_size("win")
    receiver_blocks = route_blocks(white, partner[0, 0], levels)
    out = pair_terms(white[:, :SRC], receiver_blocks, table)
    stacked = lax.psum_scatter(out, "win", scatter_dimension=1, tiled=True)
    return (stacked / math.sqrt(windows))[None, None]


def solution(mesh):
    body = pair_body if mesh.shape["win"] == 4 else general_body
    return jax.shard_map(
        body,
        mesh=mesh,
        in_specs=(P("win", "chan", None, None), P("chan"), P()),
        out_specs=P("chan", None, None, "win", None),
        check_vma=False,
    )
```

```python
import functools
import math

import jax
import jax.numpy as jnp
import numpy as np
from jax import lax
from jax.experimental import pallas as pl
from jax.experimental.pallas import tpu as pltpu
from jax.sharding import PartitionSpec as P

LAGS = 16
SRC = 160
HALF = LAGS // 2
VMEM_LIMIT = 16 * 1024 * 1024


def from_partner(value, axis, stride):
    return lax.ppermute(value, axis, [(i, i ^ 1 << stride) for i in range(lax.axis_size(axis))])


def whiten_local(spectra, count):
    values = spectra.astype(jnp.float32)
    block_size = spectra.shape[1]
    freqs = spectra.shape[3]
    valid = (jnp.arange(block_size, dtype=jnp.int32) < count).astype(jnp.float32)
    freq = jnp.arange(freqs, dtype=jnp.float32)
    taper = 0.75 - 0.25 * jnp.cos(2.0 * math.pi * (freq + 0.5) / freqs)
    power = jnp.mean(values * values, axis=(2, 3))
    scale = valid[None, :] / jnp.sqrt(power + 1e-05)
    return (values * taper * scale[:, :, None, None]).astype(jnp.bfloat16)


def shift_tables(freqs):
    freq = np.arange(freqs, dtype=np.float64) + freqs // 4
    shift = np.arange(1, HALF + 1, dtype=np.float64)
    phase = 2.0 * np.pi * shift[:, None] * freq[None, :] / (4.0 * freqs)
    return np.cos(phase).astype(np.float32), np.sin(phase).astype(np.float32)


def place_of_core():
    spot = lax.axis_index("win")
    return spot // 2, spot % 2


def whole():
    return pl.BlockSpec(memory_space=pltpu.VMEM)


def anywhere():
    return pl.BlockSpec(memory_space=pl.ANY)


def kernel_params():
    return pltpu.CompilerParams(vmem_limit_bytes=VMEM_LIMIT)


def fetch_kernel(source_ref, out_ref, sems):
    windows, parts = out_ref.shape[0], sems.shape[1]
    step = out_ref.shape[1] // parts
    copies = []
    for w in range(windows):
        for i in range(parts):
            part = (w, pl.ds(i * step, step))
            copies.append(
                pltpu.make_async_copy(source_ref.at[part], out_ref.at[part], sems.at[w, i])
            )
            copies[-1].start()
    for copy in copies:
        copy.wait()


def fetch(value):
    return pl.pallas_call(
        fetch_kernel,
        in_specs=[pl.BlockSpec(memory_space=pltpu.HBM)],
        out_specs=whole(),
        out_shape=jax.ShapeDtypeStruct(value.shape, value.dtype),
        scratch_shapes=[pltpu.SemaphoreType.DMA((value.shape[0], 4))],
        compiler_params=kernel_params(),
        name="fetch",
    )(pltpu.with_memory_space_constraint(value, pltpu.HBM))


def whiten_kernel(count_ref, raw_ref, taper_ref, white_ref, *refs):
    *piece_refs, count, sem = refs
    copy = pltpu.make_async_copy(count_ref, count, sem)
    copy.start()
    x, core = place_of_core()
    windows, channels, width = raw_ref.shape
    mine = SRC // 4
    step = 2 * mine
    copy.wait()
    for w in range(windows):
        for index in range(channels // step):
            block = (1 - x, x)[index] if index * step < SRC else index
            begin = block * step
            line = pl.ds(pl.multiple_of(begin, step), step)
            values = raw_ref[w, line, :].astype(jnp.float32)
            power = jnp.sum(values * values, axis=1, keepdims=True) * (1.0 / width)
            row = begin + lax.broadcasted_iota(jnp.int32, (step, 1), 0)
            valid = (row < count[0]).astype(jnp.float32)
            scale = valid / jnp.sqrt(power + 1e-05)
            values = values * taper_ref[...] * scale
            white_ref[w, line, :] = values.astype(jnp.bfloat16)
            if index * step < SRC:
                low, high = values[:mine], values[mine:]
                first = core == 0
                near_ref, far_ref = piece_refs[2 * index:2 * index + 2]
                near_ref[w] = jnp.where(first, low, high).astype(jnp.bfloat16)
                far_ref[w] = jnp.where(first, high, low).astype(jnp.bfloat16)


def whiten(spectra, counts):
    windows, channels, two, freqs = spectra.shape
    width = two * freqs
    freq = np.arange(freqs, dtype=np.float64)
    taper = 0.75 - 0.25 * np.cos(2.0 * np.pi * (freq + 0.5) / freqs)
    taper = np.tile(taper.astype(np.float32), two)[None, :]
    piece = jax.ShapeDtypeStruct((windows, SRC // 4, width), jnp.bfloat16)
    return pl.pallas_call(
        whiten_kernel,
        in_specs=[anywhere(), whole(), whole()],
        out_specs=[whole()] * 5,
        out_shape=[jax.ShapeDtypeStruct((windows, channels, width), jnp.bfloat16)]
        + [piece] * 4,
        scratch_shapes=[pltpu.SMEM((1,), jnp.int32), pltpu.SemaphoreType.DMA],
        compiler_params=kernel_params(),
        name="whiten",
    )(counts, fetch(spectra).reshape(windows, channels, width), jnp.asarray(taper))


def mix(m_ref, piece, cos_ref, sin_ref, start):
    rows, width = piece.shape
    freqs = width // 2
    vrow = v_row(rows)
    low = slice(start, start + 128)
    high = slice(freqs + start, freqs + start + 128)
    real = piece[:, low].astype(jnp.float32)
    imag = piece[:, high].astype(jnp.float32)

    def put(where, cols, values):
        m_ref[where, cols] = jnp.concatenate(values, axis=0).astype(jnp.bfloat16)

    for m in range(0, HALF, 2):
        c = [cos_ref[m + i:m + i + 1, low] for i in range(2)]
        s = [sin_ref[m + i:m + i + 1, low] for i in range(2)]
        line = slice(m * rows, (m + 2) * rows)
        vline = slice(vrow + m * rows, vrow + (m + 2) * rows)
        put(line, low, [real * v for v in c])
        put(line, high, [imag * v for v in c])
        put(vline, low, [imag * -v for v in s])
        put(vline, high, [real * v for v in s])
    fill = jnp.zeros((vrow - (HALF + 1) * rows, 128), jnp.float32)
    for value, cols in ((real, low), (imag, high)):
        put(slice(HALF * rows, vrow), cols, [value, fill])


def v_row(rows):
    return -(-(HALF + 1) * rows // 128) * 128


def times(lhs, rhs):
    return lax.dot_general(
        lhs, rhs, (((1,), (1,)), ((), ())), preferred_element_type=jnp.float32
    )


def terms_kernel(second, scale, recv_ref, cos_ref, sin_ref, *refs):
    if second:
        white_ref, sibling_ref, *refs, even_ref, odd_ref, acc_ref = refs
    else:
        both_ref, *refs, even_ref, acc_ref = refs
    back_ref, here_ref, core_ref, cross_ref, *rest = refs
    x, core = place_of_core()
    steps, rows, width = recv_ref.shape
    vrow = v_row(rows)
    wide = HALF * rows
    tile = 256
    starts = range(0, width // 2, 128)

    def multiply(lhs_ref, now_ref, next_ref, later):
        todo = list(starts)
        for n in range(0, acc_ref.shape[1], tile):
            cols = slice(n, min(n + tile, acc_ref.shape[1]))
            acc_ref[:, cols] += times(lhs_ref[...], now_ref[cols, :])
            for start in todo[:2]:
                mix(next_ref, recv_ref.at[later], cos_ref, sin_ref, start)
            todo = todo[2:]

    acc_ref[...] = jnp.zeros_like(acc_ref)
    if second:
        for start in starts:
            mix(even_ref, recv_ref.at[0], cos_ref, sin_ref, start)

        half = steps // 2

        @pl.loop(0, half)
        def _(w):
            multiply(white_ref.at[w], even_ref, odd_ref, half + w)
            multiply(sibling_ref.at[w], odd_ref, even_ref, jnp.minimum(w + 1, half - 1))
    else:
        even_ref[vrow + wide:, :] = jnp.zeros_like(even_ref[vrow + wide:, :])

        @pl.loop(0, steps)
        def _(w):
            for start in starts:
                mix(even_ref, recv_ref.at[w], cos_ref, sin_ref, start)

            @pl.loop(0, acc_ref.shape[1], step=tile)
            def _(n):
                cols = pl.ds(pl.multiple_of(n, tile), tile)
                acc_ref[:, cols] += times(both_ref[w], even_ref[cols, :])

    def split(line):
        u, v = acc_ref[line, :wide] * scale, acc_ref[line, vrow:vrow + wide] * scale
        still = acc_ref[line, wide:wide + rows] * scale
        return u + v, u - v, still

    def pack(first, last, still):
        return jnp.concatenate([first, last[:, :wide - rows], still], axis=1)

    plus, minus, still = split(pl.ds(SRC, acc_ref.shape[0] - SRC))
    back = pack(minus, plus, still)
    mine = SRC // 4
    own = []
    for group in (x, 1 - x):
        for spot in (core, 1 - core):
            line = pl.ds(pl.multiple_of((2 * group + spot) * mine, 8), mine)
            own.append(pack(*split(line)))
    here, over, chip, cross = own
    if second:
        back_ref[...] = back
        chip_ref, = rest
        chip_ref[...] = chip.astype(chip_ref.dtype)
    else:
        back_ref[...] = jnp.concatenate([back, chip], axis=0).astype(back_ref.dtype)
    here_ref[...] = here
    core_ref[...] = over.astype(core_ref.dtype)
    cross_ref[...] = cross.astype(cross_ref.dtype)


def terms(lhs, recv, tables, scale, second):
    steps, rows, width = recv.shape
    channels = lhs[0].shape[1]
    wide = 2 * HALF * rows
    columns = v_row(rows) + HALF * rows
    mine = SRC // 4
    if not second:
        columns += (-columns) % 256
    rest = channels - SRC
    if second:
        out = [((rest, wide), jnp.float32)]
    else:
        out = [((rest + mine, wide), jnp.bfloat16)]
    out += [((mine, wide), jnp.float32)] + [((mine, wide), jnp.bfloat16)] * (3 if second else 2)
    return pl.pallas_call(
        functools.partial(terms_kernel, second, scale),
        in_specs=[whole()] * (3 + len(lhs)),
        out_specs=[whole()] * len(out),
        out_shape=[jax.ShapeDtypeStruct(*v) for v in out],
        scratch_shapes=[pltpu.VMEM((columns, width), jnp.bfloat16)] * (2 if second else 1)
        + [pltpu.VMEM((channels, columns), jnp.float32)],
        compiler_params=kernel_params(),
        cost_estimate=pl.CostEstimate(
            flops=2 * steps * channels * columns * width,
            bytes_accessed=2 * steps * channels * width,
            transcendentals=0,
        ),
        name="terms_second" if second else "terms_first",
    )(recv, *tables, *lhs)


def after_kernel(*refs):
    del refs


def keep_kernel(*refs):
    count = len(refs) // 2
    for source_ref, out_ref in zip(refs[:count], refs[count:]):
        out_ref[...] = source_ref[...]


def keep(*values):
    return pl.pallas_call(
        keep_kernel,
        in_specs=[whole()] * len(values),
        out_specs=[whole()] * len(values),
        out_shape=[jax.ShapeDtypeStruct(v.shape, v.dtype) for v in values],
        compiler_params=kernel_params(),
        name="keep",
    )(*values)


def after(done, values):
    count = len(values)
    return pl.pallas_call(
        after_kernel,
        in_specs=[anywhere()] * (count + len(done)),
        out_specs=[anywhere()] * count,
        out_shape=[jax.ShapeDtypeStruct(v.shape, v.dtype) for v in values],
        input_output_aliases={i: i for i in range(count)},
        name="after",
    )(*values, *done)


def join_kernel(near_ref, far_ref, out_ref):
    half = near_ref.shape[0]
    out_ref[:half] = near_ref[...]
    out_ref[half:] = far_ref[...]


def join(near, far):
    return pl.pallas_call(
        join_kernel,
        in_specs=[whole()] * 2,
        out_specs=whole(),
        out_shape=jax.ShapeDtypeStruct((2 * near.shape[0], *near.shape[1:]), near.dtype),
        compiler_params=kernel_params(),
        cost_estimate=pl.CostEstimate(flops=30 * 10**9, bytes_accessed=0, transcendentals=0),
        name="join",
    )(near, far)


def place_kernel(
    here_first, chip_first, core_first, cross_first, here_second, back_ref, *refs
):
    *last_refs, out_ref, last_ref, block_ref, last_sems, sems = refs
    last = [
        pltpu.make_async_copy(ref, last_ref.at[i], last_sems.at[i])
        for i, ref in enumerate(last_refs)
    ]
    for copy in last:
        copy.start()
    x, core = place_of_core()
    lags, mine, channels = block_ref.shape
    back = back_ref[...].astype(jnp.float32).T
    for j in range(lags):
        block_ref[lag_at(j), :, SRC:] = back[j * mine:(j + 1) * mine]
    for copy in last:
        copy.wait()
    first = [v[...].astype(jnp.float32) for v in (core_first, cross_first)]
    second = [v.astype(jnp.float32) for v in last_ref[...]]
    own = here_first[...] + second[2], here_second[...] + chip_first[SRC:, :].astype(jnp.float32)
    other = first[0] + second[1], second[0] + first[1]
    sides = []
    for q in range(2):
        mine_q, other_q = (jnp.where(x == q, v[1], v[0]) for v in (own, other))
        sides += [jnp.where(core != 0, other_q, mine_q), jnp.where(core != 0, mine_q, other_q)]
    copies = []
    for j in range(lags):
        lag = lag_at(j)
        cols = slice(j * mine, (j + 1) * mine)
        block_ref[lag, :, :SRC] = jnp.concatenate([v[:, cols] for v in sides], axis=1)
        copies.append(pltpu.make_async_copy(block_ref.at[lag], out_ref.at[lag], sems.at[lag]))
        copies[-1].start()
    for copy in copies:
        copy.wait()


def lag_at(j):
    return HALF - 1 - j if j < HALF else j + 1 if j < LAGS - 1 else HALF


def place(here_first, chip_first, core_first, cross_first, here_second, back, *last):
    mine, wide = here_first.shape
    shape = (LAGS, mine, SRC + back.shape[0])
    return pl.pallas_call(
        place_kernel,
        in_specs=[whole()] * 6 + [anywhere()] * len(last),
        out_specs=anywhere(),
        out_shape=jax.ShapeDtypeStruct(shape, jnp.float32),
        scratch_shapes=[
            pltpu.VMEM((len(last), mine, wide), jnp.bfloat16),
            pltpu.VMEM(shape, jnp.float32),
            pltpu.SemaphoreType.DMA((len(last),)),
            pltpu.SemaphoreType.DMA((LAGS,)),
        ],
        compiler_params=kernel_params(),
        name="place_lags",
    )(here_first, chip_first, core_first, cross_first, here_second, back, *last)


def pair_body(spectra, counts, partner):
    blocks = lax.axis_size("chan")
    groups = lax.axis_size("win")
    windows, channels, two, freqs = spectra.shape
    scale = 1.0 / (math.sqrt(2.0 * freqs) * math.sqrt(windows * groups))
    other_core = [(i, i ^ 1) for i in range(groups)]
    other_chip = [(i, i ^ 2) for i in range(groups)]
    other_both = [(i, i ^ 3) for i in range(groups)]

    def to_partner(t):
        return [(i, i ^ t) for i in range(blocks)]

    def to_partner_core(t):
        return [
            (i * groups + g, (i ^ t) * groups + (g ^ 1))
            for i in range(blocks)
            for g in range(groups)
        ]

    def send_piece(t, near, far):
        near = lax.ppermute(near, "chan", to_partner(t))
        return near, lax.ppermute(far, ("chan", "win"), to_partner_core(t))

    def send_own(core, cross):
        return lax.ppermute(core, "win", other_core), lax.ppermute(cross, "win", other_both)

    def send_sources(t, white, first, second):
        sibling, = keep(lax.ppermute(white, "win", other_core))
        first = send_piece(t, *first)
        second = send_piece(t, *after(first[:1], second))
        both = jnp.concatenate([white, sibling])
        chip, here, *own = terms([both], jnp.concatenate(first), tables, scale, False)
        chip = lax.ppermute(chip, "win", other_chip)
        return join(*second), here, sibling, keep(chip, *send_own(*own))

    def send_terms(t, back, core, cross, chip):
        back, = keep(lax.ppermute(back, "chan", to_partner(t)))
        return back, *send_own(core, cross), lax.ppermute(chip, "win", other_chip)

    def by_round(run, *values):
        branches = [functools.partial(run, t) for t in range(1, blocks)]
        return lax.switch(partner[0, 0] - 1, branches, *values)

    tables = [jnp.asarray(v) for v in shift_tables(freqs)]
    white, *pieces = whiten(spectra, counts)
    recv, here_first, sibling, (chip_first, *away_first) = by_round(
        send_sources, white, pieces[:2], pieces[2:]
    )
    back, here, *own = terms([white, sibling], recv, tables, scale, True)
    back = back + chip_first[:back.shape[0]].astype(jnp.float32)
    back, *last = by_round(send_terms, back.astype(jnp.bfloat16), *own)
    return place(here_first, chip_first, *away_first, here, back, *last)[None, None]


def lag_table(freqs, lags):
    freq = jnp.arange(freqs, dtype=jnp.float32) + freqs // 4
    delay = jnp.arange(lags, dtype=jnp.float32) - lags // 2
    phase = 2.0 * math.pi * freq[:, None] * delay[None, :] / (4.0 * freqs)
    norm = 1.0 / math.sqrt(2.0 * freqs)
    return jnp.stack([jnp.cos(phase), -jnp.sin(phase)]) * norm


def blended_sources(sources, table):
    src = sources.astype(jnp.float32)
    first = src[:, :, 0][:, :, None, :]
    second = src[:, :, 1][:, :, None, :]
    cos_part = table[0].T[None, None]
    sin_part = table[1].T[None, None]
    real_mix = first * cos_part + second * sin_part
    imag_mix = second * cos_part - first * sin_part
    return jnp.stack([real_mix, imag_mix], axis=3).astype(jnp.bfloat16)


def pair_terms(sources, receiver_blocks, table):
    wins, count, two, freqs = sources.shape
    lags = table.shape[2]
    group = math.gcd(count, 32)
    flat_recv = receiver_blocks.reshape(wins, receiver_blocks.shape[1], two * freqs)
    grouped = jnp.moveaxis(sources.reshape(wins, count // group, group, two, freqs), 1, 0)

    def one_group(piece):
        mixed_spectra = blended_sources(piece, table).reshape(wins, group * lags, two * freqs)
        out = jnp.einsum(
            "wmx,wrx->mr", mixed_spectra, flat_recv, preferred_element_type=jnp.float32
        )
        return out.reshape(group, lags, receiver_blocks.shape[1])

    out = lax.map(one_group, grouped).reshape(count, lags, receiver_blocks.shape[1])
    return jnp.transpose(out, (1, 0, 2))


def route_blocks(values, round_flags, levels):
    for level in range(levels):
        moved = from_partner(values, "chan", level)
        values = jnp.where((round_flags >> level) % 2 == 1, moved, values)
    return values


def general_body(spectra, counts, partner):
    white = whiten_local(spectra, counts[0])
    table = lag_table(spectra.shape[3], LAGS)
    levels = lax.axis_size("chan").bit_length() - 1
    windows = spectra.shape[0] * lax.axis_size("win")
    receiver_blocks = route_blocks(white, partner[0, 0], levels)
    out = pair_terms(white[:, :SRC], receiver_blocks, table)
    stacked = lax.psum_scatter(out, "win", scatter_dimension=1, tiled=True)
    return (stacked / math.sqrt(windows))[None, None]


def solution(mesh):
    body = pair_body if mesh.shape["win"] == 4 else general_body
    return jax.shard_map(
        body,
        mesh=mesh,
        in_specs=(P("win", "chan", None, None), P("chan"), P()),
        out_specs=P("chan", None, None, "win", None),
        check_vma=False,
    )
```

```python
import functools
import math

import jax
import jax.numpy as jnp
import numpy as np
from jax import lax
from jax.experimental import pallas as pl
from jax.experimental.pallas import tpu as pltpu
from jax.sharding import PartitionSpec as P

LAGS = 16
SRC = 160
HALF = LAGS // 2
VMEM_LIMIT = 16 * 1024 * 1024


def from_partner(value, axis, stride):
    return lax.ppermute(value, axis, [(i, i ^ 1 << stride) for i in range(lax.axis_size(axis))])


def whiten_local(spectra, count):
    values = spectra.astype(jnp.float32)
    block_size = spectra.shape[1]
    freqs = spectra.shape[3]
    valid = (jnp.arange(block_size, dtype=jnp.int32) < count).astype(jnp.float32)
    freq = jnp.arange(freqs, dtype=jnp.float32)
    taper = 0.75 - 0.25 * jnp.cos(2.0 * math.pi * (freq + 0.5) / freqs)
    power = jnp.mean(values * values, axis=(2, 3))
    scale = valid[None, :] / jnp.sqrt(power + 1e-05)
    return (values * taper * scale[:, :, None, None]).astype(jnp.bfloat16)


def shift_tables(freqs):
    freq = np.arange(freqs, dtype=np.float64) + freqs // 4
    shift = np.arange(1, HALF + 1, dtype=np.float64)
    phase = 2.0 * np.pi * shift[:, None] * freq[None, :] / (4.0 * freqs)
    return np.cos(phase).astype(np.float32), np.sin(phase).astype(np.float32)


def place_of_core():
    spot = lax.axis_index("win")
    return spot // 2, spot % 2


def whole():
    return pl.BlockSpec(memory_space=pltpu.VMEM)


def anywhere():
    return pl.BlockSpec(memory_space=pl.ANY)


def kernel_params():
    return pltpu.CompilerParams(vmem_limit_bytes=VMEM_LIMIT)


def fetch_kernel(source_ref, out_ref, sems):
    windows, parts = out_ref.shape[0], sems.shape[1]
    step = out_ref.shape[1] // parts
    copies = []
    for w in range(windows):
        for i in range(parts):
            part = (w, pl.ds(i * step, step))
            copies.append(
                pltpu.make_async_copy(source_ref.at[part], out_ref.at[part], sems.at[w, i])
            )
            copies[-1].start()
    for copy in copies:
        copy.wait()


def fetch(value):
    return pl.pallas_call(
        fetch_kernel,
        in_specs=[pl.BlockSpec(memory_space=pltpu.HBM)],
        out_specs=whole(),
        out_shape=jax.ShapeDtypeStruct(value.shape, value.dtype),
        scratch_shapes=[pltpu.SemaphoreType.DMA((value.shape[0], 4))],
        compiler_params=kernel_params(),
        name="fetch",
    )(pltpu.with_memory_space_constraint(value, pltpu.HBM))


def whiten_kernel(count_ref, raw_ref, taper_ref, white_ref, near_ref, far_ref, count, sem):
    copy = pltpu.make_async_copy(count_ref, count, sem)
    copy.start()
    _, core = place_of_core()
    windows, channels, width = raw_ref.shape
    mine = SRC // 4
    step = 2 * mine

    copy.wait()
    for w in range(windows):
        for index in range(channels // step):
            line = slice(index * step, (index + 1) * step)
            values = raw_ref[w, line, :].astype(jnp.float32)
            power = jnp.sum(values * values, axis=1, keepdims=True) * (1.0 / width)
            row = index * step + lax.broadcasted_iota(jnp.int32, (step, 1), 0)
            valid = (row < count[0]).astype(jnp.float32)
            scale = valid / jnp.sqrt(power + 1e-05)
            values = values * taper_ref[...] * scale
            white_ref[w, line, :] = values.astype(jnp.bfloat16)
            if index * step < SRC:
                low, high = values[:mine], values[mine:]
                first = core == 0
                near_ref[w, index] = jnp.where(first, low, high).astype(jnp.bfloat16)
                far_ref[w, index] = jnp.where(first, high, low).astype(jnp.bfloat16)


def whiten(spectra, counts):
    windows, channels, two, freqs = spectra.shape
    width = two * freqs
    freq = np.arange(freqs, dtype=np.float64)
    taper = 0.75 - 0.25 * np.cos(2.0 * np.pi * (freq + 0.5) / freqs)
    taper = np.tile(taper.astype(np.float32), two)[None, :]
    piece = jax.ShapeDtypeStruct((windows, 2, SRC // 4, width), jnp.bfloat16)
    return pl.pallas_call(
        whiten_kernel,
        in_specs=[anywhere(), whole(), whole()],
        out_specs=[whole()] * 3,
        out_shape=[
            jax.ShapeDtypeStruct((windows, channels, width), jnp.bfloat16), piece, piece
        ],
        scratch_shapes=[pltpu.SMEM((1,), jnp.int32), pltpu.SemaphoreType.DMA],
        compiler_params=kernel_params(),
        name="whiten",
    )(counts, fetch(spectra).reshape(windows, channels, width), jnp.asarray(taper))


def mix(m_ref, piece, cos_ref, sin_ref, start):
    rows, width = piece.shape
    freqs = width // 2
    vrow = v_row(rows)
    low = slice(start, start + 128)
    high = slice(freqs + start, freqs + start + 128)
    real = piece[:, low].astype(jnp.float32)
    imag = piece[:, high].astype(jnp.float32)

    def put(where, cols, values):
        m_ref[where, cols] = jnp.concatenate(values, axis=0).astype(jnp.bfloat16)

    for m in range(0, HALF, 2):
        c = [cos_ref[m + i:m + i + 1, low] for i in range(2)]
        s = [sin_ref[m + i:m + i + 1, low] for i in range(2)]
        line = slice(m * rows, (m + 2) * rows)
        vline = slice(vrow + m * rows, vrow + (m + 2) * rows)
        put(line, low, [real * v for v in c])
        put(line, high, [imag * v for v in c])
        put(vline, low, [imag * -v for v in s])
        put(vline, high, [real * v for v in s])
    fill = jnp.zeros((vrow - (HALF + 1) * rows, 128), jnp.float32)
    for value, cols in ((real, low), (imag, high)):
        put(slice(HALF * rows, vrow), cols, [value, fill])


def v_row(rows):
    return -(-(HALF + 1) * rows // 128) * 128


def times(lhs, rhs):
    return lax.dot_general(
        lhs, rhs, (((1,), (1,)), ((), ())), preferred_element_type=jnp.float32
    )


def part_kernel(white_ref, recv_ref, cos_ref, sin_ref, part_ref, done_ref, mixed_ref):
    done_ref[...] = jnp.zeros_like(done_ref)
    x, _ = place_of_core()
    windows, _, rows, width = recv_ref.shape
    tile = 256
    used = v_row(rows) + HALF * rows
    part_ref[...] = jnp.zeros_like(part_ref)
    if used < mixed_ref.shape[0]:
        mixed_ref[used:, :] = jnp.zeros_like(mixed_ref[used:, :])

    @pl.loop(0, 2 * windows)
    def _(i):
        group, w = i // windows, i % windows
        q = jnp.where(group == 0, 1 - x, x)
        for start in range(0, width // 2, 128):
            mix(mixed_ref, recv_ref.at[w, q], cos_ref, sin_ref, start)

        @pl.loop(0, mixed_ref.shape[0], step=tile)
        def _(n):
            cols = pl.ds(pl.multiple_of(n, tile), tile)
            part_ref[group, :, cols] += times(white_ref[w], mixed_ref[cols, :])


def part_terms(white, recv, tables):
    windows, channels, width = white.shape
    rows = recv.shape[2]
    columns = v_row(rows) + HALF * rows
    columns += (-columns) % 256
    return pl.pallas_call(
        part_kernel,
        in_specs=[whole()] * 4,
        out_specs=[whole()] * 2,
        out_shape=[
            jax.ShapeDtypeStruct((2, channels, columns), jnp.float32),
            jax.ShapeDtypeStruct((8, 128), jnp.float32),
        ],
        scratch_shapes=[pltpu.VMEM((columns, width), jnp.bfloat16)],
        compiler_params=kernel_params(),
        cost_estimate=pl.CostEstimate(
            flops=2 * 2 * windows * channels * columns * width,
            bytes_accessed=2 * white.size,
            transcendentals=0,
        ),
        name="terms_part",
    )(white, recv, *tables)


def terms_kernel(second, scale, part_ref, sibling_ref, recv_ref, cos_ref, sin_ref, *refs):
    if second:
        refs = refs[4:]
    back_ref, *own_refs, even_ref, odd_ref, acc_ref = refs
    x, core = place_of_core()
    windows, _, rows, width = recv_ref.shape
    vrow = v_row(rows)
    wide = HALF * rows
    starts = list(range(0, width // 2, 128))
    group, q = (1, x) if second else (0, 1 - x)
    tiles = [
        slice(n, min(n + 256, acc_ref.shape[1])) for n in range(0, acc_ref.shape[1], 256)
    ]
    buffers = even_ref, odd_ref
    for start in starts:
        mix(even_ref, recv_ref.at[0, q], cos_ref, sin_ref, start)
    for w in range(windows):
        now_ref, next_ref = buffers[w % 2], buffers[1 - w % 2]
        todo = starts if w + 1 < windows else []
        for cols in tiles:
            before = part_ref[group, :, cols] if w == 0 else acc_ref[:, cols]
            acc_ref[:, cols] = before + times(sibling_ref[w], now_ref[cols, :])
            for start in todo[:2]:
                mix(next_ref, recv_ref.at[w + 1, q], cos_ref, sin_ref, start)
            todo = todo[2:]

    def split(line):
        u, v = acc_ref[line, :wide] * scale, acc_ref[line, vrow:vrow + wide] * scale
        still = acc_ref[line, wide:wide + rows] * scale
        return u + v, u - v, still

    plus, minus, still = split(pl.ds(SRC, acc_ref.shape[0] - SRC))
    back = jnp.concatenate([minus, plus[:, :wide - rows], still], axis=1)
    back_ref[...] = back.astype(back_ref.dtype)
    mine = SRC // 4
    for i, out in enumerate(own_refs):
        group, spot = (x, 1 - x)[i // 2], (core, 1 - core)[i % 2]
        line = pl.ds(pl.multiple_of((2 * group + spot) * mine, 8), mine)
        plus, minus, still = split(line)
        value = jnp.concatenate([plus, minus[:, :wide - rows], still], axis=1)
        out[1 if second else 0] = value.astype(out.dtype)


def terms(part, sibling, recv, tables, scale, first=None):
    windows, channels, width = sibling.shape
    rows = recv.shape[2]
    wide = 2 * HALF * rows
    columns = v_row(rows) + HALF * rows
    mine = SRC // 4
    second = first is not None
    own = () if first is None else tuple(first)
    return pl.pallas_call(
        functools.partial(terms_kernel, second, scale),
        in_specs=[whole()] * 5 + [anywhere()] * len(own),
        out_specs=[whole()] * 5,
        out_shape=[
            jax.ShapeDtypeStruct(
                (channels - SRC, wide), jnp.float32 if second else jnp.bfloat16
            ),
            jax.ShapeDtypeStruct((2, mine, wide), jnp.float32),
        ] + [jax.ShapeDtypeStruct((2, mine, wide), jnp.bfloat16)] * 3,
        input_output_aliases={5 + i: 1 + i for i in range(len(own))},
        scratch_shapes=[
            pltpu.VMEM((columns, width), jnp.bfloat16),
            pltpu.VMEM((columns, width), jnp.bfloat16),
            pltpu.VMEM((channels, columns), jnp.float32),
        ],
        compiler_params=kernel_params(),
        cost_estimate=pl.CostEstimate(
            flops=2 * windows * channels * columns * width,
            bytes_accessed=2 * sibling.size,
            transcendentals=0,
        ),
        name="terms_second" if second else "terms_first",
    )(part, sibling, recv, *tables, *own)


def keep_kernel(source_ref, *refs):
    refs[-1][...] = source_ref[...]


def keep(value, *done):
    return pl.pallas_call(
        keep_kernel,
        in_specs=[whole()] * (1 + len(done)),
        out_specs=whole(),
        out_shape=jax.ShapeDtypeStruct(value.shape, value.dtype),
        compiler_params=kernel_params(),
        name="keep",
    )(value, *done)


def place_kernel(
    here_ref, core_ref, chip_ref, cross_ref, back_ref, out_ref, block_ref, sems
):
    x, core = place_of_core()
    lags, mine, channels = block_ref.shape
    swap = core != 0
    sides = []
    for q in range(2):
        index = jnp.where(x == q, 1, 0)
        own = here_ref[index] + chip_ref[1 - index].astype(jnp.float32)
        other = core_ref[index].astype(jnp.float32) + cross_ref[1 - index].astype(jnp.float32)
        sides += [jnp.where(swap, other, own), jnp.where(swap, own, other)]
    back = back_ref[...].T
    copies = []
    for j in range(lags):
        lag = HALF - 1 - j if j < HALF else j + 1 if j < lags - 1 else HALF
        cols = slice(j * mine, (j + 1) * mine)
        block_ref[lag, :, :SRC] = jnp.concatenate([v[:, cols] for v in sides], axis=1)
        block_ref[lag, :, SRC:] = back[cols]
        copies.append(pltpu.make_async_copy(block_ref.at[lag], out_ref.at[lag], sems.at[lag]))
        copies[-1].start()
    for copy in copies:
        copy.wait()


def place(here, core, chip, cross, back):
    _, mine, wide = here.shape
    shape = (wide // mine, mine, SRC + back.shape[0])
    return pl.pallas_call(
        place_kernel,
        in_specs=[whole()] * 5,
        out_specs=anywhere(),
        out_shape=jax.ShapeDtypeStruct(shape, jnp.float32),
        scratch_shapes=[
            pltpu.VMEM(shape, jnp.float32), pltpu.SemaphoreType.DMA((shape[0],))
        ],
        compiler_params=kernel_params(),
        name="place_lags",
    )(here, core, chip, cross, back)


def pair_body(spectra, counts, partner):
    blocks = lax.axis_size("chan")
    groups = lax.axis_size("win")
    windows, channels, two, freqs = spectra.shape
    scale = 1.0 / (math.sqrt(2.0 * freqs) * math.sqrt(windows * groups))
    other_core = [(i, i ^ 1) for i in range(groups)]
    other_chip = [(i, i ^ 2) for i in range(groups)]
    other_both = [(i, i ^ 3) for i in range(groups)]

    def to_partner(t):
        return [(i, i ^ t) for i in range(blocks)]

    def to_partner_core(t):
        return [
            (i * groups + g, (i ^ t) * groups + (g ^ 1))
            for i in range(blocks)
            for g in range(groups)
        ]

    def send_sources(t, white, near, far):
        sibling = lax.ppermute(white, "win", other_core)
        near = lax.ppermute(near, "chan", to_partner(t))
        far = lax.ppermute(far, ("chan", "win"), to_partner_core(t))
        part, done = part_terms(white, near, tables)
        return part, keep(sibling), keep(far, done)

    def send_terms(t, back):
        return lax.ppermute(back, "chan", to_partner(t)).astype(jnp.float32)

    def by_round(run, *values):
        branches = [functools.partial(run, t) for t in range(1, blocks)]
        return lax.switch(partner[0, 0] - 1, branches, *values)

    tables = [jnp.asarray(v) for v in shift_tables(freqs)]
    sources = by_round(send_sources, *whiten(spectra, counts))
    back_send, *own = terms(*sources, tables, scale)
    back_recv = lax.ppermute(back_send, "win", other_chip)
    back_keep, here, core, chip, cross = terms(*sources, tables, scale, own)
    away = [
        lax.ppermute(value, "win", to)
        for value, to in ((core, other_core), (chip, other_chip), (cross, other_both))
    ]
    back = (back_keep + back_recv.astype(jnp.float32)).astype(jnp.bfloat16)
    back = by_round(send_terms, back)
    return place(here, *away, back)[None, None]


def lag_table(freqs, lags):
    freq = jnp.arange(freqs, dtype=jnp.float32) + freqs // 4
    delay = jnp.arange(lags, dtype=jnp.float32) - lags // 2
    phase = 2.0 * math.pi * freq[:, None] * delay[None, :] / (4.0 * freqs)
    norm = 1.0 / math.sqrt(2.0 * freqs)
    return jnp.stack([jnp.cos(phase), -jnp.sin(phase)]) * norm


def blended_sources(sources, table):
    src = sources.astype(jnp.float32)
    first = src[:, :, 0][:, :, None, :]
    second = src[:, :, 1][:, :, None, :]
    cos_part = table[0].T[None, None]
    sin_part = table[1].T[None, None]
    real_mix = first * cos_part + second * sin_part
    imag_mix = second * cos_part - first * sin_part
    return jnp.stack([real_mix, imag_mix], axis=3).astype(jnp.bfloat16)


def pair_terms(sources, receiver_blocks, table):
    wins, count, two, freqs = sources.shape
    lags = table.shape[2]
    group = math.gcd(count, 32)
    flat_recv = receiver_blocks.reshape(wins, receiver_blocks.shape[1], two * freqs)
    grouped = jnp.moveaxis(sources.reshape(wins, count // group, group, two, freqs), 1, 0)

    def one_group(piece):
        mixed_spectra = blended_sources(piece, table).reshape(wins, group * lags, two * freqs)
        out = jnp.einsum(
            "wmx,wrx->mr", mixed_spectra, flat_recv, preferred_element_type=jnp.float32
        )
        return out.reshape(group, lags, receiver_blocks.shape[1])

    out = lax.map(one_group, grouped).reshape(count, lags, receiver_blocks.shape[1])
    return jnp.transpose(out, (1, 0, 2))


def route_blocks(values, round_flags, levels):
    for level in range(levels):
        moved = from_partner(values, "chan", level)
        values = jnp.where((round_flags >> level) % 2 == 1, moved, values)
    return values


def general_body(spectra, counts, partner):
    white = whiten_local(spectra, counts[0])
    table = lag_table(spectra.shape[3], LAGS)
    levels = lax.axis_size("chan").bit_length() - 1
    windows = spectra.shape[0] * lax.axis_size("win")
    receiver_blocks = route_blocks(white, partner[0, 0], levels)
    out = pair_terms(white[:, :SRC], receiver_blocks, table)
    stacked = lax.psum_scatter(out, "win", scatter_dimension=1, tiled=True)
    return (stacked / math.sqrt(windows))[None, None]


def solution(mesh):
    body = pair_body if mesh.shape["win"] == 4 else general_body
    return jax.shard_map(
        body,
        mesh=mesh,
        in_specs=(P("win", "chan", None, None), P("chan"), P()),
        out_specs=P("chan", None, None, "win", None),
        check_vma=False,
    )
```

```python
import functools
import math

import jax
import jax.numpy as jnp
import numpy as np
from jax import lax
from jax.experimental import pallas as pl
from jax.experimental.pallas import tpu as pltpu
from jax.sharding import PartitionSpec as P

LAGS = 16
SRC = 160
HALF = LAGS // 2
VMEM_LIMIT = 16 * 1024 * 1024


def from_partner(value, axis, stride):
    return lax.ppermute(value, axis, [(i, i ^ 1 << stride) for i in range(lax.axis_size(axis))])


def whiten_local(spectra, count):
    values = spectra.astype(jnp.float32)
    block_size = spectra.shape[1]
    freqs = spectra.shape[3]
    valid = (jnp.arange(block_size, dtype=jnp.int32) < count).astype(jnp.float32)
    freq = jnp.arange(freqs, dtype=jnp.float32)
    taper = 0.75 - 0.25 * jnp.cos(2.0 * math.pi * (freq + 0.5) / freqs)
    power = jnp.mean(values * values, axis=(2, 3))
    scale = valid[None, :] / jnp.sqrt(power + 1e-05)
    return (values * taper * scale[:, :, None, None]).astype(jnp.bfloat16)


def shift_tables(freqs):
    freq = np.arange(freqs, dtype=np.float64) + freqs // 4
    shift = np.arange(1, HALF + 1, dtype=np.float64)
    phase = 2.0 * np.pi * shift[:, None] * freq[None, :] / (4.0 * freqs)
    return np.cos(phase).astype(np.float32), np.sin(phase).astype(np.float32)


def place_of_core():
    spot = lax.axis_index("win")
    return spot // 2, spot % 2


def whole():
    return pl.BlockSpec(memory_space=pltpu.VMEM)


def anywhere():
    return pl.BlockSpec(memory_space=pl.ANY)


def kernel_params():
    return pltpu.CompilerParams(vmem_limit_bytes=VMEM_LIMIT)


def fetch_kernel(source_ref, out_ref, sems):
    windows, parts = out_ref.shape[0], sems.shape[1]
    step = out_ref.shape[1] // parts
    copies = []
    for w in range(windows):
        for i in range(parts):
            part = (w, pl.ds(i * step, step))
            copies.append(
                pltpu.make_async_copy(source_ref.at[part], out_ref.at[part], sems.at[w, i])
            )
            copies[-1].start()
    for copy in copies:
        copy.wait()


def fetch(value):
    return pl.pallas_call(
        fetch_kernel,
        in_specs=[pl.BlockSpec(memory_space=pltpu.HBM)],
        out_specs=whole(),
        out_shape=jax.ShapeDtypeStruct(value.shape, value.dtype),
        scratch_shapes=[pltpu.SemaphoreType.DMA((value.shape[0], 4))],
        compiler_params=kernel_params(),
        name="fetch",
    )(pltpu.with_memory_space_constraint(value, pltpu.HBM))


def whiten_kernel(count_ref, raw_ref, taper_ref, white_ref, near_ref, far_ref, count, sem):
    copy = pltpu.make_async_copy(count_ref, count, sem)
    copy.start()
    _, core = place_of_core()
    windows, channels, width = raw_ref.shape
    mine = SRC // 4
    step = 2 * mine

    copy.wait()
    for w in range(windows):
        for index in range(channels // step):
            line = slice(index * step, (index + 1) * step)
            values = raw_ref[w, line, :].astype(jnp.float32)
            power = jnp.sum(values * values, axis=1, keepdims=True) * (1.0 / width)
            row = index * step + lax.broadcasted_iota(jnp.int32, (step, 1), 0)
            valid = (row < count[0]).astype(jnp.float32)
            scale = valid / jnp.sqrt(power + 1e-05)
            values = values * taper_ref[...] * scale
            white_ref[w, line, :] = values.astype(jnp.bfloat16)
            if index * step < SRC:
                low, high = values[:mine], values[mine:]
                first = core == 0
                near_ref[w, index] = jnp.where(first, low, high).astype(jnp.bfloat16)
                far_ref[w, index] = jnp.where(first, high, low).astype(jnp.bfloat16)


def whiten(spectra, counts):
    windows, channels, two, freqs = spectra.shape
    width = two * freqs
    freq = np.arange(freqs, dtype=np.float64)
    taper = 0.75 - 0.25 * np.cos(2.0 * np.pi * (freq + 0.5) / freqs)
    taper = np.tile(taper.astype(np.float32), two)[None, :]
    piece = jax.ShapeDtypeStruct((windows, 2, SRC // 4, width), jnp.bfloat16)
    return pl.pallas_call(
        whiten_kernel,
        in_specs=[anywhere(), whole(), whole()],
        out_specs=[whole()] * 3,
        out_shape=[
            jax.ShapeDtypeStruct((windows, channels, width), jnp.bfloat16), piece, piece
        ],
        scratch_shapes=[pltpu.SMEM((1,), jnp.int32), pltpu.SemaphoreType.DMA],
        compiler_params=kernel_params(),
        name="whiten",
    )(counts, fetch(spectra).reshape(windows, channels, width), jnp.asarray(taper))


def mix(m_ref, piece, cos_ref, sin_ref, start):
    rows, width = piece.shape
    freqs = width // 2
    vrow = v_row(rows)
    low = slice(start, start + 128)
    high = slice(freqs + start, freqs + start + 128)
    real = piece[:, low].astype(jnp.float32)
    imag = piece[:, high].astype(jnp.float32)

    def put(where, cols, values):
        m_ref[where, cols] = jnp.concatenate(values, axis=0).astype(jnp.bfloat16)

    for m in range(0, HALF, 2):
        c = [cos_ref[m + i:m + i + 1, low] for i in range(2)]
        s = [sin_ref[m + i:m + i + 1, low] for i in range(2)]
        line = slice(m * rows, (m + 2) * rows)
        vline = slice(vrow + m * rows, vrow + (m + 2) * rows)
        put(line, low, [real * v for v in c])
        put(line, high, [imag * v for v in c])
        put(vline, low, [imag * -v for v in s])
        put(vline, high, [real * v for v in s])
    fill = jnp.zeros((vrow - (HALF + 1) * rows, 128), jnp.float32)
    for value, cols in ((real, low), (imag, high)):
        put(slice(HALF * rows, vrow), cols, [value, fill])


def v_row(rows):
    return -(-(HALF + 1) * rows // 128) * 128


def times(lhs, rhs):
    return lax.dot_general(
        lhs, rhs, (((1,), (1,)), ((), ())), preferred_element_type=jnp.float32
    )


def part_kernel(white_ref, recv_ref, cos_ref, sin_ref, part_ref, done_ref, mixed_ref):
    done_ref[...] = jnp.zeros_like(done_ref)
    x, _ = place_of_core()
    windows, _, rows, width = recv_ref.shape
    tile = 256
    used = v_row(rows) + HALF * rows
    part_ref[...] = jnp.zeros_like(part_ref)
    if used < mixed_ref.shape[0]:
        mixed_ref[used:, :] = jnp.zeros_like(mixed_ref[used:, :])

    @pl.loop(0, 2 * windows)
    def _(i):
        group, w = i // windows, i % windows
        q = jnp.where(group == 0, 1 - x, x)
        for start in range(0, width // 2, 128):
            mix(mixed_ref, recv_ref.at[w, q], cos_ref, sin_ref, start)

        @pl.loop(0, mixed_ref.shape[0], step=tile)
        def _(n):
            cols = pl.ds(pl.multiple_of(n, tile), tile)
            part_ref[group, :, cols] += times(white_ref[w], mixed_ref[cols, :])


def part_terms(white, recv, tables):
    windows, channels, width = white.shape
    rows = recv.shape[2]
    columns = v_row(rows) + HALF * rows
    columns += (-columns) % 256
    return pl.pallas_call(
        part_kernel,
        in_specs=[whole()] * 4,
        out_specs=[whole()] * 2,
        out_shape=[
            jax.ShapeDtypeStruct((2, channels, columns), jnp.float32),
            jax.ShapeDtypeStruct((8, 128), jnp.float32),
        ],
        scratch_shapes=[pltpu.VMEM((columns, width), jnp.bfloat16)],
        compiler_params=kernel_params(),
        cost_estimate=pl.CostEstimate(
            flops=2 * 2 * windows * channels * columns * width,
            bytes_accessed=2 * white.size,
            transcendentals=0,
        ),
        name="terms_part",
    )(white, recv, *tables)


def terms_kernel(second, scale, part_ref, sibling_ref, recv_ref, cos_ref, sin_ref, *refs):
    if second:
        refs = refs[4:]
    back_ref, *own_refs, even_ref, odd_ref, acc_ref = refs
    x, core = place_of_core()
    windows, _, rows, width = recv_ref.shape
    vrow = v_row(rows)
    wide = HALF * rows
    starts = list(range(0, width // 2, 128))
    group, q = (1, x) if second else (0, 1 - x)
    tiles = [
        slice(n, min(n + 256, acc_ref.shape[1])) for n in range(0, acc_ref.shape[1], 256)
    ]
    buffers = even_ref, odd_ref
    for start in starts:
        mix(even_ref, recv_ref.at[0, q], cos_ref, sin_ref, start)
    for w in range(windows):
        now_ref, next_ref = buffers[w % 2], buffers[1 - w % 2]
        todo = starts if w + 1 < windows else []
        for cols in tiles:
            before = part_ref[group, :, cols] if w == 0 else acc_ref[:, cols]
            acc_ref[:, cols] = before + times(sibling_ref[w], now_ref[cols, :])
            for start in todo[:2]:
                mix(next_ref, recv_ref.at[w + 1, q], cos_ref, sin_ref, start)
            todo = todo[2:]

    def split(line):
        u, v = acc_ref[line, :wide] * scale, acc_ref[line, vrow:vrow + wide] * scale
        still = acc_ref[line, wide:wide + rows] * scale
        return u + v, u - v, still

    plus, minus, still = split(pl.ds(SRC, acc_ref.shape[0] - SRC))
    back = jnp.concatenate([minus, plus[:, :wide - rows], still], axis=1)
    back_ref[...] = back.astype(back_ref.dtype)
    mine = SRC // 4
    for i, out in enumerate(own_refs):
        group, spot = (x, 1 - x)[i // 2], (core, 1 - core)[i % 2]
        line = pl.ds(pl.multiple_of((2 * group + spot) * mine, 8), mine)
        plus, minus, still = split(line)
        value = jnp.concatenate([plus, minus[:, :wide - rows], still], axis=1)
        out[1 if second else 0] = value.astype(out.dtype)


def terms(part, sibling, recv, tables, scale, first=None):
    windows, channels, width = sibling.shape
    rows = recv.shape[2]
    wide = 2 * HALF * rows
    columns = v_row(rows) + HALF * rows
    mine = SRC // 4
    second = first is not None
    own = () if first is None else tuple(first)
    return pl.pallas_call(
        functools.partial(terms_kernel, second, scale),
        in_specs=[whole()] * 5 + [anywhere()] * len(own),
        out_specs=[whole()] * 5,
        out_shape=[
            jax.ShapeDtypeStruct(
                (channels - SRC, wide), jnp.float32 if second else jnp.bfloat16
            ),
            jax.ShapeDtypeStruct((2, mine, wide), jnp.float32),
        ] + [jax.ShapeDtypeStruct((2, mine, wide), jnp.bfloat16)] * 3,
        input_output_aliases={5 + i: 1 + i for i in range(len(own))},
        scratch_shapes=[
            pltpu.VMEM((columns, width), jnp.bfloat16),
            pltpu.VMEM((columns, width), jnp.bfloat16),
            pltpu.VMEM((channels, columns), jnp.float32),
        ],
        compiler_params=kernel_params(),
        cost_estimate=pl.CostEstimate(
            flops=2 * windows * channels * columns * width,
            bytes_accessed=2 * sibling.size,
            transcendentals=0,
        ),
        name="terms_second" if second else "terms_first",
    )(part, sibling, recv, *tables, *own)


def keep_kernel(source_ref, *refs):
    refs[-1][...] = source_ref[...]


def keep(value, *done):
    return pl.pallas_call(
        keep_kernel,
        in_specs=[whole()] * (1 + len(done)),
        out_specs=whole(),
        out_shape=jax.ShapeDtypeStruct(value.shape, value.dtype),
        compiler_params=kernel_params(),
        name="keep",
    )(value, *done)


def place_kernel(
    here_ref, core_ref, chip_ref, cross_ref, back_ref, out_ref, block_ref, sems
):
    x, core = place_of_core()
    lags, mine, channels = block_ref.shape
    swap = core != 0
    sides = []
    for q in range(2):
        index = jnp.where(x == q, 1, 0)
        own = here_ref[index] + chip_ref[1 - index].astype(jnp.float32)
        other = core_ref[index].astype(jnp.float32) + cross_ref[1 - index].astype(jnp.float32)
        sides += [jnp.where(swap, other, own), jnp.where(swap, own, other)]
    back = back_ref[...].astype(jnp.float32).T
    copies = []
    for j in range(lags):
        lag = HALF - 1 - j if j < HALF else j + 1 if j < lags - 1 else HALF
        cols = slice(j * mine, (j + 1) * mine)
        block_ref[lag, :, :SRC] = jnp.concatenate([v[:, cols] for v in sides], axis=1)
        block_ref[lag, :, SRC:] = back[cols]
        copies.append(pltpu.make_async_copy(block_ref.at[lag], out_ref.at[lag], sems.at[lag]))
        copies[-1].start()
    for copy in copies:
        copy.wait()


def place(here, core, chip, cross, back):
    _, mine, wide = here.shape
    shape = (wide // mine, mine, SRC + back.shape[0])
    return pl.pallas_call(
        place_kernel,
        in_specs=[whole()] * 5,
        out_specs=anywhere(),
        out_shape=jax.ShapeDtypeStruct(shape, jnp.float32),
        scratch_shapes=[
            pltpu.VMEM(shape, jnp.float32), pltpu.SemaphoreType.DMA((shape[0],))
        ],
        compiler_params=kernel_params(),
        name="place_lags",
    )(here, core, chip, cross, back)


def pair_body(spectra, counts, partner):
    blocks = lax.axis_size("chan")
    groups = lax.axis_size("win")
    windows, channels, two, freqs = spectra.shape
    scale = 1.0 / (math.sqrt(2.0 * freqs) * math.sqrt(windows * groups))
    other_core = [(i, i ^ 1) for i in range(groups)]
    other_chip = [(i, i ^ 2) for i in range(groups)]
    other_both = [(i, i ^ 3) for i in range(groups)]

    def to_partner(t):
        return [(i, i ^ t) for i in range(blocks)]

    def to_partner_core(t):
        return [
            (i * groups + g, (i ^ t) * groups + (g ^ 1))
            for i in range(blocks)
            for g in range(groups)
        ]

    def send_sources(t, white, near, far):
        sibling = lax.ppermute(white, "win", other_core)
        near = lax.ppermute(near, "chan", to_partner(t))
        far = lax.ppermute(far, ("chan", "win"), to_partner_core(t))
        part, done = part_terms(white, near, tables)
        return part, keep(sibling), keep(far, done)

    def send_terms(t, back, chip, cross):
        back = lax.ppermute(back, "chan", to_partner(t))
        chip = lax.ppermute(chip, "win", other_chip)
        cross = lax.ppermute(cross, "win", other_both)
        return keep(chip), keep(cross), keep(back)

    def by_round(run, *values):
        branches = [functools.partial(run, t) for t in range(1, blocks)]
        return lax.switch(partner[0, 0] - 1, branches, *values)

    tables = [jnp.asarray(v) for v in shift_tables(freqs)]
    sources = by_round(send_sources, *whiten(spectra, counts))
    back_send, *own = terms(*sources, tables, scale)
    back_recv = lax.ppermute(back_send, "win", other_chip)
    back_keep, here, core, chip, cross = terms(*sources, tables, scale, own)
    core = lax.ppermute(core, "win", other_core)
    back = (back_keep + back_recv.astype(jnp.float32)).astype(jnp.bfloat16)
    return place(here, core, *by_round(send_terms, back, chip, cross))[None, None]


def lag_table(freqs, lags):
    freq = jnp.arange(freqs, dtype=jnp.float32) + freqs // 4
    delay = jnp.arange(lags, dtype=jnp.float32) - lags // 2
    phase = 2.0 * math.pi * freq[:, None] * delay[None, :] / (4.0 * freqs)
    norm = 1.0 / math.sqrt(2.0 * freqs)
    return jnp.stack([jnp.cos(phase), -jnp.sin(phase)]) * norm


def blended_sources(sources, table):
    src = sources.astype(jnp.float32)
    first = src[:, :, 0][:, :, None, :]
    second = src[:, :, 1][:, :, None, :]
    cos_part = table[0].T[None, None]
    sin_part = table[1].T[None, None]
    real_mix = first * cos_part + second * sin_part
    imag_mix = second * cos_part - first * sin_part
    return jnp.stack([real_mix, imag_mix], axis=3).astype(jnp.bfloat16)


def pair_terms(sources, receiver_blocks, table):
    wins, count, two, freqs = sources.shape
    lags = table.shape[2]
    group = math.gcd(count, 32)
    flat_recv = receiver_blocks.reshape(wins, receiver_blocks.shape[1], two * freqs)
    grouped = jnp.moveaxis(sources.reshape(wins, count // group, group, two, freqs), 1, 0)

    def one_group(piece):
        mixed_spectra = blended_sources(piece, table).reshape(wins, group * lags, two * freqs)
        out = jnp.einsum(
            "wmx,wrx->mr", mixed_spectra, flat_recv, preferred_element_type=jnp.float32
        )
        return out.reshape(group, lags, receiver_blocks.shape[1])

    out = lax.map(one_group, grouped).reshape(count, lags, receiver_blocks.shape[1])
    return jnp.transpose(out, (1, 0, 2))


def route_blocks(values, round_flags, levels):
    for level in range(levels):
        moved = from_partner(values, "chan", level)
        values = jnp.where((round_flags >> level) % 2 == 1, moved, values)
    return values


def general_body(spectra, counts, partner):
    white = whiten_local(spectra, counts[0])
    table = lag_table(spectra.shape[3], LAGS)
    levels = lax.axis_size("chan").bit_length() - 1
    windows = spectra.shape[0] * lax.axis_size("win")
    receiver_blocks = route_blocks(white, partner[0, 0], levels)
    out = pair_terms(white[:, :SRC], receiver_blocks, table)
    stacked = lax.psum_scatter(out, "win", scatter_dimension=1, tiled=True)
    return (stacked / math.sqrt(windows))[None, None]


def solution(mesh):
    body = pair_body if mesh.shape["win"] == 4 else general_body
    return jax.shard_map(
        body,
        mesh=mesh,
        in_specs=(P("win", "chan", None, None), P("chan"), P()),
        out_specs=P("chan", None, None, "win", None),
        check_vma=False,
    )
```

```python
import functools
import math

import jax
import jax.numpy as jnp
import numpy as np
from jax import lax
from jax.experimental import pallas as pl
from jax.experimental.pallas import tpu as pltpu
from jax.sharding import PartitionSpec as P

LAGS = 16
SRC = 160
HALF = LAGS // 2
VMEM_LIMIT = 16 * 1024 * 1024


def from_partner(value, axis, stride):
    return lax.ppermute(value, axis, [(i, i ^ 1 << stride) for i in range(lax.axis_size(axis))])


def whiten_local(spectra, count):
    values = spectra.astype(jnp.float32)
    block_size = spectra.shape[1]
    freqs = spectra.shape[3]
    valid = (jnp.arange(block_size, dtype=jnp.int32) < count).astype(jnp.float32)
    freq = jnp.arange(freqs, dtype=jnp.float32)
    taper = 0.75 - 0.25 * jnp.cos(2.0 * math.pi * (freq + 0.5) / freqs)
    power = jnp.mean(values * values, axis=(2, 3))
    scale = valid[None, :] / jnp.sqrt(power + 1e-05)
    return (values * taper * scale[:, :, None, None]).astype(jnp.bfloat16)


def shift_tables(freqs):
    freq = np.arange(freqs, dtype=np.float64) + freqs // 4
    shift = np.arange(1, HALF + 1, dtype=np.float64)
    phase = 2.0 * np.pi * shift[:, None] * freq[None, :] / (4.0 * freqs)
    return np.cos(phase).astype(np.float32), np.sin(phase).astype(np.float32)


def place_of_core():
    spot = lax.axis_index("win")
    return spot // 2, spot % 2


def whole():
    return pl.BlockSpec(memory_space=pltpu.VMEM)


def anywhere():
    return pl.BlockSpec(memory_space=pl.ANY)


def kernel_params():
    return pltpu.CompilerParams(vmem_limit_bytes=VMEM_LIMIT)


def fetch_kernel(source_ref, out_ref, sems):
    windows, parts = out_ref.shape[0], sems.shape[1]
    step = out_ref.shape[1] // parts
    copies = []
    for w in range(windows):
        for i in range(parts):
            part = (w, pl.ds(i * step, step))
            copies.append(
                pltpu.make_async_copy(source_ref.at[part], out_ref.at[part], sems.at[w, i])
            )
            copies[-1].start()
    for copy in copies:
        copy.wait()


def fetch(value):
    return pl.pallas_call(
        fetch_kernel,
        in_specs=[pl.BlockSpec(memory_space=pltpu.HBM)],
        out_specs=whole(),
        out_shape=jax.ShapeDtypeStruct(value.shape, value.dtype),
        scratch_shapes=[pltpu.SemaphoreType.DMA((value.shape[0], 4))],
        compiler_params=kernel_params(),
        name="fetch",
    )(pltpu.with_memory_space_constraint(value, pltpu.HBM))


def whiten_kernel(count_ref, raw_ref, taper_ref, white_ref, *refs):
    *piece_refs, count, sem = refs
    copy = pltpu.make_async_copy(count_ref, count, sem)
    copy.start()
    x, core = place_of_core()
    windows, channels, width = raw_ref.shape
    mine = SRC // 4
    step = 2 * mine
    copy.wait()
    for w in range(windows):
        for index in range(channels // step):
            block = (1 - x, x)[index] if index * step < SRC else index
            begin = block * step
            line = pl.ds(pl.multiple_of(begin, step), step)
            values = raw_ref[w, line, :].astype(jnp.float32)
            power = jnp.sum(values * values, axis=1, keepdims=True) * (1.0 / width)
            row = begin + lax.broadcasted_iota(jnp.int32, (step, 1), 0)
            valid = (row < count[0]).astype(jnp.float32)
            scale = valid / jnp.sqrt(power + 1e-05)
            values = values * taper_ref[...] * scale
            white_ref[w, line, :] = values.astype(jnp.bfloat16)
            if index * step < SRC:
                low, high = values[:mine], values[mine:]
                first = core == 0
                near_ref, far_ref = piece_refs[2 * index:2 * index + 2]
                near_ref[w] = jnp.where(first, low, high).astype(jnp.bfloat16)
                far_ref[w] = jnp.where(first, high, low).astype(jnp.bfloat16)


def whiten(spectra, counts):
    windows, channels, two, freqs = spectra.shape
    width = two * freqs
    freq = np.arange(freqs, dtype=np.float64)
    taper = 0.75 - 0.25 * np.cos(2.0 * np.pi * (freq + 0.5) / freqs)
    taper = np.tile(taper.astype(np.float32), two)[None, :]
    piece = jax.ShapeDtypeStruct((windows, SRC // 4, width), jnp.bfloat16)
    return pl.pallas_call(
        whiten_kernel,
        in_specs=[anywhere(), whole(), whole()],
        out_specs=[whole()] * 5,
        out_shape=[jax.ShapeDtypeStruct((windows, channels, width), jnp.bfloat16)]
        + [piece] * 4,
        scratch_shapes=[pltpu.SMEM((1,), jnp.int32), pltpu.SemaphoreType.DMA],
        compiler_params=kernel_params(),
        name="whiten",
    )(counts, fetch(spectra).reshape(windows, channels, width), jnp.asarray(taper))


def mix(m_ref, piece, cos_ref, sin_ref, start):
    rows, width = piece.shape
    freqs = width // 2
    vrow = v_row(rows)
    low = slice(start, start + 128)
    high = slice(freqs + start, freqs + start + 128)
    real = piece[:, low].astype(jnp.float32)
    imag = piece[:, high].astype(jnp.float32)

    def put(where, cols, values):
        m_ref[where, cols] = jnp.concatenate(values, axis=0).astype(jnp.bfloat16)

    for m in range(0, HALF, 2):
        c = [cos_ref[m + i:m + i + 1, low] for i in range(2)]
        s = [sin_ref[m + i:m + i + 1, low] for i in range(2)]
        line = slice(m * rows, (m + 2) * rows)
        vline = slice(vrow + m * rows, vrow + (m + 2) * rows)
        put(line, low, [real * v for v in c])
        put(line, high, [imag * v for v in c])
        put(vline, low, [imag * -v for v in s])
        put(vline, high, [real * v for v in s])
    fill = jnp.zeros((vrow - (HALF + 1) * rows, 128), jnp.float32)
    for value, cols in ((real, low), (imag, high)):
        put(slice(HALF * rows, vrow), cols, [value, fill])


def v_row(rows):
    return -(-(HALF + 1) * rows // 128) * 128


def times(lhs, rhs):
    return lax.dot_general(
        lhs, rhs, (((1,), (1,)), ((), ())), preferred_element_type=jnp.float32
    )


def add_products(acc_ref, lhs_ref, piece_ref, cos_ref, sin_ref, mixed_ref):
    windows, rows, width = piece_ref.shape
    tile = 256
    used = v_row(rows) + HALF * rows
    if used < mixed_ref.shape[0]:
        mixed_ref[used:, :] = jnp.zeros_like(mixed_ref[used:, :])

    @pl.loop(0, windows)
    def _(w):
        for start in range(0, width // 2, 128):
            mix(mixed_ref, piece_ref.at[w], cos_ref, sin_ref, start)

        @pl.loop(0, mixed_ref.shape[0], step=tile)
        def _(n):
            cols = pl.ds(pl.multiple_of(n, tile), tile)
            acc_ref[:, cols] += times(lhs_ref[w], mixed_ref[cols, :])


def part_kernel(white_ref, piece_ref, cos_ref, sin_ref, _, part_ref, done_ref, mixed_ref):
    done_ref[...] = jnp.zeros_like(done_ref)
    part_ref[...] = jnp.zeros_like(part_ref)
    add_products(part_ref, white_ref, piece_ref, cos_ref, sin_ref, mixed_ref)


def part_columns(rows):
    columns = v_row(rows) + HALF * rows
    return columns + (-columns) % 256


def part_terms(white, piece, tables, done):
    windows, channels, width = white.shape
    columns = part_columns(piece.shape[1])
    return pl.pallas_call(
        part_kernel,
        in_specs=[whole()] * 5,
        out_specs=[whole()] * 2,
        out_shape=[jax.ShapeDtypeStruct((channels, columns), jnp.float32), TOKEN],
        scratch_shapes=[pltpu.VMEM((columns, width), jnp.bfloat16)],
        compiler_params=kernel_params(),
        cost_estimate=pl.CostEstimate(
            flops=2 * windows * channels * columns * width,
            bytes_accessed=2 * white.size,
            transcendentals=0,
        ),
        name="terms_part",
    )(white, piece, *tables, done)


TOKEN = jax.ShapeDtypeStruct((8, 128), jnp.float32)


def write_terms(acc_ref, rows, scale, back_ref, own_refs):
    x, core = place_of_core()
    vrow = v_row(rows)
    wide = HALF * rows

    def split(line):
        u, v = acc_ref[line, :wide] * scale, acc_ref[line, vrow:vrow + wide] * scale
        still = acc_ref[line, wide:wide + rows] * scale
        return u + v, u - v, still

    plus, minus, still = split(pl.ds(SRC, acc_ref.shape[0] - SRC))
    back = jnp.concatenate([minus, plus[:, :wide - rows], still], axis=1)
    back_ref[...] = back.astype(back_ref.dtype)
    mine = SRC // 4
    for i, out in enumerate(own_refs):
        group, spot = (x, 1 - x)[i // 2], (core, 1 - core)[i % 2]
        line = pl.ds(pl.multiple_of((2 * group + spot) * mine, 8), mine)
        plus, minus, still = split(line)
        value = jnp.concatenate([plus, minus[:, :wide - rows], still], axis=1)
        out[...] = value.astype(out.dtype)


def first_kernel(
    scale, part_ref, sibling_ref, piece_ref, cos_ref, sin_ref, _, back_ref, *refs
):
    *own_refs, done_ref, mixed_ref, acc_ref = refs
    done_ref[...] = jnp.zeros_like(done_ref)
    acc_ref[...] = part_ref[...]
    add_products(acc_ref, sibling_ref, piece_ref, cos_ref, sin_ref, mixed_ref)
    write_terms(acc_ref, piece_ref.shape[1], scale, back_ref, own_refs)


def second_kernel(scale, part_ref, sibling_ref, piece_ref, cos_ref, sin_ref, *refs):
    first_refs = refs[:4]
    back_ref, *own_refs, even_ref, odd_ref, acc_ref = refs[4:]
    windows, rows, width = piece_ref.shape
    starts = list(range(0, width // 2, 128))
    tiles = [
        slice(n, min(n + 256, acc_ref.shape[1])) for n in range(0, acc_ref.shape[1], 256)
    ]
    buffers = even_ref, odd_ref
    for start in starts:
        mix(even_ref, piece_ref.at[0], cos_ref, sin_ref, start)
    for w in range(windows):
        now_ref, next_ref = buffers[w % 2], buffers[1 - w % 2]
        todo = starts if w + 1 < windows else []
        for cols in tiles:
            before = part_ref[:, cols] if w == 0 else acc_ref[:, cols]
            acc_ref[:, cols] = before + times(sibling_ref[w], now_ref[cols, :])
            for start in todo[:2]:
                mix(next_ref, piece_ref.at[w + 1], cos_ref, sin_ref, start)
            todo = todo[2:]
    write_terms(acc_ref, rows, scale, back_ref, [out.at[1] for out in own_refs])
    for out, first_ref in zip(own_refs, first_refs):
        out[0] = first_ref[...]


def terms(part, sibling, piece, tables, scale, done=None, first=None):
    windows, channels, width = sibling.shape
    rows = piece.shape[1]
    wide = 2 * HALF * rows
    mine = SRC // 4
    second = first is not None
    columns = v_row(rows) + HALF * rows if second else part_columns(rows)
    own = (2, mine, wide) if second else (mine, wide)
    back = ((channels - SRC, wide), jnp.float32 if second else jnp.bfloat16)
    out = [jax.ShapeDtypeStruct(*back), jax.ShapeDtypeStruct(own, jnp.float32)]
    out += [jax.ShapeDtypeStruct(own, jnp.bfloat16)] * 3 + ([] if second else [TOKEN])
    more = tuple(first) if second else (done,)
    return pl.pallas_call(
        functools.partial(second_kernel if second else first_kernel, scale),
        in_specs=[whole()] * (5 + len(more)),
        out_specs=[whole()] * len(out),
        out_shape=out,
        scratch_shapes=[pltpu.VMEM((columns, width), jnp.bfloat16)] * (2 if second else 1)
        + [pltpu.VMEM((channels, columns), jnp.float32)],
        compiler_params=kernel_params(),
        cost_estimate=pl.CostEstimate(
            flops=2 * windows * channels * columns * width,
            bytes_accessed=2 * sibling.size,
            transcendentals=0,
        ),
        name="terms_second" if second else "terms_first",
    )(part, sibling, piece, *tables, *more)


def keep_kernel(source_ref, *refs):
    *_, out_ref, done_ref = refs
    out_ref[...] = source_ref[...]
    done_ref[...] = jnp.zeros_like(done_ref)


def keep(value, *done):
    return pl.pallas_call(
        keep_kernel,
        in_specs=[whole()] * (1 + len(done)),
        out_specs=[whole()] * 2,
        out_shape=[jax.ShapeDtypeStruct(value.shape, value.dtype), TOKEN],
        compiler_params=kernel_params(),
        name="keep",
    )(value, *done)


def place_kernel(
    here_ref, core_ref, chip_ref, cross_ref, back_ref, out_ref, block_ref, sems
):
    x, core = place_of_core()
    lags, mine, channels = block_ref.shape
    swap = core != 0
    sides = []
    for q in range(2):
        index = jnp.where(x == q, 1, 0)
        own = here_ref[index] + chip_ref[1 - index].astype(jnp.float32)
        other = core_ref[index].astype(jnp.float32) + cross_ref[1 - index].astype(jnp.float32)
        sides += [jnp.where(swap, other, own), jnp.where(swap, own, other)]
    back = back_ref[...].astype(jnp.float32).T
    copies = []
    for j in range(lags):
        lag = HALF - 1 - j if j < HALF else j + 1 if j < lags - 1 else HALF
        cols = slice(j * mine, (j + 1) * mine)
        block_ref[lag, :, :SRC] = jnp.concatenate([v[:, cols] for v in sides], axis=1)
        block_ref[lag, :, SRC:] = back[cols]
        copies.append(pltpu.make_async_copy(block_ref.at[lag], out_ref.at[lag], sems.at[lag]))
        copies[-1].start()
    for copy in copies:
        copy.wait()


def place(here, core, chip, cross, back):
    _, mine, wide = here.shape
    shape = (wide // mine, mine, SRC + back.shape[0])
    return pl.pallas_call(
        place_kernel,
        in_specs=[whole()] * 5,
        out_specs=anywhere(),
        out_shape=jax.ShapeDtypeStruct(shape, jnp.float32),
        scratch_shapes=[
            pltpu.VMEM(shape, jnp.float32), pltpu.SemaphoreType.DMA((shape[0],))
        ],
        compiler_params=kernel_params(),
        name="place_lags",
    )(here, core, chip, cross, back)


def pair_body(spectra, counts, partner):
    blocks = lax.axis_size("chan")
    groups = lax.axis_size("win")
    windows, channels, two, freqs = spectra.shape
    scale = 1.0 / (math.sqrt(2.0 * freqs) * math.sqrt(windows * groups))
    other_core = [(i, i ^ 1) for i in range(groups)]
    other_chip = [(i, i ^ 2) for i in range(groups)]
    other_both = [(i, i ^ 3) for i in range(groups)]

    def to_partner(t):
        return [(i, i ^ t) for i in range(blocks)]

    def to_partner_core(t):
        return [
            (i * groups + g, (i ^ t) * groups + (g ^ 1))
            for i in range(blocks)
            for g in range(groups)
        ]

    def send_sources(t, white, near, far, near_more, far_more):
        def straight(value):
            return lax.ppermute(value, "chan", to_partner(t))

        def crossed(value):
            return lax.ppermute(value, ("chan", "win"), to_partner_core(t))

        sibling = lax.ppermute(white, "win", other_core)
        near, far = straight(near), crossed(far)
        near_more, done = keep(near_more, near)
        near_more = straight(near_more)
        part, done = part_terms(white, near, tables, done)
        far_more, done = keep(far_more, far, done)
        far_more = crossed(far_more)
        back, *own, done = terms(part, sibling, far, tables, scale, done)
        back = lax.ppermute(back, "win", other_chip)
        part, done = part_terms(white, near_more, tables, done)
        return part, keep(sibling)[0], keep(far_more, done)[0], keep(back)[0], own

    def send_terms(t, back, chip, cross):
        back = lax.ppermute(back, "chan", to_partner(t))
        chip = lax.ppermute(chip, "win", other_chip)
        cross = lax.ppermute(cross, "win", other_both)
        return keep(chip)[0], keep(cross)[0], keep(back)[0]

    def by_round(run, *values):
        branches = [functools.partial(run, t) for t in range(1, blocks)]
        return lax.switch(partner[0, 0] - 1, branches, *values)

    tables = [jnp.asarray(v) for v in shift_tables(freqs)]
    part, sibling, piece, back_recv, own = by_round(
        send_sources, *whiten(spectra, counts)
    )
    back_keep, here, core, chip, cross = terms(part, sibling, piece, tables, scale, first=own)
    core = lax.ppermute(core, "win", other_core)
    back = (back_keep + back_recv.astype(jnp.float32)).astype(jnp.bfloat16)
    return place(here, core, *by_round(send_terms, back, chip, cross))[None, None]


def lag_table(freqs, lags):
    freq = jnp.arange(freqs, dtype=jnp.float32) + freqs // 4
    delay = jnp.arange(lags, dtype=jnp.float32) - lags // 2
    phase = 2.0 * math.pi * freq[:, None] * delay[None, :] / (4.0 * freqs)
    norm = 1.0 / math.sqrt(2.0 * freqs)
    return jnp.stack([jnp.cos(phase), -jnp.sin(phase)]) * norm


def blended_sources(sources, table):
    src = sources.astype(jnp.float32)
    first = src[:, :, 0][:, :, None, :]
    second = src[:, :, 1][:, :, None, :]
    cos_part = table[0].T[None, None]
    sin_part = table[1].T[None, None]
    real_mix = first * cos_part + second * sin_part
    imag_mix = second * cos_part - first * sin_part
    return jnp.stack([real_mix, imag_mix], axis=3).astype(jnp.bfloat16)


def pair_terms(sources, receiver_blocks, table):
    wins, count, two, freqs = sources.shape
    lags = table.shape[2]
    group = math.gcd(count, 32)
    flat_recv = receiver_blocks.reshape(wins, receiver_blocks.shape[1], two * freqs)
    grouped = jnp.moveaxis(sources.reshape(wins, count // group, group, two, freqs), 1, 0)

    def one_group(piece):
        mixed_spectra = blended_sources(piece, table).reshape(wins, group * lags, two * freqs)
        out = jnp.einsum(
            "wmx,wrx->mr", mixed_spectra, flat_recv, preferred_element_type=jnp.float32
        )
        return out.reshape(group, lags, receiver_blocks.shape[1])

    out = lax.map(one_group, grouped).reshape(count, lags, receiver_blocks.shape[1])
    return jnp.transpose(out, (1, 0, 2))


def route_blocks(values, round_flags, levels):
    for level in range(levels):
        moved = from_partner(values, "chan", level)
        values = jnp.where((round_flags >> level) % 2 == 1, moved, values)
    return values


def general_body(spectra, counts, partner):
    white = whiten_local(spectra, counts[0])
    table = lag_table(spectra.shape[3], LAGS)
    levels = lax.axis_size("chan").bit_length() - 1
    windows = spectra.shape[0] * lax.axis_size("win")
    receiver_blocks = route_blocks(white, partner[0, 0], levels)
    out = pair_terms(white[:, :SRC], receiver_blocks, table)
    stacked = lax.psum_scatter(out, "win", scatter_dimension=1, tiled=True)
    return (stacked / math.sqrt(windows))[None, None]


def solution(mesh):
    body = pair_body if mesh.shape["win"] == 4 else general_body
    return jax.shard_map(
        body,
        mesh=mesh,
        in_specs=(P("win", "chan", None, None), P("chan"), P()),
        out_specs=P("chan", None, None, "win", None),
        check_vma=False,
    )
```

```python
import functools
import math

import jax
import jax.numpy as jnp
import numpy as np
from jax import lax
from jax.experimental import pallas as pl
from jax.experimental.pallas import tpu as pltpu
from jax.sharding import PartitionSpec as P

LAGS = 16
SRC = 160
HALF = LAGS // 2
VMEM_LIMIT = 16 * 1024 * 1024


def from_partner(value, axis, stride):
    return lax.ppermute(value, axis, [(i, i ^ 1 << stride) for i in range(lax.axis_size(axis))])


def whiten_local(spectra, count):
    values = spectra.astype(jnp.float32)
    block_size = spectra.shape[1]
    freqs = spectra.shape[3]
    valid = (jnp.arange(block_size, dtype=jnp.int32) < count).astype(jnp.float32)
    freq = jnp.arange(freqs, dtype=jnp.float32)
    taper = 0.75 - 0.25 * jnp.cos(2.0 * math.pi * (freq + 0.5) / freqs)
    power = jnp.mean(values * values, axis=(2, 3))
    scale = valid[None, :] / jnp.sqrt(power + 1e-05)
    return (values * taper * scale[:, :, None, None]).astype(jnp.bfloat16)


def shift_tables(freqs):
    freq = np.arange(freqs, dtype=np.float64) + freqs // 4
    shift = np.arange(1, HALF + 1, dtype=np.float64)
    phase = 2.0 * np.pi * shift[:, None] * freq[None, :] / (4.0 * freqs)
    return np.cos(phase).astype(np.float32), np.sin(phase).astype(np.float32)


def place_of_core():
    spot = lax.axis_index("win")
    return spot // 2, spot % 2


def whole():
    return pl.BlockSpec(memory_space=pltpu.VMEM)


def anywhere():
    return pl.BlockSpec(memory_space=pl.ANY)


def kernel_params():
    return pltpu.CompilerParams(vmem_limit_bytes=VMEM_LIMIT)


def fetch_kernel(source_ref, out_ref, sems):
    windows, parts = out_ref.shape[0], sems.shape[1]
    step = out_ref.shape[1] // parts
    copies = []
    for w in range(windows):
        for i in range(parts):
            part = (w, pl.ds(i * step, step))
            copies.append(
                pltpu.make_async_copy(source_ref.at[part], out_ref.at[part], sems.at[w, i])
            )
            copies[-1].start()
    for copy in copies:
        copy.wait()


def fetch(value):
    return pl.pallas_call(
        fetch_kernel,
        in_specs=[pl.BlockSpec(memory_space=pltpu.HBM)],
        out_specs=whole(),
        out_shape=jax.ShapeDtypeStruct(value.shape, value.dtype),
        scratch_shapes=[pltpu.SemaphoreType.DMA((value.shape[0], 4))],
        compiler_params=kernel_params(),
        name="fetch",
    )(pltpu.with_memory_space_constraint(value, pltpu.HBM))


def whiten_kernel(count_ref, raw_ref, taper_ref, white_ref, *refs):
    *piece_refs, count, sem = refs
    copy = pltpu.make_async_copy(count_ref, count, sem)
    copy.start()
    x, core = place_of_core()
    windows, channels, width = raw_ref.shape
    mine = SRC // 4
    step = 2 * mine
    copy.wait()
    for w in range(windows):
        for index in range(channels // step):
            block = (1 - x, x)[index] if index * step < SRC else index
            begin = block * step
            line = pl.ds(pl.multiple_of(begin, step), step)
            values = raw_ref[w, line, :].astype(jnp.float32)
            power = jnp.sum(values * values, axis=1, keepdims=True) * (1.0 / width)
            row = begin + lax.broadcasted_iota(jnp.int32, (step, 1), 0)
            valid = (row < count[0]).astype(jnp.float32)
            scale = valid / jnp.sqrt(power + 1e-05)
            values = values * taper_ref[...] * scale
            white_ref[w, line, :] = values.astype(jnp.bfloat16)
            if index * step < SRC:
                low, high = values[:mine], values[mine:]
                first = core == 0
                near_ref, far_ref = piece_refs[2 * index:2 * index + 2]
                near_ref[w] = jnp.where(first, low, high).astype(jnp.bfloat16)
                far_ref[w] = jnp.where(first, high, low).astype(jnp.bfloat16)


def whiten(spectra, counts):
    windows, channels, two, freqs = spectra.shape
    width = two * freqs
    freq = np.arange(freqs, dtype=np.float64)
    taper = 0.75 - 0.25 * np.cos(2.0 * np.pi * (freq + 0.5) / freqs)
    taper = np.tile(taper.astype(np.float32), two)[None, :]
    piece = jax.ShapeDtypeStruct((windows, SRC // 4, width), jnp.bfloat16)
    return pl.pallas_call(
        whiten_kernel,
        in_specs=[anywhere(), whole(), whole()],
        out_specs=[whole()] * 5,
        out_shape=[jax.ShapeDtypeStruct((windows, channels, width), jnp.bfloat16)]
        + [piece] * 4,
        scratch_shapes=[pltpu.SMEM((1,), jnp.int32), pltpu.SemaphoreType.DMA],
        compiler_params=kernel_params(),
        name="whiten",
    )(counts, fetch(spectra).reshape(windows, channels, width), jnp.asarray(taper))


def mix(m_ref, piece, cos_ref, sin_ref, low, high):
    rows = piece.shape[0]
    vrow = v_row(rows)
    real = piece[:, low].astype(jnp.float32)
    imag = piece[:, high].astype(jnp.float32)

    def put(where, cols, values):
        m_ref[where, cols] = jnp.concatenate(values, axis=0).astype(jnp.bfloat16)

    for m in range(0, HALF, 2):
        c = [cos_ref[m + i:m + i + 1, low] for i in range(2)]
        s = [sin_ref[m + i:m + i + 1, low] for i in range(2)]
        line = slice(m * rows, (m + 2) * rows)
        vline = slice(vrow + m * rows, vrow + (m + 2) * rows)
        put(line, low, [real * v for v in c])
        put(line, high, [imag * v for v in c])
        put(vline, low, [imag * -v for v in s])
        put(vline, high, [real * v for v in s])
    fill = jnp.zeros((vrow - (HALF + 1) * rows, 128), jnp.float32)
    for value, cols in ((real, low), (imag, high)):
        put(slice(HALF * rows, vrow), cols, [value, fill])


def v_row(rows):
    return -(-(HALF + 1) * rows // 128) * 128


def times(lhs, rhs):
    return lax.dot_general(
        lhs, rhs, (((1,), (1,)), ((), ())), preferred_element_type=jnp.float32
    )


def add_products(acc_ref, lhs_ref, piece_ref, cos_ref, sin_ref, mixed_ref):
    windows, rows, width = piece_ref.shape
    tile = 256
    used = v_row(rows) + HALF * rows
    if used < mixed_ref.shape[0]:
        mixed_ref[used:, :] = jnp.zeros_like(mixed_ref[used:, :])

    @pl.loop(0, windows)
    def _(w):
        @pl.loop(0, width // 2, step=128)
        def _(start):
            low = pl.ds(pl.multiple_of(start, 128), 128)
            high = pl.ds(pl.multiple_of(width // 2 + start, 128), 128)
            mix(mixed_ref, piece_ref.at[w], cos_ref, sin_ref, low, high)

        @pl.loop(0, mixed_ref.shape[0], step=tile)
        def _(n):
            cols = pl.ds(pl.multiple_of(n, tile), tile)
            acc_ref[:, cols] += times(lhs_ref[w], mixed_ref[cols, :])


def part_kernel(white_ref, piece_ref, cos_ref, sin_ref, _, part_ref, done_ref, mixed_ref):
    done_ref[...] = jnp.zeros_like(done_ref)
    part_ref[...] = jnp.zeros_like(part_ref)
    add_products(part_ref, white_ref, piece_ref, cos_ref, sin_ref, mixed_ref)


def part_columns(rows):
    columns = v_row(rows) + HALF * rows
    return columns + (-columns) % 256


def part_terms(white, piece, tables, done):
    windows, channels, width = white.shape
    columns = part_columns(piece.shape[1])
    return pl.pallas_call(
        part_kernel,
        in_specs=[whole()] * 5,
        out_specs=[whole()] * 2,
        out_shape=[jax.ShapeDtypeStruct((channels, columns), jnp.float32), TOKEN],
        scratch_shapes=[pltpu.VMEM((columns, width), jnp.bfloat16)],
        compiler_params=kernel_params(),
        cost_estimate=pl.CostEstimate(
            flops=2 * windows * channels * columns * width,
            bytes_accessed=2 * white.size,
            transcendentals=0,
        ),
        name="terms_part",
    )(white, piece, *tables, done)


TOKEN = jax.ShapeDtypeStruct((8, 128), jnp.float32)


def pack(acc_ref, line, rows, scale, later):
    wide = HALF * rows
    vrow = v_row(rows)
    u, v = acc_ref[line, :wide] * scale, acc_ref[line, vrow:vrow + wide] * scale
    still = acc_ref[line, wide:wide + rows] * scale
    first, last = (u - v, u + v) if later else (u + v, u - v)
    return jnp.concatenate([first, last[:, :wide - rows], still], axis=1)


def first_kernel(
    scale, part_ref, sibling_ref, piece_ref, cos_ref, sin_ref, _, back_ref, own_ref,
    done_ref, mixed_ref, acc_ref,
):
    done_ref[...] = jnp.zeros_like(done_ref)
    acc_ref[...] = part_ref[...]
    add_products(acc_ref, sibling_ref, piece_ref, cos_ref, sin_ref, mixed_ref)
    line = pl.ds(SRC, acc_ref.shape[0] - SRC)
    back = pack(acc_ref, line, piece_ref.shape[1], scale, True)
    back_ref[...] = back.astype(back_ref.dtype)
    own_ref[...] = acc_ref[:SRC, :]


def second_kernel(scale, part_ref, sibling_ref, piece_ref, cos_ref, sin_ref, first_ref, *refs):
    back_ref, *own_refs, even_ref, odd_ref, acc_ref = refs
    x, core = place_of_core()
    windows, rows, width = piece_ref.shape
    freqs = width // 2
    starts = [
        (slice(n, n + 128), slice(freqs + n, freqs + n + 128)) for n in range(0, freqs, 128)
    ]
    tiles = [
        slice(n, min(n + 256, acc_ref.shape[1])) for n in range(0, acc_ref.shape[1], 256)
    ]
    buffers = even_ref, odd_ref
    for start in starts:
        mix(even_ref, piece_ref.at[0], cos_ref, sin_ref, *start)
    for w in range(windows):
        now_ref, next_ref = buffers[w % 2], buffers[1 - w % 2]
        todo = starts if w + 1 < windows else []
        for cols in tiles:
            before = part_ref[:, cols] if w == 0 else acc_ref[:, cols]
            acc_ref[:, cols] = before + times(sibling_ref[w], now_ref[cols, :])
            for start in todo[:2]:
                mix(next_ref, piece_ref.at[w + 1], cos_ref, sin_ref, *start)
            todo = todo[2:]
    back_ref[...] = pack(acc_ref, pl.ds(SRC, acc_ref.shape[0] - SRC), rows, scale, True)
    mine = SRC // 4
    for i, out in enumerate(own_refs):
        group, spot = (x, 1 - x)[i // 2], (core, 1 - core)[i % 2]
        line = pl.ds(pl.multiple_of((2 * group + spot) * mine, 8), mine)
        for quarter, ref in enumerate((first_ref, acc_ref)):
            out[quarter] = pack(ref, line, rows, scale, False).astype(out.dtype)


def terms(part, sibling, piece, tables, scale, done=None, first=None):
    windows, channels, width = sibling.shape
    rows = piece.shape[1]
    wide = 2 * HALF * rows
    mine = SRC // 4
    second = first is not None
    columns = v_row(rows) + HALF * rows if second else part_columns(rows)
    if second:
        out = [((channels - SRC, wide), jnp.float32), ((2, mine, wide), jnp.float32)]
        out += [((2, mine, wide), jnp.bfloat16)] * 3
    else:
        out = [((channels - SRC, wide), jnp.bfloat16), ((SRC, columns), jnp.float32)]
    out = [jax.ShapeDtypeStruct(*v) for v in out] + ([] if second else [TOKEN])
    return pl.pallas_call(
        functools.partial(second_kernel if second else first_kernel, scale),
        in_specs=[whole()] * 6,
        out_specs=[whole()] * len(out),
        out_shape=out,
        scratch_shapes=[pltpu.VMEM((columns, width), jnp.bfloat16)] * (2 if second else 1)
        + [pltpu.VMEM((channels, columns), jnp.float32)],
        compiler_params=kernel_params(),
        cost_estimate=pl.CostEstimate(
            flops=2 * windows * channels * columns * width,
            bytes_accessed=2 * sibling.size,
            transcendentals=0,
        ),
        name="terms_second" if second else "terms_first",
    )(part, sibling, piece, *tables, first if second else done)


def keep_kernel(*refs):
    *sources, sem = refs
    outs = sources[len(sources) // 2:]
    for source_ref, out_ref in zip(sources, outs):
        copy = pltpu.make_async_copy(source_ref, out_ref, sem)
        copy.start()
        copy.wait()


def hold_kernel(source_ref, *refs):
    *_, out_ref, done_ref, sem = refs
    copy = pltpu.make_async_copy(source_ref, out_ref, sem)
    copy.start()
    copy.wait()
    done_ref[...] = jnp.zeros_like(done_ref)


def keep(*values):
    return pl.pallas_call(
        keep_kernel,
        in_specs=[whole()] * len(values),
        out_specs=[whole()] * len(values),
        out_shape=[jax.ShapeDtypeStruct(v.shape, v.dtype) for v in values],
        scratch_shapes=[pltpu.SemaphoreType.DMA],
        compiler_params=kernel_params(),
        name="keep",
    )(*values)


def hold(value, *done):
    return pl.pallas_call(
        hold_kernel,
        in_specs=[whole()] * (1 + len(done)),
        out_specs=[whole()] * 2,
        out_shape=[jax.ShapeDtypeStruct(value.shape, value.dtype), TOKEN],
        scratch_shapes=[pltpu.SemaphoreType.DMA],
        compiler_params=kernel_params(),
        name="hold",
    )(value, *done)


def keep_after(value, done):
    return pl.pallas_call(
        lambda source_ref, _, out_ref, sem: keep_kernel(source_ref, out_ref, sem),
        in_specs=[whole()] * 2,
        out_specs=whole(),
        out_shape=jax.ShapeDtypeStruct(value.shape, value.dtype),
        scratch_shapes=[pltpu.SemaphoreType.DMA],
        compiler_params=kernel_params(),
        name="keep_after",
    )(value, done)


def place_kernel(
    here_ref, core_ref, chip_ref, cross_ref, back_ref, out_ref, block_ref, sems
):
    x, core = place_of_core()
    lags, mine, channels = block_ref.shape
    swap = core != 0
    sides = []
    for q in range(2):
        index = jnp.where(x == q, 1, 0)
        own = here_ref[index] + chip_ref[1 - index].astype(jnp.float32)
        other = core_ref[index].astype(jnp.float32) + cross_ref[1 - index].astype(jnp.float32)
        sides += [jnp.where(swap, other, own), jnp.where(swap, own, other)]
    back = back_ref[...].astype(jnp.float32).T
    copies = []
    for j in range(lags):
        lag = HALF - 1 - j if j < HALF else j + 1 if j < lags - 1 else HALF
        cols = slice(j * mine, (j + 1) * mine)
        block_ref[lag, :, :SRC] = jnp.concatenate([v[:, cols] for v in sides], axis=1)
        block_ref[lag, :, SRC:] = back[cols]
        copies.append(pltpu.make_async_copy(block_ref.at[lag], out_ref.at[lag], sems.at[lag]))
        copies[-1].start()
    for copy in copies:
        copy.wait()


def place(here, core, chip, cross, back):
    _, mine, wide = here.shape
    shape = (wide // mine, mine, SRC + back.shape[0])
    return pl.pallas_call(
        place_kernel,
        in_specs=[whole()] * 5,
        out_specs=anywhere(),
        out_shape=jax.ShapeDtypeStruct(shape, jnp.float32),
        scratch_shapes=[
            pltpu.VMEM(shape, jnp.float32), pltpu.SemaphoreType.DMA((shape[0],))
        ],
        compiler_params=kernel_params(),
        name="place_lags",
    )(here, core, chip, cross, back)


def pair_body(spectra, counts, partner):
    blocks = lax.axis_size("chan")
    groups = lax.axis_size("win")
    windows, channels, two, freqs = spectra.shape
    scale = 1.0 / (math.sqrt(2.0 * freqs) * math.sqrt(windows * groups))
    other_core = [(i, i ^ 1) for i in range(groups)]
    other_chip = [(i, i ^ 2) for i in range(groups)]
    other_both = [(i, i ^ 3) for i in range(groups)]

    def to_partner(t):
        return [(i, i ^ t) for i in range(blocks)]

    def to_partner_core(t):
        return [
            (i * groups + g, (i ^ t) * groups + (g ^ 1))
            for i in range(blocks)
            for g in range(groups)
        ]

    def send_sources(t, white, near, far, near_more, far_more):
        def straight(value):
            return lax.ppermute(value, "chan", to_partner(t))

        def crossed(value):
            return lax.ppermute(value, ("chan", "win"), to_partner_core(t))

        sibling = lax.ppermute(white, "win", other_core)
        near, far = straight(near), crossed(far)
        near_more, done = hold(near_more, near)
        near_more = straight(near_more)
        part, done = part_terms(white, near, tables, done)
        far_more, done = hold(far_more, far, done)
        far_more = crossed(far_more)
        back, own, done = terms(part, sibling, far, tables, scale, done)
        back = lax.ppermute(back, "win", other_chip)
        part, done = part_terms(white, near_more, tables, done)
        return part, *keep(sibling), keep_after(far_more, done), *keep(back), own

    def send_terms(t, back, chip, cross):
        back = lax.ppermute(back, "chan", to_partner(t))
        chip = lax.ppermute(chip, "win", other_chip)
        cross = lax.ppermute(cross, "win", other_both)
        return *keep(chip, cross), *keep(back)

    def by_round(run, *values):
        branches = [functools.partial(run, t) for t in range(1, blocks)]
        return lax.switch(partner[0, 0] - 1, branches, *values)

    tables = [jnp.asarray(v) for v in shift_tables(freqs)]
    part, sibling, piece, back_recv, own = by_round(
        send_sources, *whiten(spectra, counts)
    )
    back_keep, here, core, chip, cross = terms(part, sibling, piece, tables, scale, first=own)
    core = lax.ppermute(core, "win", other_core)
    back = (back_keep + back_recv.astype(jnp.float32)).astype(jnp.bfloat16)
    return place(here, core, *by_round(send_terms, back, chip, cross))[None, None]


def lag_table(freqs, lags):
    freq = jnp.arange(freqs, dtype=jnp.float32) + freqs // 4
    delay = jnp.arange(lags, dtype=jnp.float32) - lags // 2
    phase = 2.0 * math.pi * freq[:, None] * delay[None, :] / (4.0 * freqs)
    norm = 1.0 / math.sqrt(2.0 * freqs)
    return jnp.stack([jnp.cos(phase), -jnp.sin(phase)]) * norm


def blended_sources(sources, table):
    src = sources.astype(jnp.float32)
    first = src[:, :, 0][:, :, None, :]
    second = src[:, :, 1][:, :, None, :]
    cos_part = table[0].T[None, None]
    sin_part = table[1].T[None, None]
    real_mix = first * cos_part + second * sin_part
    imag_mix = second * cos_part - first * sin_part
    return jnp.stack([real_mix, imag_mix], axis=3).astype(jnp.bfloat16)


def pair_terms(sources, receiver_blocks, table):
    wins, count, two, freqs = sources.shape
    lags = table.shape[2]
    group = math.gcd(count, 32)
    flat_recv = receiver_blocks.reshape(wins, receiver_blocks.shape[1], two * freqs)
    grouped = jnp.moveaxis(sources.reshape(wins, count // group, group, two, freqs), 1, 0)

    def one_group(piece):
        mixed_spectra = blended_sources(piece, table).reshape(wins, group * lags, two * freqs)
        out = jnp.einsum(
            "wmx,wrx->mr", mixed_spectra, flat_recv, preferred_element_type=jnp.float32
        )
        return out.reshape(group, lags, receiver_blocks.shape[1])

    out = lax.map(one_group, grouped).reshape(count, lags, receiver_blocks.shape[1])
    return jnp.transpose(out, (1, 0, 2))


def route_blocks(values, round_flags, levels):
    for level in range(levels):
        moved = from_partner(values, "chan", level)
        values = jnp.where((round_flags >> level) % 2 == 1, moved, values)
    return values


def general_body(spectra, counts, partner):
    white = whiten_local(spectra, counts[0])
    table = lag_table(spectra.shape[3], LAGS)
    levels = lax.axis_size("chan").bit_length() - 1
    windows = spectra.shape[0] * lax.axis_size("win")
    receiver_blocks = route_blocks(white, partner[0, 0], levels)
    out = pair_terms(white[:, :SRC], receiver_blocks, table)
    stacked = lax.psum_scatter(out, "win", scatter_dimension=1, tiled=True)
    return (stacked / math.sqrt(windows))[None, None]


def solution(mesh):
    body = pair_body if mesh.shape["win"] == 4 else general_body
    return jax.shard_map(
        body,
        mesh=mesh,
        in_specs=(P("win", "chan", None, None), P("chan"), P()),
        out_specs=P("chan", None, None, "win", None),
        check_vma=False,
    )
```

```python
import functools
import math

import jax
import jax.numpy as jnp
import numpy as np
from jax import lax
from jax.experimental import pallas as pl
from jax.experimental.pallas import tpu as pltpu
from jax.sharding import PartitionSpec as P

LAGS = 16
SRC = 160
HALF = LAGS // 2
VMEM_LIMIT = 16 * 1024 * 1024


def from_partner(value, axis, stride):
    return lax.ppermute(value, axis, [(i, i ^ 1 << stride) for i in range(lax.axis_size(axis))])


def whiten_local(spectra, count):
    values = spectra.astype(jnp.float32)
    block_size = spectra.shape[1]
    freqs = spectra.shape[3]
    valid = (jnp.arange(block_size, dtype=jnp.int32) < count).astype(jnp.float32)
    freq = jnp.arange(freqs, dtype=jnp.float32)
    taper = 0.75 - 0.25 * jnp.cos(2.0 * math.pi * (freq + 0.5) / freqs)
    power = jnp.mean(values * values, axis=(2, 3))
    scale = valid[None, :] / jnp.sqrt(power + 1e-05)
    return (values * taper * scale[:, :, None, None]).astype(jnp.bfloat16)


def shift_tables(freqs):
    freq = np.arange(freqs, dtype=np.float64) + freqs // 4
    shift = np.arange(1, HALF + 1, dtype=np.float64)
    phase = 2.0 * np.pi * shift[:, None] * freq[None, :] / (4.0 * freqs)
    return np.cos(phase).astype(np.float32), np.sin(phase).astype(np.float32)


def place_of_core():
    spot = lax.axis_index("win")
    return spot // 2, spot % 2


def whole():
    return pl.BlockSpec(memory_space=pltpu.VMEM)


def anywhere():
    return pl.BlockSpec(memory_space=pl.ANY)


def kernel_params():
    return pltpu.CompilerParams(vmem_limit_bytes=VMEM_LIMIT)


def fetch_kernel(source_ref, out_ref, sems):
    windows, parts = out_ref.shape[0], sems.shape[1]
    step = out_ref.shape[1] // parts
    copies = []
    for w in range(windows):
        for i in range(parts):
            part = (w, pl.ds(i * step, step))
            copies.append(
                pltpu.make_async_copy(source_ref.at[part], out_ref.at[part], sems.at[w, i])
            )
            copies[-1].start()
    for copy in copies:
        copy.wait()


def fetch(value):
    return pl.pallas_call(
        fetch_kernel,
        in_specs=[pl.BlockSpec(memory_space=pltpu.HBM)],
        out_specs=whole(),
        out_shape=jax.ShapeDtypeStruct(value.shape, value.dtype),
        scratch_shapes=[pltpu.SemaphoreType.DMA((value.shape[0], 10))],
        compiler_params=kernel_params(),
        name="fetch",
    )(pltpu.with_memory_space_constraint(value, pltpu.HBM))


def whiten_kernel(count_ref, raw_ref, taper_ref, white_ref, *refs):
    *piece_refs, count, sem = refs
    copy = pltpu.make_async_copy(count_ref, count, sem)
    copy.start()
    x, core = place_of_core()
    windows, channels, width = raw_ref.shape
    mine = SRC // 4
    step = 2 * mine
    copy.wait()
    for w in range(windows):
        for index in range(channels // step):
            block = (1 - x, x)[index] if index * step < SRC else index
            begin = block * step
            line = pl.ds(pl.multiple_of(begin, step), step)
            values = raw_ref[w, line, :].astype(jnp.float32)
            power = jnp.sum(values * values, axis=1, keepdims=True) * (1.0 / width)
            row = begin + lax.broadcasted_iota(jnp.int32, (step, 1), 0)
            valid = (row < count[0]).astype(jnp.float32)
            scale = valid / jnp.sqrt(power + 1e-05)
            values = values * taper_ref[...] * scale
            white_ref[w, line, :] = values.astype(jnp.bfloat16)
            if index * step < SRC:
                low, high = values[:mine], values[mine:]
                first = core == 0
                near_ref, far_ref = piece_refs[2 * index:2 * index + 2]
                near_ref[w] = jnp.where(first, low, high).astype(jnp.bfloat16)
                far_ref[w] = jnp.where(first, high, low).astype(jnp.bfloat16)


def whiten(spectra, counts):
    windows, channels, two, freqs = spectra.shape
    width = two * freqs
    freq = np.arange(freqs, dtype=np.float64)
    taper = 0.75 - 0.25 * np.cos(2.0 * np.pi * (freq + 0.5) / freqs)
    taper = np.tile(taper.astype(np.float32), two)[None, :]
    piece = jax.ShapeDtypeStruct((windows, SRC // 4, width), jnp.bfloat16)
    return pl.pallas_call(
        whiten_kernel,
        in_specs=[anywhere(), whole(), whole()],
        out_specs=[whole()] * 5,
        out_shape=[jax.ShapeDtypeStruct((windows, channels, width), jnp.bfloat16)]
        + [piece] * 4,
        scratch_shapes=[pltpu.SMEM((1,), jnp.int32), pltpu.SemaphoreType.DMA],
        compiler_params=kernel_params(),
        name="whiten",
    )(counts, fetch(spectra).reshape(windows, channels, width), jnp.asarray(taper))


def mix(m_ref, piece, cos_ref, sin_ref, low, high):
    rows = piece.shape[0]
    vrow = v_row(rows)
    real = piece[:, low].astype(jnp.float32)
    imag = piece[:, high].astype(jnp.float32)

    def put(where, cols, values):
        m_ref[where, cols] = jnp.concatenate(values, axis=0).astype(jnp.bfloat16)

    for m in range(0, HALF, 2):
        c = [cos_ref[m + i:m + i + 1, low] for i in range(2)]
        s = [sin_ref[m + i:m + i + 1, low] for i in range(2)]
        line = slice(m * rows, (m + 2) * rows)
        vline = slice(vrow + m * rows, vrow + (m + 2) * rows)
        put(line, low, [real * v for v in c])
        put(line, high, [imag * v for v in c])
        put(vline, low, [imag * -v for v in s])
        put(vline, high, [real * v for v in s])
    fill = jnp.zeros((vrow - (HALF + 1) * rows, 128), jnp.float32)
    for value, cols in ((real, low), (imag, high)):
        put(slice(HALF * rows, vrow), cols, [value, fill])


def v_row(rows):
    return -(-(HALF + 1) * rows // 128) * 128


def times(lhs, rhs):
    return lax.dot_general(
        lhs, rhs, (((1,), (1,)), ((), ())), preferred_element_type=jnp.float32
    )


def add_products(acc_ref, lhs_ref, piece_ref, cos_ref, sin_ref, mixed_ref):
    windows, rows, width = piece_ref.shape
    tile = 256
    used = v_row(rows) + HALF * rows
    if used < mixed_ref.shape[0]:
        mixed_ref[used:, :] = jnp.zeros_like(mixed_ref[used:, :])

    @pl.loop(0, windows)
    def _(w):
        @pl.loop(0, width // 2, step=128)
        def _(start):
            low = pl.ds(pl.multiple_of(start, 128), 128)
            high = pl.ds(pl.multiple_of(width // 2 + start, 128), 128)
            mix(mixed_ref, piece_ref.at[w], cos_ref, sin_ref, low, high)

        @pl.loop(0, mixed_ref.shape[0], step=tile)
        def _(n):
            cols = pl.ds(pl.multiple_of(n, tile), tile)
            acc_ref[:, cols] += times(lhs_ref[w], mixed_ref[cols, :])


def part_kernel(white_ref, piece_ref, cos_ref, sin_ref, _, part_ref, done_ref, mixed_ref):
    done_ref[...] = jnp.zeros_like(done_ref)
    part_ref[...] = jnp.zeros_like(part_ref)
    add_products(part_ref, white_ref, piece_ref, cos_ref, sin_ref, mixed_ref)


def part_columns(rows):
    columns = v_row(rows) + HALF * rows
    return columns + (-columns) % 256


def part_terms(white, piece, tables, done):
    windows, channels, width = white.shape
    columns = part_columns(piece.shape[1])
    return pl.pallas_call(
        part_kernel,
        in_specs=[whole()] * 5,
        out_specs=[whole()] * 2,
        out_shape=[jax.ShapeDtypeStruct((channels, columns), jnp.float32), TOKEN],
        scratch_shapes=[pltpu.VMEM((columns, width), jnp.bfloat16)],
        compiler_params=kernel_params(),
        cost_estimate=LATE,
        name="terms_part",
    )(white, piece, *tables, done)


TOKEN = jax.ShapeDtypeStruct((8, 128), jnp.float32)
LATE = pl.CostEstimate(flops=30 * 10**9, bytes_accessed=0, transcendentals=0)


def pack(acc_ref, line, rows, scale, later):
    wide = HALF * rows
    vrow = v_row(rows)
    u, v = acc_ref[line, :wide] * scale, acc_ref[line, vrow:vrow + wide] * scale
    still = acc_ref[line, wide:wide + rows] * scale
    first, last = (u - v, u + v) if later else (u + v, u - v)
    return jnp.concatenate([first, last[:, :wide - rows], still], axis=1)


def first_kernel(
    scale, part_ref, sibling_ref, piece_ref, cos_ref, sin_ref, _, back_ref, own_ref,
    done_ref, mixed_ref, acc_ref,
):
    done_ref[...] = jnp.zeros_like(done_ref)
    acc_ref[...] = part_ref[...]
    add_products(acc_ref, sibling_ref, piece_ref, cos_ref, sin_ref, mixed_ref)
    line = pl.ds(SRC, acc_ref.shape[0] - SRC)
    back = pack(acc_ref, line, piece_ref.shape[1], scale, True)
    back_ref[...] = back.astype(back_ref.dtype)
    own_ref[...] = acc_ref[:SRC, :]


def second_kernel(scale, part_ref, sibling_ref, piece_ref, cos_ref, sin_ref, *refs):
    back_ref, own_ref, even_ref, odd_ref, acc_ref = refs
    windows, rows, width = piece_ref.shape
    freqs = width // 2
    starts = [
        (slice(n, n + 128), slice(freqs + n, freqs + n + 128)) for n in range(0, freqs, 128)
    ]
    tiles = [
        slice(n, min(n + 256, acc_ref.shape[1])) for n in range(0, acc_ref.shape[1], 256)
    ]
    buffers = even_ref, odd_ref
    for start in starts:
        mix(even_ref, piece_ref.at[0], cos_ref, sin_ref, *start)
    for w in range(windows):
        now_ref, next_ref = buffers[w % 2], buffers[1 - w % 2]
        todo = starts if w + 1 < windows else []
        for cols in tiles:
            before = part_ref[:, cols] if w == 0 else acc_ref[:, cols]
            acc_ref[:, cols] = before + times(sibling_ref[w], now_ref[cols, :])
            for start in todo[:2]:
                mix(next_ref, piece_ref.at[w + 1], cos_ref, sin_ref, *start)
            todo = todo[2:]
    back_ref[...] = pack(acc_ref, pl.ds(SRC, acc_ref.shape[0] - SRC), rows, scale, True)
    own_ref[...] = acc_ref[:SRC, :]


def own_kernel(scale, rows, first_ref, second_ref, *refs):
    *out_refs, packed_ref = refs
    x, core = place_of_core()
    mine = SRC // 4

    @pl.loop(0, SRC, step=mine)
    def _(start):
        line = pl.ds(pl.multiple_of(start, 8), mine)
        for quarter, ref in enumerate((first_ref, second_ref)):
            packed_ref[quarter, line, :] = pack(ref, line, rows, scale, False)

    for i, out_ref in enumerate(out_refs):
        spot = 2 * (x, 1 - x)[i // 2] + (core, 1 - core)[i % 2]
        line = pl.ds(pl.multiple_of(spot * mine, 8), mine)
        for quarter in range(2):
            out_ref[quarter] = packed_ref[quarter, line, :].astype(out_ref.dtype)


def own_terms(first, second, rows, scale):
    mine, wide = SRC // 4, 2 * HALF * rows
    return pl.pallas_call(
        functools.partial(own_kernel, scale, rows),
        in_specs=[whole()] * 2,
        out_specs=[whole()] * 4,
        out_shape=[
            jax.ShapeDtypeStruct((2, mine, wide), jnp.float32 if i == 0 else jnp.bfloat16)
            for i in range(4)
        ],
        scratch_shapes=[pltpu.VMEM((2, SRC, wide), jnp.float32)],
        compiler_params=kernel_params(),
        name="own_terms",
    )(first, second)


def terms(part, sibling, piece, tables, scale, done=None):
    windows, channels, width = sibling.shape
    rows = piece.shape[1]
    second = done is None
    columns = v_row(rows) + HALF * rows if second else part_columns(rows)
    back = ((channels - SRC, 2 * HALF * rows), jnp.float32 if second else jnp.bfloat16)
    out = [jax.ShapeDtypeStruct(*back), jax.ShapeDtypeStruct((SRC, columns), jnp.float32)]
    out += [] if second else [TOKEN]
    more = () if second else (done,)
    return pl.pallas_call(
        functools.partial(second_kernel if second else first_kernel, scale),
        in_specs=[whole()] * (5 + len(more)),
        out_specs=[whole()] * len(out),
        out_shape=out,
        scratch_shapes=[pltpu.VMEM((columns, width), jnp.bfloat16)] * (2 if second else 1)
        + [pltpu.VMEM((channels, columns), jnp.float32)],
        compiler_params=kernel_params(),
        cost_estimate=LATE,
        name="terms_second" if second else "terms_first",
    )(part, sibling, piece, *tables, *more)


def keep_kernel(*refs):
    *refs, sems = refs
    half = len(refs) // 2
    copies = [
        pltpu.make_async_copy(refs[i], refs[half + i], sems.at[i]) for i in range(half)
    ]
    for copy in copies:
        copy.start()
    for copy in copies:
        copy.wait()


def hold_kernel(source_ref, *refs):
    *_, out_ref, done_ref, sem = refs
    copy = pltpu.make_async_copy(source_ref, out_ref, sem)
    copy.start()
    copy.wait()
    done_ref[...] = jnp.zeros_like(done_ref)


def keep(*values):
    return pl.pallas_call(
        keep_kernel,
        in_specs=[whole()] * len(values),
        out_specs=[whole()] * len(values),
        out_shape=[jax.ShapeDtypeStruct(v.shape, v.dtype) for v in values],
        scratch_shapes=[pltpu.SemaphoreType.DMA((len(values),))],
        compiler_params=kernel_params(),
        name="keep",
    )(*values)


def hold(value, *done):
    return pl.pallas_call(
        hold_kernel,
        in_specs=[whole()] * (1 + len(done)),
        out_specs=[whole()] * 2,
        out_shape=[jax.ShapeDtypeStruct(value.shape, value.dtype), TOKEN],
        scratch_shapes=[pltpu.SemaphoreType.DMA],
        compiler_params=kernel_params(),
        name="hold",
    )(value, *done)


def keep_after(value, done):
    return pl.pallas_call(
        lambda source_ref, _, out_ref, sems: keep_kernel(source_ref, out_ref, sems),
        in_specs=[whole()] * 2,
        out_specs=whole(),
        out_shape=jax.ShapeDtypeStruct(value.shape, value.dtype),
        scratch_shapes=[pltpu.SemaphoreType.DMA((1,))],
        compiler_params=kernel_params(),
        name="keep_after",
    )(value, done)


def place_kernel(
    here_ref, core_ref, chip_ref, cross_ref, back_ref, out_ref, block_ref, sems
):
    x, core = place_of_core()
    lags, mine, channels = block_ref.shape
    swap = core != 0
    sides = []
    for q in range(2):
        index = jnp.where(x == q, 1, 0)
        own = here_ref[index] + chip_ref[1 - index].astype(jnp.float32)
        other = core_ref[index].astype(jnp.float32) + cross_ref[1 - index].astype(jnp.float32)
        sides += [jnp.where(swap, other, own), jnp.where(swap, own, other)]
    back = back_ref[...].astype(jnp.float32).T
    copies = []
    for j in range(lags):
        lag = HALF - 1 - j if j < HALF else j + 1 if j < lags - 1 else HALF
        cols = slice(j * mine, (j + 1) * mine)
        block_ref[lag, :, :SRC] = jnp.concatenate([v[:, cols] for v in sides], axis=1)
        block_ref[lag, :, SRC:] = back[cols]
        copies.append(pltpu.make_async_copy(block_ref.at[lag], out_ref.at[lag], sems.at[lag]))
        copies[-1].start()
    for copy in copies:
        copy.wait()


def place(here, core, chip, cross, back):
    _, mine, wide = here.shape
    shape = (wide // mine, mine, SRC + back.shape[0])
    return pl.pallas_call(
        place_kernel,
        in_specs=[whole()] * 5,
        out_specs=anywhere(),
        out_shape=jax.ShapeDtypeStruct(shape, jnp.float32),
        scratch_shapes=[
            pltpu.VMEM(shape, jnp.float32), pltpu.SemaphoreType.DMA((shape[0],))
        ],
        compiler_params=kernel_params(),
        name="place_lags",
    )(here, core, chip, cross, back)


def pair_body(spectra, counts, partner):
    blocks = lax.axis_size("chan")
    groups = lax.axis_size("win")
    windows, channels, two, freqs = spectra.shape
    scale = 1.0 / (math.sqrt(2.0 * freqs) * math.sqrt(windows * groups))
    other_core = [(i, i ^ 1) for i in range(groups)]
    other_chip = [(i, i ^ 2) for i in range(groups)]
    other_both = [(i, i ^ 3) for i in range(groups)]

    def to_partner(t):
        return [(i, i ^ t) for i in range(blocks)]

    def to_partner_core(t):
        return [
            (i * groups + g, (i ^ t) * groups + (g ^ 1))
            for i in range(blocks)
            for g in range(groups)
        ]

    def send_sources(t, white, near, far, near_more, far_more):
        def straight(value):
            return lax.ppermute(value, "chan", to_partner(t))

        def crossed(value):
            return lax.ppermute(value, ("chan", "win"), to_partner_core(t))

        sibling = lax.ppermute(white, "win", other_core)
        near, far = straight(near), crossed(far)
        near_more, done = hold(near_more, near)
        near_more = straight(near_more)
        part, done = part_terms(white, near, tables, done)
        far_more, done = hold(far_more, far, done)
        far_more = crossed(far_more)
        back, own, done = terms(part, sibling, far, tables, scale, done)
        back = lax.ppermute(back, "win", other_chip)
        part, done = part_terms(white, near_more, tables, done)
        return part, *keep(sibling), keep_after(far_more, done), *keep(back), own

    def send_terms(t, back, first, second):
        back = lax.ppermute(back, "chan", to_partner(t))
        here, core, chip, cross = own_terms(first, second, SRC // groups, scale)
        core = lax.ppermute(core, "win", other_core)
        chip = lax.ppermute(chip, "win", other_chip)
        cross = lax.ppermute(cross, "win", other_both)
        return here, *keep(core, chip, cross, back)

    def by_round(run, *values):
        branches = [functools.partial(run, t) for t in range(1, blocks)]
        return lax.switch(partner[0, 0] - 1, branches, *values)

    tables = [jnp.asarray(v) for v in shift_tables(freqs)]
    part, sibling, piece, back_recv, first = by_round(
        send_sources, *whiten(spectra, counts)
    )
    back, second = terms(part, sibling, piece, tables, scale)
    back = (back + back_recv.astype(jnp.float32)).astype(jnp.bfloat16)
    return place(*by_round(send_terms, back, first, second))[None, None]


def lag_table(freqs, lags):
    freq = jnp.arange(freqs, dtype=jnp.float32) + freqs // 4
    delay = jnp.arange(lags, dtype=jnp.float32) - lags // 2
    phase = 2.0 * math.pi * freq[:, None] * delay[None, :] / (4.0 * freqs)
    norm = 1.0 / math.sqrt(2.0 * freqs)
    return jnp.stack([jnp.cos(phase), -jnp.sin(phase)]) * norm


def blended_sources(sources, table):
    src = sources.astype(jnp.float32)
    first = src[:, :, 0][:, :, None, :]
    second = src[:, :, 1][:, :, None, :]
    cos_part = table[0].T[None, None]
    sin_part = table[1].T[None, None]
    real_mix = first * cos_part + second * sin_part
    imag_mix = second * cos_part - first * sin_part
    return jnp.stack([real_mix, imag_mix], axis=3).astype(jnp.bfloat16)


def pair_terms(sources, receiver_blocks, table):
    wins, count, two, freqs = sources.shape
    lags = table.shape[2]
    group = math.gcd(count, 32)
    flat_recv = receiver_blocks.reshape(wins, receiver_blocks.shape[1], two * freqs)
    grouped = jnp.moveaxis(sources.reshape(wins, count // group, group, two, freqs), 1, 0)

    def one_group(piece):
        mixed_spectra = blended_sources(piece, table).reshape(wins, group * lags, two * freqs)
        out = jnp.einsum(
            "wmx,wrx->mr", mixed_spectra, flat_recv, preferred_element_type=jnp.float32
        )
        return out.reshape(group, lags, receiver_blocks.shape[1])

    out = lax.map(one_group, grouped).reshape(count, lags, receiver_blocks.shape[1])
    return jnp.transpose(out, (1, 0, 2))


def route_blocks(values, round_flags, levels):
    for level in range(levels):
        moved = from_partner(values, "chan", level)
        values = jnp.where((round_flags >> level) % 2 == 1, moved, values)
    return values


def general_body(spectra, counts, partner):
    white = whiten_local(spectra, counts[0])
    table = lag_table(spectra.shape[3], LAGS)
    levels = lax.axis_size("chan").bit_length() - 1
    windows = spectra.shape[0] * lax.axis_size("win")
    receiver_blocks = route_blocks(white, partner[0, 0], levels)
    out = pair_terms(white[:, :SRC], receiver_blocks, table)
    stacked = lax.psum_scatter(out, "win", scatter_dimension=1, tiled=True)
    return (stacked / math.sqrt(windows))[None, None]


def solution(mesh):
    body = pair_body if mesh.shape["win"] == 4 else general_body
    return jax.shard_map(
        body,
        mesh=mesh,
        in_specs=(P("win", "chan", None, None), P("chan"), P()),
        out_specs=P("chan", None, None, "win", None),
        check_vma=False,
    )
```

```python
import functools
import math

import jax
import jax.numpy as jnp
import numpy as np
from jax import lax
from jax.experimental import pallas as pl
from jax.experimental.pallas import tpu as pltpu
from jax.sharding import PartitionSpec as P

LAGS = 16
SRC = 160
HALF = LAGS // 2
VMEM_LIMIT = 16 * 1024 * 1024


def from_partner(value, axis, stride):
    return lax.ppermute(value, axis, [(i, i ^ 1 << stride) for i in range(lax.axis_size(axis))])


def whiten_local(spectra, count):
    values = spectra.astype(jnp.float32)
    block_size = spectra.shape[1]
    freqs = spectra.shape[3]
    valid = (jnp.arange(block_size, dtype=jnp.int32) < count).astype(jnp.float32)
    freq = jnp.arange(freqs, dtype=jnp.float32)
    taper = 0.75 - 0.25 * jnp.cos(2.0 * math.pi * (freq + 0.5) / freqs)
    power = jnp.mean(values * values, axis=(2, 3))
    scale = valid[None, :] / jnp.sqrt(power + 1e-05)
    return (values * taper * scale[:, :, None, None]).astype(jnp.bfloat16)


def shift_tables(freqs):
    freq = np.arange(freqs, dtype=np.float64) + freqs // 4
    shift = np.arange(1, HALF + 1, dtype=np.float64)
    phase = 2.0 * np.pi * shift[:, None] * freq[None, :] / (4.0 * freqs)
    return np.cos(phase).astype(np.float32), np.sin(phase).astype(np.float32)


def place_of_core():
    spot = lax.axis_index("win")
    return spot // 2, spot % 2


def whole():
    return pl.BlockSpec(memory_space=pltpu.VMEM)


def anywhere():
    return pl.BlockSpec(memory_space=pl.ANY)


def kernel_params():
    return pltpu.CompilerParams(vmem_limit_bytes=VMEM_LIMIT)


def fetch_kernel(source_ref, out_ref, sems):
    windows, parts = out_ref.shape[0], sems.shape[1]
    step = out_ref.shape[1] // parts
    copies = []
    for w in range(windows):
        for i in range(parts):
            part = (w, pl.ds(i * step, step))
            copies.append(
                pltpu.make_async_copy(source_ref.at[part], out_ref.at[part], sems.at[w, i])
            )
            copies[-1].start()
    for copy in copies:
        copy.wait()


def fetch(value):
    return pl.pallas_call(
        fetch_kernel,
        in_specs=[pl.BlockSpec(memory_space=pltpu.HBM)],
        out_specs=whole(),
        out_shape=jax.ShapeDtypeStruct(value.shape, value.dtype),
        scratch_shapes=[pltpu.SemaphoreType.DMA((value.shape[0], 4))],
        compiler_params=kernel_params(),
        name="fetch",
    )(pltpu.with_memory_space_constraint(value, pltpu.HBM))


def whiten_kernel(count_ref, raw_ref, taper_ref, white_ref, *refs):
    *piece_refs, count, sem = refs
    copy = pltpu.make_async_copy(count_ref, count, sem)
    copy.start()
    x, core = place_of_core()
    windows, channels, width = raw_ref.shape
    mine = SRC // 4
    step = 2 * mine
    copy.wait()
    for w in range(windows):
        for index in range(channels // step):
            block = (1 - x, x)[index] if index * step < SRC else index
            begin = block * step
            line = pl.ds(pl.multiple_of(begin, step), step)
            values = raw_ref[w, line, :].astype(jnp.float32)
            power = jnp.sum(values * values, axis=1, keepdims=True) * (1.0 / width)
            row = begin + lax.broadcasted_iota(jnp.int32, (step, 1), 0)
            valid = (row < count[0]).astype(jnp.float32)
            scale = valid / jnp.sqrt(power + 1e-05)
            values = values * taper_ref[...] * scale
            white_ref[w, line, :] = values.astype(jnp.bfloat16)
            if index * step < SRC:
                low, high = values[:mine], values[mine:]
                first = core == 0
                near_ref, far_ref = piece_refs[2 * index:2 * index + 2]
                near_ref[w] = jnp.where(first, low, high).astype(jnp.bfloat16)
                far_ref[w] = jnp.where(first, high, low).astype(jnp.bfloat16)


def whiten(spectra, counts):
    windows, channels, two, freqs = spectra.shape
    width = two * freqs
    freq = np.arange(freqs, dtype=np.float64)
    taper = 0.75 - 0.25 * np.cos(2.0 * np.pi * (freq + 0.5) / freqs)
    taper = np.tile(taper.astype(np.float32), two)[None, :]
    piece = jax.ShapeDtypeStruct((windows, SRC // 4, width), jnp.bfloat16)
    return pl.pallas_call(
        whiten_kernel,
        in_specs=[anywhere(), whole(), whole()],
        out_specs=[whole()] * 5,
        out_shape=[jax.ShapeDtypeStruct((windows, channels, width), jnp.bfloat16)]
        + [piece] * 4,
        scratch_shapes=[pltpu.SMEM((1,), jnp.int32), pltpu.SemaphoreType.DMA],
        compiler_params=kernel_params(),
        name="whiten",
    )(counts, fetch(spectra).reshape(windows, channels, width), jnp.asarray(taper))


def mix(m_ref, piece, cos_ref, sin_ref, low, high):
    rows = piece.shape[0]
    vrow = v_row(rows)
    real = piece[:, low].astype(jnp.float32)
    imag = piece[:, high].astype(jnp.float32)

    def put(where, cols, values):
        m_ref[where, cols] = jnp.concatenate(values, axis=0).astype(jnp.bfloat16)

    for m in range(0, HALF, 2):
        c = [cos_ref[m + i:m + i + 1, low] for i in range(2)]
        s = [sin_ref[m + i:m + i + 1, low] for i in range(2)]
        line = slice(m * rows, (m + 2) * rows)
        vline = slice(vrow + m * rows, vrow + (m + 2) * rows)
        put(line, low, [real * v for v in c])
        put(line, high, [imag * v for v in c])
        put(vline, low, [imag * -v for v in s])
        put(vline, high, [real * v for v in s])
    fill = jnp.zeros((vrow - (HALF + 1) * rows, 128), jnp.float32)
    for value, cols in ((real, low), (imag, high)):
        put(slice(HALF * rows, vrow), cols, [value, fill])


def v_row(rows):
    return -(-(HALF + 1) * rows // 128) * 128


def times(lhs, rhs):
    return lax.dot_general(
        lhs, rhs, (((1,), (1,)), ((), ())), preferred_element_type=jnp.float32
    )


def add_products(acc_ref, lhs_ref, piece_ref, cos_ref, sin_ref, mixed_ref):
    windows, rows, width = piece_ref.shape
    tile = 256
    used = v_row(rows) + HALF * rows
    if used < mixed_ref.shape[0]:
        mixed_ref[used:, :] = jnp.zeros_like(mixed_ref[used:, :])

    @pl.loop(0, windows)
    def _(w):
        @pl.loop(0, width // 2, step=128)
        def _(start):
            low = pl.ds(pl.multiple_of(start, 128), 128)
            high = pl.ds(pl.multiple_of(width // 2 + start, 128), 128)
            mix(mixed_ref, piece_ref.at[w], cos_ref, sin_ref, low, high)

        @pl.loop(0, mixed_ref.shape[0], step=tile)
        def _(n):
            cols = pl.ds(pl.multiple_of(n, tile), tile)
            acc_ref[:, cols] += times(lhs_ref[w], mixed_ref[cols, :])


def part_kernel(white_ref, piece_ref, cos_ref, sin_ref, _, part_ref, done_ref, mixed_ref):
    done_ref[...] = jnp.zeros_like(done_ref)
    part_ref[...] = jnp.zeros_like(part_ref)
    add_products(part_ref, white_ref, piece_ref, cos_ref, sin_ref, mixed_ref)


def part_columns(rows):
    columns = v_row(rows) + HALF * rows
    return columns + (-columns) % 256


def part_terms(white, piece, tables, done):
    windows, channels, width = white.shape
    columns = part_columns(piece.shape[1])
    return pl.pallas_call(
        part_kernel,
        in_specs=[whole()] * 5,
        out_specs=[whole()] * 2,
        out_shape=[jax.ShapeDtypeStruct((channels, columns), jnp.float32), TOKEN],
        scratch_shapes=[pltpu.VMEM((columns, width), jnp.bfloat16)],
        compiler_params=kernel_params(),
        cost_estimate=LATE,
        name="terms_part",
    )(white, piece, *tables, done)


TOKEN = jax.ShapeDtypeStruct((8, 128), jnp.float32)
LATE = pl.CostEstimate(flops=30 * 10**9, bytes_accessed=0, transcendentals=0)


def pack(acc_ref, line, rows, scale, later):
    wide = HALF * rows
    vrow = v_row(rows)
    u, v = acc_ref[line, :wide] * scale, acc_ref[line, vrow:vrow + wide] * scale
    still = acc_ref[line, wide:wide + rows] * scale
    first, last = (u - v, u + v) if later else (u + v, u - v)
    return jnp.concatenate([first, last[:, :wide - rows], still], axis=1)


def first_kernel(
    scale, part_ref, sibling_ref, piece_ref, cos_ref, sin_ref, _, back_ref, own_ref,
    done_ref, mixed_ref, acc_ref,
):
    done_ref[...] = jnp.zeros_like(done_ref)
    acc_ref[...] = part_ref[...]
    add_products(acc_ref, sibling_ref, piece_ref, cos_ref, sin_ref, mixed_ref)
    line = pl.ds(SRC, acc_ref.shape[0] - SRC)
    back = pack(acc_ref, line, piece_ref.shape[1], scale, True)
    back_ref[...] = back.astype(back_ref.dtype)
    own_ref[...] = acc_ref[:SRC, :]


def second_kernel(scale, part_ref, sibling_ref, piece_ref, cos_ref, sin_ref, *refs):
    back_ref, own_ref, even_ref, odd_ref, acc_ref = refs
    windows, rows, width = piece_ref.shape
    freqs = width // 2
    starts = [
        (slice(n, n + 128), slice(freqs + n, freqs + n + 128)) for n in range(0, freqs, 128)
    ]
    tiles = [
        slice(n, min(n + 256, acc_ref.shape[1])) for n in range(0, acc_ref.shape[1], 256)
    ]
    buffers = even_ref, odd_ref
    for start in starts:
        mix(even_ref, piece_ref.at[0], cos_ref, sin_ref, *start)
    for w in range(windows):
        now_ref, next_ref = buffers[w % 2], buffers[1 - w % 2]
        todo = starts if w + 1 < windows else []
        for cols in tiles:
            before = part_ref[:, cols] if w == 0 else acc_ref[:, cols]
            acc_ref[:, cols] = before + times(sibling_ref[w], now_ref[cols, :])
            for start in todo[:2]:
                mix(next_ref, piece_ref.at[w + 1], cos_ref, sin_ref, *start)
            todo = todo[2:]
    back_ref[...] = pack(acc_ref, pl.ds(SRC, acc_ref.shape[0] - SRC), rows, scale, True)
    own_ref[...] = acc_ref[:SRC, :]


def own_kernel(scale, rows, first_ref, second_ref, *refs):
    *out_refs, packed_ref = refs
    x, core = place_of_core()
    mine = SRC // 4

    @pl.loop(0, SRC, step=mine)
    def _(start):
        line = pl.ds(pl.multiple_of(start, 8), mine)
        for quarter, ref in enumerate((first_ref, second_ref)):
            packed_ref[quarter, line, :] = pack(ref, line, rows, scale, False)

    for i, out_ref in enumerate(out_refs):
        spot = 2 * (x, 1 - x)[i // 2] + (core, 1 - core)[i % 2]
        line = pl.ds(pl.multiple_of(spot * mine, 8), mine)
        for quarter in range(2):
            out_ref[quarter] = packed_ref[quarter, line, :].astype(out_ref.dtype)


def own_terms(first, second, rows, scale):
    mine, wide = SRC // 4, 2 * HALF * rows
    return pl.pallas_call(
        functools.partial(own_kernel, scale, rows),
        in_specs=[whole()] * 2,
        out_specs=[whole()] * 4,
        out_shape=[
            jax.ShapeDtypeStruct((2, mine, wide), jnp.float32 if i == 0 else jnp.bfloat16)
            for i in range(4)
        ],
        scratch_shapes=[pltpu.VMEM((2, SRC, wide), jnp.float32)],
        compiler_params=kernel_params(),
        name="own_terms",
    )(first, second)


def terms(part, sibling, piece, tables, scale, done=None):
    windows, channels, width = sibling.shape
    rows = piece.shape[1]
    second = done is None
    columns = v_row(rows) + HALF * rows if second else part_columns(rows)
    back = ((channels - SRC, 2 * HALF * rows), jnp.float32 if second else jnp.bfloat16)
    out = [jax.ShapeDtypeStruct(*back), jax.ShapeDtypeStruct((SRC, columns), jnp.float32)]
    out += [] if second else [TOKEN]
    more = () if second else (done,)
    return pl.pallas_call(
        functools.partial(second_kernel if second else first_kernel, scale),
        in_specs=[whole()] * (5 + len(more)),
        out_specs=[whole()] * len(out),
        out_shape=out,
        scratch_shapes=[pltpu.VMEM((columns, width), jnp.bfloat16)] * (2 if second else 1)
        + [pltpu.VMEM((channels, columns), jnp.float32)],
        compiler_params=kernel_params(),
        cost_estimate=LATE,
        name="terms_second" if second else "terms_first",
    )(part, sibling, piece, *tables, *more)


def copy_rows(source_ref, out_ref):
    rows = source_ref.shape[-2]
    if rows % 4:
        out_ref[...] = source_ref[...]
        return
    step = rows // 4 if rows % 64 == 0 else rows

    @pl.loop(0, rows, step=step)
    def _(start):
        line = pl.ds(pl.multiple_of(start, 16 if step % 16 == 0 else 8), step)
        out_ref[..., line, :] = source_ref[..., line, :]


def keep_kernel(*refs):
    half = len(refs) // 2
    for source_ref, out_ref in zip(refs[:half], refs[half:]):
        copy_rows(source_ref, out_ref)


def hold_kernel(source_ref, *refs):
    *_, out_ref, done_ref = refs
    copy_rows(source_ref, out_ref)
    done_ref[...] = jnp.zeros_like(done_ref)


def keep(*values):
    return pl.pallas_call(
        keep_kernel,
        in_specs=[whole()] * len(values),
        out_specs=[whole()] * len(values),
        out_shape=[jax.ShapeDtypeStruct(v.shape, v.dtype) for v in values],
        compiler_params=kernel_params(),
        name="keep",
    )(*values)


def hold(value, *done):
    return pl.pallas_call(
        hold_kernel,
        in_specs=[whole()] * (1 + len(done)),
        out_specs=[whole()] * 2,
        out_shape=[jax.ShapeDtypeStruct(value.shape, value.dtype), TOKEN],
        compiler_params=kernel_params(),
        name="hold",
    )(value, *done)


def keep_after(value, done):
    return pl.pallas_call(
        lambda source_ref, _, out_ref: copy_rows(source_ref, out_ref),
        in_specs=[whole()] * 2,
        out_specs=whole(),
        out_shape=jax.ShapeDtypeStruct(value.shape, value.dtype),
        compiler_params=kernel_params(),
        name="keep_after",
    )(value, done)


def place_kernel(
    here_ref, core_ref, chip_ref, cross_ref, back_ref, out_ref, block_ref, sems
):
    x, core = place_of_core()
    lags, mine, channels = block_ref.shape
    swap = core != 0
    sides = []
    for q in range(2):
        index = jnp.where(x == q, 1, 0)
        own = here_ref[index] + chip_ref[1 - index].astype(jnp.float32)
        other = core_ref[index].astype(jnp.float32) + cross_ref[1 - index].astype(jnp.float32)
        sides += [jnp.where(swap, other, own), jnp.where(swap, own, other)]
    back = back_ref[...].astype(jnp.float32).T
    copies = []
    for j in range(lags):
        lag = HALF - 1 - j if j < HALF else j + 1 if j < lags - 1 else HALF
        cols = slice(j * mine, (j + 1) * mine)
        block_ref[lag, :, :SRC] = jnp.concatenate([v[:, cols] for v in sides], axis=1)
        block_ref[lag, :, SRC:] = back[cols]
        copies.append(pltpu.make_async_copy(block_ref.at[lag], out_ref.at[lag], sems.at[lag]))
        copies[-1].start()
    for copy in copies:
        copy.wait()


def place(here, core, chip, cross, back):
    _, mine, wide = here.shape
    shape = (wide // mine, mine, SRC + back.shape[0])
    return pl.pallas_call(
        place_kernel,
        in_specs=[whole()] * 5,
        out_specs=anywhere(),
        out_shape=jax.ShapeDtypeStruct(shape, jnp.float32),
        scratch_shapes=[
            pltpu.VMEM(shape, jnp.float32), pltpu.SemaphoreType.DMA((shape[0],))
        ],
        compiler_params=kernel_params(),
        name="place_lags",
    )(here, core, chip, cross, back)


def pair_body(spectra, counts, partner):
    blocks = lax.axis_size("chan")
    groups = lax.axis_size("win")
    windows, channels, two, freqs = spectra.shape
    scale = 1.0 / (math.sqrt(2.0 * freqs) * math.sqrt(windows * groups))
    other_core = [(i, i ^ 1) for i in range(groups)]
    other_chip = [(i, i ^ 2) for i in range(groups)]
    other_both = [(i, i ^ 3) for i in range(groups)]

    def to_partner(t):
        return [(i, i ^ t) for i in range(blocks)]

    def to_partner_core(t):
        return [
            (i * groups + g, (i ^ t) * groups + (g ^ 1))
            for i in range(blocks)
            for g in range(groups)
        ]

    def send_sources(t, white, near, far, near_more, far_more):
        def straight(value):
            return lax.ppermute(value, "chan", to_partner(t))

        def crossed(value):
            return lax.ppermute(value, ("chan", "win"), to_partner_core(t))

        sibling = lax.ppermute(white, "win", other_core)
        near, far = straight(near), crossed(far)
        near_more, done = hold(near_more, near)
        near_more = straight(near_more)
        part, done = part_terms(white, near, tables, done)
        far_more, done = hold(far_more, far, done)
        far_more = crossed(far_more)
        back, own, done = terms(part, sibling, far, tables, scale, done)
        back = lax.ppermute(back, "win", other_chip)
        part, done = part_terms(white, near_more, tables, done)
        return part, *keep(sibling), keep_after(far_more, done), *keep(back), own

    def send_terms(t, back, first, second):
        back = lax.ppermute(back, "chan", to_partner(t))
        here, core, chip, cross = own_terms(first, second, SRC // groups, scale)
        core = lax.ppermute(core, "win", other_core)
        chip = lax.ppermute(chip, "win", other_chip)
        cross = lax.ppermute(cross, "win", other_both)
        return here, *keep(core, chip, cross, back)

    def by_round(run, *values):
        branches = [functools.partial(run, t) for t in range(1, blocks)]
        return lax.switch(partner[0, 0] - 1, branches, *values)

    tables = [jnp.asarray(v) for v in shift_tables(freqs)]
    part, sibling, piece, back_recv, first = by_round(
        send_sources, *whiten(spectra, counts)
    )
    back, second = terms(part, sibling, piece, tables, scale)
    back = (back + back_recv.astype(jnp.float32)).astype(jnp.bfloat16)
    return place(*by_round(send_terms, back, first, second))[None, None]


def lag_table(freqs, lags):
    freq = jnp.arange(freqs, dtype=jnp.float32) + freqs // 4
    delay = jnp.arange(lags, dtype=jnp.float32) - lags // 2
    phase = 2.0 * math.pi * freq[:, None] * delay[None, :] / (4.0 * freqs)
    norm = 1.0 / math.sqrt(2.0 * freqs)
    return jnp.stack([jnp.cos(phase), -jnp.sin(phase)]) * norm


def blended_sources(sources, table):
    src = sources.astype(jnp.float32)
    first = src[:, :, 0][:, :, None, :]
    second = src[:, :, 1][:, :, None, :]
    cos_part = table[0].T[None, None]
    sin_part = table[1].T[None, None]
    real_mix = first * cos_part + second * sin_part
    imag_mix = second * cos_part - first * sin_part
    return jnp.stack([real_mix, imag_mix], axis=3).astype(jnp.bfloat16)


def pair_terms(sources, receiver_blocks, table):
    wins, count, two, freqs = sources.shape
    lags = table.shape[2]
    group = math.gcd(count, 32)
    flat_recv = receiver_blocks.reshape(wins, receiver_blocks.shape[1], two * freqs)
    grouped = jnp.moveaxis(sources.reshape(wins, count // group, group, two, freqs), 1, 0)

    def one_group(piece):
        mixed_spectra = blended_sources(piece, table).reshape(wins, group * lags, two * freqs)
        out = jnp.einsum(
            "wmx,wrx->mr", mixed_spectra, flat_recv, preferred_element_type=jnp.float32
        )
        return out.reshape(group, lags, receiver_blocks.shape[1])

    out = lax.map(one_group, grouped).reshape(count, lags, receiver_blocks.shape[1])
    return jnp.transpose(out, (1, 0, 2))


def route_blocks(values, round_flags, levels):
    for level in range(levels):
        moved = from_partner(values, "chan", level)
        values = jnp.where((round_flags >> level) % 2 == 1, moved, values)
    return values


def general_body(spectra, counts, partner):
    white = whiten_local(spectra, counts[0])
    table = lag_table(spectra.shape[3], LAGS)
    levels = lax.axis_size("chan").bit_length() - 1
    windows = spectra.shape[0] * lax.axis_size("win")
    receiver_blocks = route_blocks(white, partner[0, 0], levels)
    out = pair_terms(white[:, :SRC], receiver_blocks, table)
    stacked = lax.psum_scatter(out, "win", scatter_dimension=1, tiled=True)
    return (stacked / math.sqrt(windows))[None, None]


def solution(mesh):
    body = pair_body if mesh.shape["win"] == 4 else general_body
    return jax.shard_map(
        body,
        mesh=mesh,
        in_specs=(P("win", "chan", None, None), P("chan"), P()),
        out_specs=P("chan", None, None, "win", None),
        check_vma=False,
    )
```

```python
import functools
import math

import jax
import jax.numpy as jnp
import numpy as np
from jax import lax
from jax.experimental import pallas as pl
from jax.experimental.pallas import tpu as pltpu
from jax.sharding import PartitionSpec as P

LAGS = 16
SRC = 160
HALF = LAGS // 2
VMEM_LIMIT = 16 * 1024 * 1024


def from_partner(value, axis, stride):
    return lax.ppermute(value, axis, [(i, i ^ 1 << stride) for i in range(lax.axis_size(axis))])


def whiten_local(spectra, count):
    values = spectra.astype(jnp.float32)
    block_size = spectra.shape[1]
    freqs = spectra.shape[3]
    valid = (jnp.arange(block_size, dtype=jnp.int32) < count).astype(jnp.float32)
    freq = jnp.arange(freqs, dtype=jnp.float32)
    taper = 0.75 - 0.25 * jnp.cos(2.0 * math.pi * (freq + 0.5) / freqs)
    power = jnp.mean(values * values, axis=(2, 3))
    scale = valid[None, :] / jnp.sqrt(power + 1e-05)
    return (values * taper * scale[:, :, None, None]).astype(jnp.bfloat16)


def shift_tables(freqs):
    freq = np.arange(freqs, dtype=np.float64) + freqs // 4
    shift = np.arange(1, HALF + 1, dtype=np.float64)
    phase = 2.0 * np.pi * shift[:, None] * freq[None, :] / (4.0 * freqs)
    return np.cos(phase).astype(np.float32), np.sin(phase).astype(np.float32)


def place_of_core():
    spot = lax.axis_index("win")
    return spot // 2, spot % 2


def whole():
    return pl.BlockSpec(memory_space=pltpu.VMEM)


def anywhere():
    return pl.BlockSpec(memory_space=pl.ANY)


def kernel_params():
    return pltpu.CompilerParams(vmem_limit_bytes=VMEM_LIMIT)


def fetch_kernel(source_ref, out_ref, sems):
    windows, parts = out_ref.shape[0], sems.shape[1]
    step = out_ref.shape[1] // parts
    copies = []
    for w in range(windows):
        for i in range(parts):
            part = (w, pl.ds(i * step, step))
            copies.append(
                pltpu.make_async_copy(source_ref.at[part], out_ref.at[part], sems.at[w, i])
            )
            copies[-1].start()
    for copy in copies:
        copy.wait()


def fetch(value):
    return pl.pallas_call(
        fetch_kernel,
        in_specs=[pl.BlockSpec(memory_space=pltpu.HBM)],
        out_specs=whole(),
        out_shape=jax.ShapeDtypeStruct(value.shape, value.dtype),
        scratch_shapes=[pltpu.SemaphoreType.DMA((value.shape[0], 4))],
        compiler_params=kernel_params(),
        name="fetch",
    )(pltpu.with_memory_space_constraint(value, pltpu.HBM))


def whiten_kernel(count_ref, raw_ref, taper_ref, white_ref, *refs):
    *piece_refs, count, sem = refs
    copy = pltpu.make_async_copy(count_ref, count, sem)
    copy.start()
    x, core = place_of_core()
    windows, channels, width = raw_ref.shape
    mine = SRC // 4
    step = 2 * mine
    copy.wait()
    for w in range(windows):
        for index in range(channels // step):
            block = (1 - x, x)[index] if index * step < SRC else index
            begin = block * step
            line = pl.ds(pl.multiple_of(begin, step), step)
            values = raw_ref[w, line, :].astype(jnp.float32)
            power = jnp.sum(values * values, axis=1, keepdims=True) * (1.0 / width)
            row = begin + lax.broadcasted_iota(jnp.int32, (step, 1), 0)
            valid = (row < count[0]).astype(jnp.float32)
            scale = valid / jnp.sqrt(power + 1e-05)
            values = values * taper_ref[...] * scale
            white_ref[w, line, :] = values.astype(jnp.bfloat16)
            if index * step < SRC:
                low, high = values[:mine], values[mine:]
                first = core == 0
                near_ref, far_ref = piece_refs[2 * index:2 * index + 2]
                near_ref[w] = jnp.where(first, low, high).astype(jnp.bfloat16)
                far_ref[w] = jnp.where(first, high, low).astype(jnp.bfloat16)


def whiten(spectra, counts):
    windows, channels, two, freqs = spectra.shape
    width = two * freqs
    freq = np.arange(freqs, dtype=np.float64)
    taper = 0.75 - 0.25 * np.cos(2.0 * np.pi * (freq + 0.5) / freqs)
    taper = np.tile(taper.astype(np.float32), two)[None, :]
    piece = jax.ShapeDtypeStruct((windows, SRC // 4, width), jnp.bfloat16)
    return pl.pallas_call(
        whiten_kernel,
        in_specs=[anywhere(), whole(), whole()],
        out_specs=[whole()] * 5,
        out_shape=[jax.ShapeDtypeStruct((windows, channels, width), jnp.bfloat16)]
        + [piece] * 4,
        scratch_shapes=[pltpu.SMEM((1,), jnp.int32), pltpu.SemaphoreType.DMA],
        compiler_params=kernel_params(),
        name="whiten",
    )(counts, fetch(spectra).reshape(windows, channels, width), jnp.asarray(taper))


def mix(m_ref, piece, cos_ref, sin_ref, low, high):
    rows = piece.shape[0]
    vrow = v_row(rows)
    real = piece[:, low].astype(jnp.float32)
    imag = piece[:, high].astype(jnp.float32)

    def put(where, cols, values):
        m_ref[where, cols] = jnp.concatenate(values, axis=0).astype(jnp.bfloat16)

    for m in range(0, HALF, 2):
        c = [cos_ref[m + i:m + i + 1, low] for i in range(2)]
        s = [sin_ref[m + i:m + i + 1, low] for i in range(2)]
        line = slice(m * rows, (m + 2) * rows)
        vline = slice(vrow + m * rows, vrow + (m + 2) * rows)
        put(line, low, [real * v for v in c])
        put(line, high, [imag * v for v in c])
        put(vline, low, [imag * -v for v in s])
        put(vline, high, [real * v for v in s])
    fill = jnp.zeros((vrow - (HALF + 1) * rows, 128), jnp.float32)
    for value, cols in ((real, low), (imag, high)):
        put(slice(HALF * rows, vrow), cols, [value, fill])


def v_row(rows):
    return -(-(HALF + 1) * rows // 128) * 128


def times(lhs, rhs):
    return lax.dot_general(
        lhs, rhs, (((1,), (1,)), ((), ())), preferred_element_type=jnp.float32
    )


def add_products(acc_ref, lhs_ref, piece_ref, cos_ref, sin_ref, mixed_ref):
    windows, rows, width = piece_ref.shape
    tile = 256
    used = v_row(rows) + HALF * rows
    if used < mixed_ref.shape[0]:
        mixed_ref[used:, :] = jnp.zeros_like(mixed_ref[used:, :])

    @pl.loop(0, windows)
    def _(w):
        @pl.loop(0, width // 2, step=128)
        def _(start):
            low = pl.ds(pl.multiple_of(start, 128), 128)
            high = pl.ds(pl.multiple_of(width // 2 + start, 128), 128)
            mix(mixed_ref, piece_ref.at[w], cos_ref, sin_ref, low, high)

        @pl.loop(0, mixed_ref.shape[0], step=tile)
        def _(n):
            cols = pl.ds(pl.multiple_of(n, tile), tile)
            acc_ref[:, cols] += times(lhs_ref[w], mixed_ref[cols, :])


def part_kernel(white_ref, piece_ref, cos_ref, sin_ref, part_ref, done_ref, mixed_ref):
    done_ref[...] = jnp.zeros_like(done_ref)
    part_ref[...] = jnp.zeros_like(part_ref)
    add_products(part_ref, white_ref, piece_ref, cos_ref, sin_ref, mixed_ref)


def part_columns(rows):
    columns = v_row(rows) + HALF * rows
    return columns + (-columns) % 256


def part_terms(white, piece, tables):
    windows, channels, width = white.shape
    columns = part_columns(piece.shape[1])
    return pl.pallas_call(
        part_kernel,
        in_specs=[whole()] * 4,
        out_specs=[whole()] * 2,
        out_shape=[jax.ShapeDtypeStruct((channels, columns), jnp.float32), TOKEN],
        scratch_shapes=[pltpu.VMEM((columns, width), jnp.bfloat16)],
        compiler_params=kernel_params(),
        cost_estimate=COST,
        name="terms_part",
    )(white, piece, *tables)


TOKEN = jax.ShapeDtypeStruct((8, 128), jnp.float32)
COST = pl.CostEstimate(flops=10**9, bytes_accessed=0, transcendentals=0)


def pack(acc_ref, line, rows, scale, later):
    wide = HALF * rows
    vrow = v_row(rows)
    u, v = acc_ref[line, :wide] * scale, acc_ref[line, vrow:vrow + wide] * scale
    still = acc_ref[line, wide:wide + rows] * scale
    first, last = (u - v, u + v) if later else (u + v, u - v)
    return jnp.concatenate([first, last[:, :wide - rows], still], axis=1)


def first_kernel(
    scale, part_ref, sibling_ref, piece_ref, cos_ref, sin_ref, back_ref, own_ref,
    done_ref, mixed_ref, acc_ref,
):
    done_ref[...] = jnp.zeros_like(done_ref)
    acc_ref[...] = part_ref[...]
    add_products(acc_ref, sibling_ref, piece_ref, cos_ref, sin_ref, mixed_ref)
    line = pl.ds(SRC, acc_ref.shape[0] - SRC)
    back = pack(acc_ref, line, piece_ref.shape[1], scale, True)
    back_ref[...] = back.astype(back_ref.dtype)
    own_ref[...] = acc_ref[:SRC, :]


def second_kernel(scale, part_ref, sibling_ref, piece_ref, cos_ref, sin_ref, *refs):
    back_ref, own_ref, even_ref, odd_ref, acc_ref = refs
    windows, rows, width = piece_ref.shape
    freqs = width // 2
    starts = [
        (slice(n, n + 128), slice(freqs + n, freqs + n + 128)) for n in range(0, freqs, 128)
    ]
    tiles = [
        slice(n, min(n + 256, acc_ref.shape[1])) for n in range(0, acc_ref.shape[1], 256)
    ]
    buffers = even_ref, odd_ref
    for start in starts:
        mix(even_ref, piece_ref.at[0], cos_ref, sin_ref, *start)
    for w in range(windows):
        now_ref, next_ref = buffers[w % 2], buffers[1 - w % 2]
        todo = starts if w + 1 < windows else []
        for cols in tiles:
            before = part_ref[:, cols] if w == 0 else acc_ref[:, cols]
            acc_ref[:, cols] = before + times(sibling_ref[w], now_ref[cols, :])
            for start in todo[:2]:
                mix(next_ref, piece_ref.at[w + 1], cos_ref, sin_ref, *start)
            todo = todo[2:]
    back_ref[...] = pack(acc_ref, pl.ds(SRC, acc_ref.shape[0] - SRC), rows, scale, True)
    own_ref[...] = acc_ref[:SRC, :]


def own_kernel(scale, rows, first_ref, second_ref, *refs):
    *out_refs, packed_ref = refs
    x, core = place_of_core()
    mine = SRC // 4

    @pl.loop(0, SRC, step=mine)
    def _(start):
        line = pl.ds(pl.multiple_of(start, 8), mine)
        for quarter, ref in enumerate((first_ref, second_ref)):
            packed_ref[quarter, line, :] = pack(ref, line, rows, scale, False)

    for i, out_ref in enumerate(out_refs):
        spot = 2 * (x, 1 - x)[i // 2] + (core, 1 - core)[i % 2]
        line = pl.ds(pl.multiple_of(spot * mine, 8), mine)
        for quarter in range(2):
            out_ref[quarter] = packed_ref[quarter, line, :].astype(out_ref.dtype)


def own_terms(first, second, rows, scale):
    mine, wide = SRC // 4, 2 * HALF * rows
    return pl.pallas_call(
        functools.partial(own_kernel, scale, rows),
        in_specs=[whole()] * 2,
        out_specs=[whole()] * 4,
        out_shape=[
            jax.ShapeDtypeStruct((2, mine, wide), jnp.float32 if i == 0 else jnp.bfloat16)
            for i in range(4)
        ],
        scratch_shapes=[pltpu.VMEM((2, SRC, wide), jnp.float32)],
        compiler_params=kernel_params(),
        name="own_terms",
    )(first, second)


def terms(part, sibling, piece, tables, scale, short):
    windows, channels, width = sibling.shape
    rows = piece.shape[1]
    second = not short
    columns = v_row(rows) + HALF * rows if second else part_columns(rows)
    back = ((channels - SRC, 2 * HALF * rows), jnp.float32 if second else jnp.bfloat16)
    out = [jax.ShapeDtypeStruct(*back), jax.ShapeDtypeStruct((SRC, columns), jnp.float32)]
    out += [] if second else [TOKEN]
    return pl.pallas_call(
        functools.partial(second_kernel if second else first_kernel, scale),
        in_specs=[whole()] * 5,
        out_specs=[whole()] * len(out),
        out_shape=out,
        scratch_shapes=[pltpu.VMEM((columns, width), jnp.bfloat16)] * (2 if second else 1)
        + [pltpu.VMEM((channels, columns), jnp.float32)],
        compiler_params=kernel_params(),
        cost_estimate=COST,
        name="terms_second" if second else "terms_first",
    )(part, sibling, piece, *tables)


def copy_rows(source_ref, out_ref):
    rows = source_ref.shape[-2]
    if rows % 4:
        out_ref[...] = source_ref[...]
        return
    step = rows // 4 if rows % 64 == 0 else rows

    @pl.loop(0, rows, step=step)
    def _(start):
        line = pl.ds(pl.multiple_of(start, 16 if step % 16 == 0 else 8), step)
        out_ref[..., line, :] = source_ref[..., line, :]


def keep_kernel(*refs):
    half = len(refs) // 2
    for source_ref, out_ref in zip(refs[:half], refs[half:]):
        copy_rows(source_ref, out_ref)


def keep(*values):
    return pl.pallas_call(
        keep_kernel,
        in_specs=[whole()] * len(values),
        out_specs=[whole()] * len(values),
        out_shape=[jax.ShapeDtypeStruct(v.shape, v.dtype) for v in values],
        compiler_params=kernel_params(),
        name="keep",
    )(*values)


def hold(value, done):
    return pl.pallas_call(
        lambda source_ref, _, out_ref: copy_rows(source_ref, out_ref),
        in_specs=[whole()] * 2,
        out_specs=whole(),
        out_shape=jax.ShapeDtypeStruct(value.shape, value.dtype),
        compiler_params=kernel_params(),
        name="hold",
    )(value, done)


def place_kernel(
    here_ref, core_ref, chip_ref, cross_ref, back_ref, out_ref, block_ref, sems
):
    x, core = place_of_core()
    lags, mine, channels = block_ref.shape
    swap = core != 0
    sides = []
    for q in range(2):
        index = jnp.where(x == q, 1, 0)
        own = here_ref[index] + chip_ref[1 - index].astype(jnp.float32)
        other = core_ref[index].astype(jnp.float32) + cross_ref[1 - index].astype(jnp.float32)
        sides += [jnp.where(swap, other, own), jnp.where(swap, own, other)]
    back = back_ref[...].astype(jnp.float32).T
    copies = []
    for j in range(lags):
        lag = HALF - 1 - j if j < HALF else j + 1 if j < lags - 1 else HALF
        cols = slice(j * mine, (j + 1) * mine)
        block_ref[lag, :, :SRC] = jnp.concatenate([v[:, cols] for v in sides], axis=1)
        block_ref[lag, :, SRC:] = back[cols]
        copies.append(pltpu.make_async_copy(block_ref.at[lag], out_ref.at[lag], sems.at[lag]))
        copies[-1].start()
    for copy in copies:
        copy.wait()


def place(here, core, chip, cross, back):
    _, mine, wide = here.shape
    shape = (wide // mine, mine, SRC + back.shape[0])
    return pl.pallas_call(
        place_kernel,
        in_specs=[whole()] * 5,
        out_specs=anywhere(),
        out_shape=jax.ShapeDtypeStruct(shape, jnp.float32),
        scratch_shapes=[
            pltpu.VMEM(shape, jnp.float32), pltpu.SemaphoreType.DMA((shape[0],))
        ],
        compiler_params=kernel_params(),
        name="place_lags",
    )(here, core, chip, cross, back)


def pair_body(spectra, counts, partner):
    blocks = lax.axis_size("chan")
    groups = lax.axis_size("win")
    windows, channels, two, freqs = spectra.shape
    scale = 1.0 / (math.sqrt(2.0 * freqs) * math.sqrt(windows * groups))
    other_core = [(i, i ^ 1) for i in range(groups)]
    other_chip = [(i, i ^ 2) for i in range(groups)]
    other_both = [(i, i ^ 3) for i in range(groups)]

    def to_partner(t):
        return [(i, i ^ t) for i in range(blocks)]

    def to_partner_core(t):
        return [
            (i * groups + g, (i ^ t) * groups + (g ^ 1))
            for i in range(blocks)
            for g in range(groups)
        ]

    def send_sources(t, white, near, far, near_more, far_more):
        def straight(value):
            return lax.ppermute(value, "chan", to_partner(t))

        def crossed(value):
            return lax.ppermute(value, ("chan", "win"), to_partner_core(t))

        sibling = lax.ppermute(white, "win", other_core)
        near, far = straight(near), crossed(far)
        part, done = part_terms(white, near, tables)
        near_more = straight(hold(near_more, done))
        back, own, done = terms(part, sibling, far, tables, scale, True)
        back = lax.ppermute(back, "win", other_chip)
        far_more = crossed(hold(far_more, done))
        part, done = part_terms(white, near_more, tables)
        return part, *keep(sibling), hold(far_more, done), *keep(back), own

    def send_terms(t, back, first, second):
        back = lax.ppermute(back, "chan", to_partner(t))
        here, core, chip, cross = own_terms(first, second, SRC // groups, scale)
        core = lax.ppermute(core, "win", other_core)
        chip = lax.ppermute(chip, "win", other_chip)
        cross = lax.ppermute(cross, "win", other_both)
        return here, *keep(core, chip, cross, back)

    def by_round(run, *values):
        branches = [functools.partial(run, t) for t in range(1, blocks)]
        return lax.switch(partner[0, 0] - 1, branches, *values)

    tables = [jnp.asarray(v) for v in shift_tables(freqs)]
    part, sibling, piece, back_recv, first = by_round(
        send_sources, *whiten(spectra, counts)
    )
    back, second = terms(part, sibling, piece, tables, scale, False)
    back = (back + back_recv.astype(jnp.float32)).astype(jnp.bfloat16)
    return place(*by_round(send_terms, back, first, second))[None, None]


def lag_table(freqs, lags):
    freq = jnp.arange(freqs, dtype=jnp.float32) + freqs // 4
    delay = jnp.arange(lags, dtype=jnp.float32) - lags // 2
    phase = 2.0 * math.pi * freq[:, None] * delay[None, :] / (4.0 * freqs)
    norm = 1.0 / math.sqrt(2.0 * freqs)
    return jnp.stack([jnp.cos(phase), -jnp.sin(phase)]) * norm


def blended_sources(sources, table):
    src = sources.astype(jnp.float32)
    first = src[:, :, 0][:, :, None, :]
    second = src[:, :, 1][:, :, None, :]
    cos_part = table[0].T[None, None]
    sin_part = table[1].T[None, None]
    real_mix = first * cos_part + second * sin_part
    imag_mix = second * cos_part - first * sin_part
    return jnp.stack([real_mix, imag_mix], axis=3).astype(jnp.bfloat16)


def pair_terms(sources, receiver_blocks, table):
    wins, count, two, freqs = sources.shape
    lags = table.shape[2]
    group = math.gcd(count, 32)
    flat_recv = receiver_blocks.reshape(wins, receiver_blocks.shape[1], two * freqs)
    grouped = jnp.moveaxis(sources.reshape(wins, count // group, group, two, freqs), 1, 0)

    def one_group(piece):
        mixed_spectra = blended_sources(piece, table).reshape(wins, group * lags, two * freqs)
        out = jnp.einsum(
            "wmx,wrx->mr", mixed_spectra, flat_recv, preferred_element_type=jnp.float32
        )
        return out.reshape(group, lags, receiver_blocks.shape[1])

    out = lax.map(one_group, grouped).reshape(count, lags, receiver_blocks.shape[1])
    return jnp.transpose(out, (1, 0, 2))


def route_blocks(values, round_flags, levels):
    for level in range(levels):
        moved = from_partner(values, "chan", level)
        values = jnp.where((round_flags >> level) % 2 == 1, moved, values)
    return values


def general_body(spectra, counts, partner):
    white = whiten_local(spectra, counts[0])
    table = lag_table(spectra.shape[3], LAGS)
    levels = lax.axis_size("chan").bit_length() - 1
    windows = spectra.shape[0] * lax.axis_size("win")
    receiver_blocks = route_blocks(white, partner[0, 0], levels)
    out = pair_terms(white[:, :SRC], receiver_blocks, table)
    stacked = lax.psum_scatter(out, "win", scatter_dimension=1, tiled=True)
    return (stacked / math.sqrt(windows))[None, None]


def solution(mesh):
    body = pair_body if mesh.shape["win"] == 4 else general_body
    return jax.shard_map(
        body,
        mesh=mesh,
        in_specs=(P("win", "chan", None, None), P("chan"), P()),
        out_specs=P("chan", None, None, "win", None),
        check_vma=False,
    )
```

```python
import functools
import math

import jax
import jax.numpy as jnp
import numpy as np
from jax import lax
from jax.experimental import pallas as pl
from jax.experimental.pallas import tpu as pltpu
from jax.sharding import PartitionSpec as P

LAGS = 16
SRC = 160
HALF = LAGS // 2
VMEM_LIMIT = 16 * 1024 * 1024


def from_partner(value, axis, stride):
    return lax.ppermute(value, axis, [(i, i ^ 1 << stride) for i in range(lax.axis_size(axis))])


def whiten_local(spectra, count):
    values = spectra.astype(jnp.float32)
    block_size = spectra.shape[1]
    freqs = spectra.shape[3]
    valid = (jnp.arange(block_size, dtype=jnp.int32) < count).astype(jnp.float32)
    freq = jnp.arange(freqs, dtype=jnp.float32)
    taper = 0.75 - 0.25 * jnp.cos(2.0 * math.pi * (freq + 0.5) / freqs)
    power = jnp.mean(values * values, axis=(2, 3))
    scale = valid[None, :] / jnp.sqrt(power + 1e-05)
    return (values * taper * scale[:, :, None, None]).astype(jnp.bfloat16)


def shift_tables(freqs):
    freq = np.arange(freqs, dtype=np.float64) + freqs // 4
    shift = np.arange(1, HALF + 1, dtype=np.float64)
    phase = 2.0 * np.pi * shift[:, None] * freq[None, :] / (4.0 * freqs)
    return np.cos(phase).astype(np.float32), np.sin(phase).astype(np.float32)


def place_of_core():
    spot = lax.axis_index("win")
    return spot // 2, spot % 2


def whole():
    return pl.BlockSpec(memory_space=pltpu.VMEM)


def anywhere():
    return pl.BlockSpec(memory_space=pl.ANY)


def kernel_params():
    return pltpu.CompilerParams(vmem_limit_bytes=VMEM_LIMIT)


def fetch_kernel(source_ref, out_ref, sems):
    windows, parts = out_ref.shape[0], sems.shape[1]
    step = out_ref.shape[1] // parts
    copies = []
    for w in range(windows):
        for i in range(parts):
            part = (w, pl.ds(i * step, step))
            copies.append(
                pltpu.make_async_copy(source_ref.at[part], out_ref.at[part], sems.at[w, i])
            )
            copies[-1].start()
    for copy in copies:
        copy.wait()


def fetch(value):
    return pl.pallas_call(
        fetch_kernel,
        in_specs=[pl.BlockSpec(memory_space=pltpu.HBM)],
        out_specs=whole(),
        out_shape=jax.ShapeDtypeStruct(value.shape, value.dtype),
        scratch_shapes=[pltpu.SemaphoreType.DMA((value.shape[0], 4))],
        compiler_params=kernel_params(),
        name="fetch",
    )(pltpu.with_memory_space_constraint(value, pltpu.HBM))


def whiten_kernel(count_ref, raw_ref, taper_ref, white_ref, *refs):
    *piece_refs, count, sem = refs
    copy = pltpu.make_async_copy(count_ref, count, sem)
    copy.start()
    x, core = place_of_core()
    windows, channels, width = raw_ref.shape
    mine = SRC // 4
    step = 2 * mine
    copy.wait()
    for w in range(windows):
        for index in range(channels // step):
            block = (1 - x, x)[index] if index * step < SRC else index
            begin = block * step
            line = pl.ds(pl.multiple_of(begin, step), step)
            values = raw_ref[w, line, :].astype(jnp.float32)
            power = jnp.sum(values * values, axis=1, keepdims=True) * (1.0 / width)
            row = begin + lax.broadcasted_iota(jnp.int32, (step, 1), 0)
            valid = (row < count[0]).astype(jnp.float32)
            scale = valid / jnp.sqrt(power + 1e-05)
            values = values * taper_ref[...] * scale
            white_ref[w, line, :] = values.astype(jnp.bfloat16)
            if index * step < SRC:
                low, high = values[:mine], values[mine:]
                first = core == 0
                near_ref, far_ref = piece_refs[2 * index:2 * index + 2]
                near_ref[w] = jnp.where(first, low, high).astype(jnp.bfloat16)
                far_ref[w] = jnp.where(first, high, low).astype(jnp.bfloat16)


def whiten(spectra, counts):
    windows, channels, two, freqs = spectra.shape
    width = two * freqs
    freq = np.arange(freqs, dtype=np.float64)
    taper = 0.75 - 0.25 * np.cos(2.0 * np.pi * (freq + 0.5) / freqs)
    taper = np.tile(taper.astype(np.float32), two)[None, :]
    piece = jax.ShapeDtypeStruct((windows, SRC // 4, width), jnp.bfloat16)
    return pl.pallas_call(
        whiten_kernel,
        in_specs=[anywhere(), whole(), whole()],
        out_specs=[whole()] * 5,
        out_shape=[jax.ShapeDtypeStruct((windows, channels, width), jnp.bfloat16)]
        + [piece] * 4,
        scratch_shapes=[pltpu.SMEM((1,), jnp.int32), pltpu.SemaphoreType.DMA],
        compiler_params=kernel_params(),
        name="whiten",
    )(counts, fetch(spectra).reshape(windows, channels, width), jnp.asarray(taper))


def mix(m_ref, piece, cos_ref, sin_ref, low, high):
    rows = piece.shape[0]
    vrow = v_row(rows)
    real = piece[:, low].astype(jnp.float32)
    imag = piece[:, high].astype(jnp.float32)

    def put(where, cols, values):
        m_ref[where, cols] = jnp.concatenate(values, axis=0).astype(jnp.bfloat16)

    for m in range(0, HALF, 2):
        c = [cos_ref[m + i:m + i + 1, low] for i in range(2)]
        s = [sin_ref[m + i:m + i + 1, low] for i in range(2)]
        line = slice(m * rows, (m + 2) * rows)
        vline = slice(vrow + m * rows, vrow + (m + 2) * rows)
        put(line, low, [real * v for v in c])
        put(line, high, [imag * v for v in c])
        put(vline, low, [imag * -v for v in s])
        put(vline, high, [real * v for v in s])
    fill = jnp.zeros((vrow - (HALF + 1) * rows, 128), jnp.float32)
    for value, cols in ((real, low), (imag, high)):
        put(slice(HALF * rows, vrow), cols, [value, fill])


def v_row(rows):
    return -(-(HALF + 1) * rows // 128) * 128


def times(lhs, rhs):
    return lax.dot_general(
        lhs, rhs, (((1,), (1,)), ((), ())), preferred_element_type=jnp.float32
    )


def add_products(acc_ref, lhs_ref, piece_ref, cos_ref, sin_ref, mixed_ref):
    windows, rows, width = piece_ref.shape
    tile = 256
    used = v_row(rows) + HALF * rows
    if used < mixed_ref.shape[0]:
        mixed_ref[used:, :] = jnp.zeros_like(mixed_ref[used:, :])

    @pl.loop(0, windows)
    def _(w):
        @pl.loop(0, width // 2, step=128)
        def _(start):
            low = pl.ds(pl.multiple_of(start, 128), 128)
            high = pl.ds(pl.multiple_of(width // 2 + start, 128), 128)
            mix(mixed_ref, piece_ref.at[w], cos_ref, sin_ref, low, high)

        @pl.loop(0, mixed_ref.shape[0], step=tile)
        def _(n):
            cols = pl.ds(pl.multiple_of(n, tile), tile)
            acc_ref[:, cols] += times(lhs_ref[w], mixed_ref[cols, :])


def part_kernel(white_ref, piece_ref, cos_ref, sin_ref, _, part_ref, done_ref, mixed_ref):
    done_ref[...] = jnp.zeros_like(done_ref)
    part_ref[...] = jnp.zeros_like(part_ref)
    add_products(part_ref, white_ref, piece_ref, cos_ref, sin_ref, mixed_ref)


def part_columns(rows):
    columns = v_row(rows) + HALF * rows
    return columns + (-columns) % 256


def part_terms(white, piece, tables, done):
    windows, channels, width = white.shape
    columns = part_columns(piece.shape[1])
    return pl.pallas_call(
        part_kernel,
        in_specs=[whole()] * 5,
        out_specs=[whole()] * 2,
        out_shape=[jax.ShapeDtypeStruct((channels, columns), jnp.float32), TOKEN],
        scratch_shapes=[pltpu.VMEM((columns, width), jnp.bfloat16)],
        compiler_params=kernel_params(),
        cost_estimate=LATE,
        name="terms_part",
    )(white, piece, *tables, done)


TOKEN = jax.ShapeDtypeStruct((8, 128), jnp.float32)
LATE = pl.CostEstimate(flops=30 * 10**9, bytes_accessed=0, transcendentals=0)


def pack(acc_ref, line, rows, scale, later):
    wide = HALF * rows
    vrow = v_row(rows)
    u, v = acc_ref[line, :wide] * scale, acc_ref[line, vrow:vrow + wide] * scale
    still = acc_ref[line, wide:wide + rows] * scale
    first, last = (u - v, u + v) if later else (u + v, u - v)
    return jnp.concatenate([first, last[:, :wide - rows], still], axis=1)


def first_kernel(
    scale, part_ref, sibling_ref, piece_ref, cos_ref, sin_ref, _, back_ref, own_ref,
    done_ref, mixed_ref, acc_ref,
):
    done_ref[...] = jnp.zeros_like(done_ref)
    acc_ref[...] = part_ref[...]
    add_products(acc_ref, sibling_ref, piece_ref, cos_ref, sin_ref, mixed_ref)
    line = pl.ds(SRC, acc_ref.shape[0] - SRC)
    back = pack(acc_ref, line, piece_ref.shape[1], scale, True)
    back_ref[...] = back.astype(back_ref.dtype)
    own_ref[...] = acc_ref[:SRC, :]


def second_kernel(scale, part_ref, sibling_ref, piece_ref, cos_ref, sin_ref, *refs):
    back_ref, own_ref, even_ref, odd_ref, acc_ref = refs
    windows, rows, width = piece_ref.shape
    freqs = width // 2
    starts = [
        (slice(n, n + 128), slice(freqs + n, freqs + n + 128)) for n in range(0, freqs, 128)
    ]
    tiles = [
        slice(n, min(n + 256, acc_ref.shape[1])) for n in range(0, acc_ref.shape[1], 256)
    ]
    buffers = even_ref, odd_ref
    for start in starts:
        mix(even_ref, piece_ref.at[0], cos_ref, sin_ref, *start)
    for w in range(windows):
        now_ref, next_ref = buffers[w % 2], buffers[1 - w % 2]
        todo = starts if w + 1 < windows else []
        for cols in tiles:
            before = part_ref[:, cols] if w == 0 else acc_ref[:, cols]
            acc_ref[:, cols] = before + times(sibling_ref[w], now_ref[cols, :])
            for start in todo[:2]:
                mix(next_ref, piece_ref.at[w + 1], cos_ref, sin_ref, *start)
            todo = todo[2:]
    back_ref[...] = pack(acc_ref, pl.ds(SRC, acc_ref.shape[0] - SRC), rows, scale, True)
    own_ref[...] = acc_ref[:SRC, :]


def own_kernel(scale, rows, first_ref, second_ref, *refs):
    *out_refs, packed_ref = refs
    x, core = place_of_core()
    mine = SRC // 4

    @pl.loop(0, SRC, step=mine)
    def _(start):
        line = pl.ds(pl.multiple_of(start, 8), mine)
        for quarter, ref in enumerate((first_ref, second_ref)):
            packed_ref[quarter, line, :] = pack(ref, line, rows, scale, False)

    for i, out_ref in enumerate(out_refs):
        spot = 2 * (x, 1 - x)[i // 2] + (core, 1 - core)[i % 2]
        line = pl.ds(pl.multiple_of(spot * mine, 8), mine)
        for quarter in range(2):
            out_ref[quarter] = packed_ref[quarter, line, :].astype(out_ref.dtype)


def own_terms(first, second, rows, scale):
    mine, wide = SRC // 4, 2 * HALF * rows
    return pl.pallas_call(
        functools.partial(own_kernel, scale, rows),
        in_specs=[whole()] * 2,
        out_specs=[whole()] * 4,
        out_shape=[
            jax.ShapeDtypeStruct((2, mine, wide), jnp.float32 if i == 0 else jnp.bfloat16)
            for i in range(4)
        ],
        scratch_shapes=[pltpu.VMEM((2, SRC, wide), jnp.float32)],
        compiler_params=kernel_params(),
        name="own_terms",
    )(first, second)


def terms(part, sibling, piece, tables, scale, done=None):
    windows, channels, width = sibling.shape
    rows = piece.shape[1]
    second = done is None
    columns = v_row(rows) + HALF * rows if second else part_columns(rows)
    back = ((channels - SRC, 2 * HALF * rows), jnp.float32 if second else jnp.bfloat16)
    out = [jax.ShapeDtypeStruct(*back), jax.ShapeDtypeStruct((SRC, columns), jnp.float32)]
    out += [] if second else [TOKEN]
    more = () if second else (done,)
    return pl.pallas_call(
        functools.partial(second_kernel if second else first_kernel, scale),
        in_specs=[whole()] * (5 + len(more)),
        out_specs=[whole()] * len(out),
        out_shape=out,
        scratch_shapes=[pltpu.VMEM((columns, width), jnp.bfloat16)] * (2 if second else 1)
        + [pltpu.VMEM((channels, columns), jnp.float32)],
        compiler_params=kernel_params(),
        cost_estimate=LATE,
        name="terms_second" if second else "terms_first",
    )(part, sibling, piece, *tables, *more)


def copy_rows(source_ref, out_ref):
    rows = source_ref.shape[-2]
    if rows % 4:
        out_ref[...] = source_ref[...]
        return
    step = rows // 4 if rows % 64 == 0 else rows

    @pl.loop(0, rows, step=step)
    def _(start):
        line = pl.ds(pl.multiple_of(start, 16 if step % 16 == 0 else 8), step)
        out_ref[..., line, :] = source_ref[..., line, :]


def keep_kernel(*refs):
    half = len(refs) // 2
    for source_ref, out_ref in zip(refs[:half], refs[half:]):
        copy_rows(source_ref, out_ref)


def hold_kernel(source_ref, *refs):
    *_, out_ref, done_ref = refs
    copy_rows(source_ref, out_ref)
    done_ref[...] = jnp.zeros_like(done_ref)


def keep(*values):
    return pl.pallas_call(
        keep_kernel,
        in_specs=[whole()] * len(values),
        out_specs=[whole()] * len(values),
        out_shape=[jax.ShapeDtypeStruct(v.shape, v.dtype) for v in values],
        compiler_params=kernel_params(),
        name="keep",
    )(*values)


def hold(value, *done):
    return pl.pallas_call(
        hold_kernel,
        in_specs=[whole()] * (1 + len(done)),
        out_specs=[whole()] * 2,
        out_shape=[jax.ShapeDtypeStruct(value.shape, value.dtype), TOKEN],
        compiler_params=kernel_params(),
        name="hold",
    )(value, *done)


def keep_after(value, done):
    return pl.pallas_call(
        lambda source_ref, _, out_ref: copy_rows(source_ref, out_ref),
        in_specs=[whole()] * 2,
        out_specs=whole(),
        out_shape=jax.ShapeDtypeStruct(value.shape, value.dtype),
        compiler_params=kernel_params(),
        name="keep_after",
    )(value, done)


def place_kernel(
    here_ref, core_ref, chip_ref, cross_ref, back_ref, out_ref, block_ref, sems
):
    x, core = place_of_core()
    lags, mine, channels = block_ref.shape
    swap = core != 0
    sides = []
    for q in range(2):
        index = jnp.where(x == q, 1, 0)
        own = here_ref[index] + chip_ref[1 - index].astype(jnp.float32)
        other = core_ref[index].astype(jnp.float32) + cross_ref[1 - index].astype(jnp.float32)
        sides += [jnp.where(swap, other, own), jnp.where(swap, own, other)]
    back = back_ref[...].astype(jnp.float32).T
    copies = []
    for j in range(lags):
        lag = HALF - 1 - j if j < HALF else j + 1 if j < lags - 1 else HALF
        cols = slice(j * mine, (j + 1) * mine)
        block_ref[lag, :, :SRC] = jnp.concatenate([v[:, cols] for v in sides], axis=1)
        block_ref[lag, :, SRC:] = back[cols]
        copies.append(pltpu.make_async_copy(block_ref.at[lag], out_ref.at[lag], sems.at[lag]))
        copies[-1].start()
    for copy in copies:
        copy.wait()


def place(here, core, chip, cross, back):
    _, mine, wide = here.shape
    shape = (wide // mine, mine, SRC + back.shape[0])
    return pl.pallas_call(
        place_kernel,
        in_specs=[whole()] * 5,
        out_specs=anywhere(),
        out_shape=jax.ShapeDtypeStruct(shape, jnp.float32),
        scratch_shapes=[
            pltpu.VMEM(shape, jnp.float32), pltpu.SemaphoreType.DMA((shape[0],))
        ],
        compiler_params=kernel_params(),
        name="place_lags",
    )(here, core, chip, cross, back)


def pair_body(spectra, counts, partner):
    blocks = lax.axis_size("chan")
    groups = lax.axis_size("win")
    windows, channels, two, freqs = spectra.shape
    scale = 1.0 / (math.sqrt(2.0 * freqs) * math.sqrt(windows * groups))
    other_core = [(i, i ^ 1) for i in range(groups)]
    other_chip = [(i, i ^ 2) for i in range(groups)]
    other_both = [(i, i ^ 3) for i in range(groups)]

    def to_partner(t):
        return [(i, i ^ t) for i in range(blocks)]

    def to_partner_core(t):
        return [
            (i * groups + g, (i ^ t) * groups + (g ^ 1))
            for i in range(blocks)
            for g in range(groups)
        ]

    def send_sources(t, white, near, far, near_more, far_more):
        def straight(value):
            return lax.ppermute(value, "chan", to_partner(t))

        def crossed(value):
            return lax.ppermute(value, ("chan", "win"), to_partner_core(t))

        sibling = lax.ppermute(white, "win", other_core)
        near, far = straight(near), crossed(far)
        near_more, done = hold(near_more, near)
        near_more = straight(near_more)
        part, done = part_terms(white, near, tables, done)
        far_more, done = hold(far_more, far, done)
        far_more = crossed(far_more)
        back, own, done = terms(part, sibling, far, tables, scale, done)
        back = lax.ppermute(back, "win", other_chip)
        part, done = part_terms(white, near_more, tables, done)
        return part, *keep(sibling), keep_after(far_more, done), *keep(back), own

    def send_terms(t, back):
        return keep(lax.ppermute(back, "chan", to_partner(t)))[0]

    def by_round(run, *values):
        branches = [functools.partial(run, t) for t in range(1, blocks)]
        return lax.switch(partner[0, 0] - 1, branches, *values)

    tables = [jnp.asarray(v) for v in shift_tables(freqs)]
    part, sibling, piece, back_recv, first = by_round(
        send_sources, *whiten(spectra, counts)
    )
    back, second = terms(part, sibling, piece, tables, scale)
    here, core, chip, cross = own_terms(first, second, SRC // groups, scale)
    core = lax.ppermute(core, "win", other_core)
    chip = lax.ppermute(chip, "win", other_chip)
    cross = lax.ppermute(cross, "win", other_both)
    back = (back + back_recv.astype(jnp.float32)).astype(jnp.bfloat16)
    return place(here, core, chip, cross, by_round(send_terms, back))[None, None]


def lag_table(freqs, lags):
    freq = jnp.arange(freqs, dtype=jnp.float32) + freqs // 4
    delay = jnp.arange(lags, dtype=jnp.float32) - lags // 2
    phase = 2.0 * math.pi * freq[:, None] * delay[None, :] / (4.0 * freqs)
    norm = 1.0 / math.sqrt(2.0 * freqs)
    return jnp.stack([jnp.cos(phase), -jnp.sin(phase)]) * norm


def blended_sources(sources, table):
    src = sources.astype(jnp.float32)
    first = src[:, :, 0][:, :, None, :]
    second = src[:, :, 1][:, :, None, :]
    cos_part = table[0].T[None, None]
    sin_part = table[1].T[None, None]
    real_mix = first * cos_part + second * sin_part
    imag_mix = second * cos_part - first * sin_part
    return jnp.stack([real_mix, imag_mix], axis=3).astype(jnp.bfloat16)


def pair_terms(sources, receiver_blocks, table):
    wins, count, two, freqs = sources.shape
    lags = table.shape[2]
    group = math.gcd(count, 32)
    flat_recv = receiver_blocks.reshape(wins, receiver_blocks.shape[1], two * freqs)
    grouped = jnp.moveaxis(sources.reshape(wins, count // group, group, two, freqs), 1, 0)

    def one_group(piece):
        mixed_spectra = blended_sources(piece, table).reshape(wins, group * lags, two * freqs)
        out = jnp.einsum(
            "wmx,wrx->mr", mixed_spectra, flat_recv, preferred_element_type=jnp.float32
        )
        return out.reshape(group, lags, receiver_blocks.shape[1])

    out = lax.map(one_group, grouped).reshape(count, lags, receiver_blocks.shape[1])
    return jnp.transpose(out, (1, 0, 2))


def route_blocks(values, round_flags, levels):
    for level in range(levels):
        moved = from_partner(values, "chan", level)
        values = jnp.where((round_flags >> level) % 2 == 1, moved, values)
    return values


def general_body(spectra, counts, partner):
    white = whiten_local(spectra, counts[0])
    table = lag_table(spectra.shape[3], LAGS)
    levels = lax.axis_size("chan").bit_length() - 1
    windows = spectra.shape[0] * lax.axis_size("win")
    receiver_blocks = route_blocks(white, partner[0, 0], levels)
    out = pair_terms(white[:, :SRC], receiver_blocks, table)
    stacked = lax.psum_scatter(out, "win", scatter_dimension=1, tiled=True)
    return (stacked / math.sqrt(windows))[None, None]


def solution(mesh):
    body = pair_body if mesh.shape["win"] == 4 else general_body
    return jax.shard_map(
        body,
        mesh=mesh,
        in_specs=(P("win", "chan", None, None), P("chan"), P()),
        out_specs=P("chan", None, None, "win", None),
        check_vma=False,
    )
```

```python
import functools
import math

import jax
import jax.numpy as jnp
import numpy as np
from jax import lax
from jax.experimental import pallas as pl
from jax.experimental.pallas import tpu as pltpu
from jax.sharding import PartitionSpec as P

LAGS = 16
SRC = 160
HALF = LAGS // 2
VMEM_LIMIT = 16 * 1024 * 1024


def from_partner(value, axis, stride):
    return lax.ppermute(value, axis, [(i, i ^ 1 << stride) for i in range(lax.axis_size(axis))])


def whiten_local(spectra, count):
    values = spectra.astype(jnp.float32)
    block_size = spectra.shape[1]
    freqs = spectra.shape[3]
    valid = (jnp.arange(block_size, dtype=jnp.int32) < count).astype(jnp.float32)
    freq = jnp.arange(freqs, dtype=jnp.float32)
    taper = 0.75 - 0.25 * jnp.cos(2.0 * math.pi * (freq + 0.5) / freqs)
    power = jnp.mean(values * values, axis=(2, 3))
    scale = valid[None, :] / jnp.sqrt(power + 1e-05)
    return (values * taper * scale[:, :, None, None]).astype(jnp.bfloat16)


def shift_tables(freqs):
    freq = np.arange(freqs, dtype=np.float64) + freqs // 4
    shift = np.arange(1, HALF + 1, dtype=np.float64)
    phase = 2.0 * np.pi * shift[:, None] * freq[None, :] / (4.0 * freqs)
    return np.cos(phase).astype(np.float32), np.sin(phase).astype(np.float32)


def place_of_core():
    spot = lax.axis_index("win")
    return spot // 2, spot % 2


def whole():
    return pl.BlockSpec(memory_space=pltpu.VMEM)


def anywhere():
    return pl.BlockSpec(memory_space=pl.ANY)


def kernel_params():
    return pltpu.CompilerParams(vmem_limit_bytes=VMEM_LIMIT)


def fetch_kernel(source_ref, out_ref, sems):
    windows, parts = out_ref.shape[0], sems.shape[1]
    step = out_ref.shape[1] // parts
    copies = []
    for w in range(windows):
        for i in range(parts):
            part = (w, pl.ds(i * step, step))
            copies.append(
                pltpu.make_async_copy(source_ref.at[part], out_ref.at[part], sems.at[w, i])
            )
            copies[-1].start()
    for copy in copies:
        copy.wait()


def fetch(value):
    return pl.pallas_call(
        fetch_kernel,
        in_specs=[pl.BlockSpec(memory_space=pltpu.HBM)],
        out_specs=whole(),
        out_shape=jax.ShapeDtypeStruct(value.shape, value.dtype),
        scratch_shapes=[pltpu.SemaphoreType.DMA((value.shape[0], 4))],
        compiler_params=kernel_params(),
        name="fetch",
    )(pltpu.with_memory_space_constraint(value, pltpu.HBM))


def whiten_kernel(count_ref, raw_ref, taper_ref, white_ref, *refs):
    *piece_refs, count, sem = refs
    copy = pltpu.make_async_copy(count_ref, count, sem)
    copy.start()
    x, core = place_of_core()
    windows, channels, width = raw_ref.shape
    mine = SRC // 4
    step = 2 * mine
    copy.wait()
    for w in range(windows):
        for index in range(channels // step):
            block = (1 - x, x)[index] if index * step < SRC else index
            begin = block * step
            line = pl.ds(pl.multiple_of(begin, step), step)
            values = raw_ref[w, line, :].astype(jnp.float32)
            power = jnp.sum(values * values, axis=1, keepdims=True) * (1.0 / width)
            row = begin + lax.broadcasted_iota(jnp.int32, (step, 1), 0)
            valid = (row < count[0]).astype(jnp.float32)
            scale = valid / jnp.sqrt(power + 1e-05)
            values = values * taper_ref[...] * scale
            white_ref[w, line, :] = values.astype(jnp.bfloat16)
            if index * step < SRC:
                low, high = values[:mine], values[mine:]
                first = core == 0
                near_ref, far_ref = piece_refs[2 * index:2 * index + 2]
                near_ref[w] = jnp.where(first, low, high).astype(jnp.bfloat16)
                far_ref[w] = jnp.where(first, high, low).astype(jnp.bfloat16)


def whiten(spectra, counts):
    windows, channels, two, freqs = spectra.shape
    width = two * freqs
    freq = np.arange(freqs, dtype=np.float64)
    taper = 0.75 - 0.25 * np.cos(2.0 * np.pi * (freq + 0.5) / freqs)
    taper = np.tile(taper.astype(np.float32), two)[None, :]
    piece = jax.ShapeDtypeStruct((windows, SRC // 4, width), jnp.bfloat16)
    return pl.pallas_call(
        whiten_kernel,
        in_specs=[anywhere(), whole(), whole()],
        out_specs=[whole()] * 5,
        out_shape=[jax.ShapeDtypeStruct((windows, channels, width), jnp.bfloat16)]
        + [piece] * 4,
        scratch_shapes=[pltpu.SMEM((1,), jnp.int32), pltpu.SemaphoreType.DMA],
        compiler_params=kernel_params(),
        name="whiten",
    )(counts, fetch(spectra).reshape(windows, channels, width), jnp.asarray(taper))


def mix(m_ref, piece, cos_ref, sin_ref, low, high):
    rows = piece.shape[0]
    vrow = v_row(rows)
    real = piece[:, low].astype(jnp.float32)
    imag = piece[:, high].astype(jnp.float32)

    def put(where, cols, values):
        m_ref[where, cols] = jnp.concatenate(values, axis=0).astype(jnp.bfloat16)

    for m in range(0, HALF, 2):
        c = [cos_ref[m + i:m + i + 1, low] for i in range(2)]
        s = [sin_ref[m + i:m + i + 1, low] for i in range(2)]
        line = slice(m * rows, (m + 2) * rows)
        vline = slice(vrow + m * rows, vrow + (m + 2) * rows)
        put(line, low, [real * v for v in c])
        put(line, high, [imag * v for v in c])
        put(vline, low, [imag * -v for v in s])
        put(vline, high, [real * v for v in s])
    fill = jnp.zeros((vrow - (HALF + 1) * rows, 128), jnp.float32)
    for value, cols in ((real, low), (imag, high)):
        put(slice(HALF * rows, vrow), cols, [value, fill])


def v_row(rows):
    return -(-(HALF + 1) * rows // 128) * 128


def times(lhs, rhs):
    return lax.dot_general(
        lhs, rhs, (((1,), (1,)), ((), ())), preferred_element_type=jnp.float32
    )


def add_products(acc_ref, lhs_ref, piece_ref, cos_ref, sin_ref, mixed_ref):
    windows, rows, width = piece_ref.shape
    tile = 256
    used = v_row(rows) + HALF * rows
    if used < mixed_ref.shape[0]:
        mixed_ref[used:, :] = jnp.zeros_like(mixed_ref[used:, :])

    @pl.loop(0, windows)
    def _(w):
        @pl.loop(0, width // 2, step=128)
        def _(start):
            low = pl.ds(pl.multiple_of(start, 128), 128)
            high = pl.ds(pl.multiple_of(width // 2 + start, 128), 128)
            mix(mixed_ref, piece_ref.at[w], cos_ref, sin_ref, low, high)

        @pl.loop(0, mixed_ref.shape[0], step=tile)
        def _(n):
            cols = pl.ds(pl.multiple_of(n, tile), tile)
            acc_ref[:, cols] += times(lhs_ref[w], mixed_ref[cols, :])


def part_kernel(white_ref, piece_ref, cos_ref, sin_ref, _, part_ref, done_ref, mixed_ref):
    done_ref[...] = jnp.zeros_like(done_ref)
    part_ref[...] = jnp.zeros_like(part_ref)
    add_products(part_ref, white_ref, piece_ref, cos_ref, sin_ref, mixed_ref)


def part_columns(rows):
    columns = v_row(rows) + HALF * rows
    return columns + (-columns) % 256


def part_terms(white, piece, tables, done):
    windows, channels, width = white.shape
    columns = part_columns(piece.shape[1])
    return pl.pallas_call(
        part_kernel,
        in_specs=[whole()] * 5,
        out_specs=[whole()] * 2,
        out_shape=[jax.ShapeDtypeStruct((channels, columns), jnp.float32), TOKEN],
        scratch_shapes=[pltpu.VMEM((columns, width), jnp.bfloat16)],
        compiler_params=kernel_params(),
        cost_estimate=LATE,
        name="terms_part",
    )(white, piece, *tables, done)


TOKEN = jax.ShapeDtypeStruct((8, 128), jnp.float32)
LATE = pl.CostEstimate(flops=30 * 10**9, bytes_accessed=0, transcendentals=0)


def pack(acc_ref, line, rows, scale, later):
    wide = HALF * rows
    vrow = v_row(rows)
    u, v = acc_ref[line, :wide] * scale, acc_ref[line, vrow:vrow + wide] * scale
    still = acc_ref[line, wide:wide + rows] * scale
    first, last = (u - v, u + v) if later else (u + v, u - v)
    return jnp.concatenate([first, last[:, :wide - rows], still], axis=1)


def first_kernel(
    scale, part_ref, sibling_ref, piece_ref, cos_ref, sin_ref, _, back_ref, own_ref,
    done_ref, mixed_ref, acc_ref,
):
    done_ref[...] = jnp.zeros_like(done_ref)
    acc_ref[...] = part_ref[...]
    add_products(acc_ref, sibling_ref, piece_ref, cos_ref, sin_ref, mixed_ref)
    line = pl.ds(SRC, acc_ref.shape[0] - SRC)
    back = pack(acc_ref, line, piece_ref.shape[1], scale, True)
    back_ref[...] = back.astype(back_ref.dtype)
    own_ref[...] = acc_ref[:SRC, :]


def second_kernel(scale, part_ref, sibling_ref, piece_ref, cos_ref, sin_ref, *refs):
    back_ref, own_ref, even_ref, odd_ref, acc_ref = refs
    windows, rows, width = piece_ref.shape
    freqs = width // 2
    starts = [
        (slice(n, n + 128), slice(freqs + n, freqs + n + 128)) for n in range(0, freqs, 128)
    ]
    tiles = [
        slice(n, min(n + 256, acc_ref.shape[1])) for n in range(0, acc_ref.shape[1], 256)
    ]
    buffers = even_ref, odd_ref
    for start in starts:
        mix(even_ref, piece_ref.at[0], cos_ref, sin_ref, *start)
    for w in range(windows):
        now_ref, next_ref = buffers[w % 2], buffers[1 - w % 2]
        todo = starts if w + 1 < windows else []
        for cols in tiles:
            before = part_ref[:, cols] if w == 0 else acc_ref[:, cols]
            acc_ref[:, cols] = before + times(sibling_ref[w], now_ref[cols, :])
            for start in todo[:2]:
                mix(next_ref, piece_ref.at[w + 1], cos_ref, sin_ref, *start)
            todo = todo[2:]
    back_ref[...] = pack(acc_ref, pl.ds(SRC, acc_ref.shape[0] - SRC), rows, scale, True)
    own_ref[...] = acc_ref[:SRC, :]


def own_kernel(scale, rows, first_ref, second_ref, *refs):
    *out_refs, packed_ref = refs
    x, core = place_of_core()
    mine = SRC // 4

    @pl.loop(0, SRC, step=mine)
    def _(start):
        line = pl.ds(pl.multiple_of(start, 8), mine)
        for quarter, ref in enumerate((first_ref, second_ref)):
            packed_ref[quarter, line, :] = pack(ref, line, rows, scale, False)

    for i, out_ref in enumerate(out_refs):
        spot = 2 * (x, 1 - x)[i // 2] + (core, 1 - core)[i % 2]
        line = pl.ds(pl.multiple_of(spot * mine, 8), mine)
        for quarter in range(2):
            out_ref[quarter] = packed_ref[quarter, line, :].astype(out_ref.dtype)


def own_terms(first, second, rows, scale):
    mine, wide = SRC // 4, 2 * HALF * rows
    return pl.pallas_call(
        functools.partial(own_kernel, scale, rows),
        in_specs=[whole()] * 2,
        out_specs=[whole()] * 4,
        out_shape=[
            jax.ShapeDtypeStruct((2, mine, wide), jnp.float32 if i == 0 else jnp.bfloat16)
            for i in range(4)
        ],
        scratch_shapes=[pltpu.VMEM((2, SRC, wide), jnp.float32)],
        compiler_params=kernel_params(),
        name="own_terms",
    )(first, second)


def terms(part, sibling, piece, tables, scale, done=None):
    windows, channels, width = sibling.shape
    rows = piece.shape[1]
    second = done is None
    columns = v_row(rows) + HALF * rows if second else part_columns(rows)
    back = ((channels - SRC, 2 * HALF * rows), jnp.float32 if second else jnp.bfloat16)
    out = [jax.ShapeDtypeStruct(*back), jax.ShapeDtypeStruct((SRC, columns), jnp.float32)]
    out += [] if second else [TOKEN]
    more = () if second else (done,)
    return pl.pallas_call(
        functools.partial(second_kernel if second else first_kernel, scale),
        in_specs=[whole()] * (5 + len(more)),
        out_specs=[whole()] * len(out),
        out_shape=out,
        scratch_shapes=[pltpu.VMEM((columns, width), jnp.bfloat16)] * (2 if second else 1)
        + [pltpu.VMEM((channels, columns), jnp.float32)],
        compiler_params=kernel_params(),
        cost_estimate=LATE,
        name="terms_second" if second else "terms_first",
    )(part, sibling, piece, *tables, *more)


def copy_rows(source_ref, out_ref):
    rows = source_ref.shape[-2]
    if rows % 4:
        out_ref[...] = source_ref[...]
        return
    step = rows // 4 if rows % 64 == 0 else rows

    @pl.loop(0, rows, step=step)
    def _(start):
        line = pl.ds(pl.multiple_of(start, 16 if step % 16 == 0 else 8), step)
        out_ref[..., line, :] = source_ref[..., line, :]


def keep_kernel(*refs):
    half = len(refs) // 2
    for source_ref, out_ref in zip(refs[:half], refs[half:]):
        copy_rows(source_ref, out_ref)


def hold_kernel(source_ref, *refs):
    *_, out_ref, done_ref = refs
    copy_rows(source_ref, out_ref)
    done_ref[...] = jnp.zeros_like(done_ref)


def keep(*values):
    return pl.pallas_call(
        keep_kernel,
        in_specs=[whole()] * len(values),
        out_specs=[whole()] * len(values),
        out_shape=[jax.ShapeDtypeStruct(v.shape, v.dtype) for v in values],
        compiler_params=kernel_params(),
        name="keep",
    )(*values)


def hold(value, *done):
    return pl.pallas_call(
        hold_kernel,
        in_specs=[whole()] * (1 + len(done)),
        out_specs=[whole()] * 2,
        out_shape=[jax.ShapeDtypeStruct(value.shape, value.dtype), TOKEN],
        compiler_params=kernel_params(),
        name="hold",
    )(value, *done)


def keep_after(value, done):
    return pl.pallas_call(
        lambda source_ref, _, out_ref: copy_rows(source_ref, out_ref),
        in_specs=[whole()] * 2,
        out_specs=whole(),
        out_shape=jax.ShapeDtypeStruct(value.shape, value.dtype),
        compiler_params=kernel_params(),
        name="keep_after",
    )(value, done)


def place_kernel(
    here_ref, core_ref, chip_ref, cross_ref, back_ref, out_ref, block_ref, sems
):
    x, core = place_of_core()
    lags, mine, channels = block_ref.shape
    swap = core != 0
    sides = []
    for q in range(2):
        index = jnp.where(x == q, 1, 0)
        own = here_ref[index] + chip_ref[1 - index].astype(jnp.float32)
        other = core_ref[index].astype(jnp.float32) + cross_ref[1 - index].astype(jnp.float32)
        sides += [jnp.where(swap, other, own), jnp.where(swap, own, other)]
    back = back_ref[...].astype(jnp.float32).T
    copies = []
    for j in range(lags):
        lag = HALF - 1 - j if j < HALF else j + 1 if j < lags - 1 else HALF
        cols = slice(j * mine, (j + 1) * mine)
        block_ref[lag, :, :SRC] = jnp.concatenate([v[:, cols] for v in sides], axis=1)
        block_ref[lag, :, SRC:] = back[cols]
        copies.append(pltpu.make_async_copy(block_ref.at[lag], out_ref.at[lag], sems.at[lag]))
        copies[-1].start()
    for copy in copies:
        copy.wait()


def place(here, core, chip, cross, back):
    _, mine, wide = here.shape
    shape = (wide // mine, mine, SRC + back.shape[0])
    return pl.pallas_call(
        place_kernel,
        in_specs=[whole()] * 5,
        out_specs=anywhere(),
        out_shape=jax.ShapeDtypeStruct(shape, jnp.float32),
        scratch_shapes=[
            pltpu.VMEM(shape, jnp.float32), pltpu.SemaphoreType.DMA((shape[0],))
        ],
        compiler_params=kernel_params(),
        name="place_lags",
    )(here, core, chip, cross, back)


def pair_body(spectra, counts, partner):
    blocks = lax.axis_size("chan")
    groups = lax.axis_size("win")
    windows, channels, two, freqs = spectra.shape
    scale = 1.0 / (math.sqrt(2.0 * freqs) * math.sqrt(windows * groups))
    other_core = [(i, i ^ 1) for i in range(groups)]
    other_chip = [(i, i ^ 2) for i in range(groups)]
    other_both = [(i, i ^ 3) for i in range(groups)]

    def to_partner(t):
        return [(i, i ^ t) for i in range(blocks)]

    def to_partner_core(t):
        return [
            (i * groups + g, (i ^ t) * groups + (g ^ 1))
            for i in range(blocks)
            for g in range(groups)
        ]

    def send_sources(t, white, near, far, near_more, far_more):
        def straight(value):
            return lax.ppermute(value, "chan", to_partner(t))

        def crossed(value):
            return lax.ppermute(value, ("chan", "win"), to_partner_core(t))

        sibling = lax.ppermute(white, "win", other_core)
        near, far = straight(near), crossed(far)
        in_line = t < blocks // 2
        if not in_line:
            near_more, done = hold(near_more, sibling)
            far_more, done = hold(far_more, done)
            near_more, far_more = straight(near_more), crossed(far_more)
        else:
            near_more, done = hold(near_more, near)
            near_more = straight(near_more)
        part, done = part_terms(white, near, tables, done)
        if in_line:
            far_more, done = hold(far_more, far, done)
            far_more = crossed(far_more)
        back, own, done = terms(part, sibling, far, tables, scale, done)
        back = lax.ppermute(back, "win", other_chip)
        if in_line:
            part, done = part_terms(white, near_more, tables, done)
            last = *keep(sibling), keep_after(far_more, done)
        else:
            part, done = part_terms(sibling, far_more, tables, done)
            last = *keep(white), keep_after(near_more, done)
        return part, *last, *keep(back), own

    def send_terms(t, back, first, second):
        back = lax.ppermute(back, "chan", to_partner(t))
        here, core, chip, cross = own_terms(first, second, SRC // groups, scale)
        core = lax.ppermute(core, "win", other_core)
        chip = lax.ppermute(chip, "win", other_chip)
        cross = lax.ppermute(cross, "win", other_both)
        return here, *keep(core, chip, cross, back)

    def by_round(run, *values):
        branches = [functools.partial(run, t) for t in range(1, blocks)]
        return lax.switch(partner[0, 0] - 1, branches, *values)

    tables = [jnp.asarray(v) for v in shift_tables(freqs)]
    part, last, piece, back_recv, first = by_round(
        send_sources, *whiten(spectra, counts)
    )
    back, second = terms(part, last, piece, tables, scale)
    back = (back + back_recv.astype(jnp.float32)).astype(jnp.bfloat16)
    return place(*by_round(send_terms, back, first, second))[None, None]


def lag_table(freqs, lags):
    freq = jnp.arange(freqs, dtype=jnp.float32) + freqs // 4
    delay = jnp.arange(lags, dtype=jnp.float32) - lags // 2
    phase = 2.0 * math.pi * freq[:, None] * delay[None, :] / (4.0 * freqs)
    norm = 1.0 / math.sqrt(2.0 * freqs)
    return jnp.stack([jnp.cos(phase), -jnp.sin(phase)]) * norm


def blended_sources(sources, table):
    src = sources.astype(jnp.float32)
    first = src[:, :, 0][:, :, None, :]
    second = src[:, :, 1][:, :, None, :]
    cos_part = table[0].T[None, None]
    sin_part = table[1].T[None, None]
    real_mix = first * cos_part + second * sin_part
    imag_mix = second * cos_part - first * sin_part
    return jnp.stack([real_mix, imag_mix], axis=3).astype(jnp.bfloat16)


def pair_terms(sources, receiver_blocks, table):
    wins, count, two, freqs = sources.shape
    lags = table.shape[2]
    group = math.gcd(count, 32)
    flat_recv = receiver_blocks.reshape(wins, receiver_blocks.shape[1], two * freqs)
    grouped = jnp.moveaxis(sources.reshape(wins, count // group, group, two, freqs), 1, 0)

    def one_group(piece):
        mixed_spectra = blended_sources(piece, table).reshape(wins, group * lags, two * freqs)
        out = jnp.einsum(
            "wmx,wrx->mr", mixed_spectra, flat_recv, preferred_element_type=jnp.float32
        )
        return out.reshape(group, lags, receiver_blocks.shape[1])

    out = lax.map(one_group, grouped).reshape(count, lags, receiver_blocks.shape[1])
    return jnp.transpose(out, (1, 0, 2))


def route_blocks(values, round_flags, levels):
    for level in range(levels):
        moved = from_partner(values, "chan", level)
        values = jnp.where((round_flags >> level) % 2 == 1, moved, values)
    return values


def general_body(spectra, counts, partner):
    white = whiten_local(spectra, counts[0])
    table = lag_table(spectra.shape[3], LAGS)
    levels = lax.axis_size("chan").bit_length() - 1
    windows = spectra.shape[0] * lax.axis_size("win")
    receiver_blocks = route_blocks(white, partner[0, 0], levels)
    out = pair_terms(white[:, :SRC], receiver_blocks, table)
    stacked = lax.psum_scatter(out, "win", scatter_dimension=1, tiled=True)
    return (stacked / math.sqrt(windows))[None, None]


def solution(mesh):
    body = pair_body if mesh.shape["win"] == 4 else general_body
    return jax.shard_map(
        body,
        mesh=mesh,
        in_specs=(P("win", "chan", None, None), P("chan"), P()),
        out_specs=P("chan", None, None, "win", None),
        check_vma=False,
    )
```

```python
import functools
import math

import jax
import jax.numpy as jnp
import numpy as np
from jax import lax
from jax.experimental import pallas as pl
from jax.experimental.pallas import tpu as pltpu
from jax.sharding import PartitionSpec as P

LAGS = 16
SRC = 160
HALF = LAGS // 2
VMEM_LIMIT = 16 * 1024 * 1024


def from_partner(value, axis, stride):
    return lax.ppermute(value, axis, [(i, i ^ 1 << stride) for i in range(lax.axis_size(axis))])


def whiten_local(spectra, count):
    values = spectra.astype(jnp.float32)
    block_size = spectra.shape[1]
    freqs = spectra.shape[3]
    valid = (jnp.arange(block_size, dtype=jnp.int32) < count).astype(jnp.float32)
    freq = jnp.arange(freqs, dtype=jnp.float32)
    taper = 0.75 - 0.25 * jnp.cos(2.0 * math.pi * (freq + 0.5) / freqs)
    power = jnp.mean(values * values, axis=(2, 3))
    scale = valid[None, :] / jnp.sqrt(power + 1e-05)
    return (values * taper * scale[:, :, None, None]).astype(jnp.bfloat16)


def shift_tables(freqs):
    freq = np.arange(freqs, dtype=np.float64) + freqs // 4
    shift = np.arange(1, HALF + 1, dtype=np.float64)
    phase = 2.0 * np.pi * shift[:, None] * freq[None, :] / (4.0 * freqs)
    return np.cos(phase).astype(np.float32), np.sin(phase).astype(np.float32)


def place_of_core():
    spot = lax.axis_index("win")
    return spot // 2, spot % 2


def whole():
    return pl.BlockSpec(memory_space=pltpu.VMEM)


def anywhere():
    return pl.BlockSpec(memory_space=pl.ANY)


def kernel_params():
    return pltpu.CompilerParams(vmem_limit_bytes=VMEM_LIMIT)


def fetch_kernel(source_ref, out_ref, sems):
    windows, channels = out_ref.shape[:2]
    parts = sems.shape[1]
    step = channels // parts
    copies = []
    for w in range(windows):
        for i in range(parts):
            part = (w, pl.ds(i * step, step))
            copies.append(
                pltpu.make_async_copy(source_ref.at[part], out_ref.at[part], sems.at[w, i])
            )
            copies[-1].start()
    for copy in copies:
        copy.wait()


def fetch_sources(spectra):
    windows, _, *rest = spectra.shape
    return pl.pallas_call(
        fetch_kernel,
        in_specs=[pl.BlockSpec(memory_space=pltpu.HBM)],
        out_specs=whole(),
        out_shape=jax.ShapeDtypeStruct((windows, SRC, *rest), spectra.dtype),
        scratch_shapes=[pltpu.SemaphoreType.DMA((windows, 4))],
        compiler_params=kernel_params(),
        name="fetch",
    )(spectra)


def white_block(raw_ref, taper_ref, count, w, line, first_row):
    values = raw_ref[w, line, :].astype(jnp.float32)
    rows, width = values.shape
    power = jnp.sum(values * values, axis=1, keepdims=True) * (1.0 / width)
    row = first_row + lax.broadcasted_iota(jnp.int32, (rows, 1), 0)
    valid = (row < count).astype(jnp.float32)
    scale = valid / jnp.sqrt(power + 1e-05)
    return values * taper_ref[...] * scale


def whiten_kernel(count_ref, raw_ref, taper_ref, white_ref, *refs):
    *piece_refs, count, sem = refs
    copy = pltpu.make_async_copy(count_ref, count, sem)
    copy.start()
    x, core = place_of_core()
    mine = SRC // 4
    step = 2 * mine
    copy.wait()
    for w in range(raw_ref.shape[0]):
        for index, group in enumerate((1 - x, x)):
            line = pl.ds(pl.multiple_of(group * step, step), step)
            values = white_block(raw_ref, taper_ref, count[0], w, line, group * step)
            white_ref[w, line, :] = values.astype(jnp.bfloat16)
            low, high = values[:mine], values[mine:]
            first = core == 0
            near_ref, far_ref = piece_refs[2 * index:2 * index + 2]
            near_ref[w] = jnp.where(first, low, high).astype(jnp.bfloat16)
            far_ref[w] = jnp.where(first, high, low).astype(jnp.bfloat16)


def rest_kernel(
    count_ref, spectra_ref, taper_ref, sources_ref, white_ref, raw_ref, count, sems
):
    windows, channels, two, freqs = raw_ref.shape
    copies = [pltpu.make_async_copy(count_ref, count, sems.at[windows])]
    for w in range(windows):
        part = spectra_ref.at[w, pl.ds(SRC, channels)]
        copies.append(pltpu.make_async_copy(part, raw_ref.at[w], sems.at[w]))
    for copy in copies:
        copy.start()
    step = 32

    @pl.loop(0, windows)
    def _(w):
        @pl.loop(0, SRC, step=step)
        def _(start):
            line = pl.ds(pl.multiple_of(start, step), step)
            white_ref[w, line, :] = sources_ref[w, line, :]

    for copy in copies:
        copy.wait()

    @pl.loop(0, windows)
    def _(w):
        @pl.loop(0, channels, step=step)
        def _(start):
            line = pl.ds(pl.multiple_of(start, step), step)
            parts = [raw_ref[w, line, p, :].astype(jnp.float32) for p in range(two)]
            power = sum(jnp.sum(v * v, axis=1, keepdims=True) for v in parts)
            row = SRC + start + lax.broadcasted_iota(jnp.int32, (step, 1), 0)
            valid = (row < count[0]).astype(jnp.float32)
            scale = valid / jnp.sqrt(power * (1.0 / (two * freqs)) + 1e-05)
            out = pl.ds(pl.multiple_of(SRC + start, step), step)
            for p, v in enumerate(parts):
                cols = slice(p * freqs, (p + 1) * freqs)
                white_ref[w, out, cols] = (v * taper_ref[:, cols] * scale).astype(jnp.bfloat16)


def whiten_rest(counts, spectra, taper, sources):
    windows, channels, two, freqs = spectra.shape
    return pl.pallas_call(
        rest_kernel,
        in_specs=[anywhere(), pl.BlockSpec(memory_space=pltpu.HBM), whole(), whole()],
        out_specs=whole(),
        out_shape=jax.ShapeDtypeStruct((windows, channels, two * freqs), jnp.bfloat16),
        scratch_shapes=[
            pltpu.VMEM((windows, channels - SRC, two, freqs), spectra.dtype),
            pltpu.SMEM((1,), jnp.int32),
            pltpu.SemaphoreType.DMA((windows + 1,)),
        ],
        compiler_params=kernel_params(),
        name="whiten_rest",
    )(counts, spectra, taper, sources)


def whiten_sources(out_shape, counts, raw, taper):
    windows, channels, two, freqs = raw.shape
    return pl.pallas_call(
        whiten_kernel,
        in_specs=[anywhere()] + [whole()] * 2,
        out_specs=[whole()] * len(out_shape),
        out_shape=out_shape,
        scratch_shapes=[pltpu.SMEM((1,), jnp.int32), pltpu.SemaphoreType.DMA],
        compiler_params=kernel_params(),
        name="whiten",
    )(counts, raw.reshape(windows, channels, two * freqs), taper)


def taper_row(two, freqs):
    freq = np.arange(freqs, dtype=np.float64)
    taper = 0.75 - 0.25 * np.cos(2.0 * np.pi * (freq + 0.5) / freqs)
    return jnp.asarray(np.tile(taper.astype(np.float32), two)[None, :])


def mix(m_ref, piece, cos_ref, sin_ref, low, high):
    rows = piece.shape[0]
    vrow = v_row(rows)
    real = piece[:, low].astype(jnp.float32)
    imag = piece[:, high].astype(jnp.float32)

    def put(where, cols, values):
        m_ref[where, cols] = jnp.concatenate(values, axis=0).astype(jnp.bfloat16)

    for m in range(0, HALF, 2):
        c = [cos_ref[m + i:m + i + 1, low] for i in range(2)]
        s = [sin_ref[m + i:m + i + 1, low] for i in range(2)]
        line = slice(m * rows, (m + 2) * rows)
        vline = slice(vrow + m * rows, vrow + (m + 2) * rows)
        put(line, low, [real * v for v in c])
        put(line, high, [imag * v for v in c])
        put(vline, low, [imag * -v for v in s])
        put(vline, high, [real * v for v in s])
    fill = jnp.zeros((vrow - (HALF + 1) * rows, 128), jnp.float32)
    for value, cols in ((real, low), (imag, high)):
        put(slice(HALF * rows, vrow), cols, [value, fill])


def v_row(rows):
    return -(-(HALF + 1) * rows // 128) * 128


def times(lhs, rhs):
    return lax.dot_general(
        lhs, rhs, (((1,), (1,)), ((), ())), preferred_element_type=jnp.float32
    )


def add_products(acc_ref, lhs_ref, piece_ref, cos_ref, sin_ref, mixed_ref):
    windows, rows, width = piece_ref.shape
    tile = 256
    used = v_row(rows) + HALF * rows
    if used < mixed_ref.shape[0]:
        mixed_ref[used:, :] = jnp.zeros_like(mixed_ref[used:, :])

    @pl.loop(0, windows)
    def _(w):
        @pl.loop(0, width // 2, step=128)
        def _(start):
            low = pl.ds(pl.multiple_of(start, 128), 128)
            high = pl.ds(pl.multiple_of(width // 2 + start, 128), 128)
            mix(mixed_ref, piece_ref.at[w], cos_ref, sin_ref, low, high)

        @pl.loop(0, mixed_ref.shape[0], step=tile)
        def _(n):
            cols = pl.ds(pl.multiple_of(n, tile), tile)
            acc_ref[:, cols] += times(lhs_ref[w], mixed_ref[cols, :])


def part_kernel(white_ref, piece_ref, cos_ref, sin_ref, _, part_ref, done_ref, mixed_ref):
    done_ref[...] = jnp.zeros_like(done_ref)
    part_ref[...] = jnp.zeros_like(part_ref)
    add_products(part_ref, white_ref, piece_ref, cos_ref, sin_ref, mixed_ref)


def part_columns(rows):
    columns = v_row(rows) + HALF * rows
    return columns + (-columns) % 256


def part_terms(white, piece, tables, done):
    windows, channels, width = white.shape
    columns = part_columns(piece.shape[1])
    return pl.pallas_call(
        part_kernel,
        in_specs=[whole()] * 5,
        out_specs=[whole()] * 2,
        out_shape=[jax.ShapeDtypeStruct((channels, columns), jnp.float32), TOKEN],
        scratch_shapes=[pltpu.VMEM((columns, width), jnp.bfloat16)],
        compiler_params=kernel_params(),
        cost_estimate=LATE,
        name="terms_part",
    )(white, piece, *tables, done)


TOKEN = jax.ShapeDtypeStruct((8, 128), jnp.float32)
LATE = pl.CostEstimate(flops=30 * 10**9, bytes_accessed=0, transcendentals=0)


def pack(acc_ref, line, rows, scale, later):
    wide = HALF * rows
    vrow = v_row(rows)
    u, v = acc_ref[line, :wide] * scale, acc_ref[line, vrow:vrow + wide] * scale
    still = acc_ref[line, wide:wide + rows] * scale
    first, last = (u - v, u + v) if later else (u + v, u - v)
    return jnp.concatenate([first, last[:, :wide - rows], still], axis=1)


def first_kernel(
    scale, part_ref, sibling_ref, piece_ref, cos_ref, sin_ref, _, back_ref, own_ref,
    done_ref, mixed_ref, acc_ref,
):
    done_ref[...] = jnp.zeros_like(done_ref)
    acc_ref[...] = part_ref[...]
    add_products(acc_ref, sibling_ref, piece_ref, cos_ref, sin_ref, mixed_ref)
    line = pl.ds(SRC, acc_ref.shape[0] - SRC)
    back = pack(acc_ref, line, piece_ref.shape[1], scale, True)
    back_ref[...] = back.astype(back_ref.dtype)
    own_ref[...] = acc_ref[:SRC, :]


def second_kernel(scale, part_ref, sibling_ref, piece_ref, cos_ref, sin_ref, *refs):
    back_ref, own_ref, even_ref, odd_ref, acc_ref = refs
    windows, rows, width = piece_ref.shape
    freqs = width // 2
    starts = [
        (slice(n, n + 128), slice(freqs + n, freqs + n + 128)) for n in range(0, freqs, 128)
    ]
    tiles = [
        slice(n, min(n + 256, acc_ref.shape[1])) for n in range(0, acc_ref.shape[1], 256)
    ]
    buffers = even_ref, odd_ref
    for start in starts:
        mix(even_ref, piece_ref.at[0], cos_ref, sin_ref, *start)
    for w in range(windows):
        now_ref, next_ref = buffers[w % 2], buffers[1 - w % 2]
        todo = starts if w + 1 < windows else []
        for cols in tiles:
            before = part_ref[:, cols] if w == 0 else acc_ref[:, cols]
            acc_ref[:, cols] = before + times(sibling_ref[w], now_ref[cols, :])
            for start in todo[:2]:
                mix(next_ref, piece_ref.at[w + 1], cos_ref, sin_ref, *start)
            todo = todo[2:]
    back_ref[...] = pack(acc_ref, pl.ds(SRC, acc_ref.shape[0] - SRC), rows, scale, True)
    own_ref[...] = acc_ref[:SRC, :]


def own_kernel(scale, rows, first_ref, second_ref, *refs):
    *out_refs, packed_ref = refs
    x, core = place_of_core()
    mine = SRC // 4

    @pl.loop(0, SRC, step=mine)
    def _(start):
        line = pl.ds(pl.multiple_of(start, 8), mine)
        for quarter, ref in enumerate((first_ref, second_ref)):
            packed_ref[quarter, line, :] = pack(ref, line, rows, scale, False)

    for i, out_ref in enumerate(out_refs):
        spot = 2 * (x, 1 - x)[i // 2] + (core, 1 - core)[i % 2]
        line = pl.ds(pl.multiple_of(spot * mine, 8), mine)
        for quarter in range(2):
            out_ref[quarter] = packed_ref[quarter, line, :].astype(out_ref.dtype)


def own_terms(first, second, rows, scale):
    mine, wide = SRC // 4, 2 * HALF * rows
    return pl.pallas_call(
        functools.partial(own_kernel, scale, rows),
        in_specs=[whole()] * 2,
        out_specs=[whole()] * 4,
        out_shape=[
            jax.ShapeDtypeStruct((2, mine, wide), jnp.float32 if i == 0 else jnp.bfloat16)
            for i in range(4)
        ],
        scratch_shapes=[pltpu.VMEM((2, SRC, wide), jnp.float32)],
        compiler_params=kernel_params(),
        name="own_terms",
    )(first, second)


def terms(part, sibling, piece, tables, scale, done=None):
    windows, channels, width = sibling.shape
    rows = piece.shape[1]
    second = done is None
    columns = v_row(rows) + HALF * rows if second else part_columns(rows)
    back = ((channels - SRC, 2 * HALF * rows), jnp.float32 if second else jnp.bfloat16)
    out = [jax.ShapeDtypeStruct(*back), jax.ShapeDtypeStruct((SRC, columns), jnp.float32)]
    out += [] if second else [TOKEN]
    more = () if second else (done,)
    return pl.pallas_call(
        functools.partial(second_kernel if second else first_kernel, scale),
        in_specs=[whole()] * (5 + len(more)),
        out_specs=[whole()] * len(out),
        out_shape=out,
        scratch_shapes=[pltpu.VMEM((columns, width), jnp.bfloat16)] * (2 if second else 1)
        + [pltpu.VMEM((channels, columns), jnp.float32)],
        compiler_params=kernel_params(),
        cost_estimate=LATE,
        name="terms_second" if second else "terms_first",
    )(part, sibling, piece, *tables, *more)


def copy_rows(source_ref, out_ref):
    rows = source_ref.shape[-2]
    if rows % 4:
        out_ref[...] = source_ref[...]
        return
    step = rows // 4 if rows % 64 == 0 else rows

    @pl.loop(0, rows, step=step)
    def _(start):
        line = pl.ds(pl.multiple_of(start, 16 if step % 16 == 0 else 8), step)
        out_ref[..., line, :] = source_ref[..., line, :]


def keep_kernel(*refs):
    half = len(refs) // 2
    for source_ref, out_ref in zip(refs[:half], refs[half:]):
        copy_rows(source_ref, out_ref)


def hold_kernel(source_ref, *refs):
    *_, out_ref, done_ref = refs
    copy_rows(source_ref, out_ref)
    done_ref[...] = jnp.zeros_like(done_ref)


def keep(*values):
    return pl.pallas_call(
        keep_kernel,
        in_specs=[whole()] * len(values),
        out_specs=[whole()] * len(values),
        out_shape=[jax.ShapeDtypeStruct(v.shape, v.dtype) for v in values],
        compiler_params=kernel_params(),
        name="keep",
    )(*values)


def hold(value, *done):
    return pl.pallas_call(
        hold_kernel,
        in_specs=[whole()] * (1 + len(done)),
        out_specs=[whole()] * 2,
        out_shape=[jax.ShapeDtypeStruct(value.shape, value.dtype), TOKEN],
        compiler_params=kernel_params(),
        name="hold",
    )(value, *done)


def keep_after(value, done):
    return pl.pallas_call(
        lambda source_ref, _, out_ref: copy_rows(source_ref, out_ref),
        in_specs=[whole()] * 2,
        out_specs=whole(),
        out_shape=jax.ShapeDtypeStruct(value.shape, value.dtype),
        compiler_params=kernel_params(),
        name="keep_after",
    )(value, done)


def place_kernel(
    here_ref, core_ref, chip_ref, cross_ref, back_ref, out_ref, block_ref, sems
):
    x, core = place_of_core()
    lags, mine, channels = block_ref.shape
    swap = core != 0
    sides = []
    for q in range(2):
        index = jnp.where(x == q, 1, 0)
        own = here_ref[index] + chip_ref[1 - index].astype(jnp.float32)
        other = core_ref[index].astype(jnp.float32) + cross_ref[1 - index].astype(jnp.float32)
        sides += [jnp.where(swap, other, own), jnp.where(swap, own, other)]
    back = back_ref[...].astype(jnp.float32).T
    copies = []
    for j in range(lags):
        lag = HALF - 1 - j if j < HALF else j + 1 if j < lags - 1 else HALF
        cols = slice(j * mine, (j + 1) * mine)
        block_ref[lag, :, :SRC] = jnp.concatenate([v[:, cols] for v in sides], axis=1)
        block_ref[lag, :, SRC:] = back[cols]
        copies.append(pltpu.make_async_copy(block_ref.at[lag], out_ref.at[lag], sems.at[lag]))
        copies[-1].start()
    for copy in copies:
        copy.wait()


def place(here, core, chip, cross, back):
    _, mine, wide = here.shape
    shape = (wide // mine, mine, SRC + back.shape[0])
    return pl.pallas_call(
        place_kernel,
        in_specs=[whole()] * 5,
        out_specs=anywhere(),
        out_shape=jax.ShapeDtypeStruct(shape, jnp.float32),
        scratch_shapes=[
            pltpu.VMEM(shape, jnp.float32), pltpu.SemaphoreType.DMA((shape[0],))
        ],
        compiler_params=kernel_params(),
        name="place_lags",
    )(here, core, chip, cross, back)


def pair_body(spectra, counts, partner):
    blocks = lax.axis_size("chan")
    groups = lax.axis_size("win")
    windows, channels, two, freqs = spectra.shape
    scale = 1.0 / (math.sqrt(2.0 * freqs) * math.sqrt(windows * groups))
    other_core = [(i, i ^ 1) for i in range(groups)]
    other_chip = [(i, i ^ 2) for i in range(groups)]
    other_both = [(i, i ^ 3) for i in range(groups)]

    def to_partner(t):
        return [(i, i ^ t) for i in range(blocks)]

    def to_partner_core(t):
        return [
            (i * groups + g, (i ^ t) * groups + (g ^ 1))
            for i in range(blocks)
            for g in range(groups)
        ]

    def send_sources(t, counts, raw, sources, near, far, near_more, far_more):
        def straight(value):
            return lax.ppermute(value, "chan", to_partner(t))

        def crossed(value):
            return lax.ppermute(value, ("chan", "win"), to_partner_core(t))

        near, far = straight(near), crossed(far)
        white = whiten_rest(counts, raw, taper, sources)
        sibling = lax.ppermute(white, "win", other_core)
        near_more, done = hold(near_more, near)
        near_more = straight(near_more)
        part, done = part_terms(white, near, tables, done)
        far_more, done = hold(far_more, far, done)
        far_more = crossed(far_more)
        back, own, done = terms(part, sibling, far, tables, scale, done)
        back = lax.ppermute(back, "win", other_chip)
        part, done = part_terms(white, near_more, tables, done)
        return part, *keep(sibling), keep_after(far_more, done), *keep(back), own

    def send_terms(t, back, first, second):
        back = lax.ppermute(back, "chan", to_partner(t))
        here, core, chip, cross = own_terms(first, second, SRC // groups, scale)
        core = lax.ppermute(core, "win", other_core)
        chip = lax.ppermute(chip, "win", other_chip)
        cross = lax.ppermute(cross, "win", other_both)
        return here, *keep(core, chip, cross, back)

    def by_round(run, *values):
        branches = [functools.partial(run, t) for t in range(1, blocks)]
        return lax.switch(partner[0, 0] - 1, branches, *values)

    tables = [jnp.asarray(v) for v in shift_tables(freqs)]
    taper = taper_row(two, freqs)
    piece = jax.ShapeDtypeStruct((windows, SRC // 4, two * freqs), jnp.bfloat16)
    sources = jax.ShapeDtypeStruct((windows, SRC, two * freqs), jnp.bfloat16)
    raw = pltpu.with_memory_space_constraint(spectra, pltpu.HBM)
    sources = whiten_sources([sources] + [piece] * 4, counts, fetch_sources(raw), taper)
    part, sibling, piece, back_recv, first = by_round(send_sources, counts, raw, *sources)
    back, second = terms(part, sibling, piece, tables, scale)
    back = (back + back_recv.astype(jnp.float32)).astype(jnp.bfloat16)
    return place(*by_round(send_terms, back, first, second))[None, None]


def lag_table(freqs, lags):
    freq = jnp.arange(freqs, dtype=jnp.float32) + freqs // 4
    delay = jnp.arange(lags, dtype=jnp.float32) - lags // 2
    phase = 2.0 * math.pi * freq[:, None] * delay[None, :] / (4.0 * freqs)
    norm = 1.0 / math.sqrt(2.0 * freqs)
    return jnp.stack([jnp.cos(phase), -jnp.sin(phase)]) * norm


def blended_sources(sources, table):
    src = sources.astype(jnp.float32)
    first = src[:, :, 0][:, :, None, :]
    second = src[:, :, 1][:, :, None, :]
    cos_part = table[0].T[None, None]
    sin_part = table[1].T[None, None]
    real_mix = first * cos_part + second * sin_part
    imag_mix = second * cos_part - first * sin_part
    return jnp.stack([real_mix, imag_mix], axis=3).astype(jnp.bfloat16)


def pair_terms(sources, receiver_blocks, table):
    wins, count, two, freqs = sources.shape
    lags = table.shape[2]
    group = math.gcd(count, 32)
    flat_recv = receiver_blocks.reshape(wins, receiver_blocks.shape[1], two * freqs)
    grouped = jnp.moveaxis(sources.reshape(wins, count // group, group, two, freqs), 1, 0)

    def one_group(piece):
        mixed_spectra = blended_sources(piece, table).reshape(wins, group * lags, two * freqs)
        out = jnp.einsum(
            "wmx,wrx->mr", mixed_spectra, flat_recv, preferred_element_type=jnp.float32
        )
        return out.reshape(group, lags, receiver_blocks.shape[1])

    out = lax.map(one_group, grouped).reshape(count, lags, receiver_blocks.shape[1])
    return jnp.transpose(out, (1, 0, 2))


def route_blocks(values, round_flags, levels):
    for level in range(levels):
        moved = from_partner(values, "chan", level)
        values = jnp.where((round_flags >> level) % 2 == 1, moved, values)
    return values


def general_body(spectra, counts, partner):
    white = whiten_local(spectra, counts[0])
    table = lag_table(spectra.shape[3], LAGS)
    levels = lax.axis_size("chan").bit_length() - 1
    windows = spectra.shape[0] * lax.axis_size("win")
    receiver_blocks = route_blocks(white, partner[0, 0], levels)
    out = pair_terms(white[:, :SRC], receiver_blocks, table)
    stacked = lax.psum_scatter(out, "win", scatter_dimension=1, tiled=True)
    return (stacked / math.sqrt(windows))[None, None]


def solution(mesh):
    body = pair_body if mesh.shape["win"] == 4 else general_body
    return jax.shard_map(
        body,
        mesh=mesh,
        in_specs=(P("win", "chan", None, None), P("chan"), P()),
        out_specs=P("chan", None, None, "win", None),
        check_vma=False,
    )
```

```python
import functools
import math

import jax
import jax.numpy as jnp
import numpy as np
from jax import lax
from jax.experimental import pallas as pl
from jax.experimental.pallas import tpu as pltpu
from jax.sharding import PartitionSpec as P

LAGS = 16
SRC = 160
HALF = LAGS // 2
VMEM_LIMIT = 16 * 1024 * 1024


def from_partner(value, axis, stride):
    return lax.ppermute(value, axis, [(i, i ^ 1 << stride) for i in range(lax.axis_size(axis))])


def whiten_local(spectra, count):
    values = spectra.astype(jnp.float32)
    block_size = spectra.shape[1]
    freqs = spectra.shape[3]
    valid = (jnp.arange(block_size, dtype=jnp.int32) < count).astype(jnp.float32)
    freq = jnp.arange(freqs, dtype=jnp.float32)
    taper = 0.75 - 0.25 * jnp.cos(2.0 * math.pi * (freq + 0.5) / freqs)
    power = jnp.mean(values * values, axis=(2, 3))
    scale = valid[None, :] / jnp.sqrt(power + 1e-05)
    return (values * taper * scale[:, :, None, None]).astype(jnp.bfloat16)


def shift_tables(freqs):
    freq = np.arange(freqs, dtype=np.float64) + freqs // 4
    shift = np.arange(1, HALF + 1, dtype=np.float64)
    phase = 2.0 * np.pi * shift[:, None] * freq[None, :] / (4.0 * freqs)
    return np.cos(phase).astype(np.float32), np.sin(phase).astype(np.float32)


def place_of_core():
    spot = lax.axis_index("win")
    return spot // 2, spot % 2


def whole():
    return pl.BlockSpec(memory_space=pltpu.VMEM)


def anywhere():
    return pl.BlockSpec(memory_space=pl.ANY)


def kernel_params():
    return pltpu.CompilerParams(vmem_limit_bytes=VMEM_LIMIT)


def fetch_kernel(source_ref, out_ref, sems):
    windows, channels = out_ref.shape[:2]
    parts = sems.shape[1]
    step = channels // parts
    copies = []
    for w in range(windows):
        for i in range(parts):
            part = (w, pl.ds(i * step, step))
            copies.append(
                pltpu.make_async_copy(source_ref.at[part], out_ref.at[part], sems.at[w, i])
            )
            copies[-1].start()
    for copy in copies:
        copy.wait()


def fetch_sources(spectra):
    windows, _, *rest = spectra.shape
    return pl.pallas_call(
        fetch_kernel,
        in_specs=[pl.BlockSpec(memory_space=pltpu.HBM)],
        out_specs=whole(),
        out_shape=jax.ShapeDtypeStruct((windows, SRC, *rest), spectra.dtype),
        scratch_shapes=[pltpu.SemaphoreType.DMA((windows, 4))],
        compiler_params=kernel_params(),
        name="fetch",
    )(spectra)


def white_block(raw_ref, taper_ref, count, w, line, first_row):
    values = raw_ref[w, line, :].astype(jnp.float32)
    rows, width = values.shape
    power = jnp.sum(values * values, axis=1, keepdims=True) * (1.0 / width)
    row = first_row + lax.broadcasted_iota(jnp.int32, (rows, 1), 0)
    valid = (row < count).astype(jnp.float32)
    scale = valid / jnp.sqrt(power + 1e-05)
    return values * taper_ref[...] * scale


def whiten_kernel(count_ref, raw_ref, taper_ref, white_ref, *refs):
    *piece_refs, count, sem = refs
    copy = pltpu.make_async_copy(count_ref, count, sem)
    copy.start()
    x, core = place_of_core()
    mine = SRC // 4
    step = 2 * mine
    copy.wait()
    for w in range(raw_ref.shape[0]):
        for index, group in enumerate((1 - x, x)):
            line = pl.ds(pl.multiple_of(group * step, step), step)
            values = white_block(raw_ref, taper_ref, count[0], w, line, group * step)
            white_ref[w, line, :] = values.astype(jnp.bfloat16)
            low, high = values[:mine], values[mine:]
            first = core == 0
            near_ref, far_ref = piece_refs[2 * index:2 * index + 2]
            near_ref[w] = jnp.where(first, low, high).astype(jnp.bfloat16)
            far_ref[w] = jnp.where(first, high, low).astype(jnp.bfloat16)


def rest_kernel(
    count_ref, spectra_ref, taper_ref, sources_ref, white_ref, raw_ref, count, sems
):
    windows, channels, two, freqs = raw_ref.shape
    copies = [pltpu.make_async_copy(count_ref, count, sems.at[windows])]
    for w in range(windows):
        part = spectra_ref.at[w, pl.ds(SRC, channels)]
        copies.append(pltpu.make_async_copy(part, raw_ref.at[w], sems.at[w]))
    for copy in copies:
        copy.start()
    step = 32

    @pl.loop(0, windows)
    def _(w):
        @pl.loop(0, SRC, step=step)
        def _(start):
            line = pl.ds(pl.multiple_of(start, step), step)
            white_ref[w, line, :] = sources_ref[w, line, :]

    for copy in copies:
        copy.wait()

    @pl.loop(0, windows)
    def _(w):
        @pl.loop(0, channels, step=step)
        def _(start):
            line = pl.ds(pl.multiple_of(start, step), step)
            parts = [raw_ref[w, line, p, :].astype(jnp.float32) for p in range(two)]
            power = sum(jnp.sum(v * v, axis=1, keepdims=True) for v in parts)
            row = SRC + start + lax.broadcasted_iota(jnp.int32, (step, 1), 0)
            valid = (row < count[0]).astype(jnp.float32)
            scale = valid / jnp.sqrt(power * (1.0 / (two * freqs)) + 1e-05)
            out = pl.ds(pl.multiple_of(SRC + start, step), step)
            for p, v in enumerate(parts):
                cols = slice(p * freqs, (p + 1) * freqs)
                white_ref[w, out, cols] = (v * taper_ref[:, cols] * scale).astype(jnp.bfloat16)


def whiten_rest(counts, spectra, taper, sources):
    windows, channels, two, freqs = spectra.shape
    return pl.pallas_call(
        rest_kernel,
        in_specs=[anywhere(), pl.BlockSpec(memory_space=pltpu.HBM), whole(), whole()],
        out_specs=whole(),
        out_shape=jax.ShapeDtypeStruct((windows, channels, two * freqs), jnp.bfloat16),
        scratch_shapes=[
            pltpu.VMEM((windows, channels - SRC, two, freqs), spectra.dtype),
            pltpu.SMEM((1,), jnp.int32),
            pltpu.SemaphoreType.DMA((windows + 1,)),
        ],
        compiler_params=kernel_params(),
        name="whiten_rest",
    )(counts, spectra, taper, sources)


def whiten_sources(out_shape, counts, raw, taper):
    windows, channels, two, freqs = raw.shape
    return pl.pallas_call(
        whiten_kernel,
        in_specs=[anywhere()] + [whole()] * 2,
        out_specs=[whole()] * len(out_shape),
        out_shape=out_shape,
        scratch_shapes=[pltpu.SMEM((1,), jnp.int32), pltpu.SemaphoreType.DMA],
        compiler_params=kernel_params(),
        name="whiten",
    )(counts, raw.reshape(windows, channels, two * freqs), taper)


def taper_row(two, freqs):
    freq = np.arange(freqs, dtype=np.float64)
    taper = 0.75 - 0.25 * np.cos(2.0 * np.pi * (freq + 0.5) / freqs)
    return jnp.asarray(np.tile(taper.astype(np.float32), two)[None, :])


def mix(m_ref, piece, cos_ref, sin_ref, low, high):
    rows = piece.shape[0]
    vrow = v_row(rows)
    real = piece[:, low].astype(jnp.float32)
    imag = piece[:, high].astype(jnp.float32)

    def put(where, cols, values):
        m_ref[where, cols] = jnp.concatenate(values, axis=0).astype(jnp.bfloat16)

    for m in range(0, HALF, 2):
        c = [cos_ref[m + i:m + i + 1, low] for i in range(2)]
        s = [sin_ref[m + i:m + i + 1, low] for i in range(2)]
        line = slice(m * rows, (m + 2) * rows)
        vline = slice(vrow + m * rows, vrow + (m + 2) * rows)
        put(line, low, [real * v for v in c])
        put(line, high, [imag * v for v in c])
        put(vline, low, [imag * -v for v in s])
        put(vline, high, [real * v for v in s])
    fill = jnp.zeros((vrow - (HALF + 1) * rows, 128), jnp.float32)
    for value, cols in ((real, low), (imag, high)):
        put(slice(HALF * rows, vrow), cols, [value, fill])


def v_row(rows):
    return -(-(HALF + 1) * rows // 128) * 128


def times(lhs, rhs):
    return lax.dot_general(
        lhs, rhs, (((1,), (1,)), ((), ())), preferred_element_type=jnp.float32
    )


def add_products(acc_ref, lhs_ref, piece_ref, cos_ref, sin_ref, mixed_ref):
    windows, rows, width = piece_ref.shape
    tile = 256
    used = v_row(rows) + HALF * rows
    if used < mixed_ref.shape[0]:
        mixed_ref[used:, :] = jnp.zeros_like(mixed_ref[used:, :])

    @pl.loop(0, windows)
    def _(w):
        @pl.loop(0, width // 2, step=128)
        def _(start):
            low = pl.ds(pl.multiple_of(start, 128), 128)
            high = pl.ds(pl.multiple_of(width // 2 + start, 128), 128)
            mix(mixed_ref, piece_ref.at[w], cos_ref, sin_ref, low, high)

        @pl.loop(0, mixed_ref.shape[0], step=tile)
        def _(n):
            cols = pl.ds(pl.multiple_of(n, tile), tile)
            acc_ref[:, cols] += times(lhs_ref[w], mixed_ref[cols, :])


def part_kernel(white_ref, piece_ref, cos_ref, sin_ref, _, part_ref, done_ref, mixed_ref):
    done_ref[...] = jnp.zeros_like(done_ref)
    part_ref[...] = jnp.zeros_like(part_ref)
    add_products(part_ref, white_ref, piece_ref, cos_ref, sin_ref, mixed_ref)


def part_columns(rows):
    columns = v_row(rows) + HALF * rows
    return columns + (-columns) % 256


def part_terms(white, piece, tables, done):
    windows, channels, width = white.shape
    columns = part_columns(piece.shape[1])
    return pl.pallas_call(
        part_kernel,
        in_specs=[whole()] * 5,
        out_specs=[whole()] * 2,
        out_shape=[jax.ShapeDtypeStruct((channels, columns), jnp.float32), TOKEN],
        scratch_shapes=[pltpu.VMEM((columns, width), jnp.bfloat16)],
        compiler_params=kernel_params(),
        cost_estimate=LATE,
        name="terms_part",
    )(white, piece, *tables, done)


TOKEN = jax.ShapeDtypeStruct((8, 128), jnp.float32)
LATE = pl.CostEstimate(flops=30 * 10**9, bytes_accessed=0, transcendentals=0)


def pack(acc_ref, line, rows, scale, later):
    wide = HALF * rows
    vrow = v_row(rows)
    u, v = acc_ref[line, :wide] * scale, acc_ref[line, vrow:vrow + wide] * scale
    still = acc_ref[line, wide:wide + rows] * scale
    first, last = (u - v, u + v) if later else (u + v, u - v)
    return jnp.concatenate([first, last[:, :wide - rows], still], axis=1)


def first_kernel(
    scale, part_ref, sibling_ref, piece_ref, cos_ref, sin_ref, _, back_ref, own_ref,
    done_ref, mixed_ref, acc_ref,
):
    done_ref[...] = jnp.zeros_like(done_ref)
    acc_ref[...] = part_ref[...]
    add_products(acc_ref, sibling_ref, piece_ref, cos_ref, sin_ref, mixed_ref)
    line = pl.ds(SRC, acc_ref.shape[0] - SRC)
    back = pack(acc_ref, line, piece_ref.shape[1], scale, True)
    back_ref[...] = back.astype(back_ref.dtype)
    own_ref[...] = acc_ref[:SRC, :]


def second_kernel(scale, part_ref, sibling_ref, piece_ref, cos_ref, sin_ref, *refs):
    back_ref, own_ref, even_ref, odd_ref, acc_ref = refs
    windows, rows, width = piece_ref.shape
    freqs = width // 2
    starts = [
        (slice(n, n + 128), slice(freqs + n, freqs + n + 128)) for n in range(0, freqs, 128)
    ]
    tiles = [
        slice(n, min(n + 256, acc_ref.shape[1])) for n in range(0, acc_ref.shape[1], 256)
    ]
    buffers = even_ref, odd_ref
    for start in starts:
        mix(even_ref, piece_ref.at[0], cos_ref, sin_ref, *start)
    for w in range(windows):
        now_ref, next_ref = buffers[w % 2], buffers[1 - w % 2]
        todo = starts if w + 1 < windows else []
        for cols in tiles:
            before = part_ref[:, cols] if w == 0 else acc_ref[:, cols]
            acc_ref[:, cols] = before + times(sibling_ref[w], now_ref[cols, :])
            for start in todo[:2]:
                mix(next_ref, piece_ref.at[w + 1], cos_ref, sin_ref, *start)
            todo = todo[2:]
    back_ref[...] = pack(acc_ref, pl.ds(SRC, acc_ref.shape[0] - SRC), rows, scale, True)
    own_ref[...] = acc_ref[:SRC, :]


def own_kernel(scale, rows, first_ref, second_ref, *refs):
    *out_refs, packed_ref = refs
    x, core = place_of_core()
    mine = SRC // 4

    @pl.loop(0, SRC, step=mine)
    def _(start):
        line = pl.ds(pl.multiple_of(start, 8), mine)
        for quarter, ref in enumerate((first_ref, second_ref)):
            packed_ref[quarter, line, :] = pack(ref, line, rows, scale, False)

    for i, out_ref in enumerate(out_refs):
        spot = 2 * (x, 1 - x)[i // 2] + (core, 1 - core)[i % 2]
        line = pl.ds(pl.multiple_of(spot * mine, 8), mine)
        for quarter in range(2):
            out_ref[quarter] = packed_ref[quarter, line, :].astype(out_ref.dtype)


def own_terms(first, second, rows, scale):
    mine, wide = SRC // 4, 2 * HALF * rows
    return pl.pallas_call(
        functools.partial(own_kernel, scale, rows),
        in_specs=[whole()] * 2,
        out_specs=[whole()] * 4,
        out_shape=[
            jax.ShapeDtypeStruct((2, mine, wide), jnp.float32 if i == 0 else jnp.bfloat16)
            for i in range(4)
        ],
        scratch_shapes=[pltpu.VMEM((2, SRC, wide), jnp.float32)],
        compiler_params=kernel_params(),
        name="own_terms",
    )(first, second)


def terms(part, sibling, piece, tables, scale, done=None):
    windows, channels, width = sibling.shape
    rows = piece.shape[1]
    second = done is None
    columns = v_row(rows) + HALF * rows if second else part_columns(rows)
    back = ((channels - SRC, 2 * HALF * rows), jnp.float32 if second else jnp.bfloat16)
    out = [jax.ShapeDtypeStruct(*back), jax.ShapeDtypeStruct((SRC, columns), jnp.float32)]
    out += [] if second else [TOKEN]
    more = () if second else (done,)
    return pl.pallas_call(
        functools.partial(second_kernel if second else first_kernel, scale),
        in_specs=[whole()] * (5 + len(more)),
        out_specs=[whole()] * len(out),
        out_shape=out,
        scratch_shapes=[pltpu.VMEM((columns, width), jnp.bfloat16)] * (2 if second else 1)
        + [pltpu.VMEM((channels, columns), jnp.float32)],
        compiler_params=kernel_params(),
        cost_estimate=LATE,
        name="terms_second" if second else "terms_first",
    )(part, sibling, piece, *tables, *more)


def copy_rows(source_ref, out_ref):
    rows = source_ref.shape[-2]
    if rows % 4:
        out_ref[...] = source_ref[...]
        return
    step = rows // 4 if rows % 64 == 0 else rows

    @pl.loop(0, rows, step=step)
    def _(start):
        line = pl.ds(pl.multiple_of(start, 16 if step % 16 == 0 else 8), step)
        out_ref[..., line, :] = source_ref[..., line, :]


def keep_kernel(*refs):
    half = len(refs) // 2
    for source_ref, out_ref in zip(refs[:half], refs[half:]):
        copy_rows(source_ref, out_ref)


def hold_kernel(source_ref, *refs):
    *_, out_ref, done_ref = refs
    copy_rows(source_ref, out_ref)
    done_ref[...] = jnp.zeros_like(done_ref)


def keep(*values):
    return pl.pallas_call(
        keep_kernel,
        in_specs=[whole()] * len(values),
        out_specs=[whole()] * len(values),
        out_shape=[jax.ShapeDtypeStruct(v.shape, v.dtype) for v in values],
        compiler_params=kernel_params(),
        name="keep",
    )(*values)


def hold(value, *done):
    return pl.pallas_call(
        hold_kernel,
        in_specs=[whole()] * (1 + len(done)),
        out_specs=[whole()] * 2,
        out_shape=[jax.ShapeDtypeStruct(value.shape, value.dtype), TOKEN],
        compiler_params=kernel_params(),
        name="hold",
    )(value, *done)


def keep_after(value, done):
    return pl.pallas_call(
        lambda source_ref, _, out_ref: copy_rows(source_ref, out_ref),
        in_specs=[whole()] * 2,
        out_specs=whole(),
        out_shape=jax.ShapeDtypeStruct(value.shape, value.dtype),
        compiler_params=kernel_params(),
        name="keep_after",
    )(value, done)


def place_kernel(
    here_ref, core_ref, chip_ref, cross_ref, back_ref, out_ref, block_ref, sems
):
    x, core = place_of_core()
    lags, mine, channels = block_ref.shape
    swap = core != 0
    sides = []
    for q in range(2):
        index = jnp.where(x == q, 1, 0)
        own = here_ref[index] + chip_ref[1 - index].astype(jnp.float32)
        other = core_ref[index].astype(jnp.float32) + cross_ref[1 - index].astype(jnp.float32)
        sides += [jnp.where(swap, other, own), jnp.where(swap, own, other)]
    back = back_ref[...].astype(jnp.float32).T
    copies = []
    for j in range(lags):
        lag = HALF - 1 - j if j < HALF else j + 1 if j < lags - 1 else HALF
        cols = slice(j * mine, (j + 1) * mine)
        block_ref[lag, :, :SRC] = jnp.concatenate([v[:, cols] for v in sides], axis=1)
        block_ref[lag, :, SRC:] = back[cols]
        copies.append(pltpu.make_async_copy(block_ref.at[lag], out_ref.at[lag], sems.at[lag]))
        copies[-1].start()
    for copy in copies:
        copy.wait()


def place(here, core, chip, cross, back):
    _, mine, wide = here.shape
    shape = (wide // mine, mine, SRC + back.shape[0])
    return pl.pallas_call(
        place_kernel,
        in_specs=[whole()] * 5,
        out_specs=anywhere(),
        out_shape=jax.ShapeDtypeStruct(shape, jnp.float32),
        scratch_shapes=[
            pltpu.VMEM(shape, jnp.float32), pltpu.SemaphoreType.DMA((shape[0],))
        ],
        compiler_params=kernel_params(),
        name="place_lags",
    )(here, core, chip, cross, back)


def pair_body(spectra, counts, partner):
    blocks = lax.axis_size("chan")
    groups = lax.axis_size("win")
    windows, channels, two, freqs = spectra.shape
    scale = 1.0 / (math.sqrt(2.0 * freqs) * math.sqrt(windows * groups))
    other_core = [(i, i ^ 1) for i in range(groups)]
    other_chip = [(i, i ^ 2) for i in range(groups)]
    other_both = [(i, i ^ 3) for i in range(groups)]

    def to_partner(t):
        return [(i, i ^ t) for i in range(blocks)]

    def to_partner_core(t):
        return [
            (i * groups + g, (i ^ t) * groups + (g ^ 1))
            for i in range(blocks)
            for g in range(groups)
        ]

    def send_sources(t, counts, raw, sources, near, far, near_more, far_more):
        def straight(value):
            return lax.ppermute(value, "chan", to_partner(t))

        def crossed(value):
            return lax.ppermute(value, ("chan", "win"), to_partner_core(t))

        near, far = straight(near), crossed(far)
        white = whiten_rest(counts, raw, taper, sources)
        sibling = lax.ppermute(white, "win", other_core)
        in_line = t < blocks // 2
        if in_line:
            near_more, done = hold(near_more, near)
            near_more = straight(near_more)
        else:
            near_more, done = hold(near_more, white)
            far_more, done = hold(far_more, done)
            near_more, far_more = straight(near_more), crossed(far_more)
        part, done = part_terms(white, near, tables, done)
        if in_line:
            far_more, done = hold(far_more, far, done)
            far_more = crossed(far_more)
        back, own, done = terms(part, sibling, far, tables, scale, done)
        back = lax.ppermute(back, "win", other_chip)
        if in_line:
            part, done = part_terms(white, near_more, tables, done)
            last = *keep(sibling), keep_after(far_more, done)
        else:
            part, done = part_terms(sibling, far_more, tables, done)
            last = *keep(white), keep_after(near_more, done)
        return part, *last, *keep(back), own

    def send_terms(t, back, first, second):
        back = lax.ppermute(back, "chan", to_partner(t))
        here, core, chip, cross = own_terms(first, second, SRC // groups, scale)
        core = lax.ppermute(core, "win", other_core)
        chip = lax.ppermute(chip, "win", other_chip)
        cross = lax.ppermute(cross, "win", other_both)
        return here, *keep(core, chip, cross, back)

    def by_round(run, *values):
        branches = [functools.partial(run, t) for t in range(1, blocks)]
        return lax.switch(partner[0, 0] - 1, branches, *values)

    tables = [jnp.asarray(v) for v in shift_tables(freqs)]
    taper = taper_row(two, freqs)
    piece = jax.ShapeDtypeStruct((windows, SRC // 4, two * freqs), jnp.bfloat16)
    sources = jax.ShapeDtypeStruct((windows, SRC, two * freqs), jnp.bfloat16)
    raw = pltpu.with_memory_space_constraint(spectra, pltpu.HBM)
    sources = whiten_sources([sources] + [piece] * 4, counts, fetch_sources(raw), taper)
    part, last, piece, back_recv, first = by_round(send_sources, counts, raw, *sources)
    back, second = terms(part, last, piece, tables, scale)
    back = (back + back_recv.astype(jnp.float32)).astype(jnp.bfloat16)
    return place(*by_round(send_terms, back, first, second))[None, None]


def lag_table(freqs, lags):
    freq = jnp.arange(freqs, dtype=jnp.float32) + freqs // 4
    delay = jnp.arange(lags, dtype=jnp.float32) - lags // 2
    phase = 2.0 * math.pi * freq[:, None] * delay[None, :] / (4.0 * freqs)
    norm = 1.0 / math.sqrt(2.0 * freqs)
    return jnp.stack([jnp.cos(phase), -jnp.sin(phase)]) * norm


def blended_sources(sources, table):
    src = sources.astype(jnp.float32)
    first = src[:, :, 0][:, :, None, :]
    second = src[:, :, 1][:, :, None, :]
    cos_part = table[0].T[None, None]
    sin_part = table[1].T[None, None]
    real_mix = first * cos_part + second * sin_part
    imag_mix = second * cos_part - first * sin_part
    return jnp.stack([real_mix, imag_mix], axis=3).astype(jnp.bfloat16)


def pair_terms(sources, receiver_blocks, table):
    wins, count, two, freqs = sources.shape
    lags = table.shape[2]
    group = math.gcd(count, 32)
    flat_recv = receiver_blocks.reshape(wins, receiver_blocks.shape[1], two * freqs)
    grouped = jnp.moveaxis(sources.reshape(wins, count // group, group, two, freqs), 1, 0)

    def one_group(piece):
        mixed_spectra = blended_sources(piece, table).reshape(wins, group * lags, two * freqs)
        out = jnp.einsum(
            "wmx,wrx->mr", mixed_spectra, flat_recv, preferred_element_type=jnp.float32
        )
        return out.reshape(group, lags, receiver_blocks.shape[1])

    out = lax.map(one_group, grouped).reshape(count, lags, receiver_blocks.shape[1])
    return jnp.transpose(out, (1, 0, 2))


def route_blocks(values, round_flags, levels):
    for level in range(levels):
        moved = from_partner(values, "chan", level)
        values = jnp.where((round_flags >> level) % 2 == 1, moved, values)
    return values


def general_body(spectra, counts, partner):
    white = whiten_local(spectra, counts[0])
    table = lag_table(spectra.shape[3], LAGS)
    levels = lax.axis_size("chan").bit_length() - 1
    windows = spectra.shape[0] * lax.axis_size("win")
    receiver_blocks = route_blocks(white, partner[0, 0], levels)
    out = pair_terms(white[:, :SRC], receiver_blocks, table)
    stacked = lax.psum_scatter(out, "win", scatter_dimension=1, tiled=True)
    return (stacked / math.sqrt(windows))[None, None]


def solution(mesh):
    body = pair_body if mesh.shape["win"] == 4 else general_body
    return jax.shard_map(
        body,
        mesh=mesh,
        in_specs=(P("win", "chan", None, None), P("chan"), P()),
        out_specs=P("chan", None, None, "win", None),
        check_vma=False,
    )
```

```python
import functools
import math

import jax
import jax.numpy as jnp
import numpy as np
from jax import lax
from jax.experimental import pallas as pl
from jax.experimental.pallas import tpu as pltpu
from jax.sharding import PartitionSpec as P

LAGS = 16
SRC = 160
HALF = LAGS // 2
VMEM_LIMIT = 16 * 1024 * 1024


def from_partner(value, axis, stride):
    return lax.ppermute(value, axis, [(i, i ^ 1 << stride) for i in range(lax.axis_size(axis))])


def whiten_local(spectra, count):
    values = spectra.astype(jnp.float32)
    block_size = spectra.shape[1]
    freqs = spectra.shape[3]
    valid = (jnp.arange(block_size, dtype=jnp.int32) < count).astype(jnp.float32)
    freq = jnp.arange(freqs, dtype=jnp.float32)
    taper = 0.75 - 0.25 * jnp.cos(2.0 * math.pi * (freq + 0.5) / freqs)
    power = jnp.mean(values * values, axis=(2, 3))
    scale = valid[None, :] / jnp.sqrt(power + 1e-05)
    return (values * taper * scale[:, :, None, None]).astype(jnp.bfloat16)


def shift_tables(freqs):
    freq = np.arange(freqs, dtype=np.float64) + freqs // 4
    shift = np.arange(1, HALF + 1, dtype=np.float64)
    phase = 2.0 * np.pi * shift[:, None] * freq[None, :] / (4.0 * freqs)
    return np.cos(phase).astype(np.float32), np.sin(phase).astype(np.float32)


def place_of_core():
    spot = lax.axis_index("win")
    return spot // 2, spot % 2


def whole():
    return pl.BlockSpec(memory_space=pltpu.VMEM)


def anywhere():
    return pl.BlockSpec(memory_space=pl.ANY)


def kernel_params():
    return pltpu.CompilerParams(vmem_limit_bytes=VMEM_LIMIT)


def fetch_kernel(source_ref, out_ref, sems):
    windows, channels = out_ref.shape[:2]
    parts = sems.shape[1]
    step = channels // parts
    copies = []
    for w in range(windows):
        for i in range(parts):
            part = (w, pl.ds(i * step, step))
            copies.append(
                pltpu.make_async_copy(source_ref.at[part], out_ref.at[part], sems.at[w, i])
            )
            copies[-1].start()
    for copy in copies:
        copy.wait()


def fetch_sources(spectra):
    windows, _, *rest = spectra.shape
    return pl.pallas_call(
        fetch_kernel,
        in_specs=[pl.BlockSpec(memory_space=pltpu.HBM)],
        out_specs=whole(),
        out_shape=jax.ShapeDtypeStruct((windows, SRC, *rest), spectra.dtype),
        scratch_shapes=[pltpu.SemaphoreType.DMA((windows, 4))],
        compiler_params=kernel_params(),
        name="fetch",
    )(spectra)


def white_block(raw_ref, taper_ref, count, w, line, first_row):
    values = raw_ref[w, line, :].astype(jnp.float32)
    rows, width = values.shape
    power = jnp.sum(values * values, axis=1, keepdims=True) * (1.0 / width)
    row = first_row + lax.broadcasted_iota(jnp.int32, (rows, 1), 0)
    valid = (row < count).astype(jnp.float32)
    scale = valid / jnp.sqrt(power + 1e-05)
    return values * taper_ref[...] * scale


def whiten_kernel(count_ref, raw_ref, taper_ref, white_ref, *refs):
    *piece_refs, count, sem = refs
    copy = pltpu.make_async_copy(count_ref, count, sem)
    copy.start()
    x, core = place_of_core()
    mine = SRC // 4
    step = 2 * mine
    copy.wait()
    for w in range(raw_ref.shape[0]):
        for index, group in enumerate((1 - x, x)):
            line = pl.ds(pl.multiple_of(group * step, step), step)
            values = white_block(raw_ref, taper_ref, count[0], w, line, group * step)
            white_ref[w, line, :] = values.astype(jnp.bfloat16)
            low, high = values[:mine], values[mine:]
            first = core == 0
            near_ref, far_ref = piece_refs[2 * index:2 * index + 2]
            near_ref[w] = jnp.where(first, low, high).astype(jnp.bfloat16)
            far_ref[w] = jnp.where(first, high, low).astype(jnp.bfloat16)


def rest_kernel(
    count_ref, spectra_ref, taper_ref, sources_ref, white_ref, raw_ref, count, sems
):
    windows, channels, two, freqs = raw_ref.shape
    copies = [pltpu.make_async_copy(count_ref, count, sems.at[windows])]
    for w in range(windows):
        part = spectra_ref.at[w, pl.ds(SRC, channels)]
        copies.append(pltpu.make_async_copy(part, raw_ref.at[w], sems.at[w]))
    for copy in copies:
        copy.start()
    step = 32

    @pl.loop(0, windows)
    def _(w):
        @pl.loop(0, SRC, step=step)
        def _(start):
            line = pl.ds(pl.multiple_of(start, step), step)
            white_ref[w, line, :] = sources_ref[w, line, :]

    for copy in copies:
        copy.wait()

    @pl.loop(0, windows)
    def _(w):
        @pl.loop(0, channels, step=step)
        def _(start):
            line = pl.ds(pl.multiple_of(start, step), step)
            parts = [raw_ref[w, line, p, :].astype(jnp.float32) for p in range(two)]
            power = sum(jnp.sum(v * v, axis=1, keepdims=True) for v in parts)
            row = SRC + start + lax.broadcasted_iota(jnp.int32, (step, 1), 0)
            valid = (row < count[0]).astype(jnp.float32)
            scale = valid / jnp.sqrt(power * (1.0 / (two * freqs)) + 1e-05)
            out = pl.ds(pl.multiple_of(SRC + start, step), step)
            for p, v in enumerate(parts):
                cols = slice(p * freqs, (p + 1) * freqs)
                white_ref[w, out, cols] = (v * taper_ref[:, cols] * scale).astype(jnp.bfloat16)


def whiten_rest(counts, spectra, taper, sources):
    windows, channels, two, freqs = spectra.shape
    return pl.pallas_call(
        rest_kernel,
        in_specs=[anywhere(), pl.BlockSpec(memory_space=pltpu.HBM), whole(), whole()],
        out_specs=whole(),
        out_shape=jax.ShapeDtypeStruct((windows, channels, two * freqs), jnp.bfloat16),
        scratch_shapes=[
            pltpu.VMEM((windows, channels - SRC, two, freqs), spectra.dtype),
            pltpu.SMEM((1,), jnp.int32),
            pltpu.SemaphoreType.DMA((windows + 1,)),
        ],
        compiler_params=kernel_params(),
        name="whiten_rest",
    )(counts, spectra, taper, sources)


def whiten_sources(out_shape, counts, raw, taper):
    windows, channels, two, freqs = raw.shape
    return pl.pallas_call(
        whiten_kernel,
        in_specs=[anywhere()] + [whole()] * 2,
        out_specs=[whole()] * len(out_shape),
        out_shape=out_shape,
        scratch_shapes=[pltpu.SMEM((1,), jnp.int32), pltpu.SemaphoreType.DMA],
        compiler_params=kernel_params(),
        name="whiten",
    )(counts, raw.reshape(windows, channels, two * freqs), taper)


def taper_row(two, freqs):
    freq = np.arange(freqs, dtype=np.float64)
    taper = 0.75 - 0.25 * np.cos(2.0 * np.pi * (freq + 0.5) / freqs)
    return jnp.asarray(np.tile(taper.astype(np.float32), two)[None, :])


def mix(m_ref, piece, cos_ref, sin_ref, low, high):
    rows = piece.shape[0]
    vrow = v_row(rows)
    real = piece[:, low].astype(jnp.float32)
    imag = piece[:, high].astype(jnp.float32)

    def put(where, cols, values):
        m_ref[where, cols] = jnp.concatenate(values, axis=0).astype(jnp.bfloat16)

    for m in range(0, HALF, 2):
        c = [cos_ref[m + i:m + i + 1, low] for i in range(2)]
        s = [sin_ref[m + i:m + i + 1, low] for i in range(2)]
        line = slice(m * rows, (m + 2) * rows)
        vline = slice(vrow + m * rows, vrow + (m + 2) * rows)
        put(line, low, [real * v for v in c])
        put(line, high, [imag * v for v in c])
        put(vline, low, [imag * -v for v in s])
        put(vline, high, [real * v for v in s])
    fill = jnp.zeros((vrow - (HALF + 1) * rows, 128), jnp.float32)
    for value, cols in ((real, low), (imag, high)):
        put(slice(HALF * rows, vrow), cols, [value, fill])


def v_row(rows):
    return -(-(HALF + 1) * rows // 128) * 128


def times(lhs, rhs):
    return lax.dot_general(
        lhs, rhs, (((1,), (1,)), ((), ())), preferred_element_type=jnp.float32
    )


def add_products(acc_ref, lhs_ref, piece_ref, cos_ref, sin_ref, mixed_ref):
    windows, rows, width = piece_ref.shape
    tile = 256
    used = v_row(rows) + HALF * rows
    if used < mixed_ref.shape[0]:
        mixed_ref[used:, :] = jnp.zeros_like(mixed_ref[used:, :])

    @pl.loop(0, windows)
    def _(w):
        @pl.loop(0, width // 2, step=128)
        def _(start):
            low = pl.ds(pl.multiple_of(start, 128), 128)
            high = pl.ds(pl.multiple_of(width // 2 + start, 128), 128)
            mix(mixed_ref, piece_ref.at[w], cos_ref, sin_ref, low, high)

        @pl.loop(0, mixed_ref.shape[0], step=tile)
        def _(n):
            cols = pl.ds(pl.multiple_of(n, tile), tile)
            acc_ref[:, cols] += times(lhs_ref[w], mixed_ref[cols, :])


def part_kernel(white_ref, piece_ref, cos_ref, sin_ref, _, part_ref, done_ref, mixed_ref):
    done_ref[...] = jnp.zeros_like(done_ref)
    part_ref[...] = jnp.zeros_like(part_ref)
    add_products(part_ref, white_ref, piece_ref, cos_ref, sin_ref, mixed_ref)


def part_columns(rows):
    columns = v_row(rows) + HALF * rows
    return columns + (-columns) % 256


def part_terms(white, piece, tables, done):
    windows, channels, width = white.shape
    columns = part_columns(piece.shape[1])
    return pl.pallas_call(
        part_kernel,
        in_specs=[whole()] * 5,
        out_specs=[whole()] * 2,
        out_shape=[jax.ShapeDtypeStruct((channels, columns), jnp.float32), TOKEN],
        scratch_shapes=[pltpu.VMEM((columns, width), jnp.bfloat16)],
        compiler_params=kernel_params(),
        cost_estimate=COST,
        name="terms_part",
    )(white, piece, *tables, done)


TOKEN = jax.ShapeDtypeStruct((8, 128), jnp.float32)
COST = pl.CostEstimate(flops=30 * 10**9, bytes_accessed=0, transcendentals=0)


def pack(acc_ref, line, rows, scale, later):
    wide = HALF * rows
    vrow = v_row(rows)
    u, v = acc_ref[line, :wide] * scale, acc_ref[line, vrow:vrow + wide] * scale
    still = acc_ref[line, wide:wide + rows] * scale
    first, last = (u - v, u + v) if later else (u + v, u - v)
    return jnp.concatenate([first, last[:, :wide - rows], still], axis=1)


def terms_kernel(
    scale, part_ref, sibling_ref, piece_ref, cos_ref, sin_ref, _, back_ref, own_ref, *refs
):
    *done_refs, mixed_ref, acc_ref = refs
    for done_ref in done_refs:
        done_ref[...] = jnp.zeros_like(done_ref)
    acc_ref[...] = part_ref[...]
    add_products(acc_ref, sibling_ref, piece_ref, cos_ref, sin_ref, mixed_ref)
    line = pl.ds(SRC, acc_ref.shape[0] - SRC)
    back = pack(acc_ref, line, piece_ref.shape[1], scale, True)
    back_ref[...] = back.astype(back_ref.dtype)
    own_ref[...] = acc_ref[:SRC, :]


def own_kernel(scale, rows, first_ref, second_ref, *refs):
    *out_refs, packed_ref = refs
    x, core = place_of_core()
    mine = SRC // 4

    @pl.loop(0, SRC, step=mine)
    def _(start):
        line = pl.ds(pl.multiple_of(start, 8), mine)
        for quarter, ref in enumerate((first_ref, second_ref)):
            packed_ref[quarter, line, :] = pack(ref, line, rows, scale, False)

    for i, out_ref in enumerate(out_refs):
        spot = 2 * (x, 1 - x)[i // 2] + (core, 1 - core)[i % 2]
        line = pl.ds(pl.multiple_of(spot * mine, 8), mine)
        for quarter in range(2):
            out_ref[quarter] = packed_ref[quarter, line, :].astype(out_ref.dtype)


def own_terms(first, second, rows, scale):
    mine, wide = SRC // 4, 2 * HALF * rows
    return pl.pallas_call(
        functools.partial(own_kernel, scale, rows),
        in_specs=[whole()] * 2,
        out_specs=[whole()] * 4,
        out_shape=[
            jax.ShapeDtypeStruct((2, mine, wide), jnp.float32 if i == 0 else jnp.bfloat16)
            for i in range(4)
        ],
        scratch_shapes=[pltpu.VMEM((2, SRC, wide), jnp.float32)],
        compiler_params=kernel_params(),
        name="own_terms",
    )(first, second)


def terms(part, sibling, piece, tables, scale, done, last):
    windows, channels, width = sibling.shape
    rows = piece.shape[1]
    columns = part_columns(rows)
    back = ((channels - SRC, 2 * HALF * rows), jnp.float32 if last else jnp.bfloat16)
    out = [jax.ShapeDtypeStruct(*back), jax.ShapeDtypeStruct((SRC, columns), jnp.float32)]
    out += [] if last else [TOKEN]
    return pl.pallas_call(
        functools.partial(terms_kernel, scale),
        in_specs=[whole()] * 6,
        out_specs=[whole()] * len(out),
        out_shape=out,
        scratch_shapes=[
            pltpu.VMEM((columns, width), jnp.bfloat16),
            pltpu.VMEM((channels, columns), jnp.float32),
        ],
        compiler_params=kernel_params(),
        cost_estimate=COST,
        name="terms",
    )(part, sibling, piece, *tables, done)


def sum_kernel(here_ref, there_ref, out_ref):
    rows = out_ref.shape[0] // 4

    @pl.loop(0, out_ref.shape[0], step=rows)
    def _(start):
        line = pl.ds(pl.multiple_of(start, 8), rows)
        total = here_ref[line, :] + there_ref[line, :].astype(jnp.float32)
        out_ref[line, :] = total.astype(out_ref.dtype)


def sum_terms(here, there):
    return pl.pallas_call(
        sum_kernel,
        in_specs=[whole()] * 2,
        out_specs=whole(),
        out_shape=jax.ShapeDtypeStruct(there.shape, there.dtype),
        compiler_params=kernel_params(),
        name="sum_terms",
    )(here, there)


def copy_rows(source_ref, out_ref):
    rows = source_ref.shape[-2]
    if rows % 4:
        out_ref[...] = source_ref[...]
        return
    step = rows // 4 if rows % 64 == 0 else rows

    @pl.loop(0, rows, step=step)
    def _(start):
        line = pl.ds(pl.multiple_of(start, 16 if step % 16 == 0 else 8), step)
        out_ref[..., line, :] = source_ref[..., line, :]


def keep_kernel(*refs):
    half = len(refs) // 2
    for source_ref, out_ref in zip(refs[:half], refs[half:]):
        copy_rows(source_ref, out_ref)


def hold_kernel(source_ref, *refs):
    *_, out_ref, done_ref = refs
    copy_rows(source_ref, out_ref)
    done_ref[...] = jnp.zeros_like(done_ref)


def keep(*values):
    return pl.pallas_call(
        keep_kernel,
        in_specs=[whole()] * len(values),
        out_specs=[whole()] * len(values),
        out_shape=[jax.ShapeDtypeStruct(v.shape, v.dtype) for v in values],
        compiler_params=kernel_params(),
        name="keep",
    )(*values)


def hold(value, *done):
    return pl.pallas_call(
        hold_kernel,
        in_specs=[whole()] * (1 + len(done)),
        out_specs=[whole()] * 2,
        out_shape=[jax.ShapeDtypeStruct(value.shape, value.dtype), TOKEN],
        compiler_params=kernel_params(),
        name="hold",
    )(value, *done)


def place_kernel(
    here_ref, core_ref, chip_ref, cross_ref, back_ref, out_ref, block_ref, sems
):
    x, core = place_of_core()
    lags, mine, channels = block_ref.shape
    swap = core != 0
    sides = []
    for q in range(2):
        index = jnp.where(x == q, 1, 0)
        own = here_ref[index] + chip_ref[1 - index].astype(jnp.float32)
        other = core_ref[index].astype(jnp.float32) + cross_ref[1 - index].astype(jnp.float32)
        sides += [jnp.where(swap, other, own), jnp.where(swap, own, other)]
    back = back_ref[...].astype(jnp.float32).T
    copies = []
    for j in range(lags):
        lag = HALF - 1 - j if j < HALF else j + 1 if j < lags - 1 else HALF
        cols = slice(j * mine, (j + 1) * mine)
        block_ref[lag, :, :SRC] = jnp.concatenate([v[:, cols] for v in sides], axis=1)
        block_ref[lag, :, SRC:] = back[cols]
        copies.append(pltpu.make_async_copy(block_ref.at[lag], out_ref.at[lag], sems.at[lag]))
        copies[-1].start()
    for copy in copies:
        copy.wait()


def place(here, core, chip, cross, back):
    _, mine, wide = here.shape
    shape = (wide // mine, mine, SRC + back.shape[0])
    return pl.pallas_call(
        place_kernel,
        in_specs=[whole()] * 5,
        out_specs=anywhere(),
        out_shape=jax.ShapeDtypeStruct(shape, jnp.float32),
        scratch_shapes=[
            pltpu.VMEM(shape, jnp.float32), pltpu.SemaphoreType.DMA((shape[0],))
        ],
        compiler_params=kernel_params(),
        name="place_lags",
    )(here, core, chip, cross, back)


def pair_body(spectra, counts, partner):
    blocks = lax.axis_size("chan")
    groups = lax.axis_size("win")
    windows, channels, two, freqs = spectra.shape
    scale = 1.0 / (math.sqrt(2.0 * freqs) * math.sqrt(windows * groups))
    other_core = [(i, i ^ 1) for i in range(groups)]
    other_chip = [(i, i ^ 2) for i in range(groups)]
    other_both = [(i, i ^ 3) for i in range(groups)]

    def to_partner(t):
        return [(i, i ^ t) for i in range(blocks)]

    def to_partner_core(t):
        return [
            (i * groups + g, (i ^ t) * groups + (g ^ 1))
            for i in range(blocks)
            for g in range(groups)
        ]

    def send_sources(t, counts, raw, sources, near, far, near_more, far_more):
        def straight(value):
            return lax.ppermute(value, "chan", to_partner(t))

        def crossed(value):
            return lax.ppermute(value, ("chan", "win"), to_partner_core(t))

        near, far = straight(near), crossed(far)
        white = whiten_rest(counts, raw, taper, sources)
        sibling = lax.ppermute(white, "win", other_core)
        near_more, done = hold(near_more, near)
        near_more = straight(near_more)
        part, done = part_terms(white, near, tables, done)
        far_more, done = hold(far_more, far, done)
        far_more = crossed(far_more)
        there, first, done = terms(part, sibling, far, tables, scale, done, False)
        there = lax.ppermute(there, "win", other_chip)
        part, done = part_terms(white, near_more, tables, done)
        here, second = terms(part, sibling, far_more, tables, scale, done, True)
        return sum_terms(here, there), first, second

    def send_terms(t, back):
        return keep(lax.ppermute(back, "chan", to_partner(t)))[0]

    def by_round(run, *values):
        branches = [functools.partial(run, t) for t in range(1, blocks)]
        return lax.switch(partner[0, 0] - 1, branches, *values)

    tables = [jnp.asarray(v) for v in shift_tables(freqs)]
    taper = taper_row(two, freqs)
    piece = jax.ShapeDtypeStruct((windows, SRC // 4, two * freqs), jnp.bfloat16)
    sources = jax.ShapeDtypeStruct((windows, SRC, two * freqs), jnp.bfloat16)
    raw = pltpu.with_memory_space_constraint(spectra, pltpu.HBM)
    sources = whiten_sources([sources] + [piece] * 4, counts, fetch_sources(raw), taper)
    back, first, second = by_round(send_sources, counts, raw, *sources)
    here, core, chip, cross = own_terms(first, second, SRC // groups, scale)
    core = lax.ppermute(core, "win", other_core)
    chip = lax.ppermute(chip, "win", other_chip)
    cross = lax.ppermute(cross, "win", other_both)
    return place(here, core, chip, cross, by_round(send_terms, back))[None, None]


def lag_table(freqs, lags):
    freq = jnp.arange(freqs, dtype=jnp.float32) + freqs // 4
    delay = jnp.arange(lags, dtype=jnp.float32) - lags // 2
    phase = 2.0 * math.pi * freq[:, None] * delay[None, :] / (4.0 * freqs)
    norm = 1.0 / math.sqrt(2.0 * freqs)
    return jnp.stack([jnp.cos(phase), -jnp.sin(phase)]) * norm


def blended_sources(sources, table):
    src = sources.astype(jnp.float32)
    first = src[:, :, 0][:, :, None, :]
    second = src[:, :, 1][:, :, None, :]
    cos_part = table[0].T[None, None]
    sin_part = table[1].T[None, None]
    real_mix = first * cos_part + second * sin_part
    imag_mix = second * cos_part - first * sin_part
    return jnp.stack([real_mix, imag_mix], axis=3).astype(jnp.bfloat16)


def pair_terms(sources, receiver_blocks, table):
    wins, count, two, freqs = sources.shape
    lags = table.shape[2]
    group = math.gcd(count, 32)
    flat_recv = receiver_blocks.reshape(wins, receiver_blocks.shape[1], two * freqs)
    grouped = jnp.moveaxis(sources.reshape(wins, count // group, group, two, freqs), 1, 0)

    def one_group(piece):
        mixed_spectra = blended_sources(piece, table).reshape(wins, group * lags, two * freqs)
        out = jnp.einsum(
            "wmx,wrx->mr", mixed_spectra, flat_recv, preferred_element_type=jnp.float32
        )
        return out.reshape(group, lags, receiver_blocks.shape[1])

    out = lax.map(one_group, grouped).reshape(count, lags, receiver_blocks.shape[1])
    return jnp.transpose(out, (1, 0, 2))


def route_blocks(values, round_flags, levels):
    for level in range(levels):
        moved = from_partner(values, "chan", level)
        values = jnp.where((round_flags >> level) % 2 == 1, moved, values)
    return values


def general_body(spectra, counts, partner):
    white = whiten_local(spectra, counts[0])
    table = lag_table(spectra.shape[3], LAGS)
    levels = lax.axis_size("chan").bit_length() - 1
    windows = spectra.shape[0] * lax.axis_size("win")
    receiver_blocks = route_blocks(white, partner[0, 0], levels)
    out = pair_terms(white[:, :SRC], receiver_blocks, table)
    stacked = lax.psum_scatter(out, "win", scatter_dimension=1, tiled=True)
    return (stacked / math.sqrt(windows))[None, None]


def solution(mesh):
    body = pair_body if mesh.shape["win"] == 4 else general_body
    return jax.shard_map(
        body,
        mesh=mesh,
        in_specs=(P("win", "chan", None, None), P("chan"), P()),
        out_specs=P("chan", None, None, "win", None),
        check_vma=False,
    )
```

```python
import functools
import math

import jax
import jax.numpy as jnp
import numpy as np
from jax import lax
from jax.experimental import pallas as pl
from jax.experimental.pallas import tpu as pltpu
from jax.sharding import PartitionSpec as P

LAGS = 16
SRC = 160
HALF = LAGS // 2
VMEM_LIMIT = 16 * 1024 * 1024


def from_partner(value, axis, stride):
    return lax.ppermute(value, axis, [(i, i ^ 1 << stride) for i in range(lax.axis_size(axis))])


def whiten_local(spectra, count):
    values = spectra.astype(jnp.float32)
    block_size = spectra.shape[1]
    freqs = spectra.shape[3]
    valid = (jnp.arange(block_size, dtype=jnp.int32) < count).astype(jnp.float32)
    freq = jnp.arange(freqs, dtype=jnp.float32)
    taper = 0.75 - 0.25 * jnp.cos(2.0 * math.pi * (freq + 0.5) / freqs)
    power = jnp.mean(values * values, axis=(2, 3))
    scale = valid[None, :] / jnp.sqrt(power + 1e-05)
    return (values * taper * scale[:, :, None, None]).astype(jnp.bfloat16)


def shift_tables(freqs):
    freq = np.arange(freqs, dtype=np.float64) + freqs // 4
    shift = np.arange(1, HALF + 1, dtype=np.float64)
    phase = 2.0 * np.pi * shift[:, None] * freq[None, :] / (4.0 * freqs)
    return np.cos(phase).astype(np.float32), np.sin(phase).astype(np.float32)


def place_of_core():
    spot = lax.axis_index("win")
    return spot // 2, spot % 2


def whole():
    return pl.BlockSpec(memory_space=pltpu.VMEM)


def anywhere():
    return pl.BlockSpec(memory_space=pl.ANY)


def kernel_params():
    return pltpu.CompilerParams(vmem_limit_bytes=VMEM_LIMIT)


def fetch_kernel(source_ref, out_ref, sems):
    windows, channels = out_ref.shape[:2]
    parts = sems.shape[1]
    step = channels // parts
    copies = []
    for w in range(windows):
        for i in range(parts):
            part = (w, pl.ds(i * step, step))
            copies.append(
                pltpu.make_async_copy(source_ref.at[part], out_ref.at[part], sems.at[w, i])
            )
            copies[-1].start()
    for copy in copies:
        copy.wait()


def fetch_sources(spectra):
    windows, _, *rest = spectra.shape
    return pl.pallas_call(
        fetch_kernel,
        in_specs=[pl.BlockSpec(memory_space=pltpu.HBM)],
        out_specs=whole(),
        out_shape=jax.ShapeDtypeStruct((windows, SRC, *rest), spectra.dtype),
        scratch_shapes=[pltpu.SemaphoreType.DMA((windows, 4))],
        compiler_params=kernel_params(),
        name="fetch",
    )(spectra)


def white_block(raw_ref, taper_ref, count, w, line, first_row):
    values = raw_ref[w, line, :].astype(jnp.float32)
    rows, width = values.shape
    power = jnp.sum(values * values, axis=1, keepdims=True) * (1.0 / width)
    row = first_row + lax.broadcasted_iota(jnp.int32, (rows, 1), 0)
    valid = (row < count).astype(jnp.float32)
    scale = valid / jnp.sqrt(power + 1e-05)
    return values * taper_ref[...] * scale


def whiten_kernel(count_ref, raw_ref, taper_ref, white_ref, *refs):
    *piece_refs, count, sem = refs
    copy = pltpu.make_async_copy(count_ref, count, sem)
    copy.start()
    x, core = place_of_core()
    mine = SRC // 4
    step = 2 * mine
    copy.wait()
    for w in range(raw_ref.shape[0]):
        for index, group in enumerate((1 - x, x)):
            line = pl.ds(pl.multiple_of(group * step, step), step)
            values = white_block(raw_ref, taper_ref, count[0], w, line, group * step)
            white_ref[w, line, :] = values.astype(jnp.bfloat16)
            low, high = values[:mine], values[mine:]
            first = core == 0
            near_ref, far_ref = piece_refs[2 * index:2 * index + 2]
            near_ref[w] = jnp.where(first, low, high).astype(jnp.bfloat16)
            far_ref[w] = jnp.where(first, high, low).astype(jnp.bfloat16)


def rest_kernel(
    count_ref, spectra_ref, taper_ref, sources_ref, white_ref, raw_ref, count, sems
):
    windows, channels, two, freqs = raw_ref.shape
    copies = [pltpu.make_async_copy(count_ref, count, sems.at[windows])]
    for w in range(windows):
        part = spectra_ref.at[w, pl.ds(SRC, channels)]
        copies.append(pltpu.make_async_copy(part, raw_ref.at[w], sems.at[w]))
    for copy in copies:
        copy.start()
    step = 32

    @pl.loop(0, windows)
    def _(w):
        @pl.loop(0, SRC, step=step)
        def _(start):
            line = pl.ds(pl.multiple_of(start, step), step)
            white_ref[w, line, :] = sources_ref[w, line, :]

    for copy in copies:
        copy.wait()

    @pl.loop(0, windows)
    def _(w):
        @pl.loop(0, channels, step=step)
        def _(start):
            line = pl.ds(pl.multiple_of(start, step), step)
            parts = [raw_ref[w, line, p, :].astype(jnp.float32) for p in range(two)]
            power = sum(jnp.sum(v * v, axis=1, keepdims=True) for v in parts)
            row = SRC + start + lax.broadcasted_iota(jnp.int32, (step, 1), 0)
            valid = (row < count[0]).astype(jnp.float32)
            scale = valid / jnp.sqrt(power * (1.0 / (two * freqs)) + 1e-05)
            out = pl.ds(pl.multiple_of(SRC + start, step), step)
            for p, v in enumerate(parts):
                cols = slice(p * freqs, (p + 1) * freqs)
                white_ref[w, out, cols] = (v * taper_ref[:, cols] * scale).astype(jnp.bfloat16)


def whiten_rest(counts, spectra, taper, sources):
    windows, channels, two, freqs = spectra.shape
    return pl.pallas_call(
        rest_kernel,
        in_specs=[anywhere(), pl.BlockSpec(memory_space=pltpu.HBM), whole(), whole()],
        out_specs=whole(),
        out_shape=jax.ShapeDtypeStruct((windows, channels, two * freqs), jnp.bfloat16),
        scratch_shapes=[
            pltpu.VMEM((windows, channels - SRC, two, freqs), spectra.dtype),
            pltpu.SMEM((1,), jnp.int32),
            pltpu.SemaphoreType.DMA((windows + 1,)),
        ],
        compiler_params=kernel_params(),
        name="whiten_rest",
    )(counts, spectra, taper, sources)


def whiten_sources(out_shape, counts, raw, taper):
    windows, channels, two, freqs = raw.shape
    return pl.pallas_call(
        whiten_kernel,
        in_specs=[anywhere()] + [whole()] * 2,
        out_specs=[whole()] * len(out_shape),
        out_shape=out_shape,
        scratch_shapes=[pltpu.SMEM((1,), jnp.int32), pltpu.SemaphoreType.DMA],
        compiler_params=kernel_params(),
        name="whiten",
    )(counts, raw.reshape(windows, channels, two * freqs), taper)


def taper_row(two, freqs):
    freq = np.arange(freqs, dtype=np.float64)
    taper = 0.75 - 0.25 * np.cos(2.0 * np.pi * (freq + 0.5) / freqs)
    return jnp.asarray(np.tile(taper.astype(np.float32), two)[None, :])


def mix(m_ref, piece, cos_ref, sin_ref, low, high):
    rows = piece.shape[0]
    vrow = v_row(rows)
    real = piece[:, low].astype(jnp.float32)
    imag = piece[:, high].astype(jnp.float32)

    def put(where, cols, values):
        m_ref[where, cols] = jnp.concatenate(values, axis=0).astype(jnp.bfloat16)

    for m in range(0, HALF, 2):
        c = [cos_ref[m + i:m + i + 1, low] for i in range(2)]
        s = [sin_ref[m + i:m + i + 1, low] for i in range(2)]
        line = slice(m * rows, (m + 2) * rows)
        vline = slice(vrow + m * rows, vrow + (m + 2) * rows)
        put(line, low, [real * v for v in c])
        put(line, high, [imag * v for v in c])
        put(vline, low, [imag * -v for v in s])
        put(vline, high, [real * v for v in s])
    fill = jnp.zeros((vrow - (HALF + 1) * rows, 128), jnp.float32)
    for value, cols in ((real, low), (imag, high)):
        put(slice(HALF * rows, vrow), cols, [value, fill])


def v_row(rows):
    return -(-(HALF + 1) * rows // 128) * 128


def times(lhs, rhs):
    return lax.dot_general(
        lhs, rhs, (((1,), (1,)), ((), ())), preferred_element_type=jnp.float32
    )


def add_products(acc_ref, lhs_ref, piece_ref, cos_ref, sin_ref, mixed_ref):
    windows, rows, width = piece_ref.shape
    tile = 256
    used = v_row(rows) + HALF * rows
    if used < mixed_ref.shape[0]:
        mixed_ref[used:, :] = jnp.zeros_like(mixed_ref[used:, :])

    @pl.loop(0, windows)
    def _(w):
        @pl.loop(0, width // 2, step=128)
        def _(start):
            low = pl.ds(pl.multiple_of(start, 128), 128)
            high = pl.ds(pl.multiple_of(width // 2 + start, 128), 128)
            mix(mixed_ref, piece_ref.at[w], cos_ref, sin_ref, low, high)

        @pl.loop(0, mixed_ref.shape[0], step=tile)
        def _(n):
            cols = pl.ds(pl.multiple_of(n, tile), tile)
            acc_ref[:, cols] += times(lhs_ref[w], mixed_ref[cols, :])


def part_kernel(white_ref, piece_ref, cos_ref, sin_ref, _, part_ref, done_ref, mixed_ref):
    done_ref[...] = jnp.zeros_like(done_ref)
    part_ref[...] = jnp.zeros_like(part_ref)
    add_products(part_ref, white_ref, piece_ref, cos_ref, sin_ref, mixed_ref)


def part_columns(rows):
    columns = v_row(rows) + HALF * rows
    return columns + (-columns) % 256


def part_terms(white, piece, tables, done):
    windows, channels, width = white.shape
    columns = part_columns(piece.shape[1])
    return pl.pallas_call(
        part_kernel,
        in_specs=[whole()] * 5,
        out_specs=[whole()] * 2,
        out_shape=[jax.ShapeDtypeStruct((channels, columns), jnp.float32), TOKEN],
        scratch_shapes=[pltpu.VMEM((columns, width), jnp.bfloat16)],
        compiler_params=kernel_params(),
        cost_estimate=COST,
        name="terms_part",
    )(white, piece, *tables, done)


TOKEN = jax.ShapeDtypeStruct((8, 128), jnp.float32)
COST = pl.CostEstimate(flops=30 * 10**9, bytes_accessed=0, transcendentals=0)


def pack(acc_ref, line, rows, scale, later):
    wide = HALF * rows
    vrow = v_row(rows)
    u, v = acc_ref[line, :wide] * scale, acc_ref[line, vrow:vrow + wide] * scale
    still = acc_ref[line, wide:wide + rows] * scale
    first, last = (u - v, u + v) if later else (u + v, u - v)
    return jnp.concatenate([first, last[:, :wide - rows], still], axis=1)


def terms_kernel(
    scale, part_ref, sibling_ref, piece_ref, cos_ref, sin_ref, _, back_ref, own_ref, *refs
):
    *done_refs, mixed_ref, acc_ref = refs
    for done_ref in done_refs:
        done_ref[...] = jnp.zeros_like(done_ref)
    acc_ref[...] = part_ref[...]
    add_products(acc_ref, sibling_ref, piece_ref, cos_ref, sin_ref, mixed_ref)
    line = pl.ds(SRC, acc_ref.shape[0] - SRC)
    back = pack(acc_ref, line, piece_ref.shape[1], scale, True)
    back_ref[...] = back.astype(back_ref.dtype)
    own_ref[...] = acc_ref[:SRC, :]


def own_kernel(scale, rows, first_ref, second_ref, *refs):
    *out_refs, packed_ref = refs
    x, core = place_of_core()
    mine = SRC // 4

    @pl.loop(0, SRC, step=mine)
    def _(start):
        line = pl.ds(pl.multiple_of(start, 8), mine)
        for quarter, ref in enumerate((first_ref, second_ref)):
            packed_ref[quarter, line, :] = pack(ref, line, rows, scale, False)

    for i, out_ref in enumerate(out_refs):
        spot = 2 * (x, 1 - x)[i // 2] + (core, 1 - core)[i % 2]
        line = pl.ds(pl.multiple_of(spot * mine, 8), mine)
        for quarter in range(2):
            out_ref[quarter] = packed_ref[quarter, line, :].astype(out_ref.dtype)


def own_terms(first, second, rows, scale):
    mine, wide = SRC // 4, 2 * HALF * rows
    return pl.pallas_call(
        functools.partial(own_kernel, scale, rows),
        in_specs=[whole()] * 2,
        out_specs=[whole()] * 4,
        out_shape=[
            jax.ShapeDtypeStruct((2, mine, wide), jnp.float32 if i == 0 else jnp.bfloat16)
            for i in range(4)
        ],
        scratch_shapes=[pltpu.VMEM((2, SRC, wide), jnp.float32)],
        compiler_params=kernel_params(),
        name="own_terms",
    )(first, second)


def terms(part, sibling, piece, tables, scale, done, last):
    windows, channels, width = sibling.shape
    rows = piece.shape[1]
    columns = part_columns(rows)
    back = ((channels - SRC, 2 * HALF * rows), jnp.float32 if last else jnp.bfloat16)
    out = [jax.ShapeDtypeStruct(*back), jax.ShapeDtypeStruct((SRC, columns), jnp.float32)]
    out += [] if last else [TOKEN]
    return pl.pallas_call(
        functools.partial(terms_kernel, scale),
        in_specs=[whole()] * 6,
        out_specs=[whole()] * len(out),
        out_shape=out,
        scratch_shapes=[
            pltpu.VMEM((columns, width), jnp.bfloat16),
            pltpu.VMEM((channels, columns), jnp.float32),
        ],
        compiler_params=kernel_params(),
        cost_estimate=COST,
        name="terms",
    )(part, sibling, piece, *tables, done)


def sum_kernel(here_ref, there_ref, out_ref):
    rows = out_ref.shape[0] // 4

    @pl.loop(0, out_ref.shape[0], step=rows)
    def _(start):
        line = pl.ds(pl.multiple_of(start, 8), rows)
        total = here_ref[line, :] + there_ref[line, :].astype(jnp.float32)
        out_ref[line, :] = total.astype(out_ref.dtype)


def sum_terms(here, there):
    return pl.pallas_call(
        sum_kernel,
        in_specs=[whole()] * 2,
        out_specs=whole(),
        out_shape=jax.ShapeDtypeStruct(there.shape, there.dtype),
        compiler_params=kernel_params(),
        name="sum_terms",
    )(here, there)


def copy_rows(source_ref, out_ref):
    rows = source_ref.shape[-2]
    if rows % 4:
        out_ref[...] = source_ref[...]
        return
    step = rows // 4 if rows % 64 == 0 else rows

    @pl.loop(0, rows, step=step)
    def _(start):
        line = pl.ds(pl.multiple_of(start, 16 if step % 16 == 0 else 8), step)
        out_ref[..., line, :] = source_ref[..., line, :]


def keep_kernel(*refs):
    half = len(refs) // 2
    for source_ref, out_ref in zip(refs[:half], refs[half:]):
        copy_rows(source_ref, out_ref)


def hold_kernel(source_ref, *refs):
    *_, out_ref, done_ref = refs
    copy_rows(source_ref, out_ref)
    done_ref[...] = jnp.zeros_like(done_ref)


def keep(*values):
    return pl.pallas_call(
        keep_kernel,
        in_specs=[whole()] * len(values),
        out_specs=[whole()] * len(values),
        out_shape=[jax.ShapeDtypeStruct(v.shape, v.dtype) for v in values],
        compiler_params=kernel_params(),
        name="keep",
    )(*values)


def hold(value, *done):
    return pl.pallas_call(
        hold_kernel,
        in_specs=[whole()] * (1 + len(done)),
        out_specs=[whole()] * 2,
        out_shape=[jax.ShapeDtypeStruct(value.shape, value.dtype), TOKEN],
        compiler_params=kernel_params(),
        name="hold",
    )(value, *done)


def place_kernel(
    here_ref, core_ref, chip_ref, cross_ref, back_ref, out_ref, block_ref, sems
):
    x, core = place_of_core()
    lags, mine, channels = block_ref.shape
    swap = core != 0
    sides = []
    for q in range(2):
        index = jnp.where(x == q, 1, 0)
        own = here_ref[index] + chip_ref[1 - index].astype(jnp.float32)
        other = core_ref[index].astype(jnp.float32) + cross_ref[1 - index].astype(jnp.float32)
        sides += [jnp.where(swap, other, own), jnp.where(swap, own, other)]
    back = back_ref[...].astype(jnp.float32).T
    copies = []
    for j in range(lags):
        lag = HALF - 1 - j if j < HALF else j + 1 if j < lags - 1 else HALF
        cols = slice(j * mine, (j + 1) * mine)
        block_ref[lag, :, :SRC] = jnp.concatenate([v[:, cols] for v in sides], axis=1)
        block_ref[lag, :, SRC:] = back[cols]
        copies.append(pltpu.make_async_copy(block_ref.at[lag], out_ref.at[lag], sems.at[lag]))
        copies[-1].start()
    for copy in copies:
        copy.wait()


def place(here, core, chip, cross, back):
    _, mine, wide = here.shape
    shape = (wide // mine, mine, SRC + back.shape[0])
    return pl.pallas_call(
        place_kernel,
        in_specs=[whole()] * 5,
        out_specs=anywhere(),
        out_shape=jax.ShapeDtypeStruct(shape, jnp.float32),
        scratch_shapes=[
            pltpu.VMEM(shape, jnp.float32), pltpu.SemaphoreType.DMA((shape[0],))
        ],
        compiler_params=kernel_params(),
        name="place_lags",
    )(here, core, chip, cross, back)


def pair_body(spectra, counts, partner):
    blocks = lax.axis_size("chan")
    groups = lax.axis_size("win")
    windows, channels, two, freqs = spectra.shape
    scale = 1.0 / (math.sqrt(2.0 * freqs) * math.sqrt(windows * groups))
    other_core = [(i, i ^ 1) for i in range(groups)]
    other_chip = [(i, i ^ 2) for i in range(groups)]
    other_both = [(i, i ^ 3) for i in range(groups)]

    def to_partner(t):
        return [(i, i ^ t) for i in range(blocks)]

    def to_partner_core(t):
        return [
            (i * groups + g, (i ^ t) * groups + (g ^ 1))
            for i in range(blocks)
            for g in range(groups)
        ]

    def one_round(t, counts, raw, sources, near, far, near_more, far_more):
        def straight(value):
            return lax.ppermute(value, "chan", to_partner(t))

        def crossed(value):
            return lax.ppermute(value, ("chan", "win"), to_partner_core(t))

        near, far = straight(near), crossed(far)
        white = whiten_rest(counts, raw, taper, sources)
        sibling = lax.ppermute(white, "win", other_core)
        near_more, done = hold(near_more, near)
        near_more = straight(near_more)
        part, done = part_terms(white, near, tables, done)
        far_more, done = hold(far_more, far, done)
        far_more = crossed(far_more)
        there, first, done = terms(part, sibling, far, tables, scale, done, False)
        there = lax.ppermute(there, "win", other_chip)
        part, done = part_terms(white, near_more, tables, done)
        here, second = terms(part, sibling, far_more, tables, scale, done, True)
        back = lax.ppermute(sum_terms(here, there), "chan", to_partner(t))
        here, core, chip, cross = own_terms(first, second, SRC // groups, scale)
        core = lax.ppermute(core, "win", other_core)
        chip = lax.ppermute(chip, "win", other_chip)
        cross = lax.ppermute(cross, "win", other_both)
        return here, *keep(core, chip, cross, back)

    def by_round(run, *values):
        branches = [functools.partial(run, t) for t in range(1, blocks)]
        return lax.switch(partner[0, 0] - 1, branches, *values)

    tables = [jnp.asarray(v) for v in shift_tables(freqs)]
    taper = taper_row(two, freqs)
    piece = jax.ShapeDtypeStruct((windows, SRC // 4, two * freqs), jnp.bfloat16)
    sources = jax.ShapeDtypeStruct((windows, SRC, two * freqs), jnp.bfloat16)
    raw = pltpu.with_memory_space_constraint(spectra, pltpu.HBM)
    sources = whiten_sources([sources] + [piece] * 4, counts, fetch_sources(raw), taper)
    return place(*by_round(one_round, counts, raw, *sources))[None, None]


def lag_table(freqs, lags):
    freq = jnp.arange(freqs, dtype=jnp.float32) + freqs // 4
    delay = jnp.arange(lags, dtype=jnp.float32) - lags // 2
    phase = 2.0 * math.pi * freq[:, None] * delay[None, :] / (4.0 * freqs)
    norm = 1.0 / math.sqrt(2.0 * freqs)
    return jnp.stack([jnp.cos(phase), -jnp.sin(phase)]) * norm


def blended_sources(sources, table):
    src = sources.astype(jnp.float32)
    first = src[:, :, 0][:, :, None, :]
    second = src[:, :, 1][:, :, None, :]
    cos_part = table[0].T[None, None]
    sin_part = table[1].T[None, None]
    real_mix = first * cos_part + second * sin_part
    imag_mix = second * cos_part - first * sin_part
    return jnp.stack([real_mix, imag_mix], axis=3).astype(jnp.bfloat16)


def pair_terms(sources, receiver_blocks, table):
    wins, count, two, freqs = sources.shape
    lags = table.shape[2]
    group = math.gcd(count, 32)
    flat_recv = receiver_blocks.reshape(wins, receiver_blocks.shape[1], two * freqs)
    grouped = jnp.moveaxis(sources.reshape(wins, count // group, group, two, freqs), 1, 0)

    def one_group(piece):
        mixed_spectra = blended_sources(piece, table).reshape(wins, group * lags, two * freqs)
        out = jnp.einsum(
            "wmx,wrx->mr", mixed_spectra, flat_recv, preferred_element_type=jnp.float32
        )
        return out.reshape(group, lags, receiver_blocks.shape[1])

    out = lax.map(one_group, grouped).reshape(count, lags, receiver_blocks.shape[1])
    return jnp.transpose(out, (1, 0, 2))


def route_blocks(values, round_flags, levels):
    for level in range(levels):
        moved = from_partner(values, "chan", level)
        values = jnp.where((round_flags >> level) % 2 == 1, moved, values)
    return values


def general_body(spectra, counts, partner):
    white = whiten_local(spectra, counts[0])
    table = lag_table(spectra.shape[3], LAGS)
    levels = lax.axis_size("chan").bit_length() - 1
    windows = spectra.shape[0] * lax.axis_size("win")
    receiver_blocks = route_blocks(white, partner[0, 0], levels)
    out = pair_terms(white[:, :SRC], receiver_blocks, table)
    stacked = lax.psum_scatter(out, "win", scatter_dimension=1, tiled=True)
    return (stacked / math.sqrt(windows))[None, None]


def solution(mesh):
    body = pair_body if mesh.shape["win"] == 4 else general_body
    return jax.shard_map(
        body,
        mesh=mesh,
        in_specs=(P("win", "chan", None, None), P("chan"), P()),
        out_specs=P("chan", None, None, "win", None),
        check_vma=False,
    )
```

```python
import functools
import math

import jax
import jax.numpy as jnp
import numpy as np
from jax import lax
from jax.experimental import pallas as pl
from jax.experimental.pallas import tpu as pltpu
from jax.sharding import PartitionSpec as P

LAGS = 16
SRC = 160
HALF = LAGS // 2
VMEM_LIMIT = 16 * 1024 * 1024


def from_partner(value, axis, stride):
    return lax.ppermute(value, axis, [(i, i ^ 1 << stride) for i in range(lax.axis_size(axis))])


def whiten_local(spectra, count):
    values = spectra.astype(jnp.float32)
    block_size = spectra.shape[1]
    freqs = spectra.shape[3]
    valid = (jnp.arange(block_size, dtype=jnp.int32) < count).astype(jnp.float32)
    freq = jnp.arange(freqs, dtype=jnp.float32)
    taper = 0.75 - 0.25 * jnp.cos(2.0 * math.pi * (freq + 0.5) / freqs)
    power = jnp.mean(values * values, axis=(2, 3))
    scale = valid[None, :] / jnp.sqrt(power + 1e-05)
    return (values * taper * scale[:, :, None, None]).astype(jnp.bfloat16)


def shift_tables(freqs):
    freq = np.arange(freqs, dtype=np.float64) + freqs // 4
    shift = np.arange(1, HALF + 1, dtype=np.float64)
    phase = 2.0 * np.pi * shift[:, None] * freq[None, :] / (4.0 * freqs)
    return np.cos(phase).astype(np.float32), np.sin(phase).astype(np.float32)


def place_of_core():
    spot = lax.axis_index("win")
    return spot // 2, spot % 2


def whole():
    return pl.BlockSpec(memory_space=pltpu.VMEM)


def anywhere():
    return pl.BlockSpec(memory_space=pl.ANY)


def kernel_params():
    return pltpu.CompilerParams(vmem_limit_bytes=VMEM_LIMIT)


def fetch_kernel(source_ref, out_ref, sems):
    windows, channels = out_ref.shape[:2]
    parts = sems.shape[1]
    step = channels // parts
    copies = []
    for w in range(windows):
        for i in range(parts):
            part = (w, pl.ds(i * step, step))
            copies.append(
                pltpu.make_async_copy(source_ref.at[part], out_ref.at[part], sems.at[w, i])
            )
            copies[-1].start()
    for copy in copies:
        copy.wait()


def fetch_sources(spectra):
    windows, _, *rest = spectra.shape
    return pl.pallas_call(
        fetch_kernel,
        in_specs=[pl.BlockSpec(memory_space=pltpu.HBM)],
        out_specs=whole(),
        out_shape=jax.ShapeDtypeStruct((windows, SRC, *rest), spectra.dtype),
        scratch_shapes=[pltpu.SemaphoreType.DMA((windows, 4))],
        compiler_params=kernel_params(),
        name="fetch",
    )(spectra)


def white_block(raw_ref, taper_ref, count, w, line, first_row):
    values = raw_ref[w, line, :].astype(jnp.float32)
    rows, width = values.shape
    power = jnp.sum(values * values, axis=1, keepdims=True) * (1.0 / width)
    row = first_row + lax.broadcasted_iota(jnp.int32, (rows, 1), 0)
    valid = (row < count).astype(jnp.float32)
    scale = valid / jnp.sqrt(power + 1e-05)
    return values * taper_ref[...] * scale


def whiten_kernel(count_ref, raw_ref, taper_ref, white_ref, *refs):
    *piece_refs, count, sem = refs
    copy = pltpu.make_async_copy(count_ref, count, sem)
    copy.start()
    x, core = place_of_core()
    mine = SRC // 4
    step = 2 * mine
    copy.wait()
    for w in range(raw_ref.shape[0]):
        for index, group in enumerate((1 - x, x)):
            line = pl.ds(pl.multiple_of(group * step, step), step)
            values = white_block(raw_ref, taper_ref, count[0], w, line, group * step)
            white_ref[w, line, :] = values.astype(jnp.bfloat16)
            low, high = values[:mine], values[mine:]
            first = core == 0
            near_ref, far_ref = piece_refs[2 * index:2 * index + 2]
            near_ref[w] = jnp.where(first, low, high).astype(jnp.bfloat16)
            far_ref[w] = jnp.where(first, high, low).astype(jnp.bfloat16)


def rest_kernel(
    count_ref, spectra_ref, taper_ref, sources_ref, white_ref, raw_ref, count, sems
):
    windows, channels, two, freqs = raw_ref.shape
    copies = [pltpu.make_async_copy(count_ref, count, sems.at[windows])]
    for w in range(windows):
        part = spectra_ref.at[w, pl.ds(SRC, channels)]
        copies.append(pltpu.make_async_copy(part, raw_ref.at[w], sems.at[w]))
    for copy in copies:
        copy.start()
    step = 32

    @pl.loop(0, windows)
    def _(w):
        @pl.loop(0, SRC, step=step)
        def _(start):
            line = pl.ds(pl.multiple_of(start, step), step)
            white_ref[w, line, :] = sources_ref[w, line, :]

    for copy in copies:
        copy.wait()

    @pl.loop(0, windows)
    def _(w):
        @pl.loop(0, channels, step=step)
        def _(start):
            line = pl.ds(pl.multiple_of(start, step), step)
            parts = [raw_ref[w, line, p, :].astype(jnp.float32) for p in range(two)]
            power = sum(jnp.sum(v * v, axis=1, keepdims=True) for v in parts)
            row = SRC + start + lax.broadcasted_iota(jnp.int32, (step, 1), 0)
            valid = (row < count[0]).astype(jnp.float32)
            scale = valid / jnp.sqrt(power * (1.0 / (two * freqs)) + 1e-05)
            out = pl.ds(pl.multiple_of(SRC + start, step), step)
            for p, v in enumerate(parts):
                cols = slice(p * freqs, (p + 1) * freqs)
                white_ref[w, out, cols] = (v * taper_ref[:, cols] * scale).astype(jnp.bfloat16)


def whiten_rest(counts, spectra, taper, sources):
    windows, channels, two, freqs = spectra.shape
    return pl.pallas_call(
        rest_kernel,
        in_specs=[anywhere(), pl.BlockSpec(memory_space=pltpu.HBM), whole(), whole()],
        out_specs=whole(),
        out_shape=jax.ShapeDtypeStruct((windows, channels, two * freqs), jnp.bfloat16),
        scratch_shapes=[
            pltpu.VMEM((windows, channels - SRC, two, freqs), spectra.dtype),
            pltpu.SMEM((1,), jnp.int32),
            pltpu.SemaphoreType.DMA((windows + 1,)),
        ],
        compiler_params=kernel_params(),
        name="whiten_rest",
    )(counts, spectra, taper, sources)


def whiten_sources(out_shape, counts, raw, taper):
    windows, channels, two, freqs = raw.shape
    return pl.pallas_call(
        whiten_kernel,
        in_specs=[anywhere()] + [whole()] * 2,
        out_specs=[whole()] * len(out_shape),
        out_shape=out_shape,
        scratch_shapes=[pltpu.SMEM((1,), jnp.int32), pltpu.SemaphoreType.DMA],
        compiler_params=kernel_params(),
        name="whiten",
    )(counts, raw.reshape(windows, channels, two * freqs), taper)


def taper_row(two, freqs):
    freq = np.arange(freqs, dtype=np.float64)
    taper = 0.75 - 0.25 * np.cos(2.0 * np.pi * (freq + 0.5) / freqs)
    return jnp.asarray(np.tile(taper.astype(np.float32), two)[None, :])


def mix(m_ref, piece, cos_ref, sin_ref, low, high):
    rows = piece.shape[0]
    vrow = v_row(rows)
    real = piece[:, low].astype(jnp.float32)
    imag = piece[:, high].astype(jnp.float32)

    def put(where, cols, values):
        m_ref[where, cols] = jnp.concatenate(values, axis=0).astype(jnp.bfloat16)

    for m in range(0, HALF, 2):
        c = [cos_ref[m + i:m + i + 1, low] for i in range(2)]
        s = [sin_ref[m + i:m + i + 1, low] for i in range(2)]
        line = slice(m * rows, (m + 2) * rows)
        vline = slice(vrow + m * rows, vrow + (m + 2) * rows)
        put(line, low, [real * v for v in c])
        put(line, high, [imag * v for v in c])
        put(vline, low, [imag * -v for v in s])
        put(vline, high, [real * v for v in s])
    fill = jnp.zeros((vrow - (HALF + 1) * rows, 128), jnp.float32)
    for value, cols in ((real, low), (imag, high)):
        put(slice(HALF * rows, vrow), cols, [value, fill])


def v_row(rows):
    return -(-(HALF + 1) * rows // 128) * 128


def times(lhs, rhs):
    return lax.dot_general(
        lhs, rhs, (((1,), (1,)), ((), ())), preferred_element_type=jnp.float32
    )


def add_products(acc_ref, lhs_ref, piece_ref, cos_ref, sin_ref, mixed_ref):
    windows, rows, width = piece_ref.shape
    tile = 256
    used = v_row(rows) + HALF * rows
    if used < mixed_ref.shape[0]:
        mixed_ref[used:, :] = jnp.zeros_like(mixed_ref[used:, :])

    @pl.loop(0, windows)
    def _(w):
        @pl.loop(0, width // 2, step=128)
        def _(start):
            low = pl.ds(pl.multiple_of(start, 128), 128)
            high = pl.ds(pl.multiple_of(width // 2 + start, 128), 128)
            mix(mixed_ref, piece_ref.at[w], cos_ref, sin_ref, low, high)

        @pl.loop(0, mixed_ref.shape[0], step=tile)
        def _(n):
            cols = pl.ds(pl.multiple_of(n, tile), tile)
            acc_ref[:, cols] += times(lhs_ref[w], mixed_ref[cols, :])


def part_kernel(white_ref, piece_ref, cos_ref, sin_ref, _, part_ref, done_ref, mixed_ref):
    done_ref[...] = jnp.zeros_like(done_ref)
    part_ref[...] = jnp.zeros_like(part_ref)
    add_products(part_ref, white_ref, piece_ref, cos_ref, sin_ref, mixed_ref)


def part_columns(rows):
    columns = v_row(rows) + HALF * rows
    return columns + (-columns) % 256


def part_terms(white, piece, tables, done):
    windows, channels, width = white.shape
    columns = part_columns(piece.shape[1])
    return pl.pallas_call(
        part_kernel,
        in_specs=[whole()] * 5,
        out_specs=[whole()] * 2,
        out_shape=[jax.ShapeDtypeStruct((channels, columns), jnp.float32), TOKEN],
        scratch_shapes=[pltpu.VMEM((columns, width), jnp.bfloat16)],
        compiler_params=kernel_params(),
        cost_estimate=COST,
        name="terms_part",
    )(white, piece, *tables, done)


TOKEN = jax.ShapeDtypeStruct((8, 128), jnp.float32)
COST = pl.CostEstimate(flops=30 * 10**9, bytes_accessed=0, transcendentals=0)


def pack(acc_ref, line, rows, scale, later):
    wide = HALF * rows
    vrow = v_row(rows)
    u, v = acc_ref[line, :wide] * scale, acc_ref[line, vrow:vrow + wide] * scale
    still = acc_ref[line, wide:wide + rows] * scale
    first, last = (u - v, u + v) if later else (u + v, u - v)
    return jnp.concatenate([first, last[:, :wide - rows], still], axis=1)


def terms_kernel(
    scale, part_ref, sibling_ref, piece_ref, cos_ref, sin_ref, _, back_ref, own_ref, *refs
):
    *done_refs, mixed_ref, acc_ref = refs
    for done_ref in done_refs:
        done_ref[...] = jnp.zeros_like(done_ref)
    acc_ref[...] = part_ref[...]
    add_products(acc_ref, sibling_ref, piece_ref, cos_ref, sin_ref, mixed_ref)
    line = pl.ds(SRC, acc_ref.shape[0] - SRC)
    back = pack(acc_ref, line, piece_ref.shape[1], scale, True)
    back_ref[...] = back.astype(back_ref.dtype)
    own_ref[...] = acc_ref[:SRC, :]


def own_kernel(scale, rows, first_ref, second_ref, *refs):
    *out_refs, packed_ref = refs
    x, core = place_of_core()
    mine = SRC // 4

    @pl.loop(0, SRC, step=mine)
    def _(start):
        line = pl.ds(pl.multiple_of(start, 8), mine)
        for quarter, ref in enumerate((first_ref, second_ref)):
            packed_ref[quarter, line, :] = pack(ref, line, rows, scale, False)

    for i, out_ref in enumerate(out_refs):
        spot = 2 * (x, 1 - x)[i // 2] + (core, 1 - core)[i % 2]
        line = pl.ds(pl.multiple_of(spot * mine, 8), mine)
        for quarter in range(2):
            out_ref[quarter] = packed_ref[quarter, line, :].astype(out_ref.dtype)


def own_terms(first, second, rows, scale):
    mine, wide = SRC // 4, 2 * HALF * rows
    return pl.pallas_call(
        functools.partial(own_kernel, scale, rows),
        in_specs=[whole()] * 2,
        out_specs=[whole()] * 4,
        out_shape=[
            jax.ShapeDtypeStruct((2, mine, wide), jnp.float32 if i == 0 else jnp.bfloat16)
            for i in range(4)
        ],
        scratch_shapes=[pltpu.VMEM((2, SRC, wide), jnp.float32)],
        compiler_params=kernel_params(),
        name="own_terms",
    )(first, second)


def terms(part, sibling, piece, tables, scale, done, last):
    windows, channels, width = sibling.shape
    rows = piece.shape[1]
    columns = part_columns(rows)
    back = ((channels - SRC, 2 * HALF * rows), jnp.float32 if last else jnp.bfloat16)
    out = [jax.ShapeDtypeStruct(*back), jax.ShapeDtypeStruct((SRC, columns), jnp.float32)]
    out += [] if last else [TOKEN]
    return pl.pallas_call(
        functools.partial(terms_kernel, scale),
        in_specs=[whole()] * 6,
        out_specs=[whole()] * len(out),
        out_shape=out,
        scratch_shapes=[
            pltpu.VMEM((columns, width), jnp.bfloat16),
            pltpu.VMEM((channels, columns), jnp.float32),
        ],
        compiler_params=kernel_params(),
        cost_estimate=COST,
        name="terms",
    )(part, sibling, piece, *tables, done)


def sum_kernel(here_ref, there_ref, out_ref):
    rows = out_ref.shape[0] // 4

    @pl.loop(0, out_ref.shape[0], step=rows)
    def _(start):
        line = pl.ds(pl.multiple_of(start, 8), rows)
        total = here_ref[line, :] + there_ref[line, :].astype(jnp.float32)
        out_ref[line, :] = total.astype(out_ref.dtype)


def sum_terms(here, there):
    return pl.pallas_call(
        sum_kernel,
        in_specs=[whole()] * 2,
        out_specs=whole(),
        out_shape=jax.ShapeDtypeStruct(there.shape, there.dtype),
        compiler_params=kernel_params(),
        name="sum_terms",
    )(here, there)


def copy_rows(source_ref, out_ref):
    rows = source_ref.shape[-2]
    if rows % 4:
        out_ref[...] = source_ref[...]
        return
    step = rows // 4 if rows % 64 == 0 else rows

    @pl.loop(0, rows, step=step)
    def _(start):
        line = pl.ds(pl.multiple_of(start, 16 if step % 16 == 0 else 8), step)
        out_ref[..., line, :] = source_ref[..., line, :]


def keep_kernel(*refs):
    half = len(refs) // 2
    for source_ref, out_ref in zip(refs[:half], refs[half:]):
        copy_rows(source_ref, out_ref)


def hold_kernel(source_ref, *refs):
    *_, out_ref, done_ref = refs
    copy_rows(source_ref, out_ref)
    done_ref[...] = jnp.zeros_like(done_ref)


def keep(*values):
    return pl.pallas_call(
        keep_kernel,
        in_specs=[whole()] * len(values),
        out_specs=[whole()] * len(values),
        out_shape=[jax.ShapeDtypeStruct(v.shape, v.dtype) for v in values],
        compiler_params=kernel_params(),
        name="keep",
    )(*values)


def hold(value, *done):
    return pl.pallas_call(
        hold_kernel,
        in_specs=[whole()] * (1 + len(done)),
        out_specs=[whole()] * 2,
        out_shape=[jax.ShapeDtypeStruct(value.shape, value.dtype), TOKEN],
        compiler_params=kernel_params(),
        name="hold",
    )(value, *done)


def place_kernel(
    here_ref, core_ref, chip_ref, cross_ref, back_ref, out_ref, block_ref, sems
):
    x, core = place_of_core()
    lags, mine, channels = block_ref.shape
    swap = core != 0
    sides = []
    for q in range(2):
        index = jnp.where(x == q, 1, 0)
        own = here_ref[index] + chip_ref[1 - index].astype(jnp.float32)
        other = core_ref[index].astype(jnp.float32) + cross_ref[1 - index].astype(jnp.float32)
        sides += [jnp.where(swap, other, own), jnp.where(swap, own, other)]
    back = back_ref[...].astype(jnp.float32).T
    copies = []
    for j in range(lags):
        lag = HALF - 1 - j if j < HALF else j + 1 if j < lags - 1 else HALF
        cols = slice(j * mine, (j + 1) * mine)
        block_ref[lag, :, :SRC] = jnp.concatenate([v[:, cols] for v in sides], axis=1)
        block_ref[lag, :, SRC:] = back[cols]
        copies.append(pltpu.make_async_copy(block_ref.at[lag], out_ref.at[lag], sems.at[lag]))
        copies[-1].start()
    for copy in copies:
        copy.wait()


def place(here, core, chip, cross, back):
    _, mine, wide = here.shape
    shape = (wide // mine, mine, SRC + back.shape[0])
    return pl.pallas_call(
        place_kernel,
        in_specs=[whole()] * 5,
        out_specs=anywhere(),
        out_shape=jax.ShapeDtypeStruct(shape, jnp.float32),
        scratch_shapes=[
            pltpu.VMEM(shape, jnp.float32), pltpu.SemaphoreType.DMA((shape[0],))
        ],
        compiler_params=kernel_params(),
        name="place_lags",
    )(here, core, chip, cross, back)


def pair_body(spectra, counts, partner):
    blocks = lax.axis_size("chan")
    groups = lax.axis_size("win")
    windows, channels, two, freqs = spectra.shape
    scale = 1.0 / (math.sqrt(2.0 * freqs) * math.sqrt(windows * groups))
    other_core = [(i, i ^ 1) for i in range(groups)]
    other_chip = [(i, i ^ 2) for i in range(groups)]
    other_both = [(i, i ^ 3) for i in range(groups)]

    def to_partner(t):
        return [(i, i ^ t) for i in range(blocks)]

    def to_partner_core(t):
        return [
            (i * groups + g, (i ^ t) * groups + (g ^ 1))
            for i in range(blocks)
            for g in range(groups)
        ]

    def one_round(t, counts, raw, sources, near, far, near_more, far_more):
        def straight(value):
            return lax.ppermute(value, "chan", to_partner(t))

        def crossed(value):
            return lax.ppermute(value, ("chan", "win"), to_partner_core(t))

        near, far = straight(near), crossed(far)
        white = whiten_rest(counts, raw, taper, sources)
        sibling = lax.ppermute(white, "win", other_core)
        if t < blocks // 2:
            near_more, done = hold(near_more, near)
            near_more = straight(near_more)
        else:
            near_more, done = hold(near_more, white)
            far_more, done = hold(far_more, done)
            near_more, far_more = straight(near_more), crossed(far_more)
        part, done = part_terms(white, near, tables, done)
        if t < blocks // 2:
            far_more, done = hold(far_more, far, done)
            far_more = crossed(far_more)
        there, first, done = terms(part, sibling, far, tables, scale, done, False)
        there = lax.ppermute(there, "win", other_chip)
        if t < blocks // 2:
            part, done = part_terms(white, near_more, tables, done)
            here, second = terms(part, sibling, far_more, tables, scale, done, True)
        else:
            part, done = part_terms(sibling, far_more, tables, done)
            here, second = terms(part, white, near_more, tables, scale, done, True)
        back = lax.ppermute(sum_terms(here, there), "chan", to_partner(t))
        here, core, chip, cross = own_terms(first, second, SRC // groups, scale)
        core = lax.ppermute(core, "win", other_core)
        chip = lax.ppermute(chip, "win", other_chip)
        cross = lax.ppermute(cross, "win", other_both)
        return here, *keep(core, chip, cross, back)

    def by_round(run, *values):
        branches = [functools.partial(run, t) for t in range(1, blocks)]
        return lax.switch(partner[0, 0] - 1, branches, *values)

    tables = [jnp.asarray(v) for v in shift_tables(freqs)]
    taper = taper_row(two, freqs)
    piece = jax.ShapeDtypeStruct((windows, SRC // 4, two * freqs), jnp.bfloat16)
    sources = jax.ShapeDtypeStruct((windows, SRC, two * freqs), jnp.bfloat16)
    raw = pltpu.with_memory_space_constraint(spectra, pltpu.HBM)
    sources = whiten_sources([sources] + [piece] * 4, counts, fetch_sources(raw), taper)
    return place(*by_round(one_round, counts, raw, *sources))[None, None]


def lag_table(freqs, lags):
    freq = jnp.arange(freqs, dtype=jnp.float32) + freqs // 4
    delay = jnp.arange(lags, dtype=jnp.float32) - lags // 2
    phase = 2.0 * math.pi * freq[:, None] * delay[None, :] / (4.0 * freqs)
    norm = 1.0 / math.sqrt(2.0 * freqs)
    return jnp.stack([jnp.cos(phase), -jnp.sin(phase)]) * norm


def blended_sources(sources, table):
    src = sources.astype(jnp.float32)
    first = src[:, :, 0][:, :, None, :]
    second = src[:, :, 1][:, :, None, :]
    cos_part = table[0].T[None, None]
    sin_part = table[1].T[None, None]
    real_mix = first * cos_part + second * sin_part
    imag_mix = second * cos_part - first * sin_part
    return jnp.stack([real_mix, imag_mix], axis=3).astype(jnp.bfloat16)


def pair_terms(sources, receiver_blocks, table):
    wins, count, two, freqs = sources.shape
    lags = table.shape[2]
    group = math.gcd(count, 32)
    flat_recv = receiver_blocks.reshape(wins, receiver_blocks.shape[1], two * freqs)
    grouped = jnp.moveaxis(sources.reshape(wins, count // group, group, two, freqs), 1, 0)

    def one_group(piece):
        mixed_spectra = blended_sources(piece, table).reshape(wins, group * lags, two * freqs)
        out = jnp.einsum(
            "wmx,wrx->mr", mixed_spectra, flat_recv, preferred_element_type=jnp.float32
        )
        return out.reshape(group, lags, receiver_blocks.shape[1])

    out = lax.map(one_group, grouped).reshape(count, lags, receiver_blocks.shape[1])
    return jnp.transpose(out, (1, 0, 2))


def route_blocks(values, round_flags, levels):
    for level in range(levels):
        moved = from_partner(values, "chan", level)
        values = jnp.where((round_flags >> level) % 2 == 1, moved, values)
    return values


def general_body(spectra, counts, partner):
    white = whiten_local(spectra, counts[0])
    table = lag_table(spectra.shape[3], LAGS)
    levels = lax.axis_size("chan").bit_length() - 1
    windows = spectra.shape[0] * lax.axis_size("win")
    receiver_blocks = route_blocks(white, partner[0, 0], levels)
    out = pair_terms(white[:, :SRC], receiver_blocks, table)
    stacked = lax.psum_scatter(out, "win", scatter_dimension=1, tiled=True)
    return (stacked / math.sqrt(windows))[None, None]


def solution(mesh):
    body = pair_body if mesh.shape["win"] == 4 else general_body
    return jax.shard_map(
        body,
        mesh=mesh,
        in_specs=(P("win", "chan", None, None), P("chan"), P()),
        out_specs=P("chan", None, None, "win", None),
        check_vma=False,
    )
```

```python
import functools
import math

import jax
import jax.numpy as jnp
import numpy as np
from jax import lax
from jax.experimental import pallas as pl
from jax.experimental.pallas import tpu as pltpu
from jax.sharding import PartitionSpec as P

LAGS = 16
SRC = 160
HALF = LAGS // 2
VMEM_LIMIT = 16 * 1024 * 1024


def from_partner(value, axis, stride):
    return lax.ppermute(value, axis, [(i, i ^ 1 << stride) for i in range(lax.axis_size(axis))])


def whiten_local(spectra, count):
    values = spectra.astype(jnp.float32)
    block_size = spectra.shape[1]
    freqs = spectra.shape[3]
    valid = (jnp.arange(block_size, dtype=jnp.int32) < count).astype(jnp.float32)
    freq = jnp.arange(freqs, dtype=jnp.float32)
    taper = 0.75 - 0.25 * jnp.cos(2.0 * math.pi * (freq + 0.5) / freqs)
    power = jnp.mean(values * values, axis=(2, 3))
    scale = valid[None, :] / jnp.sqrt(power + 1e-05)
    return (values * taper * scale[:, :, None, None]).astype(jnp.bfloat16)


def shift_tables(freqs):
    freq = np.arange(freqs, dtype=np.float64) + freqs // 4
    shift = np.arange(1, HALF + 1, dtype=np.float64)
    phase = 2.0 * np.pi * shift[:, None] * freq[None, :] / (4.0 * freqs)
    return np.cos(phase).astype(np.float32), np.sin(phase).astype(np.float32)


def place_of_core():
    spot = lax.axis_index("win")
    return spot // 2, spot % 2


def whole():
    return pl.BlockSpec(memory_space=pltpu.VMEM)


def anywhere():
    return pl.BlockSpec(memory_space=pl.ANY)


def kernel_params():
    return pltpu.CompilerParams(vmem_limit_bytes=VMEM_LIMIT)


def fetch_kernel(source_ref, out_ref, sems):
    windows, channels = out_ref.shape[:2]
    parts = sems.shape[1]
    step = channels // parts
    copies = []
    for w in range(windows):
        for i in range(parts):
            part = (w, pl.ds(i * step, step))
            copies.append(
                pltpu.make_async_copy(source_ref.at[part], out_ref.at[part], sems.at[w, i])
            )
            copies[-1].start()
    for copy in copies:
        copy.wait()


def fetch_sources(spectra):
    windows, _, *rest = spectra.shape
    return pl.pallas_call(
        fetch_kernel,
        in_specs=[pl.BlockSpec(memory_space=pltpu.HBM)],
        out_specs=whole(),
        out_shape=jax.ShapeDtypeStruct((windows, SRC, *rest), spectra.dtype),
        scratch_shapes=[pltpu.SemaphoreType.DMA((windows, 4))],
        compiler_params=kernel_params(),
        name="fetch",
    )(spectra)


def white_block(raw_ref, taper_ref, count, w, line, first_row):
    values = raw_ref[w, line, :].astype(jnp.float32)
    rows, width = values.shape
    power = jnp.sum(values * values, axis=1, keepdims=True) * (1.0 / width)
    row = first_row + lax.broadcasted_iota(jnp.int32, (rows, 1), 0)
    valid = (row < count).astype(jnp.float32)
    scale = valid / jnp.sqrt(power + 1e-05)
    return values * taper_ref[...] * scale


def whiten_kernel(count_ref, raw_ref, taper_ref, white_ref, *refs):
    *piece_refs, count, sem = refs
    copy = pltpu.make_async_copy(count_ref, count, sem)
    copy.start()
    x, core = place_of_core()
    mine = SRC // 4
    step = 2 * mine
    copy.wait()
    for w in range(raw_ref.shape[0]):
        for index, group in enumerate((1 - x, x)):
            line = pl.ds(pl.multiple_of(group * step, step), step)
            values = white_block(raw_ref, taper_ref, count[0], w, line, group * step)
            white_ref[w, line, :] = values.astype(jnp.bfloat16)
            low, high = values[:mine], values[mine:]
            first = core == 0
            near_ref, far_ref = piece_refs[2 * index:2 * index + 2]
            near_ref[w] = jnp.where(first, low, high).astype(jnp.bfloat16)
            far_ref[w] = jnp.where(first, high, low).astype(jnp.bfloat16)


def rest_kernel(
    count_ref, spectra_ref, taper_ref, sources_ref, white_ref, raw_ref, count, sems
):
    windows, channels, two, freqs = raw_ref.shape
    copies = [pltpu.make_async_copy(count_ref, count, sems.at[windows])]
    for w in range(windows):
        part = spectra_ref.at[w, pl.ds(SRC, channels)]
        copies.append(pltpu.make_async_copy(part, raw_ref.at[w], sems.at[w]))
    for copy in copies:
        copy.start()
    step = 32

    @pl.loop(0, windows)
    def _(w):
        @pl.loop(0, SRC, step=step)
        def _(start):
            line = pl.ds(pl.multiple_of(start, step), step)
            white_ref[w, line, :] = sources_ref[w, line, :]

    for copy in copies:
        copy.wait()

    @pl.loop(0, windows)
    def _(w):
        @pl.loop(0, channels, step=step)
        def _(start):
            line = pl.ds(pl.multiple_of(start, step), step)
            parts = [raw_ref[w, line, p, :].astype(jnp.float32) for p in range(two)]
            power = sum(jnp.sum(v * v, axis=1, keepdims=True) for v in parts)
            row = SRC + start + lax.broadcasted_iota(jnp.int32, (step, 1), 0)
            valid = (row < count[0]).astype(jnp.float32)
            scale = valid / jnp.sqrt(power * (1.0 / (two * freqs)) + 1e-05)
            out = pl.ds(pl.multiple_of(SRC + start, step), step)
            for p, v in enumerate(parts):
                cols = slice(p * freqs, (p + 1) * freqs)
                white_ref[w, out, cols] = (v * taper_ref[:, cols] * scale).astype(jnp.bfloat16)


def whiten_rest(counts, spectra, taper, sources):
    windows, channels, two, freqs = spectra.shape
    return pl.pallas_call(
        rest_kernel,
        in_specs=[anywhere(), pl.BlockSpec(memory_space=pltpu.HBM), whole(), whole()],
        out_specs=whole(),
        out_shape=jax.ShapeDtypeStruct((windows, channels, two * freqs), jnp.bfloat16),
        scratch_shapes=[
            pltpu.VMEM((windows, channels - SRC, two, freqs), spectra.dtype),
            pltpu.SMEM((1,), jnp.int32),
            pltpu.SemaphoreType.DMA((windows + 1,)),
        ],
        compiler_params=kernel_params(),
        name="whiten_rest",
    )(counts, spectra, taper, sources)


def whiten_sources(out_shape, counts, raw, taper):
    windows, channels, two, freqs = raw.shape
    return pl.pallas_call(
        whiten_kernel,
        in_specs=[anywhere()] + [whole()] * 2,
        out_specs=[whole()] * len(out_shape),
        out_shape=out_shape,
        scratch_shapes=[pltpu.SMEM((1,), jnp.int32), pltpu.SemaphoreType.DMA],
        compiler_params=kernel_params(),
        name="whiten",
    )(counts, raw.reshape(windows, channels, two * freqs), taper)


def taper_row(two, freqs):
    freq = np.arange(freqs, dtype=np.float64)
    taper = 0.75 - 0.25 * np.cos(2.0 * np.pi * (freq + 0.5) / freqs)
    return jnp.asarray(np.tile(taper.astype(np.float32), two)[None, :])


def mix(m_ref, piece, cos_ref, sin_ref, low, high):
    rows = piece.shape[0]
    vrow = v_row(rows)
    real = piece[:, low].astype(jnp.float32)
    imag = piece[:, high].astype(jnp.float32)

    def put(where, cols, values):
        m_ref[where, cols] = jnp.concatenate(values, axis=0).astype(jnp.bfloat16)

    for m in range(0, HALF, 2):
        c = [cos_ref[m + i:m + i + 1, low] for i in range(2)]
        s = [sin_ref[m + i:m + i + 1, low] for i in range(2)]
        line = slice(m * rows, (m + 2) * rows)
        vline = slice(vrow + m * rows, vrow + (m + 2) * rows)
        put(line, low, [real * v for v in c])
        put(line, high, [imag * v for v in c])
        put(vline, low, [imag * -v for v in s])
        put(vline, high, [real * v for v in s])
    fill = jnp.zeros((vrow - (HALF + 1) * rows, 128), jnp.float32)
    for value, cols in ((real, low), (imag, high)):
        put(slice(HALF * rows, vrow), cols, [value, fill])


def v_row(rows):
    return -(-(HALF + 1) * rows // 128) * 128


def times(lhs, rhs):
    return lax.dot_general(
        lhs, rhs, (((1,), (1,)), ((), ())), preferred_element_type=jnp.float32
    )


def add_products(acc_ref, lhs_ref, piece_ref, cos_ref, sin_ref, mixed_ref):
    windows, rows, width = piece_ref.shape
    tile = 256
    used = v_row(rows) + HALF * rows
    if used < mixed_ref.shape[0]:
        mixed_ref[used:, :] = jnp.zeros_like(mixed_ref[used:, :])

    @pl.loop(0, windows)
    def _(w):
        @pl.loop(0, width // 2, step=128)
        def _(start):
            low = pl.ds(pl.multiple_of(start, 128), 128)
            high = pl.ds(pl.multiple_of(width // 2 + start, 128), 128)
            mix(mixed_ref, piece_ref.at[w], cos_ref, sin_ref, low, high)

        @pl.loop(0, mixed_ref.shape[0], step=tile)
        def _(n):
            cols = pl.ds(pl.multiple_of(n, tile), tile)
            acc_ref[:, cols] += times(lhs_ref[w], mixed_ref[cols, :])


def part_kernel(white_ref, piece_ref, cos_ref, sin_ref, _, part_ref, done_ref, mixed_ref):
    done_ref[...] = jnp.zeros_like(done_ref)
    part_ref[...] = jnp.zeros_like(part_ref)
    add_products(part_ref, white_ref, piece_ref, cos_ref, sin_ref, mixed_ref)


def part_columns(rows):
    columns = v_row(rows) + HALF * rows
    return columns + (-columns) % 256


def part_terms(white, piece, tables, done):
    windows, channels, width = white.shape
    columns = part_columns(piece.shape[1])
    return pl.pallas_call(
        part_kernel,
        in_specs=[whole()] * 5,
        out_specs=[whole()] * 2,
        out_shape=[jax.ShapeDtypeStruct((channels, columns), jnp.float32), TOKEN],
        scratch_shapes=[pltpu.VMEM((columns, width), jnp.bfloat16)],
        compiler_params=kernel_params(),
        cost_estimate=COST,
        name="terms_part",
    )(white, piece, *tables, done)


TOKEN = jax.ShapeDtypeStruct((8, 128), jnp.float32)
COST = pl.CostEstimate(flops=30 * 10**9, bytes_accessed=0, transcendentals=0)


def pack(acc_ref, line, rows, scale, later):
    wide = HALF * rows
    vrow = v_row(rows)
    u, v = acc_ref[line, :wide] * scale, acc_ref[line, vrow:vrow + wide] * scale
    still = acc_ref[line, wide:wide + rows] * scale
    first, last = (u - v, u + v) if later else (u + v, u - v)
    return jnp.concatenate([first, last[:, :wide - rows], still], axis=1)


def terms_kernel(
    scale, part_ref, sibling_ref, piece_ref, cos_ref, sin_ref, _, back_ref, own_ref, *refs
):
    *done_refs, mixed_ref, acc_ref = refs
    for done_ref in done_refs:
        done_ref[...] = jnp.zeros_like(done_ref)
    acc_ref[...] = part_ref[...]
    add_products(acc_ref, sibling_ref, piece_ref, cos_ref, sin_ref, mixed_ref)
    line = pl.ds(SRC, acc_ref.shape[0] - SRC)
    back = pack(acc_ref, line, piece_ref.shape[1], scale, True)
    back_ref[...] = back.astype(back_ref.dtype)
    own_ref[...] = acc_ref[:SRC, :]


def own_kernel(scale, rows, first_ref, second_ref, *refs):
    *out_refs, packed_ref = refs
    x, core = place_of_core()
    mine = SRC // 4

    @pl.loop(0, SRC, step=mine)
    def _(start):
        line = pl.ds(pl.multiple_of(start, 8), mine)
        for quarter, ref in enumerate((first_ref, second_ref)):
            packed_ref[quarter, line, :] = pack(ref, line, rows, scale, False)

    for i, out_ref in enumerate(out_refs):
        spot = 2 * (x, 1 - x, 1 - x, x)[i] + (core, core, 1 - core, 1 - core)[i]
        line = pl.ds(pl.multiple_of(spot * mine, 8), mine)
        for quarter in range(2):
            out_ref[quarter] = packed_ref[quarter, line, :].astype(out_ref.dtype)


def own_terms(first, second, rows, scale):
    mine, wide = SRC // 4, 2 * HALF * rows
    return pl.pallas_call(
        functools.partial(own_kernel, scale, rows),
        in_specs=[whole()] * 2,
        out_specs=[whole()] * 4,
        out_shape=[
            jax.ShapeDtypeStruct((2, mine, wide), jnp.float32 if i == 0 else jnp.bfloat16)
            for i in range(4)
        ],
        scratch_shapes=[pltpu.VMEM((2, SRC, wide), jnp.float32)],
        compiler_params=kernel_params(),
        name="own_terms",
    )(first, second)


def terms(part, sibling, piece, tables, scale, done, last):
    windows, channels, width = sibling.shape
    rows = piece.shape[1]
    columns = part_columns(rows)
    back = ((channels - SRC, 2 * HALF * rows), jnp.float32 if last else jnp.bfloat16)
    out = [jax.ShapeDtypeStruct(*back), jax.ShapeDtypeStruct((SRC, columns), jnp.float32)]
    out += [] if last else [TOKEN]
    return pl.pallas_call(
        functools.partial(terms_kernel, scale),
        in_specs=[whole()] * 6,
        out_specs=[whole()] * len(out),
        out_shape=out,
        scratch_shapes=[
            pltpu.VMEM((columns, width), jnp.bfloat16),
            pltpu.VMEM((channels, columns), jnp.float32),
        ],
        compiler_params=kernel_params(),
        cost_estimate=COST,
        name="terms",
    )(part, sibling, piece, *tables, done)


def sum_kernel(here_ref, there_ref, out_ref):
    rows = out_ref.shape[0] // 4

    @pl.loop(0, out_ref.shape[0], step=rows)
    def _(start):
        line = pl.ds(pl.multiple_of(start, 8), rows)
        total = here_ref[line, :] + there_ref[line, :].astype(jnp.float32)
        out_ref[line, :] = total.astype(out_ref.dtype)


def sum_terms(here, there):
    return pl.pallas_call(
        sum_kernel,
        in_specs=[whole()] * 2,
        out_specs=whole(),
        out_shape=jax.ShapeDtypeStruct(there.shape, there.dtype),
        compiler_params=kernel_params(),
        name="sum_terms",
    )(here, there)


def copy_rows(source_ref, out_ref):
    rows = source_ref.shape[-2]
    if rows % 4:
        out_ref[...] = source_ref[...]
        return
    step = rows // 4 if rows % 64 == 0 else rows

    @pl.loop(0, rows, step=step)
    def _(start):
        line = pl.ds(pl.multiple_of(start, 16 if step % 16 == 0 else 8), step)
        out_ref[..., line, :] = source_ref[..., line, :]


def keep_kernel(*refs):
    half = len(refs) // 2
    for source_ref, out_ref in zip(refs[:half], refs[half:]):
        copy_rows(source_ref, out_ref)


def hold_kernel(source_ref, *refs):
    *_, out_ref, done_ref = refs
    copy_rows(source_ref, out_ref)
    done_ref[...] = jnp.zeros_like(done_ref)


def keep(*values):
    return pl.pallas_call(
        keep_kernel,
        in_specs=[whole()] * len(values),
        out_specs=[whole()] * len(values),
        out_shape=[jax.ShapeDtypeStruct(v.shape, v.dtype) for v in values],
        compiler_params=kernel_params(),
        name="keep",
    )(*values)


def hold(value, *done):
    return pl.pallas_call(
        hold_kernel,
        in_specs=[whole()] * (1 + len(done)),
        out_specs=[whole()] * 2,
        out_shape=[jax.ShapeDtypeStruct(value.shape, value.dtype), TOKEN],
        compiler_params=kernel_params(),
        name="hold",
    )(value, *done)


def place_kernel(
    here_ref, chip_ref, cross_ref, core_ref, back_ref, out_ref, block_ref, sems
):
    x, core = place_of_core()
    lags, mine, channels = block_ref.shape
    swap = core != 0
    sides = []
    for q in range(2):
        index = jnp.where(x == q, 1, 0)
        own = here_ref[index] + chip_ref[1 - index].astype(jnp.float32)
        other = core_ref[index].astype(jnp.float32) + cross_ref[1 - index].astype(jnp.float32)
        sides += [jnp.where(swap, other, own), jnp.where(swap, own, other)]
    back = back_ref[...].astype(jnp.float32).T
    copies = []
    for j in range(lags):
        lag = HALF - 1 - j if j < HALF else j + 1 if j < lags - 1 else HALF
        cols = slice(j * mine, (j + 1) * mine)
        block_ref[lag, :, :SRC] = jnp.concatenate([v[:, cols] for v in sides], axis=1)
        block_ref[lag, :, SRC:] = back[cols]
        copies.append(pltpu.make_async_copy(block_ref.at[lag], out_ref.at[lag], sems.at[lag]))
        copies[-1].start()
    for copy in copies:
        copy.wait()


def place(here, chip, cross, core, back):
    _, mine, wide = here.shape
    shape = (wide // mine, mine, SRC + back.shape[0])
    return pl.pallas_call(
        place_kernel,
        in_specs=[whole()] * 5,
        out_specs=anywhere(),
        out_shape=jax.ShapeDtypeStruct(shape, jnp.float32),
        scratch_shapes=[
            pltpu.VMEM(shape, jnp.float32), pltpu.SemaphoreType.DMA((shape[0],))
        ],
        compiler_params=kernel_params(),
        name="place_lags",
    )(here, chip, cross, core, back)


def pair_body(spectra, counts, partner):
    blocks = lax.axis_size("chan")
    groups = lax.axis_size("win")
    windows, channels, two, freqs = spectra.shape
    scale = 1.0 / (math.sqrt(2.0 * freqs) * math.sqrt(windows * groups))
    other_core = [(i, i ^ 1) for i in range(groups)]
    other_chip = [(i, i ^ 2) for i in range(groups)]
    other_both = [(i, i ^ 3) for i in range(groups)]

    def to_partner(t):
        return [(i, i ^ t) for i in range(blocks)]

    def to_partner_core(t):
        return [
            (i * groups + g, (i ^ t) * groups + (g ^ 1))
            for i in range(blocks)
            for g in range(groups)
        ]

    def one_round(t, counts, raw, sources, near, far, near_more, far_more):
        def straight(value):
            return lax.ppermute(value, "chan", to_partner(t))

        def crossed(value):
            return lax.ppermute(value, ("chan", "win"), to_partner_core(t))

        near, far = straight(near), crossed(far)
        white = whiten_rest(counts, raw, taper, sources)
        sibling = lax.ppermute(white, "win", other_core)
        near_more, done = hold(near_more, near)
        near_more = straight(near_more)
        part, done = part_terms(white, near, tables, done)
        far_more, done = hold(far_more, far, done)
        far_more = crossed(far_more)
        there, first, done = terms(part, sibling, far, tables, scale, done, False)
        there = lax.ppermute(there, "win", other_chip)
        part, done = part_terms(white, near_more, tables, done)
        here, second = terms(part, sibling, far_more, tables, scale, done, True)
        back = lax.ppermute(sum_terms(here, there), "chan", to_partner(t))
        here, chip, cross, core = own_terms(first, second, SRC // groups, scale)
        chip = lax.ppermute(chip, "win", other_chip)
        cross = lax.ppermute(cross, "win", other_both)
        core = lax.ppermute(core, "win", other_core)
        return here, *keep(chip, cross, core, back)

    def by_round(run, *values):
        branches = [functools.partial(run, t) for t in range(1, blocks)]
        return lax.switch(partner[0, 0] - 1, branches, *values)

    tables = [jnp.asarray(v) for v in shift_tables(freqs)]
    taper = taper_row(two, freqs)
    piece = jax.ShapeDtypeStruct((windows, SRC // 4, two * freqs), jnp.bfloat16)
    sources = jax.ShapeDtypeStruct((windows, SRC, two * freqs), jnp.bfloat16)
    raw = pltpu.with_memory_space_constraint(spectra, pltpu.HBM)
    sources = whiten_sources([sources] + [piece] * 4, counts, fetch_sources(raw), taper)
    return place(*by_round(one_round, counts, raw, *sources))[None, None]


def lag_table(freqs, lags):
    freq = jnp.arange(freqs, dtype=jnp.float32) + freqs // 4
    delay = jnp.arange(lags, dtype=jnp.float32) - lags // 2
    phase = 2.0 * math.pi * freq[:, None] * delay[None, :] / (4.0 * freqs)
    norm = 1.0 / math.sqrt(2.0 * freqs)
    return jnp.stack([jnp.cos(phase), -jnp.sin(phase)]) * norm


def blended_sources(sources, table):
    src = sources.astype(jnp.float32)
    first = src[:, :, 0][:, :, None, :]
    second = src[:, :, 1][:, :, None, :]
    cos_part = table[0].T[None, None]
    sin_part = table[1].T[None, None]
    real_mix = first * cos_part + second * sin_part
    imag_mix = second * cos_part - first * sin_part
    return jnp.stack([real_mix, imag_mix], axis=3).astype(jnp.bfloat16)


def pair_terms(sources, receiver_blocks, table):
    wins, count, two, freqs = sources.shape
    lags = table.shape[2]
    group = math.gcd(count, 32)
    flat_recv = receiver_blocks.reshape(wins, receiver_blocks.shape[1], two * freqs)
    grouped = jnp.moveaxis(sources.reshape(wins, count // group, group, two, freqs), 1, 0)

    def one_group(piece):
        mixed_spectra = blended_sources(piece, table).reshape(wins, group * lags, two * freqs)
        out = jnp.einsum(
            "wmx,wrx->mr", mixed_spectra, flat_recv, preferred_element_type=jnp.float32
        )
        return out.reshape(group, lags, receiver_blocks.shape[1])

    out = lax.map(one_group, grouped).reshape(count, lags, receiver_blocks.shape[1])
    return jnp.transpose(out, (1, 0, 2))


def route_blocks(values, round_flags, levels):
    for level in range(levels):
        moved = from_partner(values, "chan", level)
        values = jnp.where((round_flags >> level) % 2 == 1, moved, values)
    return values


def general_body(spectra, counts, partner):
    white = whiten_local(spectra, counts[0])
    table = lag_table(spectra.shape[3], LAGS)
    levels = lax.axis_size("chan").bit_length() - 1
    windows = spectra.shape[0] * lax.axis_size("win")
    receiver_blocks = route_blocks(white, partner[0, 0], levels)
    out = pair_terms(white[:, :SRC], receiver_blocks, table)
    stacked = lax.psum_scatter(out, "win", scatter_dimension=1, tiled=True)
    return (stacked / math.sqrt(windows))[None, None]


def solution(mesh):
    body = pair_body if mesh.shape["win"] == 4 else general_body
    return jax.shard_map(
        body,
        mesh=mesh,
        in_specs=(P("win", "chan", None, None), P("chan"), P()),
        out_specs=P("chan", None, None, "win", None),
        check_vma=False,
    )
```

```python
import functools
import math

import jax
import jax.numpy as jnp
import numpy as np
from jax import lax
from jax.experimental import pallas as pl
from jax.experimental.pallas import tpu as pltpu
from jax.sharding import PartitionSpec as P

LAGS = 16
SRC = 160
HALF = LAGS // 2
VMEM_LIMIT = 16 * 1024 * 1024


def from_partner(value, axis, stride):
    return lax.ppermute(value, axis, [(i, i ^ 1 << stride) for i in range(lax.axis_size(axis))])


def whiten_local(spectra, count):
    values = spectra.astype(jnp.float32)
    block_size = spectra.shape[1]
    freqs = spectra.shape[3]
    valid = (jnp.arange(block_size, dtype=jnp.int32) < count).astype(jnp.float32)
    freq = jnp.arange(freqs, dtype=jnp.float32)
    taper = 0.75 - 0.25 * jnp.cos(2.0 * math.pi * (freq + 0.5) / freqs)
    power = jnp.mean(values * values, axis=(2, 3))
    scale = valid[None, :] / jnp.sqrt(power + 1e-05)
    return (values * taper * scale[:, :, None, None]).astype(jnp.bfloat16)


def shift_tables(freqs):
    freq = np.arange(freqs, dtype=np.float64) + freqs // 4
    shift = np.arange(1, HALF + 1, dtype=np.float64)
    phase = 2.0 * np.pi * shift[:, None] * freq[None, :] / (4.0 * freqs)
    return np.cos(phase).astype(np.float32), np.sin(phase).astype(np.float32)


def place_of_core():
    spot = lax.axis_index("win")
    return spot // 2, spot % 2


def whole():
    return pl.BlockSpec(memory_space=pltpu.VMEM)


def anywhere():
    return pl.BlockSpec(memory_space=pl.ANY)


def kernel_params():
    return pltpu.CompilerParams(vmem_limit_bytes=VMEM_LIMIT)


def fetch_kernel(source_ref, out_ref, sems):
    windows, channels = out_ref.shape[:2]
    parts = sems.shape[1]
    step = channels // parts
    copies = []
    for w in range(windows):
        for i in range(parts):
            part = (w, pl.ds(i * step, step))
            copies.append(
                pltpu.make_async_copy(source_ref.at[part], out_ref.at[part], sems.at[w, i])
            )
            copies[-1].start()
    for copy in copies:
        copy.wait()


def fetch_sources(spectra):
    windows, _, *rest = spectra.shape
    return pl.pallas_call(
        fetch_kernel,
        in_specs=[pl.BlockSpec(memory_space=pltpu.HBM)],
        out_specs=whole(),
        out_shape=jax.ShapeDtypeStruct((windows, SRC, *rest), spectra.dtype),
        scratch_shapes=[pltpu.SemaphoreType.DMA((windows, 4))],
        compiler_params=kernel_params(),
        name="fetch",
    )(spectra)


def white_block(raw_ref, taper_ref, count, w, line, first_row):
    values = raw_ref[w, line, :].astype(jnp.float32)
    rows, width = values.shape
    power = jnp.sum(values * values, axis=1, keepdims=True) * (1.0 / width)
    row = first_row + lax.broadcasted_iota(jnp.int32, (rows, 1), 0)
    valid = (row < count).astype(jnp.float32)
    scale = valid / jnp.sqrt(power + 1e-05)
    return values * taper_ref[...] * scale


def whiten_kernel(count_ref, raw_ref, taper_ref, white_ref, *refs):
    *piece_refs, count, sem = refs
    copy = pltpu.make_async_copy(count_ref, count, sem)
    copy.start()
    x, core = place_of_core()
    mine = SRC // 4
    step = 2 * mine
    copy.wait()
    for w in range(raw_ref.shape[0]):
        for index, group in enumerate((1 - x, x)):
            line = pl.ds(pl.multiple_of(group * step, step), step)
            values = white_block(raw_ref, taper_ref, count[0], w, line, group * step)
            white_ref[w, line, :] = values.astype(jnp.bfloat16)
            low, high = values[:mine], values[mine:]
            first = core == 0
            near_ref, far_ref = piece_refs[2 * index:2 * index + 2]
            near_ref[w] = jnp.where(first, low, high).astype(jnp.bfloat16)
            far_ref[w] = jnp.where(first, high, low).astype(jnp.bfloat16)


def rest_kernel(
    count_ref, spectra_ref, taper_ref, sources_ref, white_ref, raw_ref, count, sems
):
    windows, channels, two, freqs = raw_ref.shape
    copies = [pltpu.make_async_copy(count_ref, count, sems.at[windows])]
    for w in range(windows):
        part = spectra_ref.at[w, pl.ds(SRC, channels)]
        copies.append(pltpu.make_async_copy(part, raw_ref.at[w], sems.at[w]))
    for copy in copies:
        copy.start()
    step = 32

    @pl.loop(0, windows)
    def _(w):
        @pl.loop(0, SRC, step=step)
        def _(start):
            line = pl.ds(pl.multiple_of(start, step), step)
            white_ref[w, line, :] = sources_ref[w, line, :]

    for copy in copies:
        copy.wait()

    @pl.loop(0, windows)
    def _(w):
        @pl.loop(0, channels, step=step)
        def _(start):
            line = pl.ds(pl.multiple_of(start, step), step)
            parts = [raw_ref[w, line, p, :].astype(jnp.float32) for p in range(two)]
            power = sum(jnp.sum(v * v, axis=1, keepdims=True) for v in parts)
            row = SRC + start + lax.broadcasted_iota(jnp.int32, (step, 1), 0)
            valid = (row < count[0]).astype(jnp.float32)
            scale = valid / jnp.sqrt(power * (1.0 / (two * freqs)) + 1e-05)
            out = pl.ds(pl.multiple_of(SRC + start, step), step)
            for p, v in enumerate(parts):
                cols = slice(p * freqs, (p + 1) * freqs)
                white_ref[w, out, cols] = (v * taper_ref[:, cols] * scale).astype(jnp.bfloat16)


def whiten_rest(counts, spectra, taper, sources):
    windows, channels, two, freqs = spectra.shape
    return pl.pallas_call(
        rest_kernel,
        in_specs=[anywhere(), pl.BlockSpec(memory_space=pltpu.HBM), whole(), whole()],
        out_specs=whole(),
        out_shape=jax.ShapeDtypeStruct((windows, channels, two * freqs), jnp.bfloat16),
        scratch_shapes=[
            pltpu.VMEM((windows, channels - SRC, two, freqs), spectra.dtype),
            pltpu.SMEM((1,), jnp.int32),
            pltpu.SemaphoreType.DMA((windows + 1,)),
        ],
        compiler_params=kernel_params(),
        name="whiten_rest",
    )(counts, spectra, taper, sources)


def whiten_sources(out_shape, counts, raw, taper):
    windows, channels, two, freqs = raw.shape
    return pl.pallas_call(
        whiten_kernel,
        in_specs=[anywhere()] + [whole()] * 2,
        out_specs=[whole()] * len(out_shape),
        out_shape=out_shape,
        scratch_shapes=[pltpu.SMEM((1,), jnp.int32), pltpu.SemaphoreType.DMA],
        compiler_params=kernel_params(),
        name="whiten",
    )(counts, raw.reshape(windows, channels, two * freqs), taper)


def taper_row(two, freqs):
    freq = np.arange(freqs, dtype=np.float64)
    taper = 0.75 - 0.25 * np.cos(2.0 * np.pi * (freq + 0.5) / freqs)
    return jnp.asarray(np.tile(taper.astype(np.float32), two)[None, :])


def mix(m_ref, piece, cos_ref, sin_ref, low, high):
    rows = piece.shape[0]
    vrow = v_row(rows)
    real = piece[:, low].astype(jnp.float32)
    imag = piece[:, high].astype(jnp.float32)

    def put(where, cols, values):
        m_ref[where, cols] = jnp.concatenate(values, axis=0).astype(jnp.bfloat16)

    for m in range(0, HALF, 2):
        c = [cos_ref[m + i:m + i + 1, low] for i in range(2)]
        s = [sin_ref[m + i:m + i + 1, low] for i in range(2)]
        line = slice(m * rows, (m + 2) * rows)
        vline = slice(vrow + m * rows, vrow + (m + 2) * rows)
        put(line, low, [real * v for v in c])
        put(line, high, [imag * v for v in c])
        put(vline, low, [imag * -v for v in s])
        put(vline, high, [real * v for v in s])
    fill = jnp.zeros((vrow - (HALF + 1) * rows, 128), jnp.float32)
    for value, cols in ((real, low), (imag, high)):
        put(slice(HALF * rows, vrow), cols, [value, fill])


def v_row(rows):
    return -(-(HALF + 1) * rows // 128) * 128


def times(lhs, rhs):
    return lax.dot_general(
        lhs, rhs, (((1,), (1,)), ((), ())), preferred_element_type=jnp.float32
    )


def add_products(acc_ref, lhs_ref, piece_ref, cos_ref, sin_ref, mixed_ref):
    windows, rows, width = piece_ref.shape
    tile = 256
    used = v_row(rows) + HALF * rows
    if used < mixed_ref.shape[0]:
        mixed_ref[used:, :] = jnp.zeros_like(mixed_ref[used:, :])

    @pl.loop(0, windows)
    def _(w):
        @pl.loop(0, width // 2, step=128)
        def _(start):
            low = pl.ds(pl.multiple_of(start, 128), 128)
            high = pl.ds(pl.multiple_of(width // 2 + start, 128), 128)
            mix(mixed_ref, piece_ref.at[w], cos_ref, sin_ref, low, high)

        @pl.loop(0, mixed_ref.shape[0], step=tile)
        def _(n):
            cols = pl.ds(pl.multiple_of(n, tile), tile)
            acc_ref[:, cols] += times(lhs_ref[w], mixed_ref[cols, :])


def part_kernel(white_ref, piece_ref, cos_ref, sin_ref, _, part_ref, done_ref, mixed_ref):
    done_ref[...] = jnp.zeros_like(done_ref)
    part_ref[...] = jnp.zeros_like(part_ref)
    add_products(part_ref, white_ref, piece_ref, cos_ref, sin_ref, mixed_ref)


def part_columns(rows):
    columns = v_row(rows) + HALF * rows
    return columns + (-columns) % 256


def part_terms(white, piece, tables, done):
    windows, channels, width = white.shape
    columns = part_columns(piece.shape[1])
    return pl.pallas_call(
        part_kernel,
        in_specs=[whole()] * 5,
        out_specs=[whole()] * 2,
        out_shape=[jax.ShapeDtypeStruct((channels, columns), jnp.float32), TOKEN],
        scratch_shapes=[pltpu.VMEM((columns, width), jnp.bfloat16)],
        compiler_params=kernel_params(),
        cost_estimate=COST,
        name="terms_part",
    )(white, piece, *tables, done)


TOKEN = jax.ShapeDtypeStruct((8, 128), jnp.float32)
COST = pl.CostEstimate(flops=30 * 10**9, bytes_accessed=0, transcendentals=0)


def pack(acc_ref, line, rows, scale, later):
    wide = HALF * rows
    vrow = v_row(rows)
    u, v = acc_ref[line, :wide] * scale, acc_ref[line, vrow:vrow + wide] * scale
    still = acc_ref[line, wide:wide + rows] * scale
    first, last = (u - v, u + v) if later else (u + v, u - v)
    return jnp.concatenate([first, last[:, :wide - rows], still], axis=1)


def terms_kernel(
    scale, part_ref, sibling_ref, piece_ref, cos_ref, sin_ref, _, back_ref, own_ref, *refs
):
    *done_refs, mixed_ref, acc_ref = refs
    for done_ref in done_refs:
        done_ref[...] = jnp.zeros_like(done_ref)
    acc_ref[...] = part_ref[...]
    add_products(acc_ref, sibling_ref, piece_ref, cos_ref, sin_ref, mixed_ref)
    line = pl.ds(SRC, acc_ref.shape[0] - SRC)
    back = pack(acc_ref, line, piece_ref.shape[1], scale, True)
    back_ref[...] = back.astype(back_ref.dtype)
    own_ref[...] = acc_ref[:SRC, :]


def own_kernel(scale, rows, first_ref, second_ref, *refs):
    *out_refs, packed_ref = refs
    x, core = place_of_core()
    mine = SRC // 4

    @pl.loop(0, SRC, step=mine)
    def _(start):
        line = pl.ds(pl.multiple_of(start, 8), mine)
        for quarter, ref in enumerate((first_ref, second_ref)):
            packed_ref[quarter, line, :] = pack(ref, line, rows, scale, False)

    for i, out_ref in enumerate(out_refs):
        spot = 2 * (x, 1 - x, 1 - x, x)[i] + (core, core, 1 - core, 1 - core)[i]
        line = pl.ds(pl.multiple_of(spot * mine, 8), mine)
        for quarter in range(2):
            out_ref[quarter] = packed_ref[quarter, line, :].astype(out_ref.dtype)


def own_terms(first, second, rows, scale):
    mine, wide = SRC // 4, 2 * HALF * rows
    return pl.pallas_call(
        functools.partial(own_kernel, scale, rows),
        in_specs=[whole()] * 2,
        out_specs=[whole()] * 4,
        out_shape=[
            jax.ShapeDtypeStruct((2, mine, wide), jnp.float32 if i == 0 else jnp.bfloat16)
            for i in range(4)
        ],
        scratch_shapes=[pltpu.VMEM((2, SRC, wide), jnp.float32)],
        compiler_params=kernel_params(),
        name="own_terms",
    )(first, second)


def terms(part, sibling, piece, tables, scale, done, last):
    windows, channels, width = sibling.shape
    rows = piece.shape[1]
    columns = part_columns(rows)
    back = ((channels - SRC, 2 * HALF * rows), jnp.float32 if last else jnp.bfloat16)
    out = [jax.ShapeDtypeStruct(*back), jax.ShapeDtypeStruct((SRC, columns), jnp.float32)]
    out += [] if last else [TOKEN]
    return pl.pallas_call(
        functools.partial(terms_kernel, scale),
        in_specs=[whole()] * 6,
        out_specs=[whole()] * len(out),
        out_shape=out,
        scratch_shapes=[
            pltpu.VMEM((columns, width), jnp.bfloat16),
            pltpu.VMEM((channels, columns), jnp.float32),
        ],
        compiler_params=kernel_params(),
        cost_estimate=COST,
        name="terms",
    )(part, sibling, piece, *tables, done)


def sum_kernel(here_ref, there_ref, *refs):
    out_ref = refs[-1]
    step = 32

    @pl.loop(0, out_ref.shape[0], step=step)
    def _(start):
        line = pl.ds(pl.multiple_of(start, step), step)
        total = here_ref[line, :] + there_ref[line, :].astype(jnp.float32)
        out_ref[line, :] = total.astype(out_ref.dtype)


def sum_terms(here, there, *done):
    return pl.pallas_call(
        sum_kernel,
        in_specs=[whole()] * (2 + len(done)),
        out_specs=whole(),
        out_shape=jax.ShapeDtypeStruct(there.shape, there.dtype),
        compiler_params=kernel_params(),
        name="sum_terms",
    )(here, there, *done)


def keep_kernel(*refs):
    half = len(refs) // 2
    for source_ref, out_ref in zip(refs[:half], refs[half:]):
        out_ref[...] = source_ref[...]


def hold_kernel(source_ref, *refs):
    *_, out_ref, done_ref = refs
    out_ref[...] = source_ref[...]
    done_ref[...] = jnp.zeros_like(done_ref)


def keep(*values):
    return pl.pallas_call(
        keep_kernel,
        in_specs=[whole()] * len(values),
        out_specs=[whole()] * len(values),
        out_shape=[jax.ShapeDtypeStruct(v.shape, v.dtype) for v in values],
        compiler_params=kernel_params(),
        name="keep",
    )(*values)


def hold(value, *done):
    return pl.pallas_call(
        hold_kernel,
        in_specs=[whole()] * (1 + len(done)),
        out_specs=[whole()] * 2,
        out_shape=[jax.ShapeDtypeStruct(value.shape, value.dtype), TOKEN],
        compiler_params=kernel_params(),
        name="hold",
    )(value, *done)


def place_kernel(
    here_ref, chip_ref, cross_ref, core_ref, back_ref, out_ref, block_ref, sems
):
    x, core = place_of_core()
    lags, mine, channels = block_ref.shape
    swap = core != 0
    sides = []
    for q in range(2):
        index = jnp.where(x == q, 1, 0)
        own = here_ref[index] + chip_ref[1 - index].astype(jnp.float32)
        other = core_ref[index].astype(jnp.float32) + cross_ref[1 - index].astype(jnp.float32)
        sides += [jnp.where(swap, other, own), jnp.where(swap, own, other)]
    back = back_ref[...].astype(jnp.float32).T
    copies = []
    for j in range(lags):
        lag = HALF - 1 - j if j < HALF else j + 1 if j < lags - 1 else HALF
        cols = slice(j * mine, (j + 1) * mine)
        block_ref[lag, :, :SRC] = jnp.concatenate([v[:, cols] for v in sides], axis=1)
        block_ref[lag, :, SRC:] = back[cols]
        copies.append(pltpu.make_async_copy(block_ref.at[lag], out_ref.at[lag], sems.at[lag]))
        copies[-1].start()
    for copy in copies:
        copy.wait()


def place(here, chip, cross, core, back):
    _, mine, wide = here.shape
    shape = (wide // mine, mine, SRC + back.shape[0])
    return pl.pallas_call(
        place_kernel,
        in_specs=[whole()] * 5,
        out_specs=anywhere(),
        out_shape=jax.ShapeDtypeStruct(shape, jnp.float32),
        scratch_shapes=[
            pltpu.VMEM(shape, jnp.float32), pltpu.SemaphoreType.DMA((shape[0],))
        ],
        compiler_params=kernel_params(),
        name="place_lags",
    )(here, chip, cross, core, back)


def pair_body(spectra, counts, partner):
    blocks = lax.axis_size("chan")
    groups = lax.axis_size("win")
    windows, channels, two, freqs = spectra.shape
    scale = 1.0 / (math.sqrt(2.0 * freqs) * math.sqrt(windows * groups))
    other_core = [(i, i ^ 1) for i in range(groups)]
    other_chip = [(i, i ^ 2) for i in range(groups)]
    other_both = [(i, i ^ 3) for i in range(groups)]

    def to_partner(t):
        return [(i, i ^ t) for i in range(blocks)]

    def to_partner_core(t):
        return [
            (i * groups + g, (i ^ t) * groups + (g ^ 1))
            for i in range(blocks)
            for g in range(groups)
        ]

    def one_round(t, counts, raw, sources, near, far, near_more, far_more):
        def straight(value):
            return lax.ppermute(value, "chan", to_partner(t))

        def crossed(value):
            return lax.ppermute(value, ("chan", "win"), to_partner_core(t))

        near, far = straight(near), crossed(far)
        white = whiten_rest(counts, raw, taper, sources)
        sibling = lax.ppermute(white, "win", other_core)
        near_more, done = hold(near_more, near)
        near_more = straight(near_more)
        part, done = part_terms(white, near, tables, done)
        far_more, done = hold(far_more, far, done)
        far_more = crossed(far_more)
        there, first, done = terms(part, sibling, far, tables, scale, done, False)
        there = lax.ppermute(there, "win", other_chip)
        part, done = part_terms(white, near_more, tables, done)
        here, second = terms(part, sibling, far_more, tables, scale, done, True)
        own, chip, cross, core = own_terms(first, second, SRC // groups, scale)
        done = (core,) if t < blocks // 2 else ()
        back = lax.ppermute(sum_terms(here, there, *done), "chan", to_partner(t))
        chip = lax.ppermute(chip, "win", other_chip)
        cross = lax.ppermute(cross, "win", other_both)
        core = lax.ppermute(core, "win", other_core)
        return own, *keep(chip, cross, core, back)

    def by_round(run, *values):
        branches = [functools.partial(run, t) for t in range(1, blocks)]
        return lax.switch(partner[0, 0] - 1, branches, *values)

    tables = [jnp.asarray(v) for v in shift_tables(freqs)]
    taper = taper_row(two, freqs)
    piece = jax.ShapeDtypeStruct((windows, SRC // 4, two * freqs), jnp.bfloat16)
    sources = jax.ShapeDtypeStruct((windows, SRC, two * freqs), jnp.bfloat16)
    raw = pltpu.with_memory_space_constraint(spectra, pltpu.HBM)
    sources = whiten_sources([sources] + [piece] * 4, counts, fetch_sources(raw), taper)
    return place(*by_round(one_round, counts, raw, *sources))[None, None]


def lag_table(freqs, lags):
    freq = jnp.arange(freqs, dtype=jnp.float32) + freqs // 4
    delay = jnp.arange(lags, dtype=jnp.float32) - lags // 2
    phase = 2.0 * math.pi * freq[:, None] * delay[None, :] / (4.0 * freqs)
    norm = 1.0 / math.sqrt(2.0 * freqs)
    return jnp.stack([jnp.cos(phase), -jnp.sin(phase)]) * norm


def blended_sources(sources, table):
    src = sources.astype(jnp.float32)
    first = src[:, :, 0][:, :, None, :]
    second = src[:, :, 1][:, :, None, :]
    cos_part = table[0].T[None, None]
    sin_part = table[1].T[None, None]
    real_mix = first * cos_part + second * sin_part
    imag_mix = second * cos_part - first * sin_part
    return jnp.stack([real_mix, imag_mix], axis=3).astype(jnp.bfloat16)


def pair_terms(sources, receiver_blocks, table):
    wins, count, two, freqs = sources.shape
    lags = table.shape[2]
    group = math.gcd(count, 32)
    flat_recv = receiver_blocks.reshape(wins, receiver_blocks.shape[1], two * freqs)
    grouped = jnp.moveaxis(sources.reshape(wins, count // group, group, two, freqs), 1, 0)

    def one_group(piece):
        mixed_spectra = blended_sources(piece, table).reshape(wins, group * lags, two * freqs)
        out = jnp.einsum(
            "wmx,wrx->mr", mixed_spectra, flat_recv, preferred_element_type=jnp.float32
        )
        return out.reshape(group, lags, receiver_blocks.shape[1])

    out = lax.map(one_group, grouped).reshape(count, lags, receiver_blocks.shape[1])
    return jnp.transpose(out, (1, 0, 2))


def route_blocks(values, round_flags, levels):
    for level in range(levels):
        moved = from_partner(values, "chan", level)
        values = jnp.where((round_flags >> level) % 2 == 1, moved, values)
    return values


def general_body(spectra, counts, partner):
    white = whiten_local(spectra, counts[0])
    table = lag_table(spectra.shape[3], LAGS)
    levels = lax.axis_size("chan").bit_length() - 1
    windows = spectra.shape[0] * lax.axis_size("win")
    receiver_blocks = route_blocks(white, partner[0, 0], levels)
    out = pair_terms(white[:, :SRC], receiver_blocks, table)
    stacked = lax.psum_scatter(out, "win", scatter_dimension=1, tiled=True)
    return (stacked / math.sqrt(windows))[None, None]


def solution(mesh):
    body = pair_body if mesh.shape["win"] == 4 else general_body
    return jax.shard_map(
        body,
        mesh=mesh,
        in_specs=(P("win", "chan", None, None), P("chan"), P()),
        out_specs=P("chan", None, None, "win", None),
        check_vma=False,
    )
```

```python
import functools
import math

import jax
import jax.numpy as jnp
import numpy as np
from jax import lax
from jax.experimental import pallas as pl
from jax.experimental.pallas import tpu as pltpu
from jax.sharding import PartitionSpec as P

LAGS = 16
SRC = 160
HALF = LAGS // 2
VMEM_LIMIT = 16 * 1024 * 1024


def from_partner(value, axis, stride):
    return lax.ppermute(value, axis, [(i, i ^ 1 << stride) for i in range(lax.axis_size(axis))])


def whiten_local(spectra, count):
    values = spectra.astype(jnp.float32)
    block_size = spectra.shape[1]
    freqs = spectra.shape[3]
    valid = (jnp.arange(block_size, dtype=jnp.int32) < count).astype(jnp.float32)
    freq = jnp.arange(freqs, dtype=jnp.float32)
    taper = 0.75 - 0.25 * jnp.cos(2.0 * math.pi * (freq + 0.5) / freqs)
    power = jnp.mean(values * values, axis=(2, 3))
    scale = valid[None, :] / jnp.sqrt(power + 1e-05)
    return (values * taper * scale[:, :, None, None]).astype(jnp.bfloat16)


def shift_tables(freqs):
    freq = np.arange(freqs, dtype=np.float64) + freqs // 4
    shift = np.arange(1, HALF + 1, dtype=np.float64)
    phase = 2.0 * np.pi * shift[:, None] * freq[None, :] / (4.0 * freqs)
    return np.cos(phase).astype(np.float32), np.sin(phase).astype(np.float32)


def place_of_core():
    spot = lax.axis_index("win")
    return spot // 2, spot % 2


def whole():
    return pl.BlockSpec(memory_space=pltpu.VMEM)


def anywhere():
    return pl.BlockSpec(memory_space=pl.ANY)


def kernel_params():
    return pltpu.CompilerParams(vmem_limit_bytes=VMEM_LIMIT)


def fetch_kernel(source_ref, out_ref, sems):
    windows, channels = out_ref.shape[:2]
    parts = sems.shape[1]
    step = channels // parts
    copies = []
    for w in range(windows):
        for i in range(parts):
            part = (w, pl.ds(i * step, step))
            copies.append(
                pltpu.make_async_copy(source_ref.at[part], out_ref.at[part], sems.at[w, i])
            )
            copies[-1].start()
    for copy in copies:
        copy.wait()


def fetch_sources(spectra):
    windows, _, *rest = spectra.shape
    return pl.pallas_call(
        fetch_kernel,
        in_specs=[pl.BlockSpec(memory_space=pltpu.HBM)],
        out_specs=whole(),
        out_shape=jax.ShapeDtypeStruct((windows, SRC, *rest), spectra.dtype),
        scratch_shapes=[pltpu.SemaphoreType.DMA((windows, 4))],
        compiler_params=kernel_params(),
        name="fetch",
    )(spectra)


def white_block(raw_ref, taper_ref, count, w, line, first_row):
    values = raw_ref[w, line, :].astype(jnp.float32)
    rows, width = values.shape
    power = jnp.sum(values * values, axis=1, keepdims=True) * (1.0 / width)
    row = first_row + lax.broadcasted_iota(jnp.int32, (rows, 1), 0)
    valid = (row < count).astype(jnp.float32)
    scale = valid / jnp.sqrt(power + 1e-05)
    return values * taper_ref[...] * scale


def whiten_kernel(count_ref, raw_ref, taper_ref, white_ref, *refs):
    *piece_refs, count, sem = refs
    copy = pltpu.make_async_copy(count_ref, count, sem)
    copy.start()
    x, core = place_of_core()
    mine = SRC // 4
    step = 2 * mine
    copy.wait()
    for w in range(raw_ref.shape[0]):
        for index, group in enumerate((1 - x, x)):
            line = pl.ds(pl.multiple_of(group * step, step), step)
            values = white_block(raw_ref, taper_ref, count[0], w, line, group * step)
            white_ref[w, line, :] = values.astype(jnp.bfloat16)
            low, high = values[:mine], values[mine:]
            first = core == 0
            near_ref, far_ref = piece_refs[2 * index:2 * index + 2]
            near_ref[w] = jnp.where(first, low, high).astype(jnp.bfloat16)
            far_ref[w] = jnp.where(first, high, low).astype(jnp.bfloat16)


def rest_kernel(
    count_ref, spectra_ref, taper_ref, sources_ref, white_ref, raw_ref, count, sems
):
    windows, channels, two, freqs = raw_ref.shape
    copies = [pltpu.make_async_copy(count_ref, count, sems.at[windows])]
    for w in range(windows):
        part = spectra_ref.at[w, pl.ds(SRC, channels)]
        copies.append(pltpu.make_async_copy(part, raw_ref.at[w], sems.at[w]))
    for copy in copies:
        copy.start()
    step = 32

    @pl.loop(0, windows)
    def _(w):
        @pl.loop(0, SRC, step=step)
        def _(start):
            line = pl.ds(pl.multiple_of(start, step), step)
            white_ref[w, line, :] = sources_ref[w, line, :]

    for copy in copies:
        copy.wait()

    @pl.loop(0, windows)
    def _(w):
        @pl.loop(0, channels, step=step)
        def _(start):
            line = pl.ds(pl.multiple_of(start, step), step)
            parts = [raw_ref[w, line, p, :].astype(jnp.float32) for p in range(two)]
            power = sum(jnp.sum(v * v, axis=1, keepdims=True) for v in parts)
            row = SRC + start + lax.broadcasted_iota(jnp.int32, (step, 1), 0)
            valid = (row < count[0]).astype(jnp.float32)
            scale = valid / jnp.sqrt(power * (1.0 / (two * freqs)) + 1e-05)
            out = pl.ds(pl.multiple_of(SRC + start, step), step)
            for p, v in enumerate(parts):
                cols = slice(p * freqs, (p + 1) * freqs)
                white_ref[w, out, cols] = (v * taper_ref[:, cols] * scale).astype(jnp.bfloat16)


def whiten_rest(counts, spectra, taper, sources):
    windows, channels, two, freqs = spectra.shape
    return pl.pallas_call(
        rest_kernel,
        in_specs=[anywhere(), pl.BlockSpec(memory_space=pltpu.HBM), whole(), whole()],
        out_specs=whole(),
        out_shape=jax.ShapeDtypeStruct((windows, channels, two * freqs), jnp.bfloat16),
        scratch_shapes=[
            pltpu.VMEM((windows, channels - SRC, two, freqs), spectra.dtype),
            pltpu.SMEM((1,), jnp.int32),
            pltpu.SemaphoreType.DMA((windows + 1,)),
        ],
        compiler_params=kernel_params(),
        name="whiten_rest",
    )(counts, spectra, taper, sources)


def whiten_sources(out_shape, counts, raw, taper):
    windows, channels, two, freqs = raw.shape
    return pl.pallas_call(
        whiten_kernel,
        in_specs=[anywhere()] + [whole()] * 2,
        out_specs=[whole()] * len(out_shape),
        out_shape=out_shape,
        scratch_shapes=[pltpu.SMEM((1,), jnp.int32), pltpu.SemaphoreType.DMA],
        compiler_params=kernel_params(),
        name="whiten",
    )(counts, raw.reshape(windows, channels, two * freqs), taper)


def taper_row(two, freqs):
    freq = np.arange(freqs, dtype=np.float64)
    taper = 0.75 - 0.25 * np.cos(2.0 * np.pi * (freq + 0.5) / freqs)
    return jnp.asarray(np.tile(taper.astype(np.float32), two)[None, :])


def mix(m_ref, piece, cos_ref, sin_ref, low, high):
    rows = piece.shape[0]
    vrow = v_row(rows)
    real = piece[:, low].astype(jnp.float32)
    imag = piece[:, high].astype(jnp.float32)

    def put(where, cols, values):
        m_ref[where, cols] = jnp.concatenate(values, axis=0).astype(jnp.bfloat16)

    for m in range(0, HALF, 2):
        c = [cos_ref[m + i:m + i + 1, low] for i in range(2)]
        s = [sin_ref[m + i:m + i + 1, low] for i in range(2)]
        line = slice(m * rows, (m + 2) * rows)
        vline = slice(vrow + m * rows, vrow + (m + 2) * rows)
        put(line, low, [real * v for v in c])
        put(line, high, [imag * v for v in c])
        put(vline, low, [imag * -v for v in s])
        put(vline, high, [real * v for v in s])
    fill = jnp.zeros((vrow - (HALF + 1) * rows, 128), jnp.float32)
    for value, cols in ((real, low), (imag, high)):
        put(slice(HALF * rows, vrow), cols, [value, fill])


def v_row(rows):
    return -(-(HALF + 1) * rows // 128) * 128


def times(lhs, rhs):
    return lax.dot_general(
        lhs, rhs, (((1,), (1,)), ((), ())), preferred_element_type=jnp.float32
    )


def by_rows(count, run):
    @pl.loop(0, count, step=32)
    def _(start):
        run(pl.ds(pl.multiple_of(start, 32), 32))


def add_products(acc_ref, lhs_ref, piece_ref, cos_ref, sin_ref, mixed_ref):
    windows, rows, width = piece_ref.shape
    tile = 256
    used = v_row(rows) + HALF * rows
    if used < mixed_ref.shape[0]:
        mixed_ref[used:, :] = jnp.zeros_like(mixed_ref[used:, :])

    @pl.loop(0, windows)
    def _(w):
        @pl.loop(0, width // 2, step=128)
        def _(start):
            low = pl.ds(pl.multiple_of(start, 128), 128)
            high = pl.ds(pl.multiple_of(width // 2 + start, 128), 128)
            mix(mixed_ref, piece_ref.at[w], cos_ref, sin_ref, low, high)

        @pl.loop(0, mixed_ref.shape[0], step=tile)
        def _(n):
            cols = pl.ds(pl.multiple_of(n, tile), tile)
            acc_ref[:, cols] += times(lhs_ref[w], mixed_ref[cols, :])


def part_kernel(white_ref, piece_ref, cos_ref, sin_ref, _, part_ref, done_ref, mixed_ref):
    done_ref[...] = jnp.zeros_like(done_ref)

    def clear(line):
        part_ref[line, :] = jnp.zeros((32, part_ref.shape[1]), part_ref.dtype)

    by_rows(part_ref.shape[0], clear)
    add_products(part_ref, white_ref, piece_ref, cos_ref, sin_ref, mixed_ref)


def part_columns(rows):
    columns = v_row(rows) + HALF * rows
    return columns + (-columns) % 256


def part_terms(white, piece, tables, done):
    windows, channels, width = white.shape
    columns = part_columns(piece.shape[1])
    return pl.pallas_call(
        part_kernel,
        in_specs=[whole()] * 5,
        out_specs=[whole()] * 2,
        out_shape=[jax.ShapeDtypeStruct((channels, columns), jnp.float32), TOKEN],
        scratch_shapes=[pltpu.VMEM((columns, width), jnp.bfloat16)],
        compiler_params=kernel_params(),
        cost_estimate=COST,
        name="terms_part",
    )(white, piece, *tables, done)


TOKEN = jax.ShapeDtypeStruct((8, 128), jnp.float32)
COST = pl.CostEstimate(flops=30 * 10**9, bytes_accessed=0, transcendentals=0)


def pack(acc_ref, line, rows, scale, later):
    wide = HALF * rows
    vrow = v_row(rows)
    u, v = acc_ref[line, :wide] * scale, acc_ref[line, vrow:vrow + wide] * scale
    still = acc_ref[line, wide:wide + rows] * scale
    first, last = (u - v, u + v) if later else (u + v, u - v)
    return jnp.concatenate([first, last[:, :wide - rows], still], axis=1)


def terms_kernel(
    scale, part_ref, sibling_ref, piece_ref, cos_ref, sin_ref, _, back_ref, own_ref, *refs
):
    *done_refs, mixed_ref, acc_ref = refs
    for done_ref in done_refs:
        done_ref[...] = jnp.zeros_like(done_ref)

    def take(line):
        acc_ref[line, :] = part_ref[line, :]

    by_rows(acc_ref.shape[0], take)
    add_products(acc_ref, sibling_ref, piece_ref, cos_ref, sin_ref, mixed_ref)

    def write(line):
        behind = pl.ds(pl.multiple_of(SRC + line.start, 32), 32)
        back = pack(acc_ref, behind, piece_ref.shape[1], scale, True)
        back_ref[line, :] = back.astype(back_ref.dtype)
        own_ref[line, :] = acc_ref[line, :]

    by_rows(SRC, write)


def own_kernel(scale, rows, first_ref, second_ref, *refs):
    *out_refs, packed_ref = refs
    x, core = place_of_core()
    mine = SRC // 4

    @pl.loop(0, SRC, step=mine)
    def _(start):
        line = pl.ds(pl.multiple_of(start, 8), mine)
        for quarter, ref in enumerate((first_ref, second_ref)):
            packed_ref[quarter, line, :] = pack(ref, line, rows, scale, False)

    for i, out_ref in enumerate(out_refs):
        spot = 2 * (x, 1 - x, 1 - x, x)[i] + (core, core, 1 - core, 1 - core)[i]
        line = pl.ds(pl.multiple_of(spot * mine, 8), mine)
        for quarter in range(2):
            out_ref[quarter] = packed_ref[quarter, line, :].astype(out_ref.dtype)


def own_terms(first, second, rows, scale):
    mine, wide = SRC // 4, 2 * HALF * rows
    return pl.pallas_call(
        functools.partial(own_kernel, scale, rows),
        in_specs=[whole()] * 2,
        out_specs=[whole()] * 4,
        out_shape=[
            jax.ShapeDtypeStruct((2, mine, wide), jnp.float32 if i == 0 else jnp.bfloat16)
            for i in range(4)
        ],
        scratch_shapes=[pltpu.VMEM((2, SRC, wide), jnp.float32)],
        compiler_params=kernel_params(),
        name="own_terms",
    )(first, second)


def terms(part, sibling, piece, tables, scale, done, last):
    windows, channels, width = sibling.shape
    rows = piece.shape[1]
    columns = part_columns(rows)
    back = ((channels - SRC, 2 * HALF * rows), jnp.float32 if last else jnp.bfloat16)
    out = [jax.ShapeDtypeStruct(*back), jax.ShapeDtypeStruct((SRC, columns), jnp.float32)]
    out += [] if last else [TOKEN]
    return pl.pallas_call(
        functools.partial(terms_kernel, scale),
        in_specs=[whole()] * 6,
        out_specs=[whole()] * len(out),
        out_shape=out,
        scratch_shapes=[
            pltpu.VMEM((columns, width), jnp.bfloat16),
            pltpu.VMEM((channels, columns), jnp.float32),
        ],
        compiler_params=kernel_params(),
        cost_estimate=COST,
        name="terms",
    )(part, sibling, piece, *tables, done)


def sum_kernel(here_ref, there_ref, *refs):
    out_ref = refs[-1]

    def add(line):
        total = here_ref[line, :] + there_ref[line, :].astype(jnp.float32)
        out_ref[line, :] = total.astype(out_ref.dtype)

    by_rows(out_ref.shape[0], add)


def sum_terms(here, there, *done):
    return pl.pallas_call(
        sum_kernel,
        in_specs=[whole()] * (2 + len(done)),
        out_specs=whole(),
        out_shape=jax.ShapeDtypeStruct(there.shape, there.dtype),
        compiler_params=kernel_params(),
        name="sum_terms",
    )(here, there, *done)


def keep_kernel(*refs):
    half = len(refs) // 2
    for source_ref, out_ref in zip(refs[:half], refs[half:]):
        out_ref[...] = source_ref[...]


def hold_kernel(source_ref, *refs):
    *_, out_ref, done_ref = refs
    out_ref[...] = source_ref[...]
    done_ref[...] = jnp.zeros_like(done_ref)


def keep(*values):
    return pl.pallas_call(
        keep_kernel,
        in_specs=[whole()] * len(values),
        out_specs=[whole()] * len(values),
        out_shape=[jax.ShapeDtypeStruct(v.shape, v.dtype) for v in values],
        compiler_params=kernel_params(),
        name="keep",
    )(*values)


def hold(value, *done):
    return pl.pallas_call(
        hold_kernel,
        in_specs=[whole()] * (1 + len(done)),
        out_specs=[whole()] * 2,
        out_shape=[jax.ShapeDtypeStruct(value.shape, value.dtype), TOKEN],
        compiler_params=kernel_params(),
        name="hold",
    )(value, *done)


def place_kernel(
    here_ref, chip_ref, cross_ref, core_ref, back_ref, out_ref, block_ref, sems
):
    x, core = place_of_core()
    lags, mine, channels = block_ref.shape
    swap = core != 0
    sides = []
    for q in range(2):
        index = jnp.where(x == q, 1, 0)
        own = here_ref[index] + chip_ref[1 - index].astype(jnp.float32)
        other = core_ref[index].astype(jnp.float32) + cross_ref[1 - index].astype(jnp.float32)
        sides += [jnp.where(swap, other, own), jnp.where(swap, own, other)]
    back = back_ref[...].astype(jnp.float32).T
    copies = []
    for j in range(lags):
        lag = HALF - 1 - j if j < HALF else j + 1 if j < lags - 1 else HALF
        cols = slice(j * mine, (j + 1) * mine)
        block_ref[lag, :, :SRC] = jnp.concatenate([v[:, cols] for v in sides], axis=1)
        block_ref[lag, :, SRC:] = back[cols]
        copies.append(pltpu.make_async_copy(block_ref.at[lag], out_ref.at[lag], sems.at[lag]))
        copies[-1].start()
    for copy in copies:
        copy.wait()


def place(here, chip, cross, core, back):
    _, mine, wide = here.shape
    shape = (wide // mine, mine, SRC + back.shape[0])
    return pl.pallas_call(
        place_kernel,
        in_specs=[whole()] * 5,
        out_specs=anywhere(),
        out_shape=jax.ShapeDtypeStruct(shape, jnp.float32),
        scratch_shapes=[
            pltpu.VMEM(shape, jnp.float32), pltpu.SemaphoreType.DMA((shape[0],))
        ],
        compiler_params=kernel_params(),
        name="place_lags",
    )(here, chip, cross, core, back)


def pair_body(spectra, counts, partner):
    blocks = lax.axis_size("chan")
    groups = lax.axis_size("win")
    windows, channels, two, freqs = spectra.shape
    scale = 1.0 / (math.sqrt(2.0 * freqs) * math.sqrt(windows * groups))
    other_core = [(i, i ^ 1) for i in range(groups)]
    other_chip = [(i, i ^ 2) for i in range(groups)]
    other_both = [(i, i ^ 3) for i in range(groups)]

    def to_partner(t):
        return [(i, i ^ t) for i in range(blocks)]

    def to_partner_core(t):
        return [
            (i * groups + g, (i ^ t) * groups + (g ^ 1))
            for i in range(blocks)
            for g in range(groups)
        ]

    def one_round(t, counts, raw, sources, near, far, near_more, far_more):
        def straight(value):
            return lax.ppermute(value, "chan", to_partner(t))

        def crossed(value):
            return lax.ppermute(value, ("chan", "win"), to_partner_core(t))

        near, far = straight(near), crossed(far)
        white = whiten_rest(counts, raw, taper, sources)
        sibling = lax.ppermute(white, "win", other_core)
        near_more, done = hold(near_more, near)
        near_more = straight(near_more)
        part, done = part_terms(white, near, tables, done)
        far_more, done = hold(far_more, far, done)
        far_more = crossed(far_more)
        there, first, done = terms(part, sibling, far, tables, scale, done, False)
        there = lax.ppermute(there, "win", other_chip)
        part, done = part_terms(white, near_more, tables, done)
        here, second = terms(part, sibling, far_more, tables, scale, done, True)
        own, chip, cross, core = own_terms(first, second, SRC // groups, scale)
        done = (core,) if t < blocks // 2 else ()
        back = lax.ppermute(sum_terms(here, there, *done), "chan", to_partner(t))
        chip = lax.ppermute(chip, "win", other_chip)
        cross = lax.ppermute(cross, "win", other_both)
        core = lax.ppermute(core, "win", other_core)
        return own, *keep(chip, cross, core, back)

    def by_round(run, *values):
        branches = [functools.partial(run, t) for t in range(1, blocks)]
        return lax.switch(partner[0, 0] - 1, branches, *values)

    tables = [jnp.asarray(v) for v in shift_tables(freqs)]
    taper = taper_row(two, freqs)
    piece = jax.ShapeDtypeStruct((windows, SRC // 4, two * freqs), jnp.bfloat16)
    sources = jax.ShapeDtypeStruct((windows, SRC, two * freqs), jnp.bfloat16)
    raw = pltpu.with_memory_space_constraint(spectra, pltpu.HBM)
    sources = whiten_sources([sources] + [piece] * 4, counts, fetch_sources(raw), taper)
    return place(*by_round(one_round, counts, raw, *sources))[None, None]


def lag_table(freqs, lags):
    freq = jnp.arange(freqs, dtype=jnp.float32) + freqs // 4
    delay = jnp.arange(lags, dtype=jnp.float32) - lags // 2
    phase = 2.0 * math.pi * freq[:, None] * delay[None, :] / (4.0 * freqs)
    norm = 1.0 / math.sqrt(2.0 * freqs)
    return jnp.stack([jnp.cos(phase), -jnp.sin(phase)]) * norm


def blended_sources(sources, table):
    src = sources.astype(jnp.float32)
    first = src[:, :, 0][:, :, None, :]
    second = src[:, :, 1][:, :, None, :]
    cos_part = table[0].T[None, None]
    sin_part = table[1].T[None, None]
    real_mix = first * cos_part + second * sin_part
    imag_mix = second * cos_part - first * sin_part
    return jnp.stack([real_mix, imag_mix], axis=3).astype(jnp.bfloat16)


def pair_terms(sources, receiver_blocks, table):
    wins, count, two, freqs = sources.shape
    lags = table.shape[2]
    group = math.gcd(count, 32)
    flat_recv = receiver_blocks.reshape(wins, receiver_blocks.shape[1], two * freqs)
    grouped = jnp.moveaxis(sources.reshape(wins, count // group, group, two, freqs), 1, 0)

    def one_group(piece):
        mixed_spectra = blended_sources(piece, table).reshape(wins, group * lags, two * freqs)
        out = jnp.einsum(
            "wmx,wrx->mr", mixed_spectra, flat_recv, preferred_element_type=jnp.float32
        )
        return out.reshape(group, lags, receiver_blocks.shape[1])

    out = lax.map(one_group, grouped).reshape(count, lags, receiver_blocks.shape[1])
    return jnp.transpose(out, (1, 0, 2))


def route_blocks(values, round_flags, levels):
    for level in range(levels):
        moved = from_partner(values, "chan", level)
        values = jnp.where((round_flags >> level) % 2 == 1, moved, values)
    return values


def general_body(spectra, counts, partner):
    white = whiten_local(spectra, counts[0])
    table = lag_table(spectra.shape[3], LAGS)
    levels = lax.axis_size("chan").bit_length() - 1
    windows = spectra.shape[0] * lax.axis_size("win")
    receiver_blocks = route_blocks(white, partner[0, 0], levels)
    out = pair_terms(white[:, :SRC], receiver_blocks, table)
    stacked = lax.psum_scatter(out, "win", scatter_dimension=1, tiled=True)
    return (stacked / math.sqrt(windows))[None, None]


def solution(mesh):
    body = pair_body if mesh.shape["win"] == 4 else general_body
    return jax.shard_map(
        body,
        mesh=mesh,
        in_specs=(P("win", "chan", None, None), P("chan"), P()),
        out_specs=P("chan", None, None, "win", None),
        check_vma=False,
    )
```

```python
import functools
import math

import jax
import jax.numpy as jnp
import numpy as np
from jax import lax
from jax.experimental import pallas as pl
from jax.experimental.pallas import tpu as pltpu
from jax.sharding import PartitionSpec as P

LAGS = 16
SRC = 160
HALF = LAGS // 2
VMEM_LIMIT = 16 * 1024 * 1024


def from_partner(value, axis, stride):
    return lax.ppermute(value, axis, [(i, i ^ 1 << stride) for i in range(lax.axis_size(axis))])


def whiten_local(spectra, count):
    values = spectra.astype(jnp.float32)
    block_size = spectra.shape[1]
    freqs = spectra.shape[3]
    valid = (jnp.arange(block_size, dtype=jnp.int32) < count).astype(jnp.float32)
    freq = jnp.arange(freqs, dtype=jnp.float32)
    taper = 0.75 - 0.25 * jnp.cos(2.0 * math.pi * (freq + 0.5) / freqs)
    power = jnp.mean(values * values, axis=(2, 3))
    scale = valid[None, :] / jnp.sqrt(power + 1e-05)
    return (values * taper * scale[:, :, None, None]).astype(jnp.bfloat16)


def shift_tables(freqs):
    freq = np.arange(freqs, dtype=np.float64) + freqs // 4
    shift = np.arange(1, HALF + 1, dtype=np.float64)
    phase = 2.0 * np.pi * shift[:, None] * freq[None, :] / (4.0 * freqs)
    return np.cos(phase).astype(np.float32), np.sin(phase).astype(np.float32)


def place_of_core():
    spot = lax.axis_index("win")
    return spot // 2, spot % 2


def whole():
    return pl.BlockSpec(memory_space=pltpu.VMEM)


def anywhere():
    return pl.BlockSpec(memory_space=pl.ANY)


def kernel_params():
    return pltpu.CompilerParams(vmem_limit_bytes=VMEM_LIMIT)


def fetch_kernel(source_ref, out_ref, sems):
    windows, channels = out_ref.shape[:2]
    parts = sems.shape[1]
    step = channels // parts
    copies = []
    for w in range(windows):
        for i in range(parts):
            part = (w, pl.ds(i * step, step))
            copies.append(
                pltpu.make_async_copy(source_ref.at[part], out_ref.at[part], sems.at[w, i])
            )
            copies[-1].start()
    for copy in copies:
        copy.wait()


def fetch_sources(spectra):
    windows, _, *rest = spectra.shape
    return pl.pallas_call(
        fetch_kernel,
        in_specs=[pl.BlockSpec(memory_space=pltpu.HBM)],
        out_specs=whole(),
        out_shape=jax.ShapeDtypeStruct((windows, SRC, *rest), spectra.dtype),
        scratch_shapes=[pltpu.SemaphoreType.DMA((windows, 4))],
        compiler_params=kernel_params(),
        name="fetch",
    )(spectra)


def white_block(raw_ref, taper_ref, count, w, line, first_row):
    values = raw_ref[w, line, :].astype(jnp.float32)
    rows, width = values.shape
    power = jnp.sum(values * values, axis=1, keepdims=True) * (1.0 / width)
    row = first_row + lax.broadcasted_iota(jnp.int32, (rows, 1), 0)
    valid = (row < count).astype(jnp.float32)
    scale = valid / jnp.sqrt(power + 1e-05)
    return values * taper_ref[...] * scale


def whiten_kernel(count_ref, raw_ref, taper_ref, white_ref, *refs):
    *piece_refs, count, sem = refs
    copy = pltpu.make_async_copy(count_ref, count, sem)
    copy.start()
    x, core = place_of_core()
    mine = SRC // 4
    step = 2 * mine
    copy.wait()

    @pl.loop(0, raw_ref.shape[0])
    def _(w):
        for index, group in enumerate((1 - x, x)):
            line = pl.ds(pl.multiple_of(group * step, step), step)
            values = white_block(raw_ref, taper_ref, count[0], w, line, group * step)
            white_ref[w, line, :] = values.astype(jnp.bfloat16)
            low, high = values[:mine], values[mine:]
            first = core == 0
            near_ref, far_ref = piece_refs[2 * index:2 * index + 2]
            near_ref[w] = jnp.where(first, low, high).astype(jnp.bfloat16)
            far_ref[w] = jnp.where(first, high, low).astype(jnp.bfloat16)


def rest_kernel(
    count_ref, spectra_ref, taper_ref, sources_ref, white_ref, raw_ref, count, sems
):
    windows, channels, two, freqs = raw_ref.shape
    copies = [pltpu.make_async_copy(count_ref, count, sems.at[windows])]
    for w in range(windows):
        part = spectra_ref.at[w, pl.ds(SRC, channels)]
        copies.append(pltpu.make_async_copy(part, raw_ref.at[w], sems.at[w]))
    for copy in copies:
        copy.start()
    step = 32

    @pl.loop(0, windows)
    def _(w):
        @pl.loop(0, SRC, step=step)
        def _(start):
            line = pl.ds(pl.multiple_of(start, step), step)
            white_ref[w, line, :] = sources_ref[w, line, :]

    for copy in copies:
        copy.wait()
    step = 16

    @pl.loop(0, windows)
    def _(w):
        @pl.loop(0, channels, step=step)
        def _(start):
            line = pl.ds(pl.multiple_of(start, step), step)
            parts = [raw_ref[w, line, p, :].astype(jnp.float32) for p in range(two)]
            power = sum(jnp.sum(v * v, axis=1, keepdims=True) for v in parts)
            row = SRC + start + lax.broadcasted_iota(jnp.int32, (step, 1), 0)
            valid = (row < count[0]).astype(jnp.float32)
            scale = valid / jnp.sqrt(power * (1.0 / (two * freqs)) + 1e-05)
            out = pl.ds(pl.multiple_of(SRC + start, step), step)
            for p, v in enumerate(parts):
                cols = slice(p * freqs, (p + 1) * freqs)
                white_ref[w, out, cols] = (v * taper_ref[:, cols] * scale).astype(jnp.bfloat16)


def whiten_rest(counts, spectra, taper, sources):
    windows, channels, two, freqs = spectra.shape
    return pl.pallas_call(
        rest_kernel,
        in_specs=[anywhere(), pl.BlockSpec(memory_space=pltpu.HBM), whole(), whole()],
        out_specs=whole(),
        out_shape=jax.ShapeDtypeStruct((windows, channels, two * freqs), jnp.bfloat16),
        scratch_shapes=[
            pltpu.VMEM((windows, channels - SRC, two, freqs), spectra.dtype),
            pltpu.SMEM((1,), jnp.int32),
            pltpu.SemaphoreType.DMA((windows + 1,)),
        ],
        compiler_params=kernel_params(),
        name="whiten_rest",
    )(counts, spectra, taper, sources)


def whiten_sources(out_shape, counts, raw, taper):
    windows, channels, two, freqs = raw.shape
    return pl.pallas_call(
        whiten_kernel,
        in_specs=[anywhere()] + [whole()] * 2,
        out_specs=[whole()] * len(out_shape),
        out_shape=out_shape,
        scratch_shapes=[pltpu.SMEM((1,), jnp.int32), pltpu.SemaphoreType.DMA],
        compiler_params=kernel_params(),
        name="whiten",
    )(counts, raw.reshape(windows, channels, two * freqs), taper)


def taper_row(two, freqs):
    freq = np.arange(freqs, dtype=np.float64)
    taper = 0.75 - 0.25 * np.cos(2.0 * np.pi * (freq + 0.5) / freqs)
    return jnp.asarray(np.tile(taper.astype(np.float32), two)[None, :])


def mix(m_ref, piece, cos_ref, sin_ref, low, high):
    rows = piece.shape[0]
    vrow = v_row(rows)
    real = piece[:, low].astype(jnp.float32)
    imag = piece[:, high].astype(jnp.float32)

    def put(where, cols, values):
        m_ref[where, cols] = jnp.concatenate(values, axis=0).astype(jnp.bfloat16)

    for m in range(0, HALF, 2):
        c = [cos_ref[m + i:m + i + 1, low] for i in range(2)]
        s = [sin_ref[m + i:m + i + 1, low] for i in range(2)]
        line = slice(m * rows, (m + 2) * rows)
        vline = slice(vrow + m * rows, vrow + (m + 2) * rows)
        put(line, low, [real * v for v in c])
        put(line, high, [imag * v for v in c])
        put(vline, low, [imag * -v for v in s])
        put(vline, high, [real * v for v in s])
    fill = jnp.zeros((vrow - (HALF + 1) * rows, 128), jnp.float32)
    for value, cols in ((real, low), (imag, high)):
        put(slice(HALF * rows, vrow), cols, [value, fill])


def v_row(rows):
    return -(-(HALF + 1) * rows // 128) * 128


def times(lhs, rhs):
    return lax.dot_general(
        lhs, rhs, (((1,), (1,)), ((), ())), preferred_element_type=jnp.float32
    )


def by_rows(count, run):
    @pl.loop(0, count, step=32)
    def _(start):
        run(pl.ds(pl.multiple_of(start, 32), 32))


def add_products(acc_ref, lhs_ref, piece_ref, cos_ref, sin_ref, mixed_ref):
    windows, rows, width = piece_ref.shape
    tile = 256
    used = v_row(rows) + HALF * rows
    if used < mixed_ref.shape[0]:
        mixed_ref[used:, :] = jnp.zeros_like(mixed_ref[used:, :])

    @pl.loop(0, windows)
    def _(w):
        @pl.loop(0, width // 2, step=128)
        def _(start):
            low = pl.ds(pl.multiple_of(start, 128), 128)
            high = pl.ds(pl.multiple_of(width // 2 + start, 128), 128)
            mix(mixed_ref, piece_ref.at[w], cos_ref, sin_ref, low, high)

        @pl.loop(0, mixed_ref.shape[0], step=tile)
        def _(n):
            cols = pl.ds(pl.multiple_of(n, tile), tile)
            acc_ref[:, cols] += times(lhs_ref[w], mixed_ref[cols, :])


def part_kernel(white_ref, piece_ref, cos_ref, sin_ref, _, part_ref, done_ref, mixed_ref):
    done_ref[...] = jnp.zeros_like(done_ref)

    def clear(line):
        part_ref[line, :] = jnp.zeros((32, part_ref.shape[1]), part_ref.dtype)

    by_rows(part_ref.shape[0], clear)
    add_products(part_ref, white_ref, piece_ref, cos_ref, sin_ref, mixed_ref)


def part_columns(rows):
    columns = v_row(rows) + HALF * rows
    return columns + (-columns) % 256


def part_terms(white, piece, tables, done):
    windows, channels, width = white.shape
    columns = part_columns(piece.shape[1])
    return pl.pallas_call(
        part_kernel,
        in_specs=[whole()] * 5,
        out_specs=[whole()] * 2,
        out_shape=[jax.ShapeDtypeStruct((channels, columns), jnp.float32), TOKEN],
        scratch_shapes=[pltpu.VMEM((columns, width), jnp.bfloat16)],
        compiler_params=kernel_params(),
        cost_estimate=COST,
        name="terms_part",
    )(white, piece, *tables, done)


TOKEN = jax.ShapeDtypeStruct((8, 128), jnp.float32)
COST = pl.CostEstimate(flops=30 * 10**9, bytes_accessed=0, transcendentals=0)


def pack(acc_ref, line, rows, scale, later):
    wide = HALF * rows
    vrow = v_row(rows)
    u, v = acc_ref[line, :wide] * scale, acc_ref[line, vrow:vrow + wide] * scale
    still = acc_ref[line, wide:wide + rows] * scale
    first, last = (u - v, u + v) if later else (u + v, u - v)
    return jnp.concatenate([first, last[:, :wide - rows], still], axis=1)


def terms_kernel(
    scale, part_ref, sibling_ref, piece_ref, cos_ref, sin_ref, _, back_ref, own_ref, *refs
):
    *done_refs, mixed_ref, acc_ref = refs
    for done_ref in done_refs:
        done_ref[...] = jnp.zeros_like(done_ref)

    def take(line):
        acc_ref[line, :] = part_ref[line, :]

    by_rows(acc_ref.shape[0], take)
    add_products(acc_ref, sibling_ref, piece_ref, cos_ref, sin_ref, mixed_ref)

    def write(line):
        behind = pl.ds(pl.multiple_of(SRC + line.start, 32), 32)
        back = pack(acc_ref, behind, piece_ref.shape[1], scale, True)
        back_ref[line, :] = back.astype(back_ref.dtype)
        own_ref[line, :] = acc_ref[line, :]

    by_rows(SRC, write)


def own_kernel(scale, rows, first_ref, second_ref, *refs):
    *out_refs, packed_ref = refs
    x, core = place_of_core()
    mine = SRC // 4

    @pl.loop(0, SRC, step=mine)
    def _(start):
        line = pl.ds(pl.multiple_of(start, 8), mine)
        for quarter, ref in enumerate((first_ref, second_ref)):
            packed_ref[quarter, line, :] = pack(ref, line, rows, scale, False)

    for i, out_ref in enumerate(out_refs):
        spot = 2 * (x, 1 - x, 1 - x, x)[i] + (core, core, 1 - core, 1 - core)[i]
        line = pl.ds(pl.multiple_of(spot * mine, 8), mine)

        @pl.loop(0, 2)
        def _(quarter):
            out_ref[quarter] = packed_ref[quarter, line, :].astype(out_ref.dtype)


def own_terms(first, second, rows, scale):
    mine, wide = SRC // 4, 2 * HALF * rows
    return pl.pallas_call(
        functools.partial(own_kernel, scale, rows),
        in_specs=[whole()] * 2,
        out_specs=[whole()] * 4,
        out_shape=[
            jax.ShapeDtypeStruct((2, mine, wide), jnp.float32 if i == 0 else jnp.bfloat16)
            for i in range(4)
        ],
        scratch_shapes=[pltpu.VMEM((2, SRC, wide), jnp.float32)],
        compiler_params=kernel_params(),
        name="own_terms",
    )(first, second)


def terms(part, sibling, piece, tables, scale, done, last):
    windows, channels, width = sibling.shape
    rows = piece.shape[1]
    columns = part_columns(rows)
    back = ((channels - SRC, 2 * HALF * rows), jnp.float32 if last else jnp.bfloat16)
    out = [jax.ShapeDtypeStruct(*back), jax.ShapeDtypeStruct((SRC, columns), jnp.float32)]
    out += [] if last else [TOKEN]
    return pl.pallas_call(
        functools.partial(terms_kernel, scale),
        in_specs=[whole()] * 6,
        out_specs=[whole()] * len(out),
        out_shape=out,
        scratch_shapes=[
            pltpu.VMEM((columns, width), jnp.bfloat16),
            pltpu.VMEM((channels, columns), jnp.float32),
        ],
        compiler_params=kernel_params(),
        cost_estimate=COST,
        name="terms",
    )(part, sibling, piece, *tables, done)


def sum_kernel(here_ref, there_ref, *refs):
    out_ref = refs[-1]

    def add(line):
        total = here_ref[line, :] + there_ref[line, :].astype(jnp.float32)
        out_ref[line, :] = total.astype(out_ref.dtype)

    by_rows(out_ref.shape[0], add)


def sum_terms(here, there, *done):
    return pl.pallas_call(
        sum_kernel,
        in_specs=[whole()] * (2 + len(done)),
        out_specs=whole(),
        out_shape=jax.ShapeDtypeStruct(there.shape, there.dtype),
        compiler_params=kernel_params(),
        name="sum_terms",
    )(here, there, *done)


def copy_rows(source_ref, out_ref):
    if len(source_ref.shape) == 3:

        @pl.loop(0, source_ref.shape[0])
        def _(i):
            out_ref[i] = source_ref[i]

    else:

        def copy(line):
            out_ref[line, :] = source_ref[line, :]

        by_rows(source_ref.shape[0], copy)


def keep_kernel(*refs):
    half = len(refs) // 2
    for source_ref, out_ref in zip(refs[:half], refs[half:]):
        copy_rows(source_ref, out_ref)


def hold_kernel(source_ref, *refs):
    *_, out_ref, done_ref = refs
    copy_rows(source_ref, out_ref)
    done_ref[...] = jnp.zeros_like(done_ref)


def keep(*values):
    return pl.pallas_call(
        keep_kernel,
        in_specs=[whole()] * len(values),
        out_specs=[whole()] * len(values),
        out_shape=[jax.ShapeDtypeStruct(v.shape, v.dtype) for v in values],
        compiler_params=kernel_params(),
        name="keep",
    )(*values)


def hold(value, *done):
    return pl.pallas_call(
        hold_kernel,
        in_specs=[whole()] * (1 + len(done)),
        out_specs=[whole()] * 2,
        out_shape=[jax.ShapeDtypeStruct(value.shape, value.dtype), TOKEN],
        compiler_params=kernel_params(),
        name="hold",
    )(value, *done)


def place_kernel(
    here_ref, chip_ref, cross_ref, core_ref, back_ref, out_ref, block_ref, sems
):
    x, core = place_of_core()
    lags, mine, channels = block_ref.shape
    swap = core != 0
    sides = []
    for q in range(2):
        index = jnp.where(x == q, 1, 0)
        own = here_ref[index] + chip_ref[1 - index].astype(jnp.float32)
        other = core_ref[index].astype(jnp.float32) + cross_ref[1 - index].astype(jnp.float32)
        sides += [jnp.where(swap, other, own), jnp.where(swap, own, other)]
    back = back_ref[...].astype(jnp.float32).T
    copies = []
    for j in range(lags):
        lag = HALF - 1 - j if j < HALF else j + 1 if j < lags - 1 else HALF
        cols = slice(j * mine, (j + 1) * mine)
        block_ref[lag, :, :SRC] = jnp.concatenate([v[:, cols] for v in sides], axis=1)
        block_ref[lag, :, SRC:] = back[cols]
        copies.append(pltpu.make_async_copy(block_ref.at[lag], out_ref.at[lag], sems.at[lag]))
        copies[-1].start()
    for copy in copies:
        copy.wait()


def place(here, chip, cross, core, back):
    _, mine, wide = here.shape
    shape = (wide // mine, mine, SRC + back.shape[0])
    return pl.pallas_call(
        place_kernel,
        in_specs=[whole()] * 5,
        out_specs=anywhere(),
        out_shape=jax.ShapeDtypeStruct(shape, jnp.float32),
        scratch_shapes=[
            pltpu.VMEM(shape, jnp.float32), pltpu.SemaphoreType.DMA((shape[0],))
        ],
        compiler_params=kernel_params(),
        name="place_lags",
    )(here, chip, cross, core, back)


def pair_body(spectra, counts, partner):
    blocks = lax.axis_size("chan")
    groups = lax.axis_size("win")
    windows, channels, two, freqs = spectra.shape
    scale = 1.0 / (math.sqrt(2.0 * freqs) * math.sqrt(windows * groups))
    other_core = [(i, i ^ 1) for i in range(groups)]
    other_chip = [(i, i ^ 2) for i in range(groups)]
    other_both = [(i, i ^ 3) for i in range(groups)]

    def to_partner(t):
        return [(i, i ^ t) for i in range(blocks)]

    def to_partner_core(t):
        return [
            (i * groups + g, (i ^ t) * groups + (g ^ 1))
            for i in range(blocks)
            for g in range(groups)
        ]

    def one_round(t, counts, raw, sources, near, far, near_more, far_more):
        def straight(value):
            return lax.ppermute(value, "chan", to_partner(t))

        def crossed(value):
            return lax.ppermute(value, ("chan", "win"), to_partner_core(t))

        near, far = straight(near), crossed(far)
        white = whiten_rest(counts, raw, taper, sources)
        sibling = lax.ppermute(white, "win", other_core)
        near_more, done = hold(near_more, near)
        near_more = straight(near_more)
        part, done = part_terms(white, near, tables, done)
        far_more, done = hold(far_more, far, done)
        far_more = crossed(far_more)
        there, first, done = terms(part, sibling, far, tables, scale, done, False)
        there = lax.ppermute(there, "win", other_chip)
        part, done = part_terms(white, near_more, tables, done)
        here, second = terms(part, sibling, far_more, tables, scale, done, True)
        own, chip, cross, core = own_terms(first, second, SRC // groups, scale)
        done = (core,) if t < blocks // 2 else ()
        back = lax.ppermute(sum_terms(here, there, *done), "chan", to_partner(t))
        chip = lax.ppermute(chip, "win", other_chip)
        cross = lax.ppermute(cross, "win", other_both)
        core = lax.ppermute(core, "win", other_core)
        return own, *keep(chip, cross, core, back)

    def by_round(run, *values):
        branches = [functools.partial(run, t) for t in range(1, blocks)]
        return lax.switch(partner[0, 0] - 1, branches, *values)

    tables = [jnp.asarray(v) for v in shift_tables(freqs)]
    taper = taper_row(two, freqs)
    piece = jax.ShapeDtypeStruct((windows, SRC // 4, two * freqs), jnp.bfloat16)
    sources = jax.ShapeDtypeStruct((windows, SRC, two * freqs), jnp.bfloat16)
    raw = pltpu.with_memory_space_constraint(spectra, pltpu.HBM)
    sources = whiten_sources([sources] + [piece] * 4, counts, fetch_sources(raw), taper)
    return place(*by_round(one_round, counts, raw, *sources))[None, None]


def lag_table(freqs, lags):
    freq = jnp.arange(freqs, dtype=jnp.float32) + freqs // 4
    delay = jnp.arange(lags, dtype=jnp.float32) - lags // 2
    phase = 2.0 * math.pi * freq[:, None] * delay[None, :] / (4.0 * freqs)
    norm = 1.0 / math.sqrt(2.0 * freqs)
    return jnp.stack([jnp.cos(phase), -jnp.sin(phase)]) * norm


def blended_sources(sources, table):
    src = sources.astype(jnp.float32)
    first = src[:, :, 0][:, :, None, :]
    second = src[:, :, 1][:, :, None, :]
    cos_part = table[0].T[None, None]
    sin_part = table[1].T[None, None]
    real_mix = first * cos_part + second * sin_part
    imag_mix = second * cos_part - first * sin_part
    return jnp.stack([real_mix, imag_mix], axis=3).astype(jnp.bfloat16)


def pair_terms(sources, receiver_blocks, table):
    wins, count, two, freqs = sources.shape
    lags = table.shape[2]
    group = math.gcd(count, 32)
    flat_recv = receiver_blocks.reshape(wins, receiver_blocks.shape[1], two * freqs)
    grouped = jnp.moveaxis(sources.reshape(wins, count // group, group, two, freqs), 1, 0)

    def one_group(piece):
        mixed_spectra = blended_sources(piece, table).reshape(wins, group * lags, two * freqs)
        out = jnp.einsum(
            "wmx,wrx->mr", mixed_spectra, flat_recv, preferred_element_type=jnp.float32
        )
        return out.reshape(group, lags, receiver_blocks.shape[1])

    out = lax.map(one_group, grouped).reshape(count, lags, receiver_blocks.shape[1])
    return jnp.transpose(out, (1, 0, 2))


def route_blocks(values, round_flags, levels):
    for level in range(levels):
        moved = from_partner(values, "chan", level)
        values = jnp.where((round_flags >> level) % 2 == 1, moved, values)
    return values


def general_body(spectra, counts, partner):
    white = whiten_local(spectra, counts[0])
    table = lag_table(spectra.shape[3], LAGS)
    levels = lax.axis_size("chan").bit_length() - 1
    windows = spectra.shape[0] * lax.axis_size("win")
    receiver_blocks = route_blocks(white, partner[0, 0], levels)
    out = pair_terms(white[:, :SRC], receiver_blocks, table)
    stacked = lax.psum_scatter(out, "win", scatter_dimension=1, tiled=True)
    return (stacked / math.sqrt(windows))[None, None]


def solution(mesh):
    body = pair_body if mesh.shape["win"] == 4 else general_body
    return jax.shard_map(
        body,
        mesh=mesh,
        in_specs=(P("win", "chan", None, None), P("chan"), P()),
        out_specs=P("chan", None, None, "win", None),
        check_vma=False,
    )
```

```python
import functools
import math

import jax
import jax.numpy as jnp
import numpy as np
from jax import lax
from jax.experimental import pallas as pl
from jax.experimental.pallas import tpu as pltpu
from jax.sharding import PartitionSpec as P

LAGS = 16
SRC = 160
HALF = LAGS // 2
VMEM_LIMIT = 16 * 1024 * 1024


def from_partner(value, axis, stride):
    return lax.ppermute(value, axis, [(i, i ^ 1 << stride) for i in range(lax.axis_size(axis))])


def whiten_local(spectra, count):
    values = spectra.astype(jnp.float32)
    block_size = spectra.shape[1]
    freqs = spectra.shape[3]
    valid = (jnp.arange(block_size, dtype=jnp.int32) < count).astype(jnp.float32)
    freq = jnp.arange(freqs, dtype=jnp.float32)
    taper = 0.75 - 0.25 * jnp.cos(2.0 * math.pi * (freq + 0.5) / freqs)
    power = jnp.mean(values * values, axis=(2, 3))
    scale = valid[None, :] / jnp.sqrt(power + 1e-05)
    return (values * taper * scale[:, :, None, None]).astype(jnp.bfloat16)


def shift_tables(freqs):
    freq = np.arange(freqs, dtype=np.float64) + freqs // 4
    shift = np.arange(1, HALF + 1, dtype=np.float64)
    phase = 2.0 * np.pi * shift[:, None] * freq[None, :] / (4.0 * freqs)
    return np.cos(phase).astype(np.float32), np.sin(phase).astype(np.float32)


def place_of_core():
    spot = lax.axis_index("win")
    return spot // 2, spot % 2


def whole():
    return pl.BlockSpec(memory_space=pltpu.VMEM)


def anywhere():
    return pl.BlockSpec(memory_space=pl.ANY)


def kernel_params():
    return pltpu.CompilerParams(vmem_limit_bytes=VMEM_LIMIT)


def fetch_kernel(source_ref, out_ref, sems):
    windows, channels = out_ref.shape[:2]
    parts = sems.shape[1]
    step = channels // parts
    copies = []
    for w in range(windows):
        for i in range(parts):
            part = (w, pl.ds(i * step, step))
            copies.append(
                pltpu.make_async_copy(source_ref.at[part], out_ref.at[part], sems.at[w, i])
            )
            copies[-1].start()
    for copy in copies:
        copy.wait()


def fetch_sources(spectra):
    windows, _, *rest = spectra.shape
    return pl.pallas_call(
        fetch_kernel,
        in_specs=[pl.BlockSpec(memory_space=pltpu.HBM)],
        out_specs=whole(),
        out_shape=jax.ShapeDtypeStruct((windows, SRC, *rest), spectra.dtype),
        scratch_shapes=[pltpu.SemaphoreType.DMA((windows, 4))],
        compiler_params=kernel_params(),
        name="fetch",
    )(spectra)


def white_block(raw_ref, taper_ref, count, w, line, first_row):
    values = raw_ref[w, line, :].astype(jnp.float32)
    rows, width = values.shape
    power = jnp.sum(values * values, axis=1, keepdims=True) * (1.0 / width)
    row = first_row + lax.broadcasted_iota(jnp.int32, (rows, 1), 0)
    valid = (row < count).astype(jnp.float32)
    scale = valid / jnp.sqrt(power + 1e-05)
    return values * taper_ref[...] * scale


def whiten_kernel(count_ref, raw_ref, taper_ref, white_ref, *refs):
    *piece_refs, count, sem = refs
    copy = pltpu.make_async_copy(count_ref, count, sem)
    copy.start()
    x, core = place_of_core()
    mine = SRC // 4
    step = 2 * mine
    copy.wait()
    for w in range(raw_ref.shape[0]):
        for index, group in enumerate((1 - x, x)):
            line = pl.ds(pl.multiple_of(group * step, step), step)
            values = white_block(raw_ref, taper_ref, count[0], w, line, group * step)
            white_ref[w, line, :] = values.astype(jnp.bfloat16)
            low, high = values[:mine], values[mine:]
            first = core == 0
            near_ref, far_ref = piece_refs[2 * index:2 * index + 2]
            near_ref[w] = jnp.where(first, low, high).astype(jnp.bfloat16)
            far_ref[w] = jnp.where(first, high, low).astype(jnp.bfloat16)


def rest_kernel(
    count_ref, spectra_ref, taper_ref, sources_ref, white_ref, raw_ref, count, sems
):
    windows, channels, two, freqs = raw_ref.shape
    copies = [pltpu.make_async_copy(count_ref, count, sems.at[windows])]
    for w in range(windows):
        part = spectra_ref.at[w, pl.ds(SRC, channels)]
        copies.append(pltpu.make_async_copy(part, raw_ref.at[w], sems.at[w]))
    for copy in copies:
        copy.start()
    step = 32

    @pl.loop(0, windows)
    def _(w):
        @pl.loop(0, SRC, step=step)
        def _(start):
            line = pl.ds(pl.multiple_of(start, step), step)
            white_ref[w, line, :] = sources_ref[w, line, :]

    for copy in copies:
        copy.wait()

    @pl.loop(0, windows)
    def _(w):
        @pl.loop(0, channels, step=step)
        def _(start):
            line = pl.ds(pl.multiple_of(start, step), step)
            parts = [raw_ref[w, line, p, :].astype(jnp.float32) for p in range(two)]
            power = sum(jnp.sum(v * v, axis=1, keepdims=True) for v in parts)
            row = SRC + start + lax.broadcasted_iota(jnp.int32, (step, 1), 0)
            valid = (row < count[0]).astype(jnp.float32)
            scale = valid / jnp.sqrt(power * (1.0 / (two * freqs)) + 1e-05)
            out = pl.ds(pl.multiple_of(SRC + start, step), step)
            for p, v in enumerate(parts):
                cols = slice(p * freqs, (p + 1) * freqs)
                white_ref[w, out, cols] = (v * taper_ref[:, cols] * scale).astype(jnp.bfloat16)


def whiten_rest(counts, spectra, taper, sources):
    windows, channels, two, freqs = spectra.shape
    return pl.pallas_call(
        rest_kernel,
        in_specs=[anywhere(), pl.BlockSpec(memory_space=pltpu.HBM), whole(), whole()],
        out_specs=whole(),
        out_shape=jax.ShapeDtypeStruct((windows, channels, two * freqs), jnp.bfloat16),
        scratch_shapes=[
            pltpu.VMEM((windows, channels - SRC, two, freqs), spectra.dtype),
            pltpu.SMEM((1,), jnp.int32),
            pltpu.SemaphoreType.DMA((windows + 1,)),
        ],
        compiler_params=kernel_params(),
        name="whiten_rest",
    )(counts, spectra, taper, sources)


def whiten_sources(out_shape, counts, raw, taper):
    windows, channels, two, freqs = raw.shape
    return pl.pallas_call(
        whiten_kernel,
        in_specs=[anywhere()] + [whole()] * 2,
        out_specs=[whole()] * len(out_shape),
        out_shape=out_shape,
        scratch_shapes=[pltpu.SMEM((1,), jnp.int32), pltpu.SemaphoreType.DMA],
        compiler_params=kernel_params(),
        name="whiten",
    )(counts, raw.reshape(windows, channels, two * freqs), taper)


def taper_row(two, freqs):
    freq = np.arange(freqs, dtype=np.float64)
    taper = 0.75 - 0.25 * np.cos(2.0 * np.pi * (freq + 0.5) / freqs)
    return jnp.asarray(np.tile(taper.astype(np.float32), two)[None, :])


def mix(m_ref, piece, cos_ref, sin_ref, low, high):
    rows = piece.shape[0]
    vrow = v_row(rows)
    real = piece[:, low].astype(jnp.float32)
    imag = piece[:, high].astype(jnp.float32)

    def put(where, cols, values):
        m_ref[where, cols] = jnp.concatenate(values, axis=0).astype(jnp.bfloat16)

    for m in range(0, HALF, 2):
        c = [cos_ref[m + i:m + i + 1, low] for i in range(2)]
        s = [sin_ref[m + i:m + i + 1, low] for i in range(2)]
        line = slice(m * rows, (m + 2) * rows)
        vline = slice(vrow + m * rows, vrow + (m + 2) * rows)
        put(line, low, [real * v for v in c])
        put(line, high, [imag * v for v in c])
        put(vline, low, [imag * -v for v in s])
        put(vline, high, [real * v for v in s])
    fill = jnp.zeros((vrow - (HALF + 1) * rows, 128), jnp.float32)
    for value, cols in ((real, low), (imag, high)):
        put(slice(HALF * rows, vrow), cols, [value, fill])


def v_row(rows):
    return -(-(HALF + 1) * rows // 128) * 128


def times(lhs, rhs):
    return lax.dot_general(
        lhs, rhs, (((1,), (1,)), ((), ())), preferred_element_type=jnp.float32
    )


def add_products(acc_ref, lhs_ref, piece_ref, cos_ref, sin_ref, mixed_ref):
    windows, rows, width = piece_ref.shape
    tile = 256
    used = v_row(rows) + HALF * rows
    if used < mixed_ref.shape[0]:
        mixed_ref[used:, :] = jnp.zeros_like(mixed_ref[used:, :])

    @pl.loop(0, windows)
    def _(w):
        @pl.loop(0, width // 2, step=128)
        def _(start):
            low = pl.ds(pl.multiple_of(start, 128), 128)
            high = pl.ds(pl.multiple_of(width // 2 + start, 128), 128)
            mix(mixed_ref, piece_ref.at[w], cos_ref, sin_ref, low, high)

        @pl.loop(0, mixed_ref.shape[0], step=tile)
        def _(n):
            cols = pl.ds(pl.multiple_of(n, tile), tile)
            acc_ref[:, cols] += times(lhs_ref[w], mixed_ref[cols, :])


def part_kernel(white_ref, piece_ref, cos_ref, sin_ref, _, part_ref, done_ref, mixed_ref):
    done_ref[...] = jnp.zeros_like(done_ref)
    part_ref[...] = jnp.zeros_like(part_ref)
    add_products(part_ref, white_ref, piece_ref, cos_ref, sin_ref, mixed_ref)


def part_columns(rows):
    columns = v_row(rows) + HALF * rows
    return columns + (-columns) % 256


def part_terms(white, piece, tables, done):
    windows, channels, width = white.shape
    columns = part_columns(piece.shape[1])
    return pl.pallas_call(
        part_kernel,
        in_specs=[whole()] * 5,
        out_specs=[whole()] * 2,
        out_shape=[jax.ShapeDtypeStruct((channels, columns), jnp.float32), TOKEN],
        scratch_shapes=[pltpu.VMEM((columns, width), jnp.bfloat16)],
        compiler_params=kernel_params(),
        cost_estimate=LATE,
        name="terms_part",
    )(white, piece, *tables, done)


TOKEN = jax.ShapeDtypeStruct((8, 128), jnp.float32)
LATE = pl.CostEstimate(flops=30 * 10**9, bytes_accessed=0, transcendentals=0)


def pack(acc_ref, line, rows, scale, later):
    wide = HALF * rows
    vrow = v_row(rows)
    u, v = acc_ref[line, :wide] * scale, acc_ref[line, vrow:vrow + wide] * scale
    still = acc_ref[line, wide:wide + rows] * scale
    first, last = (u - v, u + v) if later else (u + v, u - v)
    return jnp.concatenate([first, last[:, :wide - rows], still], axis=1)


def first_kernel(
    scale, part_ref, sibling_ref, piece_ref, cos_ref, sin_ref, _, back_ref, own_ref,
    done_ref, mixed_ref, acc_ref,
):
    done_ref[...] = jnp.zeros_like(done_ref)
    acc_ref[...] = part_ref[...]
    add_products(acc_ref, sibling_ref, piece_ref, cos_ref, sin_ref, mixed_ref)
    line = pl.ds(SRC, acc_ref.shape[0] - SRC)
    back = pack(acc_ref, line, piece_ref.shape[1], scale, True)
    back_ref[...] = back.astype(back_ref.dtype)
    own_ref[...] = acc_ref[:SRC, :]


def second_kernel(scale, part_ref, sibling_ref, piece_ref, cos_ref, sin_ref, *refs):
    back_ref, own_ref, even_ref, odd_ref, acc_ref = refs
    windows, rows, width = piece_ref.shape
    freqs = width // 2
    starts = [
        (slice(n, n + 128), slice(freqs + n, freqs + n + 128)) for n in range(0, freqs, 128)
    ]
    tiles = [
        slice(n, min(n + 256, acc_ref.shape[1])) for n in range(0, acc_ref.shape[1], 256)
    ]
    buffers = even_ref, odd_ref
    for start in starts:
        mix(even_ref, piece_ref.at[0], cos_ref, sin_ref, *start)
    for w in range(windows):
        now_ref, next_ref = buffers[w % 2], buffers[1 - w % 2]
        todo = starts if w + 1 < windows else []
        for cols in tiles:
            before = part_ref[:, cols] if w == 0 else acc_ref[:, cols]
            acc_ref[:, cols] = before + times(sibling_ref[w], now_ref[cols, :])
            for start in todo[:2]:
                mix(next_ref, piece_ref.at[w + 1], cos_ref, sin_ref, *start)
            todo = todo[2:]
    back_ref[...] = pack(acc_ref, pl.ds(SRC, acc_ref.shape[0] - SRC), rows, scale, True)
    own_ref[...] = acc_ref[:SRC, :]


def own_kernel(scale, rows, first_ref, second_ref, *refs):
    *out_refs, packed_ref = refs
    x, core = place_of_core()
    mine = SRC // 4

    @pl.loop(0, SRC, step=mine)
    def _(start):
        line = pl.ds(pl.multiple_of(start, 8), mine)
        for quarter, ref in enumerate((first_ref, second_ref)):
            packed_ref[quarter, line, :] = pack(ref, line, rows, scale, False)

    for i, out_ref in enumerate(out_refs):
        spot = 2 * (x, 1 - x, 1 - x, x)[i] + (core, core, 1 - core, 1 - core)[i]
        line = pl.ds(pl.multiple_of(spot * mine, 8), mine)
        for quarter in range(2):
            out_ref[quarter] = packed_ref[quarter, line, :].astype(out_ref.dtype)


def own_terms(first, second, rows, scale):
    mine, wide = SRC // 4, 2 * HALF * rows
    return pl.pallas_call(
        functools.partial(own_kernel, scale, rows),
        in_specs=[whole()] * 2,
        out_specs=[whole()] * 4,
        out_shape=[
            jax.ShapeDtypeStruct((2, mine, wide), jnp.float32 if i == 0 else jnp.bfloat16)
            for i in range(4)
        ],
        scratch_shapes=[pltpu.VMEM((2, SRC, wide), jnp.float32)],
        compiler_params=kernel_params(),
        name="own_terms",
    )(first, second)


def terms(part, sibling, piece, tables, scale, done=None):
    windows, channels, width = sibling.shape
    rows = piece.shape[1]
    second = done is None
    columns = v_row(rows) + HALF * rows if second else part_columns(rows)
    back = ((channels - SRC, 2 * HALF * rows), jnp.float32 if second else jnp.bfloat16)
    out = [jax.ShapeDtypeStruct(*back), jax.ShapeDtypeStruct((SRC, columns), jnp.float32)]
    out += [] if second else [TOKEN]
    more = () if second else (done,)
    return pl.pallas_call(
        functools.partial(second_kernel if second else first_kernel, scale),
        in_specs=[whole()] * (5 + len(more)),
        out_specs=[whole()] * len(out),
        out_shape=out,
        scratch_shapes=[pltpu.VMEM((columns, width), jnp.bfloat16)] * (2 if second else 1)
        + [pltpu.VMEM((channels, columns), jnp.float32)],
        compiler_params=kernel_params(),
        cost_estimate=LATE,
        name="terms_second" if second else "terms_first",
    )(part, sibling, piece, *tables, *more)


def copy_rows(source_ref, out_ref):
    rows = source_ref.shape[-2]
    if rows % 4:
        out_ref[...] = source_ref[...]
        return
    step = rows // 4 if rows % 64 == 0 else rows

    @pl.loop(0, rows, step=step)
    def _(start):
        line = pl.ds(pl.multiple_of(start, 16 if step % 16 == 0 else 8), step)
        out_ref[..., line, :] = source_ref[..., line, :]


def keep_kernel(*refs):
    half = len(refs) // 2
    for source_ref, out_ref in zip(refs[:half], refs[half:]):
        copy_rows(source_ref, out_ref)


def hold_kernel(source_ref, *refs):
    *_, out_ref, done_ref = refs
    copy_rows(source_ref, out_ref)
    done_ref[...] = jnp.zeros_like(done_ref)


def keep(*values):
    return pl.pallas_call(
        keep_kernel,
        in_specs=[whole()] * len(values),
        out_specs=[whole()] * len(values),
        out_shape=[jax.ShapeDtypeStruct(v.shape, v.dtype) for v in values],
        compiler_params=kernel_params(),
        name="keep",
    )(*values)


def hold(value, *done):
    return pl.pallas_call(
        hold_kernel,
        in_specs=[whole()] * (1 + len(done)),
        out_specs=[whole()] * 2,
        out_shape=[jax.ShapeDtypeStruct(value.shape, value.dtype), TOKEN],
        compiler_params=kernel_params(),
        name="hold",
    )(value, *done)


def keep_after(value, done):
    return pl.pallas_call(
        lambda source_ref, _, out_ref: copy_rows(source_ref, out_ref),
        in_specs=[whole()] * 2,
        out_specs=whole(),
        out_shape=jax.ShapeDtypeStruct(value.shape, value.dtype),
        compiler_params=kernel_params(),
        name="keep_after",
    )(value, done)


def place_kernel(
    here_ref, chip_ref, cross_ref, core_ref, back_ref, out_ref, block_ref, sems
):
    x, core = place_of_core()
    lags, mine, channels = block_ref.shape
    swap = core != 0
    sides = []
    for q in range(2):
        index = jnp.where(x == q, 1, 0)
        own = here_ref[index] + chip_ref[1 - index].astype(jnp.float32)
        other = core_ref[index].astype(jnp.float32) + cross_ref[1 - index].astype(jnp.float32)
        sides += [jnp.where(swap, other, own), jnp.where(swap, own, other)]
    back = back_ref[...].astype(jnp.float32).T
    copies = []
    for j in range(lags):
        lag = HALF - 1 - j if j < HALF else j + 1 if j < lags - 1 else HALF
        cols = slice(j * mine, (j + 1) * mine)
        block_ref[lag, :, :SRC] = jnp.concatenate([v[:, cols] for v in sides], axis=1)
        block_ref[lag, :, SRC:] = back[cols]
        copies.append(pltpu.make_async_copy(block_ref.at[lag], out_ref.at[lag], sems.at[lag]))
        copies[-1].start()
    for copy in copies:
        copy.wait()


def place(here, chip, cross, core, back):
    _, mine, wide = here.shape
    shape = (wide // mine, mine, SRC + back.shape[0])
    return pl.pallas_call(
        place_kernel,
        in_specs=[whole()] * 5,
        out_specs=anywhere(),
        out_shape=jax.ShapeDtypeStruct(shape, jnp.float32),
        scratch_shapes=[
            pltpu.VMEM(shape, jnp.float32), pltpu.SemaphoreType.DMA((shape[0],))
        ],
        compiler_params=kernel_params(),
        name="place_lags",
    )(here, chip, cross, core, back)


def pair_body(spectra, counts, partner):
    blocks = lax.axis_size("chan")
    groups = lax.axis_size("win")
    windows, channels, two, freqs = spectra.shape
    scale = 1.0 / (math.sqrt(2.0 * freqs) * math.sqrt(windows * groups))
    other_core = [(i, i ^ 1) for i in range(groups)]
    other_chip = [(i, i ^ 2) for i in range(groups)]
    other_both = [(i, i ^ 3) for i in range(groups)]

    def to_partner(t):
        return [(i, i ^ t) for i in range(blocks)]

    def to_partner_core(t):
        return [
            (i * groups + g, (i ^ t) * groups + (g ^ 1))
            for i in range(blocks)
            for g in range(groups)
        ]

    def send_sources(t, counts, raw, sources, near, far, near_more, far_more):
        def straight(value):
            return lax.ppermute(value, "chan", to_partner(t))

        def crossed(value):
            return lax.ppermute(value, ("chan", "win"), to_partner_core(t))

        near, far = straight(near), crossed(far)
        white = whiten_rest(counts, raw, taper, sources)
        sibling = lax.ppermute(white, "win", other_core)
        near_more, done = hold(near_more, near)
        near_more = straight(near_more)
        part, done = part_terms(white, near, tables, done)
        far_more, done = hold(far_more, far, done)
        far_more = crossed(far_more)
        back, own, done = terms(part, sibling, far, tables, scale, done)
        back = lax.ppermute(back, "win", other_chip)
        part, done = part_terms(white, near_more, tables, done)
        return part, *keep(sibling), keep_after(far_more, done), *keep(back), own

    def send_terms(t, back, first, second):
        back = lax.ppermute(back, "chan", to_partner(t))
        here, chip, cross, core = own_terms(first, second, SRC // groups, scale)
        chip = lax.ppermute(chip, "win", other_chip)
        cross = lax.ppermute(cross, "win", other_both)
        core = lax.ppermute(core, "win", other_core)
        return here, *keep(chip, cross, core, back)

    def by_round(run, *values):
        branches = [functools.partial(run, t) for t in range(1, blocks)]
        return lax.switch(partner[0, 0] - 1, branches, *values)

    tables = [jnp.asarray(v) for v in shift_tables(freqs)]
    taper = taper_row(two, freqs)
    piece = jax.ShapeDtypeStruct((windows, SRC // 4, two * freqs), jnp.bfloat16)
    sources = jax.ShapeDtypeStruct((windows, SRC, two * freqs), jnp.bfloat16)
    raw = pltpu.with_memory_space_constraint(spectra, pltpu.HBM)
    sources = whiten_sources([sources] + [piece] * 4, counts, fetch_sources(raw), taper)
    part, sibling, piece, back_recv, first = by_round(send_sources, counts, raw, *sources)
    back, second = terms(part, sibling, piece, tables, scale)
    back = (back + back_recv.astype(jnp.float32)).astype(jnp.bfloat16)
    return place(*by_round(send_terms, back, first, second))[None, None]


def lag_table(freqs, lags):
    freq = jnp.arange(freqs, dtype=jnp.float32) + freqs // 4
    delay = jnp.arange(lags, dtype=jnp.float32) - lags // 2
    phase = 2.0 * math.pi * freq[:, None] * delay[None, :] / (4.0 * freqs)
    norm = 1.0 / math.sqrt(2.0 * freqs)
    return jnp.stack([jnp.cos(phase), -jnp.sin(phase)]) * norm


def blended_sources(sources, table):
    src = sources.astype(jnp.float32)
    first = src[:, :, 0][:, :, None, :]
    second = src[:, :, 1][:, :, None, :]
    cos_part = table[0].T[None, None]
    sin_part = table[1].T[None, None]
    real_mix = first * cos_part + second * sin_part
    imag_mix = second * cos_part - first * sin_part
    return jnp.stack([real_mix, imag_mix], axis=3).astype(jnp.bfloat16)


def pair_terms(sources, receiver_blocks, table):
    wins, count, two, freqs = sources.shape
    lags = table.shape[2]
    group = math.gcd(count, 32)
    flat_recv = receiver_blocks.reshape(wins, receiver_blocks.shape[1], two * freqs)
    grouped = jnp.moveaxis(sources.reshape(wins, count // group, group, two, freqs), 1, 0)

    def one_group(piece):
        mixed_spectra = blended_sources(piece, table).reshape(wins, group * lags, two * freqs)
        out = jnp.einsum(
            "wmx,wrx->mr", mixed_spectra, flat_recv, preferred_element_type=jnp.float32
        )
        return out.reshape(group, lags, receiver_blocks.shape[1])

    out = lax.map(one_group, grouped).reshape(count, lags, receiver_blocks.shape[1])
    return jnp.transpose(out, (1, 0, 2))


def route_blocks(values, round_flags, levels):
    for level in range(levels):
        moved = from_partner(values, "chan", level)
        values = jnp.where((round_flags >> level) % 2 == 1, moved, values)
    return values


def general_body(spectra, counts, partner):
    white = whiten_local(spectra, counts[0])
    table = lag_table(spectra.shape[3], LAGS)
    levels = lax.axis_size("chan").bit_length() - 1
    windows = spectra.shape[0] * lax.axis_size("win")
    receiver_blocks = route_blocks(white, partner[0, 0], levels)
    out = pair_terms(white[:, :SRC], receiver_blocks, table)
    stacked = lax.psum_scatter(out, "win", scatter_dimension=1, tiled=True)
    return (stacked / math.sqrt(windows))[None, None]


def solution(mesh):
    body = pair_body if mesh.shape["win"] == 4 else general_body
    return jax.shard_map(
        body,
        mesh=mesh,
        in_specs=(P("win", "chan", None, None), P("chan"), P()),
        out_specs=P("chan", None, None, "win", None),
        check_vma=False,
    )
```

```python
import functools
import math

import jax
import jax.numpy as jnp
import numpy as np
from jax import lax
from jax.experimental import pallas as pl
from jax.experimental.pallas import tpu as pltpu
from jax.sharding import PartitionSpec as P

LAGS = 16
SRC = 160
HALF = LAGS // 2
VMEM_LIMIT = 16 * 1024 * 1024


def from_partner(value, axis, stride):
    return lax.ppermute(value, axis, [(i, i ^ 1 << stride) for i in range(lax.axis_size(axis))])


def whiten_local(spectra, count):
    values = spectra.astype(jnp.float32)
    block_size = spectra.shape[1]
    freqs = spectra.shape[3]
    valid = (jnp.arange(block_size, dtype=jnp.int32) < count).astype(jnp.float32)
    freq = jnp.arange(freqs, dtype=jnp.float32)
    taper = 0.75 - 0.25 * jnp.cos(2.0 * math.pi * (freq + 0.5) / freqs)
    power = jnp.mean(values * values, axis=(2, 3))
    scale = valid[None, :] / jnp.sqrt(power + 1e-05)
    return (values * taper * scale[:, :, None, None]).astype(jnp.bfloat16)


def shift_tables(freqs):
    freq = np.arange(freqs, dtype=np.float64) + freqs // 4
    shift = np.arange(1, HALF + 1, dtype=np.float64)
    phase = 2.0 * np.pi * shift[:, None] * freq[None, :] / (4.0 * freqs)
    return np.cos(phase).astype(np.float32), np.sin(phase).astype(np.float32)


def place_of_core():
    spot = lax.axis_index("win")
    return spot // 2, spot % 2


def whole():
    return pl.BlockSpec(memory_space=pltpu.VMEM)


def anywhere():
    return pl.BlockSpec(memory_space=pl.ANY)


def kernel_params():
    return pltpu.CompilerParams(vmem_limit_bytes=VMEM_LIMIT)


def fetch_kernel(source_ref, out_ref, sems):
    windows, channels = out_ref.shape[:2]
    parts = sems.shape[1]
    step = channels // parts
    copies = []
    for w in range(windows):
        for i in range(parts):
            part = (w, pl.ds(i * step, step))
            copies.append(
                pltpu.make_async_copy(source_ref.at[part], out_ref.at[part], sems.at[w, i])
            )
            copies[-1].start()
    for copy in copies:
        copy.wait()


def fetch_sources(spectra):
    windows, _, *rest = spectra.shape
    return pl.pallas_call(
        fetch_kernel,
        in_specs=[pl.BlockSpec(memory_space=pltpu.HBM)],
        out_specs=whole(),
        out_shape=jax.ShapeDtypeStruct((windows, SRC, *rest), spectra.dtype),
        scratch_shapes=[pltpu.SemaphoreType.DMA((windows, 4))],
        compiler_params=kernel_params(),
        name="fetch",
    )(spectra)


def white_block(raw_ref, taper_ref, count, w, line, first_row):
    values = raw_ref[w, line, :].astype(jnp.float32)
    rows, width = values.shape
    power = jnp.sum(values * values, axis=1, keepdims=True) * (1.0 / width)
    row = first_row + lax.broadcasted_iota(jnp.int32, (rows, 1), 0)
    valid = (row < count).astype(jnp.float32)
    scale = valid / jnp.sqrt(power + 1e-05)
    return values * taper_ref[...] * scale


def whiten_kernel(count_ref, raw_ref, taper_ref, white_ref, *refs):
    *piece_refs, count, sem = refs
    copy = pltpu.make_async_copy(count_ref, count, sem)
    copy.start()
    x, core = place_of_core()
    mine = SRC // 4
    step = 2 * mine
    copy.wait()
    for w in range(raw_ref.shape[0]):
        for index, group in enumerate((1 - x, x)):
            line = pl.ds(pl.multiple_of(group * step, step), step)
            values = white_block(raw_ref, taper_ref, count[0], w, line, group * step)
            white_ref[w, line, :] = values.astype(jnp.bfloat16)
            low, high = values[:mine], values[mine:]
            first = core == 0
            near_ref, far_ref = piece_refs[2 * index:2 * index + 2]
            near_ref[w] = jnp.where(first, low, high).astype(jnp.bfloat16)
            far_ref[w] = jnp.where(first, high, low).astype(jnp.bfloat16)


def rest_kernel(
    count_ref, spectra_ref, taper_ref, sources_ref, white_ref, raw_ref, count, sems
):
    windows, channels, two, freqs = raw_ref.shape
    copies = [pltpu.make_async_copy(count_ref, count, sems.at[windows])]
    for w in range(windows):
        part = spectra_ref.at[w, pl.ds(SRC, channels)]
        copies.append(pltpu.make_async_copy(part, raw_ref.at[w], sems.at[w]))
    for copy in copies:
        copy.start()
    step = 32

    @pl.loop(0, windows)
    def _(w):
        @pl.loop(0, SRC, step=step)
        def _(start):
            line = pl.ds(pl.multiple_of(start, step), step)
            white_ref[w, line, :] = sources_ref[w, line, :]

    for copy in copies:
        copy.wait()

    @pl.loop(0, windows)
    def _(w):
        @pl.loop(0, channels, step=step)
        def _(start):
            line = pl.ds(pl.multiple_of(start, step), step)
            parts = [raw_ref[w, line, p, :].astype(jnp.float32) for p in range(two)]
            power = sum(jnp.sum(v * v, axis=1, keepdims=True) for v in parts)
            row = SRC + start + lax.broadcasted_iota(jnp.int32, (step, 1), 0)
            valid = (row < count[0]).astype(jnp.float32)
            scale = valid / jnp.sqrt(power * (1.0 / (two * freqs)) + 1e-05)
            out = pl.ds(pl.multiple_of(SRC + start, step), step)
            for p, v in enumerate(parts):
                cols = slice(p * freqs, (p + 1) * freqs)
                white_ref[w, out, cols] = (v * taper_ref[:, cols] * scale).astype(jnp.bfloat16)


def whiten_rest(counts, spectra, taper, sources):
    windows, channels, two, freqs = spectra.shape
    return pl.pallas_call(
        rest_kernel,
        in_specs=[anywhere(), pl.BlockSpec(memory_space=pltpu.HBM), whole(), whole()],
        out_specs=whole(),
        out_shape=jax.ShapeDtypeStruct((windows, channels, two * freqs), jnp.bfloat16),
        scratch_shapes=[
            pltpu.VMEM((windows, channels - SRC, two, freqs), spectra.dtype),
            pltpu.SMEM((1,), jnp.int32),
            pltpu.SemaphoreType.DMA((windows + 1,)),
        ],
        compiler_params=kernel_params(),
        name="whiten_rest",
    )(counts, spectra, taper, sources)


def whiten_sources(out_shape, counts, raw, taper):
    windows, channels, two, freqs = raw.shape
    return pl.pallas_call(
        whiten_kernel,
        in_specs=[anywhere()] + [whole()] * 2,
        out_specs=[whole()] * len(out_shape),
        out_shape=out_shape,
        scratch_shapes=[pltpu.SMEM((1,), jnp.int32), pltpu.SemaphoreType.DMA],
        compiler_params=kernel_params(),
        name="whiten",
    )(counts, raw.reshape(windows, channels, two * freqs), taper)


def taper_row(two, freqs):
    freq = np.arange(freqs, dtype=np.float64)
    taper = 0.75 - 0.25 * np.cos(2.0 * np.pi * (freq + 0.5) / freqs)
    return jnp.asarray(np.tile(taper.astype(np.float32), two)[None, :])


def mix(m_ref, piece, cos_ref, sin_ref, low, high):
    rows = piece.shape[0]
    vrow = v_row(rows)
    real = piece[:, low].astype(jnp.float32)
    imag = piece[:, high].astype(jnp.float32)

    def put(where, cols, values):
        m_ref[where, cols] = jnp.concatenate(values, axis=0).astype(jnp.bfloat16)

    for m in range(0, HALF, 2):
        c = [cos_ref[m + i:m + i + 1, low] for i in range(2)]
        s = [sin_ref[m + i:m + i + 1, low] for i in range(2)]
        line = slice(m * rows, (m + 2) * rows)
        vline = slice(vrow + m * rows, vrow + (m + 2) * rows)
        put(line, low, [real * v for v in c])
        put(line, high, [imag * v for v in c])
        put(vline, low, [imag * -v for v in s])
        put(vline, high, [real * v for v in s])
    fill = jnp.zeros((vrow - (HALF + 1) * rows, 128), jnp.float32)
    for value, cols in ((real, low), (imag, high)):
        put(slice(HALF * rows, vrow), cols, [value, fill])


def v_row(rows):
    return -(-(HALF + 1) * rows // 128) * 128


def times(lhs, rhs):
    return lax.dot_general(
        lhs, rhs, (((1,), (1,)), ((), ())), preferred_element_type=jnp.float32
    )


def add_products(acc_ref, lhs_ref, piece_ref, cos_ref, sin_ref, mixed_ref):
    windows, rows, width = piece_ref.shape
    tile = 256
    used = v_row(rows) + HALF * rows
    if used < mixed_ref.shape[0]:
        mixed_ref[used:, :] = jnp.zeros_like(mixed_ref[used:, :])

    @pl.loop(0, windows)
    def _(w):
        @pl.loop(0, width // 2, step=128)
        def _(start):
            low = pl.ds(pl.multiple_of(start, 128), 128)
            high = pl.ds(pl.multiple_of(width // 2 + start, 128), 128)
            mix(mixed_ref, piece_ref.at[w], cos_ref, sin_ref, low, high)

        @pl.loop(0, mixed_ref.shape[0], step=tile)
        def _(n):
            cols = pl.ds(pl.multiple_of(n, tile), tile)
            acc_ref[:, cols] += times(lhs_ref[w], mixed_ref[cols, :])


def part_kernel(white_ref, piece_ref, cos_ref, sin_ref, _, part_ref, done_ref, mixed_ref):
    done_ref[...] = jnp.zeros_like(done_ref)
    part_ref[...] = jnp.zeros_like(part_ref)
    add_products(part_ref, white_ref, piece_ref, cos_ref, sin_ref, mixed_ref)


def part_columns(rows):
    columns = v_row(rows) + HALF * rows
    return columns + (-columns) % 256


def part_terms(white, piece, tables, done):
    windows, channels, width = white.shape
    columns = part_columns(piece.shape[1])
    return pl.pallas_call(
        part_kernel,
        in_specs=[whole()] * 5,
        out_specs=[whole()] * 2,
        out_shape=[jax.ShapeDtypeStruct((channels, columns), jnp.float32), TOKEN],
        scratch_shapes=[pltpu.VMEM((columns, width), jnp.bfloat16)],
        compiler_params=kernel_params(),
        cost_estimate=LATE,
        name="terms_part",
    )(white, piece, *tables, done)


TOKEN = jax.ShapeDtypeStruct((8, 128), jnp.float32)
LATE = pl.CostEstimate(flops=30 * 10**9, bytes_accessed=0, transcendentals=0)


def pack(acc_ref, line, rows, scale, later):
    wide = HALF * rows
    vrow = v_row(rows)
    u, v = acc_ref[line, :wide] * scale, acc_ref[line, vrow:vrow + wide] * scale
    still = acc_ref[line, wide:wide + rows] * scale
    first, last = (u - v, u + v) if later else (u + v, u - v)
    return jnp.concatenate([first, last[:, :wide - rows], still], axis=1)


def first_kernel(
    scale, part_ref, sibling_ref, piece_ref, cos_ref, sin_ref, _, back_ref, own_ref,
    done_ref, mixed_ref, acc_ref,
):
    done_ref[...] = jnp.zeros_like(done_ref)
    acc_ref[...] = part_ref[...]
    add_products(acc_ref, sibling_ref, piece_ref, cos_ref, sin_ref, mixed_ref)
    line = pl.ds(SRC, acc_ref.shape[0] - SRC)
    back = pack(acc_ref, line, piece_ref.shape[1], scale, True)
    back_ref[...] = back.astype(back_ref.dtype)
    own_ref[...] = acc_ref[:SRC, :]


def second_kernel(scale, part_ref, sibling_ref, piece_ref, cos_ref, sin_ref, *refs):
    back_ref, own_ref, even_ref, odd_ref, acc_ref = refs
    windows, rows, width = piece_ref.shape
    freqs = width // 2
    starts = [
        (slice(n, n + 128), slice(freqs + n, freqs + n + 128)) for n in range(0, freqs, 128)
    ]
    tiles = [
        slice(n, min(n + 256, acc_ref.shape[1])) for n in range(0, acc_ref.shape[1], 256)
    ]
    buffers = even_ref, odd_ref
    for start in starts:
        mix(even_ref, piece_ref.at[0], cos_ref, sin_ref, *start)
    for w in range(windows):
        now_ref, next_ref = buffers[w % 2], buffers[1 - w % 2]
        todo = starts if w + 1 < windows else []
        for cols in tiles:
            before = part_ref[:, cols] if w == 0 else acc_ref[:, cols]
            acc_ref[:, cols] = before + times(sibling_ref[w], now_ref[cols, :])
            for start in todo[:2]:
                mix(next_ref, piece_ref.at[w + 1], cos_ref, sin_ref, *start)
            todo = todo[2:]
    back_ref[...] = pack(acc_ref, pl.ds(SRC, acc_ref.shape[0] - SRC), rows, scale, True)
    own_ref[...] = acc_ref[:SRC, :]


def own_kernel(scale, rows, first_ref, second_ref, *refs):
    *out_refs, packed_ref = refs
    x, core = place_of_core()
    mine = SRC // 4

    @pl.loop(0, SRC, step=mine)
    def _(start):
        line = pl.ds(pl.multiple_of(start, 8), mine)
        for quarter, ref in enumerate((first_ref, second_ref)):
            packed_ref[quarter, line, :] = pack(ref, line, rows, scale, False)

    for i, out_ref in enumerate(out_refs):
        spot = 2 * (x, 1 - x, 1 - x, x)[i] + (core, core, 1 - core, 1 - core)[i]
        line = pl.ds(pl.multiple_of(spot * mine, 8), mine)
        for quarter in range(2):
            out_ref[quarter] = packed_ref[quarter, line, :].astype(out_ref.dtype)


def own_terms(first, second, rows, scale):
    mine, wide = SRC // 4, 2 * HALF * rows
    return pl.pallas_call(
        functools.partial(own_kernel, scale, rows),
        in_specs=[whole()] * 2,
        out_specs=[whole()] * 4,
        out_shape=[
            jax.ShapeDtypeStruct((2, mine, wide), jnp.float32 if i == 0 else jnp.bfloat16)
            for i in range(4)
        ],
        scratch_shapes=[pltpu.VMEM((2, SRC, wide), jnp.float32)],
        compiler_params=kernel_params(),
        name="own_terms",
    )(first, second)


def terms(part, sibling, piece, tables, scale, done=None):
    windows, channels, width = sibling.shape
    rows = piece.shape[1]
    second = done is None
    columns = v_row(rows) + HALF * rows if second else part_columns(rows)
    back = ((channels - SRC, 2 * HALF * rows), jnp.float32 if second else jnp.bfloat16)
    out = [jax.ShapeDtypeStruct(*back), jax.ShapeDtypeStruct((SRC, columns), jnp.float32)]
    out += [] if second else [TOKEN]
    more = () if second else (done,)
    return pl.pallas_call(
        functools.partial(second_kernel if second else first_kernel, scale),
        in_specs=[whole()] * (5 + len(more)),
        out_specs=[whole()] * len(out),
        out_shape=out,
        scratch_shapes=[pltpu.VMEM((columns, width), jnp.bfloat16)] * (2 if second else 1)
        + [pltpu.VMEM((channels, columns), jnp.float32)],
        compiler_params=kernel_params(),
        cost_estimate=LATE,
        name="terms_second" if second else "terms_first",
    )(part, sibling, piece, *tables, *more)


def copy_rows(source_ref, out_ref):
    rows = source_ref.shape[-2]
    if rows % 4:
        out_ref[...] = source_ref[...]
        return
    step = rows // 4 if rows % 64 == 0 else rows

    @pl.loop(0, rows, step=step)
    def _(start):
        line = pl.ds(pl.multiple_of(start, 16 if step % 16 == 0 else 8), step)
        out_ref[..., line, :] = source_ref[..., line, :]


def keep_kernel(*refs):
    half = len(refs) // 2
    for source_ref, out_ref in zip(refs[:half], refs[half:]):
        copy_rows(source_ref, out_ref)


def hold_kernel(source_ref, *refs):
    *_, out_ref, done_ref = refs
    copy_rows(source_ref, out_ref)
    done_ref[...] = jnp.zeros_like(done_ref)


def keep(*values):
    return pl.pallas_call(
        keep_kernel,
        in_specs=[whole()] * len(values),
        out_specs=[whole()] * len(values),
        out_shape=[jax.ShapeDtypeStruct(v.shape, v.dtype) for v in values],
        compiler_params=kernel_params(),
        name="keep",
    )(*values)


def hold(value, *done):
    return pl.pallas_call(
        hold_kernel,
        in_specs=[whole()] * (1 + len(done)),
        out_specs=[whole()] * 2,
        out_shape=[jax.ShapeDtypeStruct(value.shape, value.dtype), TOKEN],
        compiler_params=kernel_params(),
        name="hold",
    )(value, *done)


def keep_after(value, done):
    return pl.pallas_call(
        lambda source_ref, _, out_ref: copy_rows(source_ref, out_ref),
        in_specs=[whole()] * 2,
        out_specs=whole(),
        out_shape=jax.ShapeDtypeStruct(value.shape, value.dtype),
        compiler_params=kernel_params(),
        name="keep_after",
    )(value, done)


def place_kernel(
    here_ref, chip_ref, cross_ref, core_ref, back_ref, out_ref, block_ref, sems
):
    x, core = place_of_core()
    lags, mine, channels = block_ref.shape
    swap = core != 0
    sides = []
    for q in range(2):
        index = jnp.where(x == q, 1, 0)
        own = here_ref[index] + chip_ref[1 - index].astype(jnp.float32)
        other = core_ref[index].astype(jnp.float32) + cross_ref[1 - index].astype(jnp.float32)
        sides += [jnp.where(swap, other, own), jnp.where(swap, own, other)]
    back = back_ref[...].astype(jnp.float32).T
    copies = []
    for j in range(lags):
        lag = HALF - 1 - j if j < HALF else j + 1 if j < lags - 1 else HALF
        cols = slice(j * mine, (j + 1) * mine)
        block_ref[lag, :, :SRC] = jnp.concatenate([v[:, cols] for v in sides], axis=1)
        block_ref[lag, :, SRC:] = back[cols]
        copies.append(pltpu.make_async_copy(block_ref.at[lag], out_ref.at[lag], sems.at[lag]))
        copies[-1].start()
    for copy in copies:
        copy.wait()


def place(here, chip, cross, core, back):
    _, mine, wide = here.shape
    shape = (wide // mine, mine, SRC + back.shape[0])
    return pl.pallas_call(
        place_kernel,
        in_specs=[whole()] * 5,
        out_specs=anywhere(),
        out_shape=jax.ShapeDtypeStruct(shape, jnp.float32),
        scratch_shapes=[
            pltpu.VMEM(shape, jnp.float32), pltpu.SemaphoreType.DMA((shape[0],))
        ],
        compiler_params=kernel_params(),
        name="place_lags",
    )(here, chip, cross, core, back)


def pair_body(spectra, counts, partner):
    blocks = lax.axis_size("chan")
    groups = lax.axis_size("win")
    windows, channels, two, freqs = spectra.shape
    scale = 1.0 / (math.sqrt(2.0 * freqs) * math.sqrt(windows * groups))
    other_core = [(i, i ^ 1) for i in range(groups)]
    other_chip = [(i, i ^ 2) for i in range(groups)]
    other_both = [(i, i ^ 3) for i in range(groups)]

    def to_partner(t):
        return [(i, i ^ t) for i in range(blocks)]

    def to_partner_core(t):
        return [
            (i * groups + g, (i ^ t) * groups + (g ^ 1))
            for i in range(blocks)
            for g in range(groups)
        ]

    def send_sources(t, counts, raw, sources, near, far, near_more, far_more):
        def straight(value):
            return lax.ppermute(value, "chan", to_partner(t))

        def crossed(value):
            return lax.ppermute(value, ("chan", "win"), to_partner_core(t))

        near, far = straight(near), crossed(far)
        white = whiten_rest(counts, raw, taper, sources)
        sibling = lax.ppermute(white, "win", other_core)
        near_more, done = hold(near_more, near)
        near_more = straight(near_more)
        part, done = part_terms(white, near, tables, done)
        far_more, done = hold(far_more, far, done)
        far_more = crossed(far_more)
        back, own, done = terms(part, sibling, far, tables, scale, done)
        back = lax.ppermute(back, "win", other_chip)
        part, done = part_terms(white, near_more, tables, done)
        return part, *keep(sibling), keep_after(far_more, done), *keep(back), own

    def send_terms(t, back, first, second):
        here, chip, cross, core = own_terms(first, second, SRC // groups, scale)
        if t < blocks // 2:
            back = keep_after(back, core)
        back = lax.ppermute(back, "chan", to_partner(t))
        chip = lax.ppermute(chip, "win", other_chip)
        cross = lax.ppermute(cross, "win", other_both)
        core = lax.ppermute(core, "win", other_core)
        return here, *keep(chip, cross, core, back)

    def by_round(run, *values):
        branches = [functools.partial(run, t) for t in range(1, blocks)]
        return lax.switch(partner[0, 0] - 1, branches, *values)

    tables = [jnp.asarray(v) for v in shift_tables(freqs)]
    taper = taper_row(two, freqs)
    piece = jax.ShapeDtypeStruct((windows, SRC // 4, two * freqs), jnp.bfloat16)
    sources = jax.ShapeDtypeStruct((windows, SRC, two * freqs), jnp.bfloat16)
    raw = pltpu.with_memory_space_constraint(spectra, pltpu.HBM)
    sources = whiten_sources([sources] + [piece] * 4, counts, fetch_sources(raw), taper)
    part, sibling, piece, back_recv, first = by_round(send_sources, counts, raw, *sources)
    back, second = terms(part, sibling, piece, tables, scale)
    back = (back + back_recv.astype(jnp.float32)).astype(jnp.bfloat16)
    return place(*by_round(send_terms, back, first, second))[None, None]


def lag_table(freqs, lags):
    freq = jnp.arange(freqs, dtype=jnp.float32) + freqs // 4
    delay = jnp.arange(lags, dtype=jnp.float32) - lags // 2
    phase = 2.0 * math.pi * freq[:, None] * delay[None, :] / (4.0 * freqs)
    norm = 1.0 / math.sqrt(2.0 * freqs)
    return jnp.stack([jnp.cos(phase), -jnp.sin(phase)]) * norm


def blended_sources(sources, table):
    src = sources.astype(jnp.float32)
    first = src[:, :, 0][:, :, None, :]
    second = src[:, :, 1][:, :, None, :]
    cos_part = table[0].T[None, None]
    sin_part = table[1].T[None, None]
    real_mix = first * cos_part + second * sin_part
    imag_mix = second * cos_part - first * sin_part
    return jnp.stack([real_mix, imag_mix], axis=3).astype(jnp.bfloat16)


def pair_terms(sources, receiver_blocks, table):
    wins, count, two, freqs = sources.shape
    lags = table.shape[2]
    group = math.gcd(count, 32)
    flat_recv = receiver_blocks.reshape(wins, receiver_blocks.shape[1], two * freqs)
    grouped = jnp.moveaxis(sources.reshape(wins, count // group, group, two, freqs), 1, 0)

    def one_group(piece):
        mixed_spectra = blended_sources(piece, table).reshape(wins, group * lags, two * freqs)
        out = jnp.einsum(
            "wmx,wrx->mr", mixed_spectra, flat_recv, preferred_element_type=jnp.float32
        )
        return out.reshape(group, lags, receiver_blocks.shape[1])

    out = lax.map(one_group, grouped).reshape(count, lags, receiver_blocks.shape[1])
    return jnp.transpose(out, (1, 0, 2))


def route_blocks(values, round_flags, levels):
    for level in range(levels):
        moved = from_partner(values, "chan", level)
        values = jnp.where((round_flags >> level) % 2 == 1, moved, values)
    return values


def general_body(spectra, counts, partner):
    white = whiten_local(spectra, counts[0])
    table = lag_table(spectra.shape[3], LAGS)
    levels = lax.axis_size("chan").bit_length() - 1
    windows = spectra.shape[0] * lax.axis_size("win")
    receiver_blocks = route_blocks(white, partner[0, 0], levels)
    out = pair_terms(white[:, :SRC], receiver_blocks, table)
    stacked = lax.psum_scatter(out, "win", scatter_dimension=1, tiled=True)
    return (stacked / math.sqrt(windows))[None, None]


def solution(mesh):
    body = pair_body if mesh.shape["win"] == 4 else general_body
    return jax.shard_map(
        body,
        mesh=mesh,
        in_specs=(P("win", "chan", None, None), P("chan"), P()),
        out_specs=P("chan", None, None, "win", None),
        check_vma=False,
    )
```

```python
import functools
import math

import jax
import jax.numpy as jnp
import numpy as np
from jax import lax
from jax.experimental import pallas as pl
from jax.experimental.pallas import tpu as pltpu
from jax.sharding import PartitionSpec as P

LAGS = 16
SRC = 160
HALF = LAGS // 2
VMEM_LIMIT = 16 * 1024 * 1024


def from_partner(value, axis, stride):
    return lax.ppermute(value, axis, [(i, i ^ 1 << stride) for i in range(lax.axis_size(axis))])


def whiten_local(spectra, count):
    values = spectra.astype(jnp.float32)
    block_size = spectra.shape[1]
    freqs = spectra.shape[3]
    valid = (jnp.arange(block_size, dtype=jnp.int32) < count).astype(jnp.float32)
    freq = jnp.arange(freqs, dtype=jnp.float32)
    taper = 0.75 - 0.25 * jnp.cos(2.0 * math.pi * (freq + 0.5) / freqs)
    power = jnp.mean(values * values, axis=(2, 3))
    scale = valid[None, :] / jnp.sqrt(power + 1e-05)
    return (values * taper * scale[:, :, None, None]).astype(jnp.bfloat16)


def shift_tables(freqs):
    freq = np.arange(freqs, dtype=np.float64) + freqs // 4
    shift = np.arange(1, HALF + 1, dtype=np.float64)
    phase = 2.0 * np.pi * shift[:, None] * freq[None, :] / (4.0 * freqs)
    return np.cos(phase).astype(np.float32), np.sin(phase).astype(np.float32)


def place_of_core():
    spot = lax.axis_index("win")
    return spot // 2, spot % 2


def whole():
    return pl.BlockSpec(memory_space=pltpu.VMEM)


def anywhere():
    return pl.BlockSpec(memory_space=pl.ANY)


def kernel_params():
    return pltpu.CompilerParams(vmem_limit_bytes=VMEM_LIMIT)


def fetch_kernel(source_ref, out_ref, sems):
    windows, channels = out_ref.shape[:2]
    parts = sems.shape[1]
    step = channels // parts
    copies = []
    for w in range(windows):
        for i in range(parts):
            part = (w, pl.ds(i * step, step))
            copies.append(
                pltpu.make_async_copy(source_ref.at[part], out_ref.at[part], sems.at[w, i])
            )
            copies[-1].start()
    for copy in copies:
        copy.wait()


def fetch_sources(spectra):
    windows, _, *rest = spectra.shape
    return pl.pallas_call(
        fetch_kernel,
        in_specs=[pl.BlockSpec(memory_space=pltpu.HBM)],
        out_specs=whole(),
        out_shape=jax.ShapeDtypeStruct((windows, SRC, *rest), spectra.dtype),
        scratch_shapes=[pltpu.SemaphoreType.DMA((windows, 1))],
        compiler_params=kernel_params(),
        name="fetch",
    )(spectra)


def white_block(raw_ref, taper_ref, count, w, line, first_row):
    values = raw_ref[w, line, :].astype(jnp.float32)
    rows, width = values.shape
    power = jnp.sum(values * values, axis=1, keepdims=True) * (1.0 / width)
    row = first_row + lax.broadcasted_iota(jnp.int32, (rows, 1), 0)
    valid = (row < count).astype(jnp.float32)
    scale = valid / jnp.sqrt(power + 1e-05)
    return values * taper_ref[...] * scale


def whiten_kernel(count_ref, raw_ref, taper_ref, white_ref, *refs):
    *piece_refs, count, sem = refs
    copy = pltpu.make_async_copy(count_ref, count, sem)
    copy.start()
    x, core = place_of_core()
    mine = SRC // 4
    step = 2 * mine
    copy.wait()
    for w in range(raw_ref.shape[0]):
        for index, group in enumerate((1 - x, x)):
            line = pl.ds(pl.multiple_of(group * step, step), step)
            values = white_block(raw_ref, taper_ref, count[0], w, line, group * step)
            white_ref[w, line, :] = values.astype(jnp.bfloat16)
            low, high = values[:mine], values[mine:]
            first = core == 0
            near_ref, far_ref = piece_refs[2 * index:2 * index + 2]
            near_ref[w] = jnp.where(first, low, high).astype(jnp.bfloat16)
            far_ref[w] = jnp.where(first, high, low).astype(jnp.bfloat16)


def rest_kernel(
    count_ref, spectra_ref, taper_ref, sources_ref, white_ref, raw_ref, count, sems
):
    windows, channels, two, freqs = raw_ref.shape
    copies = [pltpu.make_async_copy(count_ref, count, sems.at[windows])]
    for w in range(windows):
        part = spectra_ref.at[w, pl.ds(SRC, channels)]
        copies.append(pltpu.make_async_copy(part, raw_ref.at[w], sems.at[w]))
    for copy in copies:
        copy.start()
    step = 32

    @pl.loop(0, windows)
    def _(w):
        @pl.loop(0, SRC, step=step)
        def _(start):
            line = pl.ds(pl.multiple_of(start, step), step)
            white_ref[w, line, :] = sources_ref[w, line, :]

    for copy in copies:
        copy.wait()

    @pl.loop(0, windows)
    def _(w):
        @pl.loop(0, channels, step=step)
        def _(start):
            line = pl.ds(pl.multiple_of(start, step), step)
            parts = [raw_ref[w, line, p, :].astype(jnp.float32) for p in range(two)]
            power = sum(jnp.sum(v * v, axis=1, keepdims=True) for v in parts)
            row = SRC + start + lax.broadcasted_iota(jnp.int32, (step, 1), 0)
            valid = (row < count[0]).astype(jnp.float32)
            scale = valid / jnp.sqrt(power * (1.0 / (two * freqs)) + 1e-05)
            out = pl.ds(pl.multiple_of(SRC + start, step), step)
            for p, v in enumerate(parts):
                cols = slice(p * freqs, (p + 1) * freqs)
                white_ref[w, out, cols] = (v * taper_ref[:, cols] * scale).astype(jnp.bfloat16)


def whiten_rest(counts, spectra, taper, sources):
    windows, channels, two, freqs = spectra.shape
    return pl.pallas_call(
        rest_kernel,
        in_specs=[anywhere(), pl.BlockSpec(memory_space=pltpu.HBM), whole(), whole()],
        out_specs=whole(),
        out_shape=jax.ShapeDtypeStruct((windows, channels, two * freqs), jnp.bfloat16),
        scratch_shapes=[
            pltpu.VMEM((windows, channels - SRC, two, freqs), spectra.dtype),
            pltpu.SMEM((1,), jnp.int32),
            pltpu.SemaphoreType.DMA((windows + 1,)),
        ],
        compiler_params=kernel_params(),
        name="whiten_rest",
    )(counts, spectra, taper, sources)


def whiten_sources(out_shape, counts, raw, taper):
    windows, channels, two, freqs = raw.shape
    return pl.pallas_call(
        whiten_kernel,
        in_specs=[anywhere()] + [whole()] * 2,
        out_specs=[whole()] * len(out_shape),
        out_shape=out_shape,
        scratch_shapes=[pltpu.SMEM((1,), jnp.int32), pltpu.SemaphoreType.DMA],
        compiler_params=kernel_params(),
        name="whiten",
    )(counts, raw.reshape(windows, channels, two * freqs), taper)


def taper_row(two, freqs):
    freq = np.arange(freqs, dtype=np.float64)
    taper = 0.75 - 0.25 * np.cos(2.0 * np.pi * (freq + 0.5) / freqs)
    return jnp.asarray(np.tile(taper.astype(np.float32), two)[None, :])


def mix(m_ref, piece, cos_ref, sin_ref, low, high):
    rows = piece.shape[0]
    vrow = v_row(rows)
    real = piece[:, low].astype(jnp.float32)
    imag = piece[:, high].astype(jnp.float32)

    def put(where, cols, values):
        m_ref[where, cols] = jnp.concatenate(values, axis=0).astype(jnp.bfloat16)

    for m in range(0, HALF, 2):
        c = [cos_ref[m + i:m + i + 1, low] for i in range(2)]
        s = [sin_ref[m + i:m + i + 1, low] for i in range(2)]
        line = slice(m * rows, (m + 2) * rows)
        vline = slice(vrow + m * rows, vrow + (m + 2) * rows)
        put(line, low, [real * v for v in c])
        put(line, high, [imag * v for v in c])
        put(vline, low, [imag * -v for v in s])
        put(vline, high, [real * v for v in s])
    fill = jnp.zeros((vrow - (HALF + 1) * rows, 128), jnp.float32)
    for value, cols in ((real, low), (imag, high)):
        put(slice(HALF * rows, vrow), cols, [value, fill])


def v_row(rows):
    return -(-(HALF + 1) * rows // 128) * 128


def times(lhs, rhs):
    return lax.dot_general(
        lhs, rhs, (((1,), (1,)), ((), ())), preferred_element_type=jnp.float32
    )


def add_products(acc_ref, lhs_ref, piece_ref, cos_ref, sin_ref, mixed_ref):
    windows, rows, width = piece_ref.shape
    tile = 256
    used = v_row(rows) + HALF * rows
    if used < mixed_ref.shape[0]:
        mixed_ref[used:, :] = jnp.zeros_like(mixed_ref[used:, :])

    @pl.loop(0, windows)
    def _(w):
        @pl.loop(0, width // 2, step=128)
        def _(start):
            low = pl.ds(pl.multiple_of(start, 128), 128)
            high = pl.ds(pl.multiple_of(width // 2 + start, 128), 128)
            mix(mixed_ref, piece_ref.at[w], cos_ref, sin_ref, low, high)

        @pl.loop(0, mixed_ref.shape[0], step=tile)
        def _(n):
            cols = pl.ds(pl.multiple_of(n, tile), tile)
            acc_ref[:, cols] += times(lhs_ref[w], mixed_ref[cols, :])


def part_kernel(white_ref, piece_ref, cos_ref, sin_ref, _, part_ref, done_ref, mixed_ref):
    done_ref[...] = jnp.zeros_like(done_ref)
    part_ref[...] = jnp.zeros_like(part_ref)
    add_products(part_ref, white_ref, piece_ref, cos_ref, sin_ref, mixed_ref)


def part_columns(rows):
    columns = v_row(rows) + HALF * rows
    return columns + (-columns) % 256


def part_terms(white, piece, tables, done):
    windows, channels, width = white.shape
    columns = part_columns(piece.shape[1])
    return pl.pallas_call(
        part_kernel,
        in_specs=[whole()] * 5,
        out_specs=[whole()] * 2,
        out_shape=[jax.ShapeDtypeStruct((channels, columns), jnp.float32), TOKEN],
        scratch_shapes=[pltpu.VMEM((columns, width), jnp.bfloat16)],
        compiler_params=kernel_params(),
        cost_estimate=LATE,
        name="terms_part",
    )(white, piece, *tables, done)


TOKEN = jax.ShapeDtypeStruct((8, 128), jnp.float32)
LATE = pl.CostEstimate(flops=30 * 10**9, bytes_accessed=0, transcendentals=0)


def pack(acc_ref, line, rows, scale, later):
    wide = HALF * rows
    vrow = v_row(rows)
    u, v = acc_ref[line, :wide] * scale, acc_ref[line, vrow:vrow + wide] * scale
    still = acc_ref[line, wide:wide + rows] * scale
    first, last = (u - v, u + v) if later else (u + v, u - v)
    return jnp.concatenate([first, last[:, :wide - rows], still], axis=1)


def first_kernel(
    scale, part_ref, sibling_ref, piece_ref, cos_ref, sin_ref, _, back_ref, own_ref,
    done_ref, mixed_ref, acc_ref,
):
    done_ref[...] = jnp.zeros_like(done_ref)
    acc_ref[...] = part_ref[...]
    add_products(acc_ref, sibling_ref, piece_ref, cos_ref, sin_ref, mixed_ref)
    line = pl.ds(SRC, acc_ref.shape[0] - SRC)
    back = pack(acc_ref, line, piece_ref.shape[1], scale, True)
    back_ref[...] = back.astype(back_ref.dtype)
    own_ref[...] = acc_ref[:SRC, :]


def second_kernel(scale, part_ref, sibling_ref, piece_ref, cos_ref, sin_ref, *refs):
    back_ref, own_ref, even_ref, odd_ref, acc_ref = refs
    windows, rows, width = piece_ref.shape
    freqs = width // 2
    starts = [
        (slice(n, n + 128), slice(freqs + n, freqs + n + 128)) for n in range(0, freqs, 128)
    ]
    tiles = [
        slice(n, min(n + 256, acc_ref.shape[1])) for n in range(0, acc_ref.shape[1], 256)
    ]
    buffers = even_ref, odd_ref
    for start in starts:
        mix(even_ref, piece_ref.at[0], cos_ref, sin_ref, *start)
    for w in range(windows):
        now_ref, next_ref = buffers[w % 2], buffers[1 - w % 2]
        todo = starts if w + 1 < windows else []
        for cols in tiles:
            before = part_ref[:, cols] if w == 0 else acc_ref[:, cols]
            acc_ref[:, cols] = before + times(sibling_ref[w], now_ref[cols, :])
            for start in todo[:2]:
                mix(next_ref, piece_ref.at[w + 1], cos_ref, sin_ref, *start)
            todo = todo[2:]
    back_ref[...] = pack(acc_ref, pl.ds(SRC, acc_ref.shape[0] - SRC), rows, scale, True)
    own_ref[...] = acc_ref[:SRC, :]


def own_kernel(scale, rows, first_ref, second_ref, *refs):
    *out_refs, packed_ref = refs
    x, core = place_of_core()
    mine = SRC // 4

    @pl.loop(0, SRC, step=mine)
    def _(start):
        line = pl.ds(pl.multiple_of(start, 8), mine)
        for quarter, ref in enumerate((first_ref, second_ref)):
            packed_ref[quarter, line, :] = pack(ref, line, rows, scale, False)

    for i, out_ref in enumerate(out_refs):
        spot = 2 * (x, 1 - x, 1 - x, x)[i] + (core, core, 1 - core, 1 - core)[i]
        line = pl.ds(pl.multiple_of(spot * mine, 8), mine)
        for quarter in range(2):
            out_ref[quarter] = packed_ref[quarter, line, :].astype(out_ref.dtype)


def own_terms(first, second, rows, scale):
    mine, wide = SRC // 4, 2 * HALF * rows
    return pl.pallas_call(
        functools.partial(own_kernel, scale, rows),
        in_specs=[whole()] * 2,
        out_specs=[whole()] * 4,
        out_shape=[
            jax.ShapeDtypeStruct((2, mine, wide), jnp.float32 if i == 0 else jnp.bfloat16)
            for i in range(4)
        ],
        scratch_shapes=[pltpu.VMEM((2, SRC, wide), jnp.float32)],
        compiler_params=kernel_params(),
        name="own_terms",
    )(first, second)


def terms(part, sibling, piece, tables, scale, done=None):
    windows, channels, width = sibling.shape
    rows = piece.shape[1]
    second = done is None
    columns = v_row(rows) + HALF * rows if second else part_columns(rows)
    back = ((channels - SRC, 2 * HALF * rows), jnp.float32 if second else jnp.bfloat16)
    out = [jax.ShapeDtypeStruct(*back), jax.ShapeDtypeStruct((SRC, columns), jnp.float32)]
    out += [] if second else [TOKEN]
    more = () if second else (done,)
    return pl.pallas_call(
        functools.partial(second_kernel if second else first_kernel, scale),
        in_specs=[whole()] * (5 + len(more)),
        out_specs=[whole()] * len(out),
        out_shape=out,
        scratch_shapes=[pltpu.VMEM((columns, width), jnp.bfloat16)] * (2 if second else 1)
        + [pltpu.VMEM((channels, columns), jnp.float32)],
        compiler_params=kernel_params(),
        cost_estimate=LATE,
        name="terms_second" if second else "terms_first",
    )(part, sibling, piece, *tables, *more)


def copy_rows(source_ref, out_ref):
    rows = source_ref.shape[-2]
    if rows % 4:
        out_ref[...] = source_ref[...]
        return
    step = rows // 4 if rows % 64 == 0 else rows

    @pl.loop(0, rows, step=step)
    def _(start):
        line = pl.ds(pl.multiple_of(start, 16 if step % 16 == 0 else 8), step)
        out_ref[..., line, :] = source_ref[..., line, :]


def keep_kernel(*refs):
    half = len(refs) // 2
    for source_ref, out_ref in zip(refs[:half], refs[half:]):
        copy_rows(source_ref, out_ref)


def hold_kernel(source_ref, *refs):
    *_, out_ref, done_ref = refs
    copy_rows(source_ref, out_ref)
    done_ref[...] = jnp.zeros_like(done_ref)


def keep(*values):
    return pl.pallas_call(
        keep_kernel,
        in_specs=[whole()] * len(values),
        out_specs=[whole()] * len(values),
        out_shape=[jax.ShapeDtypeStruct(v.shape, v.dtype) for v in values],
        compiler_params=kernel_params(),
        name="keep",
    )(*values)


def hold(value, *done):
    return pl.pallas_call(
        hold_kernel,
        in_specs=[whole()] * (1 + len(done)),
        out_specs=[whole()] * 2,
        out_shape=[jax.ShapeDtypeStruct(value.shape, value.dtype), TOKEN],
        compiler_params=kernel_params(),
        name="hold",
    )(value, *done)


def keep_after(value, done):
    return pl.pallas_call(
        lambda source_ref, _, out_ref: copy_rows(source_ref, out_ref),
        in_specs=[whole()] * 2,
        out_specs=whole(),
        out_shape=jax.ShapeDtypeStruct(value.shape, value.dtype),
        compiler_params=kernel_params(),
        name="keep_after",
    )(value, done)


def place_kernel(
    here_ref, chip_ref, cross_ref, core_ref, back_ref, out_ref, block_ref, sems
):
    x, core = place_of_core()
    lags, mine, channels = block_ref.shape
    swap = core != 0
    sides = []
    for q in range(2):
        index = jnp.where(x == q, 1, 0)
        own = here_ref[index] + chip_ref[1 - index].astype(jnp.float32)
        other = core_ref[index].astype(jnp.float32) + cross_ref[1 - index].astype(jnp.float32)
        sides += [jnp.where(swap, other, own), jnp.where(swap, own, other)]
    back = back_ref[...].astype(jnp.float32).T
    copies = []
    for j in range(lags):
        lag = HALF - 1 - j if j < HALF else j + 1 if j < lags - 1 else HALF
        cols = slice(j * mine, (j + 1) * mine)
        block_ref[lag, :, :SRC] = jnp.concatenate([v[:, cols] for v in sides], axis=1)
        block_ref[lag, :, SRC:] = back[cols]
        copies.append(pltpu.make_async_copy(block_ref.at[lag], out_ref.at[lag], sems.at[lag]))
        copies[-1].start()
    for copy in copies:
        copy.wait()


def place(here, chip, cross, core, back):
    _, mine, wide = here.shape
    shape = (wide // mine, mine, SRC + back.shape[0])
    return pl.pallas_call(
        place_kernel,
        in_specs=[whole()] * 5,
        out_specs=anywhere(),
        out_shape=jax.ShapeDtypeStruct(shape, jnp.float32),
        scratch_shapes=[
            pltpu.VMEM(shape, jnp.float32), pltpu.SemaphoreType.DMA((shape[0],))
        ],
        compiler_params=kernel_params(),
        name="place_lags",
    )(here, chip, cross, core, back)


def pair_body(spectra, counts, partner):
    blocks = lax.axis_size("chan")
    groups = lax.axis_size("win")
    windows, channels, two, freqs = spectra.shape
    scale = 1.0 / (math.sqrt(2.0 * freqs) * math.sqrt(windows * groups))
    other_core = [(i, i ^ 1) for i in range(groups)]
    other_chip = [(i, i ^ 2) for i in range(groups)]
    other_both = [(i, i ^ 3) for i in range(groups)]

    def to_partner(t):
        return [(i, i ^ t) for i in range(blocks)]

    def to_partner_core(t):
        return [
            (i * groups + g, (i ^ t) * groups + (g ^ 1))
            for i in range(blocks)
            for g in range(groups)
        ]

    def send_sources(t, counts, raw, sources, near, far, near_more, far_more):
        def straight(value):
            return lax.ppermute(value, "chan", to_partner(t))

        def crossed(value):
            return lax.ppermute(value, ("chan", "win"), to_partner_core(t))

        near, far = straight(near), crossed(far)
        white = whiten_rest(counts, raw, taper, sources)
        sibling = lax.ppermute(white, "win", other_core)
        near_more, done = hold(near_more, near)
        near_more = straight(near_more)
        part, done = part_terms(white, near, tables, done)
        far_more, done = hold(far_more, far, done)
        far_more = crossed(far_more)
        back, own, done = terms(part, sibling, far, tables, scale, done)
        back = lax.ppermute(back, "win", other_chip)
        part, done = part_terms(white, near_more, tables, done)
        return part, *keep(sibling), keep_after(far_more, done), *keep(back), own

    def send_terms(t, back, first, second):
        back = lax.ppermute(back, "chan", to_partner(t))
        here, chip, cross, core = own_terms(first, second, SRC // groups, scale)
        chip = lax.ppermute(chip, "win", other_chip)
        cross = lax.ppermute(cross, "win", other_both)
        core = lax.ppermute(core, "win", other_core)
        return here, *keep(chip, cross, core, back)

    def by_round(run, *values):
        branches = [functools.partial(run, t) for t in range(1, blocks)]
        return lax.switch(partner[0, 0] - 1, branches, *values)

    tables = [jnp.asarray(v) for v in shift_tables(freqs)]
    taper = taper_row(two, freqs)
    piece = jax.ShapeDtypeStruct((windows, SRC // 4, two * freqs), jnp.bfloat16)
    sources = jax.ShapeDtypeStruct((windows, SRC, two * freqs), jnp.bfloat16)
    raw = pltpu.with_memory_space_constraint(spectra, pltpu.HBM)
    sources = whiten_sources([sources] + [piece] * 4, counts, fetch_sources(raw), taper)
    part, sibling, piece, back_recv, first = by_round(send_sources, counts, raw, *sources)
    back, second = terms(part, sibling, piece, tables, scale)
    back = (back + back_recv.astype(jnp.float32)).astype(jnp.bfloat16)
    return place(*by_round(send_terms, back, first, second))[None, None]


def lag_table(freqs, lags):
    freq = jnp.arange(freqs, dtype=jnp.float32) + freqs // 4
    delay = jnp.arange(lags, dtype=jnp.float32) - lags // 2
    phase = 2.0 * math.pi * freq[:, None] * delay[None, :] / (4.0 * freqs)
    norm = 1.0 / math.sqrt(2.0 * freqs)
    return jnp.stack([jnp.cos(phase), -jnp.sin(phase)]) * norm


def blended_sources(sources, table):
    src = sources.astype(jnp.float32)
    first = src[:, :, 0][:, :, None, :]
    second = src[:, :, 1][:, :, None, :]
    cos_part = table[0].T[None, None]
    sin_part = table[1].T[None, None]
    real_mix = first * cos_part + second * sin_part
    imag_mix = second * cos_part - first * sin_part
    return jnp.stack([real_mix, imag_mix], axis=3).astype(jnp.bfloat16)


def pair_terms(sources, receiver_blocks, table):
    wins, count, two, freqs = sources.shape
    lags = table.shape[2]
    group = math.gcd(count, 32)
    flat_recv = receiver_blocks.reshape(wins, receiver_blocks.shape[1], two * freqs)
    grouped = jnp.moveaxis(sources.reshape(wins, count // group, group, two, freqs), 1, 0)

    def one_group(piece):
        mixed_spectra = blended_sources(piece, table).reshape(wins, group * lags, two * freqs)
        out = jnp.einsum(
            "wmx,wrx->mr", mixed_spectra, flat_recv, preferred_element_type=jnp.float32
        )
        return out.reshape(group, lags, receiver_blocks.shape[1])

    out = lax.map(one_group, grouped).reshape(count, lags, receiver_blocks.shape[1])
    return jnp.transpose(out, (1, 0, 2))


def route_blocks(values, round_flags, levels):
    for level in range(levels):
        moved = from_partner(values, "chan", level)
        values = jnp.where((round_flags >> level) % 2 == 1, moved, values)
    return values


def general_body(spectra, counts, partner):
    white = whiten_local(spectra, counts[0])
    table = lag_table(spectra.shape[3], LAGS)
    levels = lax.axis_size("chan").bit_length() - 1
    windows = spectra.shape[0] * lax.axis_size("win")
    receiver_blocks = route_blocks(white, partner[0, 0], levels)
    out = pair_terms(white[:, :SRC], receiver_blocks, table)
    stacked = lax.psum_scatter(out, "win", scatter_dimension=1, tiled=True)
    return (stacked / math.sqrt(windows))[None, None]


def solution(mesh):
    body = pair_body if mesh.shape["win"] == 4 else general_body
    return jax.shard_map(
        body,
        mesh=mesh,
        in_specs=(P("win", "chan", None, None), P("chan"), P()),
        out_specs=P("chan", None, None, "win", None),
        check_vma=False,
    )
```
